32 devices in a mesh: rep: 2 (over y), shard: 4 (over x, core), ctx: 4 (over z).
Axes of the slice: x: 2, y: 2, z: 4, core: 2. Of those that a mesh axis runs over, the one named last changes fastest.
Arguments:
- tokens: bfloat16 [8, 768, 1024], P(('rep', 'shard'), 'ctx'), may hold values from -6 to 6
- lengths: int32 [8, 8], P(('rep', 'shard')), may hold values from 1 to 623, as said below
- norm_one: bfloat16 [2, 1024], P(None, ('shard', 'ctx')), may hold values from 0.5 to 1.5
- w_query: bfloat16 [2, 1024, 2048], P(None, ('shard', 'ctx')), may hold values from -0.1875 to 0.1875
- w_key: bfloat16 [2, 1024, 1024], P(None, ('shard', 'ctx')), may hold values from -0.1875 to 0.1875
- w_value: bfloat16 [2, 1024, 1024], P(None, ('shard', 'ctx')), may hold values from -0.1875 to 0.1875
- query_gain: bfloat16 [2, 128], P(None, ('shard', 'ctx')), may hold values from 0.5 to 1.5
- key_gain: bfloat16 [2, 128], P(None, ('shard', 'ctx')), may hold values from 0.5 to 1.5
- w_output: bfloat16 [2, 2048, 1024], P(None, ('shard', 'ctx')), may hold values from -0.75 to 0.75
- norm_two: bfloat16 [2, 1024], P(None, ('shard', 'ctx')), may hold values from 0.5 to 1.5
- w_gate: bfloat16 [2, 1024, 3072], P(None, ('shard', 'ctx')), may hold values from -0.1875 to 0.1875
- w_up: bfloat16 [2, 1024, 3072], P(None, ('shard', 'ctx')), may hold values from -0.1875 to 0.1875
- w_down: bfloat16 [2, 3072, 1024], P(None, ('shard', 'ctx')), may hold values from -0.109375 to 0.109375
- cotangent: bfloat16 [8, 768, 1024], P(('rep', 'shard'), 'ctx'), may hold values from -6 to 6
Outputs:
- output: bfloat16 [8, 768, 1024], P(('rep', 'shard'), 'ctx')
- grad_tokens: bfloat16 [8, 768, 1024], P(('rep', 'shard'), 'ctx')
- grad_norm_one: float32 [2, 1024], P(None, ('shard', 'ctx'))
- grad_w_query: float32 [2, 1024, 2048], P(None, ('shard', 'ctx'))
- grad_w_key: float32 [2, 1024, 1024], P(None, ('shard', 'ctx'))
- grad_w_value: float32 [2, 1024, 1024], P(None, ('shard', 'ctx'))
- grad_query_gain: float32 [2, 128], P(None, ('shard', 'ctx'))
- grad_key_gain: float32 [2, 128], P(None, ('shard', 'ctx'))
- grad_w_output: float32 [2, 2048, 1024], P(None, ('shard', 'ctx'))
- grad_norm_two: float32 [2, 1024], P(None, ('shard', 'ctx'))
- grad_w_gate: float32 [2, 1024, 3072], P(None, ('shard', 'ctx'))
- grad_w_up: float32 [2, 1024, 3072], P(None, ('shard', 'ctx'))
- grad_w_down: float32 [2, 3072, 1024], P(None, ('shard', 'ctx'))
The draws below stay inside these ranges and needn't reach their ends.
Inputs may be any that keep to these rules, and one draw needn't show every extreme that they name: `lengths`: each sequence holds 8 documents one after another from its first token, then padding of one token or more. The second document starts before token 48 and ends within the last 192 tokens.
All inputs are finite; a program needn't handle non-finite values.
Results may differ from the reference program's by a relative error of at most 0.033.
Values may be sent and summed in bfloat16 or wider, within the bound.
A program may use at most 320 MiB of HBM per device.

```python
import math
import jax
import jax.numpy as jnp
from jax import lax

D = 1024
QUERY_HEADS = 16
KEYVALUE_HEADS = 8
HEAD_SIZE = 128
FF = 3072
LAYERS = 2
NDOC = 8
TOK_DEV = 192
QD = 2048
KEY_FEATURES = 1024
SEQ_LEN = 768
SEQS = 8


def draw_lengths(key, part):
    key = jax.random.fold_in(key, 11)
    key_head, key_long, key_left, key_right, key_pick = jax.random.split(key, 5)
    rows = jnp.arange(SEQS, dtype=jnp.int32)[:, None]
    picks = jax.random.randint(key_pick, (3,), 0, SEQS)
    head_len = jax.random.randint(key_head, (SEQS, 1), 1, TOK_DEV // 4)
    head_len = jnp.where(rows == picks[0], 1, head_len)
    long_len = SEQ_LEN - TOK_DEV + jax.random.randint(key_long, (SEQS, 1), 0, TOK_DEV // 4)
    long_len = jnp.where(rows == picks[1], SEQ_LEN - TOK_DEV + TOK_DEV // 4 - 1, long_len)
    remain = SEQ_LEN - head_len - long_len
    ceiling = remain // (2 * (NDOC - 2))
    left_draw = jax.random.randint(key_left, (SEQS, NDOC - 2), 0, ceiling + 1)
    columns = jnp.arange(NDOC - 2, dtype=jnp.int32)[None, :]
    left_draw = jnp.where((rows == picks[2]) & (columns == 0), 0, left_draw)
    right_draw = jax.random.randint(key_right, (SEQS, NDOC - 2), 0, ceiling + 1)
    tail_len = 1 + left_draw * right_draw // jnp.maximum(ceiling, 1)
    return jnp.concatenate([head_len, long_len, tail_len], axis=1).astype(jnp.int32)


def level_of(stream_key, extent, cuts, least, top_value):
    gain, own = 1.0, jax.random.fold_in(stream_key, 6)
    for dim, shards_of in cuts:
        heights = jnp.exp(jax.random.uniform(jax.random.fold_in(own, dim), (shards_of,), jnp.float32, least / len(cuts), top_value / len(cuts)))
        gain = gain * jnp.repeat(heights, extent[dim] // shards_of).reshape([-1 if axis == dim else 1 for axis in range(len(extent))])
    return gain


def normal_values(stream_key, shape, width, limit, cuts=(), kind=jnp.bfloat16):
    array = jax.random.normal(stream_key, shape, jnp.float32) * width
    if len(cuts) > 0:
        array = level_of(stream_key, shape, cuts, -0.22, 0.18) * array
    return jnp.clip(array, min=-limit, max=limit).astype(kind)


def setup_inputs(seed: int = 0) -> dict:
    splits = jax.random.split(jax.random.key(seed), 15)
    tokens = normal_values(splits[0], (SEQS, SEQ_LEN, D), 1.0, 6.0, ((0, 8), (1, 4)))
    lengths = draw_lengths(jax.random.fold_in(splits[14], 71), 0)
    norm_one = jnp.clip(1.0 + 0.1 * jax.random.normal(splits[2], (LAYERS, D), jnp.float32), 0.5, 1.5).astype(jnp.bfloat16)
    w_query = normal_values(splits[3], (LAYERS, D, QD), D ** -0.5, 0.1875, ((1, 16),))
    w_key = normal_values(splits[4], (LAYERS, D, KEY_FEATURES), D ** -0.5, 0.1875, ((1, 16),))
    w_value = normal_values(splits[5], (LAYERS, D, KEY_FEATURES), D ** -0.5, 0.1875, ((1, 16),))
    query_gain = jnp.clip(1.0 + 0.1 * jax.random.normal(splits[6], (LAYERS, HEAD_SIZE), jnp.float32), 0.5, 1.5).astype(jnp.bfloat16)
    key_gain = jnp.clip(1.0 + 0.1 * jax.random.normal(splits[7], (LAYERS, HEAD_SIZE), jnp.float32), 0.5, 1.5).astype(jnp.bfloat16)
    w_output = normal_values(splits[8], (LAYERS, QD, D), (QD // 32) ** -0.5, 0.75, ((1, 16),))
    norm_two = jnp.clip(1.0 + 0.1 * jax.random.normal(splits[9], (LAYERS, D), jnp.float32), 0.5, 1.5).astype(jnp.bfloat16)
    w_gate = normal_values(splits[10], (LAYERS, D, FF), D ** -0.5, 0.1875, ((1, 16),))
    w_up = normal_values(splits[11], (LAYERS, D, FF), D ** -0.5, 0.1875, ((1, 16),))
    w_down = normal_values(splits[12], (LAYERS, FF, D), FF ** -0.5, 0.109375, ((1, 16),))
    cotangent = normal_values(splits[13], (SEQS, SEQ_LEN, D), 1.0, 6.0, ((0, 8), (1, 4)))
    return dict(tokens=tokens, lengths=lengths, norm_one=norm_one, w_query=w_query, w_key=w_key, w_value=w_value, query_gain=query_gain, key_gain=key_gain, w_output=w_output, norm_two=norm_two, w_gate=w_gate, w_up=w_up, w_down=w_down, cotangent=cotangent)


NORM_EPS = 1e-06
ROPE_BASE = 1000000.0
VERY_NEGATIVE = -1e+30

@jax.custom_vjp
def reduced_precision(v):
    return lax.optimization_barrier(v.astype(jnp.bfloat16)).astype(jnp.float32)

@jax.custom_vjp
def reduced_precision_reverse(v):
    return v

def low_keep(v):
    return (reduced_precision(v), None)

def low_pass(kept, grad):
    return (grad,)

def back_keep(v):
    return (v, None)

def back_low(kept, grad):
    return (reduced_precision(grad),)
reduced_precision.defvjp(low_keep, low_pass)
reduced_precision_reverse.defvjp(back_keep, back_low)

def doc_layout(doc_ends, token_index):
    token_segment = lax.optimization_barrier(jnp.sum((token_index[:, None] >= doc_ends[None, :]).astype(jnp.int32), axis=1)).astype(jnp.int32)
    starts = jnp.concatenate([jnp.zeros((1,), jnp.int32), doc_ends.astype(jnp.int32)]).astype(jnp.int32)
    labels = jnp.arange(starts.shape[0], dtype=jnp.int32)
    doc_begin = lax.optimization_barrier(jnp.sum(jnp.where(token_segment[:, None] == labels[None, :], starts[None, :], 0), axis=1)).astype(jnp.int32)
    return (token_segment, (token_index - doc_begin).astype(jnp.int32))

def rotary(positions, head_width):
    middle = head_width // 2
    inv_rates = jnp.exp(jnp.arange(middle, dtype=jnp.float32) * jnp.float32(-2.0 * math.log(ROPE_BASE) / head_width))
    angles = positions.astype(jnp.float32)[:, None] * inv_rates[None, :]
    cosine = jnp.cos(angles)
    sine = jnp.sin(angles)
    return (jnp.concatenate([cosine, cosine], axis=1), jnp.concatenate([sine, sine], axis=1))

def rms_scale(values, gain_vec):
    return values * lax.rsqrt(lax.optimization_barrier(jnp.mean(values * values, axis=-1, keepdims=True)) + NORM_EPS) * gain_vec

def rotate(values, cosine, sine):
    middle = values.shape[-1] // 2
    turned = jnp.concatenate([-values[..., middle:], values[..., :middle]], axis=-1)
    return values * cosine[:, None, :] + turned * sine[:, None, :]

def matrix_product(left, right):
    return jnp.dot(left, right, preferred_element_type=jnp.float32, precision=lax.Precision.HIGHEST)

def attend_tokens(query_rows, key_rows_all, values, token_segment, token_index):
    sequence_rows = query_rows.shape[0]
    block_rows = math.gcd(sequence_rows, 512)
    block_count = sequence_rows // block_rows
    score_scale = 1.0 / math.sqrt(HEAD_SIZE)

    def one_block(pieces):
        query_block, segment_block, index_block = pieces
        scores = reduced_precision_reverse(score_scale * jnp.einsum('thgd,nhd->thgn', query_block, key_rows_all, precision=lax.Precision.HIGHEST))
        allowed = ((segment_block[:, None] == token_segment[None, :]) & (index_block[:, None] >= token_index[None, :]))[:, None, None, :]
        masked = jnp.where(allowed, scores, VERY_NEGATIVE)
        row_max = lax.optimization_barrier(jnp.max(masked, axis=-1, keepdims=True))
        unnormed = jnp.where(allowed, jnp.exp(masked - row_max), 0.0)
        probability = reduced_precision(unnormed / lax.optimization_barrier(jnp.sum(unnormed, axis=-1, keepdims=True)))
        return jnp.einsum('thgn,nhd->thgd', probability, values, precision=lax.Precision.HIGHEST)
    blocks = lax.map(jax.checkpoint(one_block), (query_rows.reshape((block_count, block_rows) + query_rows.shape[1:]), token_segment.reshape(block_count, block_rows), token_index.reshape(block_count, block_rows)))
    return blocks.reshape(query_rows.shape)

def layer_forward(hidden, weights, which_layer, tables):
    cosine, sine, token_segment, token_index = tables
    gain_first, query_weight, key_matrix, value_matrix, gain_query, gain_key, output_weight, gain_second, gate_weight, up_weight, down_weight = [member[which_layer] for member in weights]
    sequence_rows = hidden.shape[0]
    normalized_rows = reduced_precision(rms_scale(hidden, gain_first))
    query_proj = reduced_precision_reverse(matrix_product(normalized_rows, query_weight)).reshape(sequence_rows, QUERY_HEADS, HEAD_SIZE)
    key_projection = reduced_precision_reverse(matrix_product(normalized_rows, key_matrix)).reshape(sequence_rows, KEYVALUE_HEADS, HEAD_SIZE)
    rows_of_values = reduced_precision_reverse(reduced_precision(matrix_product(normalized_rows, value_matrix))).reshape(sequence_rows, KEYVALUE_HEADS, HEAD_SIZE)
    query_rows = reduced_precision(rotate(rms_scale(query_proj, gain_query), cosine, sine))
    key_rows_all = reduced_precision(rotate(rms_scale(key_projection, gain_key), cosine, sine))
    attended_rows = attend_tokens(query_rows.reshape(sequence_rows, KEYVALUE_HEADS, QUERY_HEADS // KEYVALUE_HEADS, HEAD_SIZE), key_rows_all, rows_of_values, token_segment, token_index)
    attended_rows = reduced_precision_reverse(reduced_precision(attended_rows.reshape(sequence_rows, QUERY_HEADS * HEAD_SIZE)))
    hidden = hidden + reduced_precision_reverse(matrix_product(attended_rows, output_weight))
    normed_two = reduced_precision(rms_scale(hidden, gain_second))
    gate_pre = reduced_precision_reverse(matrix_product(normed_two, gate_weight))
    upward = reduced_precision_reverse(matrix_product(normed_two, up_weight))
    activated = reduced_precision(jax.nn.silu(gate_pre) * upward)
    return hidden + reduced_precision_reverse(matrix_product(activated, down_weight))

def reference(tokens, lengths, norm_one, w_query, w_key, w_value, query_gain, key_gain, w_output, norm_two, w_gate, w_up, w_down, cotangent):
    params = tuple((member.astype(jnp.float32) for member in (norm_one, w_query, w_key, w_value, query_gain, key_gain, w_output, norm_two, w_gate, w_up, w_down)))
    token_index = jnp.arange(tokens.shape[1], dtype=jnp.int32)

    def one_sequence(totals, pieces):
        inputs, doc_lengths, upstream = pieces
        doc_ends = jnp.cumsum(doc_lengths).astype(jnp.int32)
        token_segment, positions = doc_layout(doc_ends, token_index)
        cosine, sine = rotary(positions, HEAD_SIZE)
        tables = (cosine, sine, token_segment, token_index)

        def forward(start_rows, weights):
            hidden = start_rows
            for which_layer in range(LAYERS):
                hidden = layer_forward(hidden, weights, which_layer, tables)
            return hidden
        output, pullback = jax.vjp(forward, inputs.astype(jnp.float32), params)
        live_mask = (token_segment < doc_lengths.shape[0]).astype(jnp.float32)[:, None]
        grad_input, grad_weights = pullback(upstream.astype(jnp.float32) * live_mask)
        totals = tuple((running + update for running, update in zip(totals, grad_weights)))
        return (totals, (output.astype(jnp.bfloat16), grad_input.astype(jnp.bfloat16)))
    start_totals = tuple((jnp.zeros(member.shape, jnp.float32) for member in params))
    totals, stacked = lax.scan(one_sequence, start_totals, (tokens, lengths, cotangent))
    return (stacked[0], stacked[1], totals[0], totals[1], totals[2], totals[3], totals[4], totals[5], totals[6], totals[7], totals[8], totals[9], totals[10])
```

```python
import functools
import math

import jax
import jax.numpy as jnp
from jax import lax
from jax.experimental import pallas as pl
from jax.experimental.pallas import tpu as pltpu
from jax.sharding import PartitionSpec as P

QUERY_HEADS = 16
KEYVALUE_HEADS = 8
HEAD_SIZE = 128
LAYERS = 2
QD = 2048
KEY_FEATURES = 1024


NORM_EPS = 1e-06
ROPE_BASE = 1000000.0
VERY_NEGATIVE = -1e30

MESH = pl.DeviceIdType.MESH


def gather_kernel(shapes, nx, nz, *refs):
    count = len(shapes)
    shards, wholes = refs[:count], refs[count : 2 * count]
    own_sem, z_sem, x_sem, y_sem, core_sem, out_sem = refs[2 * count :]
    y = lax.axis_index("rep")
    shard = lax.axis_index("shard")
    z = lax.axis_index("ctx")
    core, x = lax.rem(shard, 2), lax.div(shard, 2)
    to_core = (y, x * 2 + 1 - core, z)
    to_y = (1 - y, shard, z)

    def to_x(step):
        return (y, shard + 2 * step, z)

    def to_z(step):
        return (y, shard, z + step)

    def rows_of(k, xs, zs, start, size, of_core=core):
        rows = shapes[k][0]
        first = ((xs * 2 + of_core) * nz + zs) * rows + start
        return wholes[k].at[pl.ds(pl.multiple_of(first, 16), size)]

    def inplane(k):
        rows, _, near = shapes[k]
        return y * (rows - near), near

    def send(src, dst, send_sem, recv_sem, device):
        pltpu.make_async_remote_copy(
            src_ref=src,
            dst_ref=dst,
            send_sem=send_sem,
            recv_sem=recv_sem,
            device_id=device,
            device_id_type=MESH,
        ).start()

    def arrived(ref, sem):
        pltpu.make_async_copy(ref, ref, sem).wait()

    def pass_z(k, src, zs, step, kind):
        start, size = inplane(k)
        send(src, rows_of(k, x, zs, start, size), out_sem.at[k, kind], z_sem.at[k, zs], to_z(step))

    def pass_x(k, src, xs, zs, step, kind):
        start, size = inplane(k)
        send(src, rows_of(k, xs, zs, start, size), out_sem.at[k, kind], x_sem.at[k, xs * nz + zs], to_x(step))

    def pass_y(k, xs, zs):
        rows, _, near = shapes[k]
        if rows > near:
            part = rows_of(k, xs, zs, y * near, rows - near)
            send(part, part, out_sem.at[k, 4], y_sem.at[k, xs * nz + zs], to_y)

    def pass_core(k, xs, zs, start, size):
        part = rows_of(k, xs, zs, start, size)
        send(part, part, out_sem.at[k, 5], core_sem.at[k], to_core)

    def stage_own(k):
        rows, _, near = shapes[k]
        start, size = inplane(k)
        part = shards[k].at[pl.ds(pl.multiple_of(start, 16), size)]

        @pl.when(z < nz - 1)
        def _():
            pass_z(k, part, z, 1, 0)

        @pl.when(z > 0)
        def _():
            pass_z(k, part, z, -1, 1)

        @pl.when(x < nx - 1)
        def _():
            pass_x(k, part, x, z, 1, 2)

        @pl.when(x > 0)
        def _():
            pass_x(k, part, x, z, -1, 3)

        send(shards[k], rows_of(k, x, z, 0, rows), out_sem.at[k, 5], core_sem.at[k], to_core)
        pltpu.make_async_copy(shards[k], rows_of(k, x, z, 0, rows), own_sem.at[k]).start()

    def stage_z(k, d):
        start, size = inplane(k)
        for step, kind in ((1, 0), (-1, 1)):
            zs = z - step * d

            @pl.when((zs >= 0) & (zs < nz))
            def _():
                part = rows_of(k, x, zs, start, size)
                arrived(part, z_sem.at[k, zs])

                @pl.when((z + step >= 0) & (z + step < nz))
                def _():
                    pass_z(k, part, zs, step, kind)

                @pl.when(x < nx - 1)
                def _():
                    pass_x(k, part, x, zs, 1, 2)

                @pl.when(x > 0)
                def _():
                    pass_x(k, part, x, zs, -1, 3)

                pass_y(k, x, zs)
                pass_core(k, x, zs, start, size)

    def stage_x(k, d):
        start, size = inplane(k)
        for step, kind in ((1, 2), (-1, 3)):
            xs = x - step * d

            @pl.when((xs >= 0) & (xs < nx))
            def _():
                def body(zs, carry):
                    part = rows_of(k, xs, zs, start, size)
                    arrived(part, x_sem.at[k, xs * nz + zs])
                    if nx > 2:

                        @pl.when((x + step >= 0) & (x + step < nx))
                        def _():
                            pass_x(k, part, xs, zs, step, kind)

                    pass_y(k, xs, zs)
                    pass_core(k, xs, zs, start, size)
                    return carry

                lax.fori_loop(0, nz, body, 0)

    def stage_y(k):
        rows, _, near = shapes[k]
        if rows > near:

            def body(i, carry):
                xs, zs = lax.div(i, nz), lax.rem(i, nz)

                @pl.when((xs != x) | (zs != z))
                def _():
                    start = (1 - y) * near
                    arrived(rows_of(k, xs, zs, start, rows - near), y_sem.at[k, i])
                    pass_core(k, xs, zs, start, rows - near)

                return carry

            lax.fori_loop(0, nx * nz, body, 0)

    def first_rows(k, size):
        return wholes[k].at[pl.ds(0, size)]

    def stage_end(k):
        rows, _, near = shapes[k]
        arrived(first_rows(k, nx * nz * rows), core_sem.at[k])
        arrived(first_rows(k, rows), own_sem.at[k])
        for zz in range(nz):

            @pl.when(z == zz)
            def _():
                if zz < nz - 1:
                    arrived(first_rows(k, (zz + 1) * near), out_sem.at[k, 0])
                if zz > 0:
                    arrived(first_rows(k, (nz - zz) * near), out_sem.at[k, 1])

        for xx in range(nx):

            @pl.when(x == xx)
            def _():
                if xx < nx - 1:
                    arrived(first_rows(k, (xx + 1) * nz * near), out_sem.at[k, 2])
                if xx > 0:
                    arrived(first_rows(k, (nx - xx) * nz * near), out_sem.at[k, 3])

        if rows > near:
            arrived(first_rows(k, (nx * nz - 1) * (rows - near)), out_sem.at[k, 4])
            arrived(
                first_rows(k, nx * nz * rows), out_sem.at[k, 5]
            )
        else:
            arrived(first_rows(k, nx * nz * rows), out_sem.at[k, 5])

    barrier = pltpu.get_barrier_semaphore()
    pl.semaphore_signal(barrier, inc=1, device_id=to_core, device_id_type=MESH)
    pl.semaphore_signal(barrier, inc=1, device_id=to_y, device_id_type=MESH)
    for here, there in ((z > 0, to_z(-1)), (z < nz - 1, to_z(1)), (x > 0, to_x(-1)), (x < nx - 1, to_x(1))):

        @pl.when(here)
        def _():
            pl.semaphore_signal(barrier, inc=1, device_id=there, device_id_type=MESH)

    greeted = 2 + (z > 0).astype(jnp.int32) + (z < nz - 1).astype(jnp.int32)
    greeted = greeted + (x > 0).astype(jnp.int32) + (x < nx - 1).astype(jnp.int32)
    pl.semaphore_wait(barrier, greeted)

    stages = [stage_own]
    stages += [functools.partial(stage_z, d=d) for d in range(1, nz)]
    stages += [functools.partial(stage_x, d=d) for d in range(1, nx)]
    stages += [stage_y]
    for tick in range(count + len(stages) - 1):
        for depth, stage in enumerate(stages):
            k = tick - depth
            if 0 <= k < count:
                stage(k)
    for k in range(count):
        stage_end(k)


def gather_weights(shards, nears, nx, nz, collective_id):
    count = len(shards)
    shapes = tuple((a.shape[0], a.shape[1], near) for a, near in zip(shards, nears))
    return pl.pallas_call(
        functools.partial(gather_kernel, shapes, nx, nz),
        out_shape=[
            jax.ShapeDtypeStruct((a.shape[0] * 2 * nx * nz, a.shape[1]), a.dtype) for a in shards
        ],
        in_specs=[pl.BlockSpec(memory_space=pl.ANY)] * count,
        out_specs=[pl.BlockSpec(memory_space=pl.ANY)] * count,
        scratch_shapes=[
            pltpu.SemaphoreType.DMA((count,)),
            pltpu.SemaphoreType.DMA((count, nz)),
            pltpu.SemaphoreType.DMA((count, nx * nz)),
            pltpu.SemaphoreType.DMA((count, nx * nz)),
            pltpu.SemaphoreType.DMA((count,)),
            pltpu.SemaphoreType.DMA((count, 6)),
        ],
        compiler_params=pltpu.CompilerParams(collective_id=collective_id, has_side_effects=True),
    )(*shards)


def segment_of(doc_ends, token_index):
    return jnp.sum((token_index[:, None] >= doc_ends[None, :]).astype(jnp.int32), axis=1)


def doc_layout(doc_ends, token_index):
    token_segment = segment_of(doc_ends, token_index)
    starts = jnp.concatenate([jnp.zeros((1,), jnp.int32), doc_ends])
    labels = jnp.arange(starts.shape[0], dtype=jnp.int32)
    doc_begin = jnp.sum(
        jnp.where(token_segment[:, None] == labels[None, :], starts[None, :], 0), axis=1
    )
    return (token_segment, token_index - doc_begin)


def rotary(positions, head_width):
    middle = head_width // 2
    inv_rates = jnp.exp(
        jnp.arange(middle, dtype=jnp.float32) * jnp.float32(-2.0 * math.log(ROPE_BASE) / head_width)
    )
    angles = positions.astype(jnp.float32)[:, None] * inv_rates[None, :]
    cosine = jnp.cos(angles)
    sine = jnp.sin(angles)
    return (jnp.concatenate([cosine, cosine], axis=1), jnp.concatenate([sine, sine], axis=1))


def rms_scale(values, gain_vec):
    return (
        values * lax.rsqrt(jnp.mean(values * values, axis=-1, keepdims=True) + NORM_EPS) * gain_vec
    )


def rotate(values, cosine, sine):
    middle = values.shape[-1] // 2
    turned = jnp.concatenate([-values[..., middle:], values[..., :middle]], axis=-1)
    return values * cosine[:, None, :] + turned * sine[:, None, :]


def swiglu(gate_pre, upward):
    return jax.nn.silu(gate_pre) * upward


def visible(token_segment, token_index, doc_ends, portion_rows):
    key_index = jnp.arange(portion_rows, dtype=jnp.int32)
    key_segment = segment_of(doc_ends, key_index)
    allowed = (token_segment[:, None] == key_segment[None, :]) & (
        token_index[:, None] >= key_index[None, :]
    )
    return allowed[:, None, None, :]


def layer_ahead(hidden, weights, tables):
    (
        gain_first,
        query_weight,
        key_matrix,
        value_matrix,
        gain_query,
        gain_key,
        output_weight,
        gain_second,
        gate_weight,
        up_weight,
        down_weight,
    ) = weights
    cosine, sine, token_segment, token_index, doc_ends, sequence_rows = tables
    token_rows = hidden.shape[0]
    query_group_size = QUERY_HEADS // KEYVALUE_HEADS
    score_scale = 1.0 / math.sqrt(HEAD_SIZE)
    normalized_rows = rms_scale(hidden, gain_first.astype(jnp.float32)).astype(jnp.bfloat16)
    query_proj = jnp.dot(normalized_rows, query_weight, preferred_element_type=jnp.float32).reshape(
        token_rows, QUERY_HEADS, HEAD_SIZE
    )
    key_projection = jnp.dot(
        normalized_rows, key_matrix, preferred_element_type=jnp.float32
    ).reshape(token_rows, KEYVALUE_HEADS, HEAD_SIZE)
    rows_of_values = jnp.dot(
        normalized_rows, value_matrix, preferred_element_type=jnp.float32
    ).astype(jnp.bfloat16)
    query_rows = (
        rotate(rms_scale(query_proj, gain_query.astype(jnp.float32)), cosine, sine)
        .astype(jnp.bfloat16)
        .reshape(token_rows, KEYVALUE_HEADS, query_group_size, HEAD_SIZE)
    )
    key_rows = (
        rotate(rms_scale(key_projection, gain_key.astype(jnp.float32)), cosine, sine)
        .astype(jnp.bfloat16)
        .reshape(token_rows, KEY_FEATURES)
    )
    running_maximum = jnp.full(
        (token_rows, KEYVALUE_HEADS, query_group_size), VERY_NEGATIVE, jnp.float32
    )
    key_portion = lax.all_gather(key_rows, "ctx", axis=0, tiled=True)
    value_portion = lax.all_gather(rows_of_values, "ctx", axis=0, tiled=True)
    portion_rows = key_portion.shape[0]
    allowed = visible(token_segment, token_index, doc_ends, portion_rows)
    scores = (
        jnp.einsum(
            "thgd,nhd->thgn",
            query_rows,
            key_portion.reshape(portion_rows, KEYVALUE_HEADS, HEAD_SIZE),
            preferred_element_type=jnp.float32,
        )
        * score_scale
    )
    masked = jnp.where(allowed, scores, VERY_NEGATIVE)
    new_max = jnp.maximum(running_maximum, jnp.max(masked, axis=-1))
    unnormed = jnp.where(allowed, jnp.exp(masked - new_max[..., None]), 0.0)
    running_sum = jnp.sum(unnormed, axis=-1)
    running_out = jnp.einsum(
        "thgn,nhd->thgd",
        unnormed.astype(jnp.bfloat16),
        value_portion.reshape(portion_rows, KEYVALUE_HEADS, HEAD_SIZE),
        preferred_element_type=jnp.float32,
    )
    running_maximum, running_sum, running_out = (new_max, running_sum, running_out)
    attended_rows = running_out / running_sum[..., None]
    log_sum = running_maximum + jnp.log(running_sum)
    attended_low = attended_rows.reshape(token_rows, QD).astype(jnp.bfloat16)
    hidden_mid = hidden + jnp.dot(attended_low, output_weight, preferred_element_type=jnp.float32)
    normed_two = rms_scale(hidden_mid, gain_second.astype(jnp.float32)).astype(jnp.bfloat16)
    gate_pre = jnp.dot(normed_two, gate_weight, preferred_element_type=jnp.float32)
    upward = jnp.dot(normed_two, up_weight, preferred_element_type=jnp.float32)
    activated = swiglu(gate_pre, upward).astype(jnp.bfloat16)
    hidden_out = hidden_mid + jnp.dot(activated, down_weight, preferred_element_type=jnp.float32)
    saved = (
        hidden,
        normalized_rows,
        query_proj,
        key_projection,
        rows_of_values,
        query_rows,
        key_rows,
        attended_rows,
        attended_low,
        log_sum,
        hidden_mid,
        normed_two,
        gate_pre,
        upward,
        activated,
    )
    return (hidden_out, saved)


def layer_back(upstream, weights, saved, tables):
    (
        gain_first,
        query_weight,
        key_matrix,
        value_matrix,
        gain_query,
        gain_key,
        output_weight,
        gain_second,
        gate_weight,
        up_weight,
        down_weight,
    ) = weights
    (
        hidden,
        normalized_rows,
        query_proj,
        key_projection,
        rows_of_values,
        query_rows,
        key_rows,
        attended_rows,
        attended_low,
        log_sum,
        hidden_mid,
        normed_two,
        gate_pre,
        upward,
        activated,
    ) = saved
    cosine, sine, token_segment, token_index, doc_ends, sequence_rows = tables
    token_rows = upstream.shape[0]
    query_group_size = QUERY_HEADS // KEYVALUE_HEADS
    score_scale = 1.0 / math.sqrt(HEAD_SIZE)
    branch_low = upstream.astype(jnp.bfloat16)
    grad_down = jnp.einsum("tf,td->fd", activated, branch_low, preferred_element_type=jnp.float32)
    grad_act = jnp.einsum("td,fd->tf", branch_low, down_weight, preferred_element_type=jnp.float32)
    ignored, swiglu_back = jax.vjp(swiglu, gate_pre, upward)
    grad_gate_pre, grad_upward = swiglu_back(grad_act)
    gate_low = grad_gate_pre.astype(jnp.bfloat16)
    up_low = grad_upward.astype(jnp.bfloat16)
    grad_gate = jnp.einsum("td,tf->df", normed_two, gate_low, preferred_element_type=jnp.float32)
    grad_up = jnp.einsum("td,tf->df", normed_two, up_low, preferred_element_type=jnp.float32)
    grad_normed_two = jnp.einsum(
        "tf,df->td", gate_low, gate_weight, preferred_element_type=jnp.float32
    ) + jnp.einsum("tf,df->td", up_low, up_weight, preferred_element_type=jnp.float32)
    ignored, second_back = jax.vjp(rms_scale, hidden_mid, gain_second.astype(jnp.float32))
    grad_mid, grad_gain_second = second_back(grad_normed_two)
    upstream_mid = upstream + grad_mid
    attn_low = upstream_mid.astype(jnp.bfloat16)
    grad_output = jnp.einsum(
        "tq,td->qd", attended_low, attn_low, preferred_element_type=jnp.float32
    )
    grad_attended = (
        jnp.einsum("td,qd->tq", attn_low, output_weight, preferred_element_type=jnp.float32)
        .astype(jnp.bfloat16)
        .reshape(token_rows, KEYVALUE_HEADS, query_group_size, HEAD_SIZE)
    )
    row_delta = jnp.sum(grad_attended.astype(jnp.float32) * attended_rows, axis=-1)
    key_portion = lax.all_gather(key_rows, "ctx", axis=0, tiled=True)
    value_portion = lax.all_gather(rows_of_values, "ctx", axis=0, tiled=True)
    portion_rows = key_portion.shape[0]
    heads_of_keys = key_portion.reshape(portion_rows, KEYVALUE_HEADS, HEAD_SIZE)
    heads_of_values = value_portion.reshape(portion_rows, KEYVALUE_HEADS, HEAD_SIZE)
    allowed = visible(token_segment, token_index, doc_ends, portion_rows)
    scores = (
        jnp.einsum("thgd,nhd->thgn", query_rows, heads_of_keys, preferred_element_type=jnp.float32)
        * score_scale
    )
    probability = jnp.where(allowed, jnp.exp(scores - log_sum[..., None]), 0.0)
    grad_prob = jnp.einsum(
        "thgd,nhd->thgn", grad_attended, heads_of_values, preferred_element_type=jnp.float32
    )
    grad_scores = (probability * (grad_prob - row_delta[..., None])).astype(jnp.bfloat16)
    grad_queries = (
        jnp.einsum("thgn,nhd->thgd", grad_scores, heads_of_keys, preferred_element_type=jnp.float32)
        * score_scale
    )
    grad_key_piece = (
        jnp.einsum("thgn,thgd->nhd", grad_scores, query_rows, preferred_element_type=jnp.float32)
        * score_scale
    )
    grad_value_piece = jnp.einsum(
        "thgn,thgd->nhd",
        probability.astype(jnp.bfloat16),
        grad_attended,
        preferred_element_type=jnp.float32,
    )
    update = jnp.concatenate(
        [
            grad_key_piece.reshape(portion_rows, KEY_FEATURES),
            grad_value_piece.reshape(portion_rows, KEY_FEATURES),
        ],
        axis=1,
    )
    grad_keyval = update
    grad_queries, grad_keyval = (grad_queries, grad_keyval)
    local_key_value = lax.psum_scatter(
        grad_keyval.astype(jnp.bfloat16), "ctx", scatter_dimension=0, tiled=True
    ).astype(jnp.float32)

    def prepare(projected, gain_vec):
        return rotate(rms_scale(projected, gain_vec), cosine, sine)

    ignored, query_back = jax.vjp(prepare, query_proj, gain_query.astype(jnp.float32))
    grad_query_proj, grad_gain_query = query_back(
        grad_queries.reshape(token_rows, QUERY_HEADS, HEAD_SIZE)
    )
    ignored, key_reverse_pass = jax.vjp(prepare, key_projection, gain_key.astype(jnp.float32))
    key_projection_gradient, key_gain_gradient = key_reverse_pass(
        local_key_value[:, :KEY_FEATURES].reshape(token_rows, KEYVALUE_HEADS, HEAD_SIZE)
    )
    query_low = grad_query_proj.reshape(token_rows, QD).astype(jnp.bfloat16)
    key_low = key_projection_gradient.reshape(token_rows, KEY_FEATURES).astype(jnp.bfloat16)
    value_low = local_key_value[:, KEY_FEATURES:].astype(jnp.bfloat16)
    grad_query = jnp.einsum(
        "td,tq->dq", normalized_rows, query_low, preferred_element_type=jnp.float32
    )
    grad_key = jnp.einsum("td,tk->dk", normalized_rows, key_low, preferred_element_type=jnp.float32)
    grad_value = jnp.einsum(
        "td,tk->dk", normalized_rows, value_low, preferred_element_type=jnp.float32
    )
    grad_normed = jnp.einsum(
        "tq,dq->td", query_low, query_weight, preferred_element_type=jnp.float32
    )
    grad_normed = grad_normed + jnp.einsum(
        "tk,dk->td", key_low, key_matrix, preferred_element_type=jnp.float32
    )
    grad_normed = grad_normed + jnp.einsum(
        "tk,dk->td", value_low, value_matrix, preferred_element_type=jnp.float32
    )
    ignored, first_back = jax.vjp(rms_scale, hidden, gain_first.astype(jnp.float32))
    grad_hidden, grad_gain_first = first_back(grad_normed)
    terms = (
        grad_gain_first,
        grad_query,
        grad_key,
        grad_value,
        grad_gain_query,
        key_gain_gradient,
        grad_output,
        grad_gain_second,
        grad_gate,
        grad_up,
        grad_down,
    )
    return (upstream_mid + grad_hidden, terms)


def near_rows(rows, share):
    return min(rows, -(-int(rows * share) // 16) * 16)


def gather_all(parts):
    nx, nz = lax.axis_size("shard") // 2, lax.axis_size("ctx")
    gains = (parts[0], parts[4], parts[5], parts[7])
    flat = jnp.concatenate([g.reshape(-1) for g in gains])
    small = jnp.zeros((16 * 128,), flat.dtype).at[: flat.shape[0]].set(flat).reshape(16, 128)
    big = (1, 2, 3, 6, 8, 9, 10)
    shares = (0.75, 0.75, 0.75, 0.6, 0.5, 0.75, 0.55)
    shards, nears = [small], [16]
    for which_layer in range(LAYERS):
        for member, share in zip(big, shares):
            shards.append(parts[member][which_layer])
            nears.append(near_rows(parts[member].shape[1], share))
    wholes = gather_weights(shards, nears, nx, nz, 0)
    every = wholes[0].reshape(2 * nx * nz, 16 * 128)[:, : flat.shape[0]]
    out, used = [[None] * 11 for _ in range(LAYERS)], 0
    for member, g in zip((0, 4, 5, 7), gains):
        here = every[:, used : used + g.size].reshape(-1, LAYERS, g.shape[1])
        used += g.size
        for which_layer in range(LAYERS):
            out[which_layer][member] = here[:, which_layer].reshape(-1)
    for which_layer in range(LAYERS):
        for i, member in enumerate(big):
            out[which_layer][member] = wholes[1 + which_layer * 7 + i]
    return out


def local(
    tokens,
    lengths,
    norm_one,
    w_query,
    w_key,
    w_value,
    query_gain,
    key_gain,
    w_output,
    norm_two,
    w_gate,
    w_up,
    w_down,
    cotangent,
):
    token_rows = tokens.shape[1]
    ctx_count = lax.axis_size("ctx")
    token_index = lax.axis_index("ctx") * token_rows + jnp.arange(token_rows, dtype=jnp.int32)
    doc_lengths = lengths[0]
    upto = jnp.arange(doc_lengths.shape[0])
    doc_ends = jnp.sum(jnp.where(upto[:, None] >= upto[None, :], doc_lengths[None, :], 0), axis=1)
    token_segment, positions = doc_layout(doc_ends, token_index)
    cosine, sine = rotary(positions, HEAD_SIZE)
    tables = (cosine, sine, token_segment, token_index, doc_ends, token_rows * ctx_count)
    hidden = tokens[0].astype(jnp.float32)
    stored = []
    held_weights = []
    gathered = gather_all((norm_one, w_query, w_key, w_value, query_gain, key_gain, w_output, norm_two, w_gate, w_up, w_down))
    for which_layer in range(LAYERS):
        weights = gathered[which_layer]
        held_weights.append(weights)
        hidden, saved = layer_ahead(hidden, weights, tables)
        stored.append(saved)
    output = hidden.astype(jnp.bfloat16)[None]
    live_mask = (token_segment < doc_lengths.shape[0]).astype(jnp.float32)
    upstream = cotangent[0].astype(jnp.float32) * live_mask[:, None]
    layer_grads = [None] * LAYERS
    for which_layer in reversed(range(LAYERS)):
        weights = gathered[which_layer]
        upstream, terms = layer_back(upstream, weights, stored[which_layer], tables)
        owned = (
            lax.psum_scatter(terms[0].astype(jnp.bfloat16), ("shard", "ctx"), scatter_dimension=0, tiled=True),
            lax.psum_scatter(terms[1].astype(jnp.bfloat16), ("shard", "ctx"), scatter_dimension=0, tiled=True),
            lax.psum_scatter(terms[2].astype(jnp.bfloat16), ("shard", "ctx"), scatter_dimension=0, tiled=True),
            lax.psum_scatter(terms[3].astype(jnp.bfloat16), ("shard", "ctx"), scatter_dimension=0, tiled=True),
            lax.psum_scatter(terms[4].astype(jnp.bfloat16), ("shard", "ctx"), scatter_dimension=0, tiled=True),
            lax.psum_scatter(terms[5].astype(jnp.bfloat16), ("shard", "ctx"), scatter_dimension=0, tiled=True),
            lax.psum_scatter(terms[6].astype(jnp.bfloat16), ("shard", "ctx"), scatter_dimension=0, tiled=True),
            lax.psum_scatter(terms[7].astype(jnp.bfloat16), ("shard", "ctx"), scatter_dimension=0, tiled=True),
            lax.psum_scatter(terms[8].astype(jnp.bfloat16), ("shard", "ctx"), scatter_dimension=0, tiled=True),
            lax.psum_scatter(terms[9].astype(jnp.bfloat16), ("shard", "ctx"), scatter_dimension=0, tiled=True),
            lax.psum_scatter(terms[10].astype(jnp.bfloat16), ("shard", "ctx"), scatter_dimension=0, tiled=True),
        )
        layer_grads[which_layer] = (
            lax.psum(owned[0].astype(jnp.bfloat16), "rep").astype(jnp.float32),
            lax.psum(owned[1].astype(jnp.bfloat16), "rep").astype(jnp.float32),
            lax.psum(owned[2].astype(jnp.bfloat16), "rep").astype(jnp.float32),
            lax.psum(owned[3].astype(jnp.bfloat16), "rep").astype(jnp.float32),
            lax.psum(owned[4].astype(jnp.bfloat16), "rep").astype(jnp.float32),
            lax.psum(owned[5].astype(jnp.bfloat16), "rep").astype(jnp.float32),
            lax.psum(owned[6].astype(jnp.bfloat16), "rep").astype(jnp.float32),
            lax.psum(owned[7].astype(jnp.bfloat16), "rep").astype(jnp.float32),
            lax.psum(owned[8].astype(jnp.bfloat16), "rep").astype(jnp.float32),
            lax.psum(owned[9].astype(jnp.bfloat16), "rep").astype(jnp.float32),
            lax.psum(owned[10].astype(jnp.bfloat16), "rep").astype(jnp.float32),
        )
    grad_tokens = upstream.astype(jnp.bfloat16)[None]
    stacked = tuple(
        (
            jnp.stack([layer_grads[which_layer][member] for which_layer in range(LAYERS)])
            for member in range(11)
        )
    )
    return (output, grad_tokens) + stacked


def solution(mesh):
    return jax.shard_map(
        local,
        mesh=mesh,
        in_specs=(
            P(("rep", "shard"), "ctx", None),
            P(("rep", "shard"), None),
            P(None, ("shard", "ctx")),
            P(None, ("shard", "ctx"), None),
            P(None, ("shard", "ctx"), None),
            P(None, ("shard", "ctx"), None),
            P(None, ("shard", "ctx")),
            P(None, ("shard", "ctx")),
            P(None, ("shard", "ctx"), None),
            P(None, ("shard", "ctx")),
            P(None, ("shard", "ctx"), None),
            P(None, ("shard", "ctx"), None),
            P(None, ("shard", "ctx"), None),
            P(("rep", "shard"), "ctx", None),
        ),
        out_specs=(
            P(("rep", "shard"), "ctx", None),
            P(("rep", "shard"), "ctx", None),
            P(None, ("shard", "ctx")),
            P(None, ("shard", "ctx"), None),
            P(None, ("shard", "ctx"), None),
            P(None, ("shard", "ctx"), None),
            P(None, ("shard", "ctx")),
            P(None, ("shard", "ctx")),
            P(None, ("shard", "ctx"), None),
            P(None, ("shard", "ctx")),
            P(None, ("shard", "ctx"), None),
            P(None, ("shard", "ctx"), None),
            P(None, ("shard", "ctx"), None),
        ),
        check_vma=False,
    )
```

```python
import functools
import math

import jax
import jax.numpy as jnp
from jax import lax
from jax.experimental import pallas as pl
from jax.experimental.pallas import tpu as pltpu
from jax.sharding import PartitionSpec as P

D = 1024
QUERY_HEADS = 16
KEYVALUE_HEADS = 8
HEAD_SIZE = 128
LAYERS = 2
QD = 2048
KEY_FEATURES = 1024


NORM_EPS = 1e-06
ROPE_BASE = 1000000.0
VERY_NEGATIVE = -1e30

MESH = pl.DeviceIdType.MESH


def gather_kernel(shapes, nx, nz, *refs):
    count = len(shapes)
    shards, wholes = refs[:count], refs[count : 2 * count]
    own_sem, z_sem, x_sem, y_sem, core_sem, out_sem = refs[2 * count :]
    y = lax.axis_index("rep")
    shard = lax.axis_index("shard")
    z = lax.axis_index("ctx")
    core, x = lax.rem(shard, 2), lax.div(shard, 2)
    to_core = (y, x * 2 + 1 - core, z)
    to_y = (1 - y, shard, z)

    def to_x(step):
        return (y, shard + 2 * step, z)

    def to_z(step):
        return (y, shard, z + step)

    def rows_of(k, xs, zs, start, size, of_core=core):
        rows = shapes[k][0]
        first = ((xs * 2 + of_core) * nz + zs) * rows + start
        return wholes[k].at[pl.ds(pl.multiple_of(first, 16), size)]

    def inplane(k):
        rows, _, near = shapes[k]
        return y * (rows - near), near

    def send(src, dst, send_sem, recv_sem, device):
        pltpu.make_async_remote_copy(
            src_ref=src,
            dst_ref=dst,
            send_sem=send_sem,
            recv_sem=recv_sem,
            device_id=device,
            device_id_type=MESH,
        ).start()

    def arrived(ref, sem):
        pltpu.make_async_copy(ref, ref, sem).wait()

    def pass_z(k, src, zs, step, kind):
        start, size = inplane(k)
        send(src, rows_of(k, x, zs, start, size), out_sem.at[k, kind], z_sem.at[k, zs], to_z(step))

    def pass_x(k, src, xs, zs, step, kind):
        start, size = inplane(k)
        send(src, rows_of(k, xs, zs, start, size), out_sem.at[k, kind], x_sem.at[k, xs * nz + zs], to_x(step))

    def pass_y(k, xs, zs):
        rows, _, near = shapes[k]
        if rows > near:
            part = rows_of(k, xs, zs, y * near, rows - near)
            send(part, part, out_sem.at[k, 4], y_sem.at[k, xs * nz + zs], to_y)

    def pass_core(k, xs, zs, start, size):
        part = rows_of(k, xs, zs, start, size)
        send(part, part, out_sem.at[k, 5], core_sem.at[k], to_core)

    def stage_own(k):
        rows, _, near = shapes[k]
        start, size = inplane(k)
        part = shards[k].at[pl.ds(pl.multiple_of(start, 16), size)]

        @pl.when(z < nz - 1)
        def _():
            pass_z(k, part, z, 1, 0)

        @pl.when(z > 0)
        def _():
            pass_z(k, part, z, -1, 1)

        @pl.when(x < nx - 1)
        def _():
            pass_x(k, part, x, z, 1, 2)

        @pl.when(x > 0)
        def _():
            pass_x(k, part, x, z, -1, 3)

        send(shards[k], rows_of(k, x, z, 0, rows), out_sem.at[k, 5], core_sem.at[k], to_core)
        pltpu.make_async_copy(shards[k], rows_of(k, x, z, 0, rows), own_sem.at[k]).start()

    def stage_z(k, d):
        start, size = inplane(k)
        for step, kind in ((1, 0), (-1, 1)):
            zs = z - step * d

            @pl.when((zs >= 0) & (zs < nz))
            def _():
                part = rows_of(k, x, zs, start, size)
                arrived(part, z_sem.at[k, zs])

                @pl.when((z + step >= 0) & (z + step < nz))
                def _():
                    pass_z(k, part, zs, step, kind)

                @pl.when(x < nx - 1)
                def _():
                    pass_x(k, part, x, zs, 1, 2)

                @pl.when(x > 0)
                def _():
                    pass_x(k, part, x, zs, -1, 3)

                pass_y(k, x, zs)
                pass_core(k, x, zs, start, size)

    def stage_x(k, d):
        start, size = inplane(k)
        for step, kind in ((1, 2), (-1, 3)):
            xs = x - step * d

            @pl.when((xs >= 0) & (xs < nx))
            def _():
                def body(zs, carry):
                    part = rows_of(k, xs, zs, start, size)
                    arrived(part, x_sem.at[k, xs * nz + zs])
                    if nx > 2:

                        @pl.when((x + step >= 0) & (x + step < nx))
                        def _():
                            pass_x(k, part, xs, zs, step, kind)

                    pass_y(k, xs, zs)
                    pass_core(k, xs, zs, start, size)
                    return carry

                lax.fori_loop(0, nz, body, 0)

    def stage_y(k):
        rows, _, near = shapes[k]
        if rows > near:

            def body(i, carry):
                xs, zs = lax.div(i, nz), lax.rem(i, nz)

                @pl.when((xs != x) | (zs != z))
                def _():
                    start = (1 - y) * near
                    arrived(rows_of(k, xs, zs, start, rows - near), y_sem.at[k, i])
                    pass_core(k, xs, zs, start, rows - near)

                return carry

            lax.fori_loop(0, nx * nz, body, 0)

    def first_rows(k, size):
        return wholes[k].at[pl.ds(0, size)]

    def stage_end(k):
        rows, _, near = shapes[k]
        arrived(first_rows(k, nx * nz * rows), core_sem.at[k])
        arrived(first_rows(k, rows), own_sem.at[k])
        for zz in range(nz):

            @pl.when(z == zz)
            def _():
                if zz < nz - 1:
                    arrived(first_rows(k, (zz + 1) * near), out_sem.at[k, 0])
                if zz > 0:
                    arrived(first_rows(k, (nz - zz) * near), out_sem.at[k, 1])

        for xx in range(nx):

            @pl.when(x == xx)
            def _():
                if xx < nx - 1:
                    arrived(first_rows(k, (xx + 1) * nz * near), out_sem.at[k, 2])
                if xx > 0:
                    arrived(first_rows(k, (nx - xx) * nz * near), out_sem.at[k, 3])

        if rows > near:
            arrived(first_rows(k, (nx * nz - 1) * (rows - near)), out_sem.at[k, 4])
            arrived(
                first_rows(k, nx * nz * rows), out_sem.at[k, 5]
            )
        else:
            arrived(first_rows(k, nx * nz * rows), out_sem.at[k, 5])

    barrier = pltpu.get_barrier_semaphore()
    pl.semaphore_signal(barrier, inc=1, device_id=to_core, device_id_type=MESH)
    pl.semaphore_signal(barrier, inc=1, device_id=to_y, device_id_type=MESH)
    for here, there in ((z > 0, to_z(-1)), (z < nz - 1, to_z(1)), (x > 0, to_x(-1)), (x < nx - 1, to_x(1))):

        @pl.when(here)
        def _():
            pl.semaphore_signal(barrier, inc=1, device_id=there, device_id_type=MESH)

    greeted = 2 + (z > 0).astype(jnp.int32) + (z < nz - 1).astype(jnp.int32)
    greeted = greeted + (x > 0).astype(jnp.int32) + (x < nx - 1).astype(jnp.int32)
    pl.semaphore_wait(barrier, greeted)

    stages = [stage_own]
    stages += [functools.partial(stage_z, d=d) for d in range(1, nz)]
    stages += [functools.partial(stage_x, d=d) for d in range(1, nx)]
    stages += [stage_y]
    for tick in range(count + len(stages) - 1):
        for depth, stage in enumerate(stages):
            k = tick - depth
            if 0 <= k < count:
                stage(k)
    for k in range(count):
        stage_end(k)


def gather_weights(shards, nears, nx, nz, collective_id):
    count = len(shards)
    shapes = tuple((a.shape[0], a.shape[1], near) for a, near in zip(shards, nears))
    return pl.pallas_call(
        functools.partial(gather_kernel, shapes, nx, nz),
        out_shape=[
            jax.ShapeDtypeStruct((a.shape[0] * 2 * nx * nz, a.shape[1]), a.dtype) for a in shards
        ],
        in_specs=[pl.BlockSpec(memory_space=pl.ANY)] * count,
        out_specs=[pl.BlockSpec(memory_space=pl.ANY)] * count,
        scratch_shapes=[
            pltpu.SemaphoreType.DMA((count,)),
            pltpu.SemaphoreType.DMA((count, nz)),
            pltpu.SemaphoreType.DMA((count, nx * nz)),
            pltpu.SemaphoreType.DMA((count, nx * nz)),
            pltpu.SemaphoreType.DMA((count,)),
            pltpu.SemaphoreType.DMA((count, 6)),
        ],
        compiler_params=pltpu.CompilerParams(collective_id=collective_id, has_side_effects=True),
    )(*shards)


SLOTS = 4
PIECES = 15
LEFTS, RIGHTS = 7, 12


def left_of(j):
    return jnp.where(j < 4, 0, jnp.where(j < 10, 1, j - 8))


def right_of(j):
    return jnp.where(j < 10, j, jnp.where(j < 12, 10, 11))


def reduce_kernel(nx, nz, layers, lefts, rights, out, left_at, right_at, total, y_in, x_in, zup_in, zdown_in, f_in, result, left_sem, right_sem, y_sem, x_sem, zup_sem, zdown_sem, f_sem, result_sem, credit):
    rows, tokens = lefts.shape[-2:]
    wide = rights.shape[-1]
    quarter = wide // 4
    kept = 3 * quarter
    pieces = layers * PIECES
    y = lax.axis_index("rep")
    shard = lax.axis_index("shard")
    z = lax.axis_index("ctx")
    core, x = lax.rem(shard, 2), lax.div(shard, 2)
    to_core = (y, x * 2 + 1 - core, z)
    to_y = (1 - y, shard, z)

    def to_x(step):
        return (y, shard + 2 * step, z)

    def to_z(step):
        return (y, shard, z + step)

    ring = total.shape[0]
    kept_at = pl.multiple_of(y * quarter, quarter)

    barrier = pltpu.get_barrier_semaphore()
    pl.semaphore_signal(barrier, inc=1, device_id=to_core, device_id_type=MESH)
    pl.semaphore_signal(barrier, inc=1, device_id=to_y, device_id_type=MESH)
    for here, there in ((z > 0, to_z(-1)), (z < nz - 1, to_z(1)), (x > 0, to_x(-1)), (x < nx - 1, to_x(1))):

        @pl.when(here)
        def _():
            pl.semaphore_signal(barrier, inc=1, device_id=there, device_id_type=MESH)

    greeted = 2 + (z > 0).astype(jnp.int32) + (z < nz - 1).astype(jnp.int32)
    greeted = greeted + (x > 0).astype(jnp.int32) + (x < nx - 1).astype(jnp.int32)
    pl.semaphore_wait(barrier, greeted)

    def left_copies(b):
        for xs in range(nx):
            mine = lefts.at[b, xs, core]
            yield pltpu.make_async_copy(mine, left_at.at[0, b, xs], left_sem.at[0, b, xs])
            yield pltpu.make_async_remote_copy(
                src_ref=lefts.at[b, xs, 1 - core],
                dst_ref=left_at.at[1, b, xs],
                send_sem=left_sem.at[2, b, xs],
                recv_sem=left_sem.at[1, b, xs],
                device_id=to_core,
                device_id_type=MESH,
            )

    def right_copies(b):
        yield pltpu.make_async_copy(rights.at[b], right_at.at[0, b], right_sem.at[0, b])
        yield pltpu.make_async_remote_copy(
            src_ref=rights.at[b],
            dst_ref=right_at.at[1, b],
            send_sem=right_sem.at[2, b],
            recv_sem=right_sem.at[1, b],
            device_id=to_core,
            device_id_type=MESH,
        )

    def first_left(j):
        return (j == 0) | (j == 4) | (j >= 10)

    def first_right(j):
        return (j <= 10) | (j == 12)

    def blocks(i):
        layer, j = lax.div(i, PIECES), lax.rem(i, PIECES)
        return layer, j, layer * LEFTS + left_of(j), layer * RIGHTS + right_of(j)

    def fetch(i, carry):
        layer, j, lb, rb = blocks(i)

        @pl.when(first_left(j))
        def _():
            for copy in left_copies(lb):
                copy.start()

        @pl.when(first_right(j))
        def _():
            for copy in right_copies(rb):
                copy.start()

        return carry

    lax.fori_loop(0, pieces, fetch, 0)

    def y_copy(i):
        return pltpu.make_async_remote_copy(
            src_ref=total.at[lax.rem(i, ring), :, :, :, pl.ds(pl.multiple_of((1 - y) * kept, quarter), quarter)],
            dst_ref=y_in.at[lax.rem(i, SLOTS)],
            send_sem=y_sem.at[0, i],
            recv_sem=y_sem.at[1, i],
            device_id=to_y,
            device_id_type=MESH,
        )

    def f_copy(i):
        return pltpu.make_async_remote_copy(
            src_ref=total.at[lax.rem(i, ring), x, z, :, pl.ds(kept_at, kept)],
            dst_ref=f_in.at[lax.rem(i, SLOTS)],
            send_sem=f_sem.at[0, i],
            recv_sem=f_sem.at[1, i],
            device_id=to_y,
            device_id_type=MESH,
        )

    def use(flow):
        pl.semaphore_wait(credit.at[flow], 1)

    def give(i, flow, device):
        @pl.when(i + SLOTS < pieces)
        def _():
            pl.semaphore_signal(credit.at[flow], inc=1, device_id=device, device_id_type=MESH)

    def spend(i, flow):
        @pl.when(i >= SLOTS)
        def _():
            use(flow)

    def product(i):
        layer, j, lb, rb = blocks(i)

        @pl.when(first_left(j))
        def _():
            for copy in left_copies(lb):
                copy.wait()

        @pl.when(first_right(j))
        def _():
            for copy in right_copies(rb):
                copy.wait()

        slot = lax.rem(i, ring)

        def tile(c, carry):
            at = pl.ds(pl.multiple_of(c * quarter, quarter), quarter)
            acc = None
            for who in range(2):
                left = left_at[who, lb].reshape(nx * nz * rows, tokens)
                part = jnp.dot(left, right_at[who, rb, :, at], preferred_element_type=jnp.float32)
                acc = part if acc is None else acc + part
            total[slot, :, :, :, at] = acc.reshape(nx, nz, rows, quarter).astype(total.dtype)
            return carry

        lax.fori_loop(0, 4, tile, 0)
        spend(i, 0)
        y_copy(i).start()

    def add(slot, xs, zs, at, width, value):
        where = (slot, xs, zs, slice(None), pl.ds(at, width))
        total[where] = (total[where].astype(jnp.float32) + value.astype(jnp.float32)).astype(total.dtype)

    def take_y(i):
        slot, small = lax.rem(i, ring), lax.rem(i, SLOTS)
        y_copy(i).wait_recv()

        def body(n, carry):
            xs, zs = lax.div(n, nz), lax.rem(n, nz)
            add(slot, xs, zs, pl.multiple_of(y * kept, quarter), quarter, y_in[small, xs, zs])
            return carry

        lax.fori_loop(0, nx * nz, body, 0)
        give(i, 0, to_y)

    def x_copy(i, up, here):
        low, high = (here + 1, nx) if up else (0, here)
        side = 0 if (up or nx == 2) else 1
        return pltpu.make_async_remote_copy(
            src_ref=total.at[lax.rem(i, ring), pl.ds(low, high - low), :, :, pl.ds(kept_at, kept)],
            dst_ref=x_in.at[lax.rem(i, SLOTS), side, pl.ds(low - (1 if up else 0), high - low)],
            send_sem=x_sem.at[0 if up else 1, i],
            recv_sem=x_sem.at[2 if up else 3, i],
            device_id=to_x(1 if up else -1),
            device_id_type=MESH,
        )

    def z_copy(i, up, here):
        low, high = (here + 1, nz) if up else (0, here)
        into = zup_in if up else zdown_in
        sems = zup_sem if up else zdown_sem
        return pltpu.make_async_remote_copy(
            src_ref=total.at[lax.rem(i, ring), x, pl.ds(low, high - low), :, pl.ds(kept_at, kept)],
            dst_ref=into.at[lax.rem(i, SLOTS), pl.ds(low - (1 if up else 0), high - low)],
            send_sem=sems.at[0, i],
            recv_sem=sems.at[1, i],
            device_id=to_z(1 if up else -1),
            device_id_type=MESH,
        )

    def x_hop(i, h):
        slot, small = lax.rem(i, ring), lax.rem(i, SLOTS)
        for up in (True, False):
            here = h if up else nx - 1 - h
            side = 0 if (up or nx == 2) else 1

            @pl.when(x == here)
            def _():
                if h > 0:
                    x_copy(i, up, here - 1 if up else here + 1).wait_recv()
                    for target in range(here, nx) if up else range(here + 1):

                        def body(zs, carry):
                            add(slot, target, zs, kept_at, kept, x_in[small, side, target - (1 if up else 0), zs])
                            return carry

                        lax.fori_loop(0, nz, body, 0)
                    give(i, 1 if up else 2, to_x(-1 if up else 1))
                if h < nx - 1:
                    spend(i, 1 if up else 2)
                    x_copy(i, up, here).start()

    def z_hop(i, h):
        slot, small = lax.rem(i, ring), lax.rem(i, SLOTS)
        for up in (True, False):
            here = h if up else nz - 1 - h

            @pl.when(z == here)
            def _():
                if h > 0:
                    z_copy(i, up, here - 1 if up else here + 1).wait_recv()
                    into = zup_in if up else zdown_in

                    def body(target, carry):
                        add(slot, x, target, kept_at, kept, into[small, target - (1 if up else 0)])
                        return carry

                    lax.fori_loop(here if up else 0, nz if up else here + 1, body, 0)
                    give(i, 3 if up else 4, to_z(-1 if up else 1))
                if h < nz - 1:
                    spend(i, 3 if up else 4)
                    z_copy(i, up, here).start()

    def send_f(i):
        spend(i, 5)
        f_copy(i).start()

    def result_copy(i):
        return pltpu.make_async_copy(result.at[lax.rem(i, 2)], out.at[i], result_sem.at[lax.rem(i, 2)])

    def finish(i):
        slot, small, two = lax.rem(i, ring), lax.rem(i, SLOTS), lax.rem(i, 2)
        f_copy(i).wait_recv()

        @pl.when(i >= 2)
        def _():
            result_copy(i - 2).wait()

        mine = total[slot, x, z].astype(jnp.float32)
        got = f_in[small].astype(jnp.float32)

        @pl.when(y == 0)
        def _():
            result[two, :, :quarter] = mine[:, :quarter]
            result[two, :, quarter:kept] = mine[:, quarter:kept] + got[:, : 2 * quarter]
            result[two, :, kept:] = got[:, 2 * quarter :]

        @pl.when(y == 1)
        def _():
            result[two, :, :quarter] = got[:, :quarter]
            result[two, :, quarter:kept] = mine[:, quarter:kept] + got[:, quarter:]
            result[two, :, kept:] = mine[:, kept:]

        give(i, 5, to_y)
        result_copy(i).start()
        y_copy(i).wait_send()
        f_copy(i).wait_send()
        for here in range(nx):

            @pl.when(x == here)
            def _():
                if here < nx - 1:
                    x_copy(i, True, here).wait_send()
                if here > 0:
                    x_copy(i, False, here).wait_send()

        for here in range(nz):

            @pl.when(z == here)
            def _():
                if here < nz - 1:
                    z_copy(i, True, here).wait_send()
                if here > 0:
                    z_copy(i, False, here).wait_send()

    plan = [[("product",)]]
    plan.append([("y",), ("x", 0)])
    for h in range(1, nx):
        plan.append([("x", h)])
    plan[-1].append(("z", 0))
    for h in range(1, nz):
        plan.append([("z", h)])
    plan[-1].append(("f",))
    plan.append([("end",)])
    does = {
        "product": product,
        "y": take_y,
        "x": x_hop,
        "z": z_hop,
        "f": send_f,
        "end": finish,
    }

    def tick(t, carry):
        for depth in [*range(1, len(plan)), 0]:
            i = t - depth

            @pl.when((i >= 0) & (i < pieces))
            def _():
                for name, *more in plan[depth]:
                    does[name](i, *more)

        return carry

    lax.fori_loop(0, pieces + len(plan) - 1, tick, 0)
    result_copy(pieces - 2).wait()
    result_copy(pieces - 1).wait()


def reduce_weights(lefts, rights, nx, nz, layers, collective_id):
    rows, tokens = lefts.shape[-2:]
    wide = rights.shape[-1]
    pieces = layers * PIECES
    kept = 3 * wide // 4
    ring = nx + nz + 2
    sides = 1 if nx == 2 else 2
    low = jnp.bfloat16
    dma = pltpu.SemaphoreType.DMA
    return pl.pallas_call(
        functools.partial(reduce_kernel, nx, nz, layers),
        out_shape=jax.ShapeDtypeStruct((pieces, rows, wide), jnp.float32),
        in_specs=[pl.BlockSpec(memory_space=pl.ANY)] * 2,
        out_specs=pl.BlockSpec(memory_space=pl.ANY),
        scratch_shapes=[
            pltpu.VMEM((2, layers * LEFTS, nx, nz, rows, tokens), low),
            pltpu.VMEM((2, layers * RIGHTS, tokens, wide), low),
            pltpu.VMEM((ring, nx, nz, rows, wide), low),
            pltpu.VMEM((SLOTS, nx, nz, rows, wide // 4), low),
            pltpu.VMEM((SLOTS, sides, nx - 1, nz, rows, kept), low),
            pltpu.VMEM((SLOTS, nz - 1, rows, kept), low),
            pltpu.VMEM((SLOTS, nz - 1, rows, kept), low),
            pltpu.VMEM((SLOTS, rows, kept), low),
            pltpu.VMEM((2, rows, wide), jnp.float32),
            dma((3, layers * LEFTS, nx)),
            dma((3, layers * RIGHTS)),
            dma((2, pieces)),
            dma((4, pieces)),
            dma((2, pieces)),
            dma((2, pieces)),
            dma((2, pieces)),
            dma((2,)),
            pltpu.SemaphoreType.REGULAR((6,)),
        ],
        compiler_params=pltpu.CompilerParams(
            collective_id=collective_id, has_side_effects=True, vmem_limit_bytes=56 * 1024 * 1024
        ),
    )(lefts, rights)


def segment_of(doc_ends, token_index):
    return jnp.sum((token_index[:, None] >= doc_ends[None, :]).astype(jnp.int32), axis=1)


def doc_layout(doc_ends, token_index):
    token_segment = segment_of(doc_ends, token_index)
    starts = jnp.concatenate([jnp.zeros((1,), jnp.int32), doc_ends])
    labels = jnp.arange(starts.shape[0], dtype=jnp.int32)
    doc_begin = jnp.sum(
        jnp.where(token_segment[:, None] == labels[None, :], starts[None, :], 0), axis=1
    )
    return (token_segment, token_index - doc_begin)


def rotary(positions, head_width):
    middle = head_width // 2
    inv_rates = jnp.exp(
        jnp.arange(middle, dtype=jnp.float32) * jnp.float32(-2.0 * math.log(ROPE_BASE) / head_width)
    )
    angles = positions.astype(jnp.float32)[:, None] * inv_rates[None, :]
    cosine = jnp.cos(angles)
    sine = jnp.sin(angles)
    return (jnp.concatenate([cosine, cosine], axis=1), jnp.concatenate([sine, sine], axis=1))


def rms_scale(values, gain_vec):
    return (
        values * lax.rsqrt(jnp.mean(values * values, axis=-1, keepdims=True) + NORM_EPS) * gain_vec
    )


def rotate(values, cosine, sine):
    middle = values.shape[-1] // 2
    turned = jnp.concatenate([-values[..., middle:], values[..., :middle]], axis=-1)
    return values * cosine[:, None, :] + turned * sine[:, None, :]


def swiglu(gate_pre, upward):
    return jax.nn.silu(gate_pre) * upward


def visible(token_segment, token_index, doc_ends, portion_rows):
    key_index = jnp.arange(portion_rows, dtype=jnp.int32)
    key_segment = segment_of(doc_ends, key_index)
    allowed = (token_segment[:, None] == key_segment[None, :]) & (
        token_index[:, None] >= key_index[None, :]
    )
    return allowed[:, None, None, :]


def layer_ahead(hidden, weights, tables):
    (
        gain_first,
        query_weight,
        key_matrix,
        value_matrix,
        gain_query,
        gain_key,
        output_weight,
        gain_second,
        gate_weight,
        up_weight,
        down_weight,
    ) = weights
    cosine, sine, token_segment, token_index, doc_ends, sequence_rows = tables
    token_rows = hidden.shape[0]
    query_group_size = QUERY_HEADS // KEYVALUE_HEADS
    score_scale = 1.0 / math.sqrt(HEAD_SIZE)
    normalized_rows = rms_scale(hidden, gain_first.astype(jnp.float32)).astype(jnp.bfloat16)
    query_proj = jnp.dot(normalized_rows, query_weight, preferred_element_type=jnp.float32).reshape(
        token_rows, QUERY_HEADS, HEAD_SIZE
    )
    key_projection = jnp.dot(
        normalized_rows, key_matrix, preferred_element_type=jnp.float32
    ).reshape(token_rows, KEYVALUE_HEADS, HEAD_SIZE)
    rows_of_values = jnp.dot(
        normalized_rows, value_matrix, preferred_element_type=jnp.float32
    ).astype(jnp.bfloat16)
    query_rows = (
        rotate(rms_scale(query_proj, gain_query.astype(jnp.float32)), cosine, sine)
        .astype(jnp.bfloat16)
        .reshape(token_rows, KEYVALUE_HEADS, query_group_size, HEAD_SIZE)
    )
    key_rows = (
        rotate(rms_scale(key_projection, gain_key.astype(jnp.float32)), cosine, sine)
        .astype(jnp.bfloat16)
        .reshape(token_rows, KEY_FEATURES)
    )
    running_maximum = jnp.full(
        (token_rows, KEYVALUE_HEADS, query_group_size), VERY_NEGATIVE, jnp.float32
    )
    key_portion = lax.all_gather(key_rows, "ctx", axis=0, tiled=True)
    value_portion = lax.all_gather(rows_of_values, "ctx", axis=0, tiled=True)
    portion_rows = key_portion.shape[0]
    allowed = visible(token_segment, token_index, doc_ends, portion_rows)
    scores = (
        jnp.einsum(
            "thgd,nhd->thgn",
            query_rows,
            key_portion.reshape(portion_rows, KEYVALUE_HEADS, HEAD_SIZE),
            preferred_element_type=jnp.float32,
        )
        * score_scale
    )
    masked = jnp.where(allowed, scores, VERY_NEGATIVE)
    new_max = jnp.maximum(running_maximum, jnp.max(masked, axis=-1))
    unnormed = jnp.where(allowed, jnp.exp(masked - new_max[..., None]), 0.0)
    running_sum = jnp.sum(unnormed, axis=-1)
    running_out = jnp.einsum(
        "thgn,nhd->thgd",
        unnormed.astype(jnp.bfloat16),
        value_portion.reshape(portion_rows, KEYVALUE_HEADS, HEAD_SIZE),
        preferred_element_type=jnp.float32,
    )
    running_maximum, running_sum, running_out = (new_max, running_sum, running_out)
    attended_rows = running_out / running_sum[..., None]
    log_sum = running_maximum + jnp.log(running_sum)
    attended_low = attended_rows.reshape(token_rows, QD).astype(jnp.bfloat16)
    hidden_mid = hidden + jnp.dot(attended_low, output_weight, preferred_element_type=jnp.float32)
    normed_two = rms_scale(hidden_mid, gain_second.astype(jnp.float32)).astype(jnp.bfloat16)
    gate_pre = jnp.dot(normed_two, gate_weight, preferred_element_type=jnp.float32)
    upward = jnp.dot(normed_two, up_weight, preferred_element_type=jnp.float32)
    activated = swiglu(gate_pre, upward).astype(jnp.bfloat16)
    hidden_out = hidden_mid + jnp.dot(activated, down_weight, preferred_element_type=jnp.float32)
    saved = (
        hidden,
        normalized_rows,
        query_proj,
        key_projection,
        rows_of_values,
        query_rows,
        key_rows,
        attended_rows,
        attended_low,
        log_sum,
        hidden_mid,
        normed_two,
        gate_pre,
        upward,
        activated,
    )
    return (hidden_out, saved)


def layer_back(upstream, weights, saved, tables):
    (
        gain_first,
        query_weight,
        key_matrix,
        value_matrix,
        gain_query,
        gain_key,
        output_weight,
        gain_second,
        gate_weight,
        up_weight,
        down_weight,
    ) = weights
    (
        hidden,
        normalized_rows,
        query_proj,
        key_projection,
        rows_of_values,
        query_rows,
        key_rows,
        attended_rows,
        attended_low,
        log_sum,
        hidden_mid,
        normed_two,
        gate_pre,
        upward,
        activated,
    ) = saved
    cosine, sine, token_segment, token_index, doc_ends, sequence_rows = tables
    token_rows = upstream.shape[0]
    query_group_size = QUERY_HEADS // KEYVALUE_HEADS
    score_scale = 1.0 / math.sqrt(HEAD_SIZE)
    branch_low = upstream.astype(jnp.bfloat16)
    grad_act = jnp.einsum("td,fd->tf", branch_low, down_weight, preferred_element_type=jnp.float32)
    ignored, swiglu_back = jax.vjp(swiglu, gate_pre, upward)
    grad_gate_pre, grad_upward = swiglu_back(grad_act)
    gate_low = grad_gate_pre.astype(jnp.bfloat16)
    up_low = grad_upward.astype(jnp.bfloat16)
    grad_normed_two = jnp.einsum(
        "tf,df->td", gate_low, gate_weight, preferred_element_type=jnp.float32
    ) + jnp.einsum("tf,df->td", up_low, up_weight, preferred_element_type=jnp.float32)
    ignored, second_back = jax.vjp(rms_scale, hidden_mid, gain_second.astype(jnp.float32))
    grad_mid, grad_gain_second = second_back(grad_normed_two)
    upstream_mid = upstream + grad_mid
    attn_low = upstream_mid.astype(jnp.bfloat16)
    grad_attended = (
        jnp.einsum("td,qd->tq", attn_low, output_weight, preferred_element_type=jnp.float32)
        .astype(jnp.bfloat16)
        .reshape(token_rows, KEYVALUE_HEADS, query_group_size, HEAD_SIZE)
    )
    row_delta = jnp.sum(grad_attended.astype(jnp.float32) * attended_rows, axis=-1)
    key_portion = lax.all_gather(key_rows, "ctx", axis=0, tiled=True)
    value_portion = lax.all_gather(rows_of_values, "ctx", axis=0, tiled=True)
    portion_rows = key_portion.shape[0]
    heads_of_keys = key_portion.reshape(portion_rows, KEYVALUE_HEADS, HEAD_SIZE)
    heads_of_values = value_portion.reshape(portion_rows, KEYVALUE_HEADS, HEAD_SIZE)
    allowed = visible(token_segment, token_index, doc_ends, portion_rows)
    scores = (
        jnp.einsum("thgd,nhd->thgn", query_rows, heads_of_keys, preferred_element_type=jnp.float32)
        * score_scale
    )
    probability = jnp.where(allowed, jnp.exp(scores - log_sum[..., None]), 0.0)
    grad_prob = jnp.einsum(
        "thgd,nhd->thgn", grad_attended, heads_of_values, preferred_element_type=jnp.float32
    )
    grad_scores = (probability * (grad_prob - row_delta[..., None])).astype(jnp.bfloat16)
    grad_queries = (
        jnp.einsum("thgn,nhd->thgd", grad_scores, heads_of_keys, preferred_element_type=jnp.float32)
        * score_scale
    )
    grad_key_piece = (
        jnp.einsum("thgn,thgd->nhd", grad_scores, query_rows, preferred_element_type=jnp.float32)
        * score_scale
    )
    grad_value_piece = jnp.einsum(
        "thgn,thgd->nhd",
        probability.astype(jnp.bfloat16),
        grad_attended,
        preferred_element_type=jnp.float32,
    )
    update = jnp.concatenate(
        [
            grad_key_piece.reshape(portion_rows, KEY_FEATURES),
            grad_value_piece.reshape(portion_rows, KEY_FEATURES),
        ],
        axis=1,
    )
    grad_keyval = update
    grad_queries, grad_keyval = (grad_queries, grad_keyval)
    local_key_value = lax.psum_scatter(
        grad_keyval.astype(jnp.bfloat16), "ctx", scatter_dimension=0, tiled=True
    ).astype(jnp.float32)

    def prepare(projected, gain_vec):
        return rotate(rms_scale(projected, gain_vec), cosine, sine)

    ignored, query_back = jax.vjp(prepare, query_proj, gain_query.astype(jnp.float32))
    grad_query_proj, grad_gain_query = query_back(
        grad_queries.reshape(token_rows, QUERY_HEADS, HEAD_SIZE)
    )
    ignored, key_reverse_pass = jax.vjp(prepare, key_projection, gain_key.astype(jnp.float32))
    key_projection_gradient, key_gain_gradient = key_reverse_pass(
        local_key_value[:, :KEY_FEATURES].reshape(token_rows, KEYVALUE_HEADS, HEAD_SIZE)
    )
    query_low = grad_query_proj.reshape(token_rows, QD).astype(jnp.bfloat16)
    key_low = key_projection_gradient.reshape(token_rows, KEY_FEATURES).astype(jnp.bfloat16)
    value_low = local_key_value[:, KEY_FEATURES:].astype(jnp.bfloat16)
    grad_normed = jnp.einsum(
        "tq,dq->td", query_low, query_weight, preferred_element_type=jnp.float32
    )
    grad_normed = grad_normed + jnp.einsum(
        "tk,dk->td", key_low, key_matrix, preferred_element_type=jnp.float32
    )
    grad_normed = grad_normed + jnp.einsum(
        "tk,dk->td", value_low, value_matrix, preferred_element_type=jnp.float32
    )
    ignored, first_back = jax.vjp(rms_scale, hidden, gain_first.astype(jnp.float32))
    grad_hidden, grad_gain_first = first_back(grad_normed)
    lefts = (normalized_rows, normed_two, attended_low, activated)
    rights = (query_low, key_low, value_low, gate_low, up_low, attn_low, branch_low)
    gains = (grad_gain_first, grad_gain_query, key_gain_gradient, grad_gain_second)
    return (upstream_mid + grad_hidden, (lefts, rights, gains))


def near_rows(rows, share):
    return min(rows, -(-int(rows * share) // 16) * 16)


def gather_all(parts):
    nx, nz = lax.axis_size("shard") // 2, lax.axis_size("ctx")
    gains = (parts[0], parts[4], parts[5], parts[7])
    flat = jnp.concatenate([g.reshape(-1) for g in gains])
    small = jnp.zeros((16 * 128,), flat.dtype).at[: flat.shape[0]].set(flat).reshape(16, 128)
    big = (1, 2, 3, 6, 8, 9, 10)
    shares = (0.75, 0.75, 0.75, 0.6, 0.5, 0.75, 0.55)
    shards, nears = [small], [16]
    for which_layer in range(LAYERS):
        for member, share in zip(big, shares):
            shards.append(parts[member][which_layer])
            nears.append(near_rows(parts[member].shape[1], share))
    wholes = gather_weights(shards, nears, nx, nz, 0)
    every = wholes[0].reshape(2 * nx * nz, 16 * 128)[:, : flat.shape[0]]
    out, used = [[None] * 11 for _ in range(LAYERS)], 0
    for member, g in zip((0, 4, 5, 7), gains):
        here = every[:, used : used + g.size].reshape(-1, LAYERS, g.shape[1])
        used += g.size
        for which_layer in range(LAYERS):
            out[which_layer][member] = here[:, which_layer].reshape(-1)
    for which_layer in range(LAYERS):
        for i, member in enumerate(big):
            out[which_layer][member] = wholes[1 + which_layer * 7 + i]
    return out


def local(
    tokens,
    lengths,
    norm_one,
    w_query,
    w_key,
    w_value,
    query_gain,
    key_gain,
    w_output,
    norm_two,
    w_gate,
    w_up,
    w_down,
    cotangent,
):
    token_rows = tokens.shape[1]
    ctx_count = lax.axis_size("ctx")
    token_index = lax.axis_index("ctx") * token_rows + jnp.arange(token_rows, dtype=jnp.int32)
    doc_lengths = lengths[0]
    upto = jnp.arange(doc_lengths.shape[0])
    doc_ends = jnp.sum(jnp.where(upto[:, None] >= upto[None, :], doc_lengths[None, :], 0), axis=1)
    token_segment, positions = doc_layout(doc_ends, token_index)
    cosine, sine = rotary(positions, HEAD_SIZE)
    tables = (cosine, sine, token_segment, token_index, doc_ends, token_rows * ctx_count)
    hidden = tokens[0].astype(jnp.float32)
    stored = []
    gathered = gather_all((norm_one, w_query, w_key, w_value, query_gain, key_gain, w_output, norm_two, w_gate, w_up, w_down))
    for which_layer in range(LAYERS):
        weights = gathered[which_layer]
        hidden, saved = layer_ahead(hidden, weights, tables)
        stored.append(saved)
    output = hidden.astype(jnp.bfloat16)[None]
    live_mask = (token_segment < doc_lengths.shape[0]).astype(jnp.float32)
    upstream = cotangent[0].astype(jnp.float32) * live_mask[:, None]
    operands = [None] * LAYERS
    for which_layer in reversed(range(LAYERS)):
        upstream, operands[which_layer] = layer_back(
            upstream, gathered[which_layer], stored[which_layer], tables
        )
    grad_tokens = upstream.astype(jnp.bfloat16)[None]
    return (output, grad_tokens) + weight_gradients(operands)


def weight_gradients(operands):
    nx, nz = lax.axis_size("shard") // 2, lax.axis_size("ctx")
    shards = 2 * nx * nz
    lefts, rights = [], []
    for layer_lefts, layer_rights, _ in operands:
        for a in layer_lefts:
            tokens, features = a.shape
            rows = D // shards
            blocks = a.T.reshape(nx, 2, nz, features // D, rows, tokens)
            lefts.append(jnp.moveaxis(blocks, 3, 0))
        for a in layer_rights:
            rights.append(jnp.moveaxis(a.reshape(a.shape[0], -1, D), 1, 0))
    pieces = reduce_weights(
        jnp.concatenate(lefts), jnp.concatenate(rights), nx, nz, LAYERS, 1
    ).reshape(LAYERS, PIECES, -1, D)

    def columns(first, count):
        part = pieces[:, first : first + count]
        return jnp.moveaxis(part, 1, 2).reshape(LAYERS, -1, count * D)

    def rows_of(first, count):
        return pieces[:, first : first + count].reshape(LAYERS, -1, D)

    flat = jnp.stack([jnp.concatenate(gains) for _, _, gains in operands])
    flat = lax.psum(flat, ("rep", "shard", "ctx"))
    here = lax.axis_index("shard") * nz + lax.axis_index("ctx")
    small, used = [], 0
    for size in (D, HEAD_SIZE, HEAD_SIZE, D):
        own = size // shards
        small.append(lax.dynamic_slice_in_dim(flat, used + here * own, own, axis=1))
        used += size
    return (
        small[0],
        columns(0, 2),
        columns(2, 1),
        columns(3, 1),
        small[1],
        small[2],
        rows_of(10, 2),
        small[3],
        columns(4, 3),
        columns(7, 3),
        rows_of(12, 3),
    )


def solution(mesh):
    return jax.shard_map(
        local,
        mesh=mesh,
        in_specs=(
            P(("rep", "shard"), "ctx", None),
            P(("rep", "shard"), None),
            P(None, ("shard", "ctx")),
            P(None, ("shard", "ctx"), None),
            P(None, ("shard", "ctx"), None),
            P(None, ("shard", "ctx"), None),
            P(None, ("shard", "ctx")),
            P(None, ("shard", "ctx")),
            P(None, ("shard", "ctx"), None),
            P(None, ("shard", "ctx")),
            P(None, ("shard", "ctx"), None),
            P(None, ("shard", "ctx"), None),
            P(None, ("shard", "ctx"), None),
            P(("rep", "shard"), "ctx", None),
        ),
        out_specs=(
            P(("rep", "shard"), "ctx", None),
            P(("rep", "shard"), "ctx", None),
            P(None, ("shard", "ctx")),
            P(None, ("shard", "ctx"), None),
            P(None, ("shard", "ctx"), None),
            P(None, ("shard", "ctx"), None),
            P(None, ("shard", "ctx")),
            P(None, ("shard", "ctx")),
            P(None, ("shard", "ctx"), None),
            P(None, ("shard", "ctx")),
            P(None, ("shard", "ctx"), None),
            P(None, ("shard", "ctx"), None),
            P(None, ("shard", "ctx"), None),
        ),
        check_vma=False,
    )
```

```python
import functools
import math

import jax
import jax.numpy as jnp
from jax import lax
from jax.experimental import pallas as pl
from jax.experimental.pallas import tpu as pltpu
from jax.sharding import PartitionSpec as P

D = 1024
QUERY_HEADS = 16
KEYVALUE_HEADS = 8
HEAD_SIZE = 128
LAYERS = 2
QD = 2048
KEY_FEATURES = 1024


NORM_EPS = 1e-06
ROPE_BASE = 1000000.0
VERY_NEGATIVE = -1e30
MESH = pl.DeviceIdType.MESH


def gather_kernel(shapes, nx, nz, *refs):
    count = len(shapes)
    shards, wholes = refs[:count], refs[count : 2 * count]
    own_sem, z_sem, x_sem, y_sem, core_sem, out_sem = refs[2 * count :]
    y = lax.axis_index("rep")
    shard = lax.axis_index("shard")
    z = lax.axis_index("ctx")
    core, x = lax.rem(shard, 2), lax.div(shard, 2)
    to_core = (y, x * 2 + 1 - core, z)
    to_y = (1 - y, shard, z)

    def to_x(step):
        return (y, shard + 2 * step, z)

    def to_z(step):
        return (y, shard, z + step)

    def rows_of(k, xs, zs, start, size, of_core=core):
        rows = shapes[k][0]
        first = ((xs * 2 + of_core) * nz + zs) * rows + start
        return wholes[k].at[pl.ds(pl.multiple_of(first, 16), size)]

    def inplane(k):
        rows, _, near = shapes[k]
        return y * (rows - near), near

    def send(src, dst, send_sem, recv_sem, device):
        pltpu.make_async_remote_copy(
            src_ref=src,
            dst_ref=dst,
            send_sem=send_sem,
            recv_sem=recv_sem,
            device_id=device,
            device_id_type=MESH,
        ).start()

    def arrived(ref, sem):
        pltpu.make_async_copy(ref, ref, sem).wait()

    def pass_z(k, src, zs, step, kind):
        start, size = inplane(k)
        send(src, rows_of(k, x, zs, start, size), out_sem.at[k, kind], z_sem.at[k, zs], to_z(step))

    def pass_x(k, src, xs, zs, step, kind):
        start, size = inplane(k)
        send(src, rows_of(k, xs, zs, start, size), out_sem.at[k, kind], x_sem.at[k, xs * nz + zs], to_x(step))

    def pass_y(k, xs, zs):
        rows, _, near = shapes[k]
        if rows > near:
            part = rows_of(k, xs, zs, y * near, rows - near)
            send(part, part, out_sem.at[k, 4], y_sem.at[k, xs * nz + zs], to_y)

    def pass_core(k, xs, zs, start, size):
        part = rows_of(k, xs, zs, start, size)
        send(part, part, out_sem.at[k, 5], core_sem.at[k], to_core)

    def stage_own(k):
        rows, _, near = shapes[k]
        start, size = inplane(k)
        part = shards[k].at[pl.ds(pl.multiple_of(start, 16), size)]

        @pl.when(z < nz - 1)
        def _():
            pass_z(k, part, z, 1, 0)

        @pl.when(z > 0)
        def _():
            pass_z(k, part, z, -1, 1)

        @pl.when(x < nx - 1)
        def _():
            pass_x(k, part, x, z, 1, 2)

        @pl.when(x > 0)
        def _():
            pass_x(k, part, x, z, -1, 3)

        send(shards[k], rows_of(k, x, z, 0, rows), out_sem.at[k, 5], core_sem.at[k], to_core)
        pltpu.make_async_copy(shards[k], rows_of(k, x, z, 0, rows), own_sem.at[k]).start()

    def stage_z(k, d):
        start, size = inplane(k)
        for step, kind in ((1, 0), (-1, 1)):
            zs = z - step * d

            @pl.when((zs >= 0) & (zs < nz))
            def _():
                part = rows_of(k, x, zs, start, size)
                arrived(part, z_sem.at[k, zs])

                @pl.when((z + step >= 0) & (z + step < nz))
                def _():
                    pass_z(k, part, zs, step, kind)

                @pl.when(x < nx - 1)
                def _():
                    pass_x(k, part, x, zs, 1, 2)

                @pl.when(x > 0)
                def _():
                    pass_x(k, part, x, zs, -1, 3)

                pass_y(k, x, zs)
                pass_core(k, x, zs, start, size)

    def stage_x(k, d):
        start, size = inplane(k)
        for step, kind in ((1, 2), (-1, 3)):
            xs = x - step * d

            @pl.when((xs >= 0) & (xs < nx))
            def _():
                def body(zs, carry):
                    part = rows_of(k, xs, zs, start, size)
                    arrived(part, x_sem.at[k, xs * nz + zs])
                    if nx > 2:

                        @pl.when((x + step >= 0) & (x + step < nx))
                        def _():
                            pass_x(k, part, xs, zs, step, kind)

                    pass_y(k, xs, zs)
                    pass_core(k, xs, zs, start, size)
                    return carry

                lax.fori_loop(0, nz, body, 0)

    def stage_y(k):
        rows, _, near = shapes[k]
        if rows > near:

            def body(i, carry):
                xs, zs = lax.div(i, nz), lax.rem(i, nz)

                @pl.when((xs != x) | (zs != z))
                def _():
                    start = (1 - y) * near
                    arrived(rows_of(k, xs, zs, start, rows - near), y_sem.at[k, i])
                    pass_core(k, xs, zs, start, rows - near)

                return carry

            lax.fori_loop(0, nx * nz, body, 0)

    def first_rows(k, size):
        return wholes[k].at[pl.ds(0, size)]

    def stage_end(k):
        rows, _, near = shapes[k]
        arrived(first_rows(k, nx * nz * rows), core_sem.at[k])
        arrived(first_rows(k, rows), own_sem.at[k])
        for zz in range(nz):

            @pl.when(z == zz)
            def _():
                if zz < nz - 1:
                    arrived(first_rows(k, (zz + 1) * near), out_sem.at[k, 0])
                if zz > 0:
                    arrived(first_rows(k, (nz - zz) * near), out_sem.at[k, 1])

        for xx in range(nx):

            @pl.when(x == xx)
            def _():
                if xx < nx - 1:
                    arrived(first_rows(k, (xx + 1) * nz * near), out_sem.at[k, 2])
                if xx > 0:
                    arrived(first_rows(k, (nx - xx) * nz * near), out_sem.at[k, 3])

        if rows > near:
            arrived(first_rows(k, (nx * nz - 1) * (rows - near)), out_sem.at[k, 4])
            arrived(
                first_rows(k, nx * nz * rows), out_sem.at[k, 5]
            )
        else:
            arrived(first_rows(k, nx * nz * rows), out_sem.at[k, 5])

    barrier = pltpu.get_barrier_semaphore()
    pl.semaphore_signal(barrier, inc=1, device_id=to_core, device_id_type=MESH)
    pl.semaphore_signal(barrier, inc=1, device_id=to_y, device_id_type=MESH)
    for here, there in ((z > 0, to_z(-1)), (z < nz - 1, to_z(1)), (x > 0, to_x(-1)), (x < nx - 1, to_x(1))):

        @pl.when(here)
        def _():
            pl.semaphore_signal(barrier, inc=1, device_id=there, device_id_type=MESH)

    greeted = 2 + (z > 0).astype(jnp.int32) + (z < nz - 1).astype(jnp.int32)
    greeted = greeted + (x > 0).astype(jnp.int32) + (x < nx - 1).astype(jnp.int32)
    pl.semaphore_wait(barrier, greeted)

    stages = [stage_own]
    stages += [functools.partial(stage_z, d=d) for d in range(1, nz)]
    stages += [functools.partial(stage_x, d=d) for d in range(1, nx)]
    stages += [stage_y]
    for tick in range(count + len(stages) - 1):
        for depth, stage in enumerate(stages):
            k = tick - depth
            if 0 <= k < count:
                stage(k)
    for k in range(count):
        stage_end(k)


def gather_weights(shards, nears, nx, nz, collective_id):
    count = len(shards)
    shapes = tuple((a.shape[0], a.shape[1], near) for a, near in zip(shards, nears))
    return pl.pallas_call(
        functools.partial(gather_kernel, shapes, nx, nz),
        out_shape=[
            jax.ShapeDtypeStruct((a.shape[0] * 2 * nx * nz, a.shape[1]), a.dtype) for a in shards
        ],
        in_specs=[pl.BlockSpec(memory_space=pl.ANY)] * count,
        out_specs=[pl.BlockSpec(memory_space=pl.ANY)] * count,
        scratch_shapes=[
            pltpu.SemaphoreType.DMA((count,)),
            pltpu.SemaphoreType.DMA((count, nz)),
            pltpu.SemaphoreType.DMA((count, nx * nz)),
            pltpu.SemaphoreType.DMA((count, nx * nz)),
            pltpu.SemaphoreType.DMA((count,)),
            pltpu.SemaphoreType.DMA((count, 6)),
        ],
        compiler_params=pltpu.CompilerParams(collective_id=collective_id, has_side_effects=True),
    )(*shards)


SLOTS = 4
PIECES = 15
LEFTS, RIGHTS = 7, 12


LEFT_BLOCKS = (1, 1, 2, 3)
RIGHT_BLOCKS = (2, 1, 1, 3, 3, 1, 1)
RIGHTS = sum(RIGHT_BLOCKS)
LEFT_FIRST = (0, 4, 10, 12)
WEIGHTS = ((0, 2, 1), (2, 1, 1), (3, 1, 1), (10, 1, 2), (4, 3, 1), (7, 3, 1), (12, 1, 3))


def right_of(j):
    return jnp.where(j < 10, j, jnp.where(j < 12, 10, 11))


def part_of(j):
    return jnp.where(j < 10, 0, jnp.where(j < 12, j - 10, j - 12))


def reduce_kernel(nx, nz, layers, *refs):
    per = len(LEFT_BLOCKS) + len(RIGHT_BLOCKS)
    operands, refs = refs[: layers * per], refs[layers * per :]
    gains, refs = refs[0], refs[1:]
    outs, refs = refs[: len(WEIGHTS)], refs[len(WEIGHTS) :]
    lefts = [operands[n * per : n * per + 4] for n in range(layers)]
    rights = [operands[n * per + 4 : (n + 1) * per] for n in range(layers)]
    gains_out, left_at, refs = refs[0], refs[1:5], refs[5:]
    right_at, turned, total, y_in, x_in, zup_in, zdown_in, f_in, result, refs = *refs[:9], refs[9:]
    gain_in, gain_up, gain_down, refs = *refs[:3], refs[3:]
    left_sem, right_sem, y_sem, x_sem, zup_sem, zdown_sem, f_sem, result_sem, gain_sem, credit = refs
    rows = total.shape[3]
    tokens, wide = right_at.shape[2:]
    quarter = wide // 4
    kept = 3 * quarter
    pieces = layers * PIECES
    y = lax.axis_index("rep")
    shard = lax.axis_index("shard")
    z = lax.axis_index("ctx")
    core, x = lax.rem(shard, 2), lax.div(shard, 2)
    to_core = (y, x * 2 + 1 - core, z)
    to_y = (1 - y, shard, z)

    def to_x(step):
        return (y, shard + 2 * step, z)

    def to_z(step):
        return (y, shard, z + step)

    ring = total.shape[0]
    kept_at = pl.multiple_of(y * quarter, quarter)

    barrier = pltpu.get_barrier_semaphore()
    pl.semaphore_signal(barrier, inc=1, device_id=to_core, device_id_type=MESH)
    pl.semaphore_signal(barrier, inc=1, device_id=to_y, device_id_type=MESH)
    for here, there in ((z > 0, to_z(-1)), (z < nz - 1, to_z(1)), (x > 0, to_x(-1)), (x < nx - 1, to_x(1))):

        @pl.when(here)
        def _():
            pl.semaphore_signal(barrier, inc=1, device_id=there, device_id_type=MESH)

    greeted = 2 + (z > 0).astype(jnp.int32) + (z < nz - 1).astype(jnp.int32)
    greeted = greeted + (x > 0).astype(jnp.int32) + (x < nx - 1).astype(jnp.int32)
    pl.semaphore_wait(barrier, greeted)

    def left_copies(k, layer, source):
        width = nz * LEFT_BLOCKS[k] * rows
        sems = layer * len(LEFT_BLOCKS) + k

        def columns(xs, of_core):
            return source.at[:, pl.ds(pl.multiple_of((xs * 2 + of_core) * width, 128), width)]

        for xs in range(nx):
            yield pltpu.make_async_copy(columns(xs, core), left_at[k].at[0, layer, xs], left_sem.at[0, sems, xs])
            yield pltpu.make_async_remote_copy(
                src_ref=columns(xs, 1 - core),
                dst_ref=left_at[k].at[1, layer, xs],
                send_sem=left_sem.at[2, sems, xs],
                recv_sem=left_sem.at[1, sems, xs],
                device_id=to_core,
                device_id_type=MESH,
            )

    def right_copies(b, source):
        yield pltpu.make_async_copy(source, right_at.at[0, b], right_sem.at[0, b])
        yield pltpu.make_async_remote_copy(
            src_ref=source,
            dst_ref=right_at.at[1, b],
            send_sem=right_sem.at[2, b],
            recv_sem=right_sem.at[1, b],
            device_id=to_core,
            device_id_type=MESH,
        )

    def first_right(j):
        return (j <= 10) | (j == 12)

    def blocks(i):
        layer, j = lax.div(i, PIECES), lax.rem(i, PIECES)
        return layer, j, part_of(j), layer * RIGHTS + right_of(j)

    for layer in range(layers):
        b = layer * RIGHTS
        for k, source in enumerate(rights[layer]):
            for k_left, first in enumerate(LEFT_FIRST):
                if first == b - layer * RIGHTS or (first == 12 and k == 6):
                    for copy in left_copies(k_left, layer, lefts[layer][k_left]):
                        copy.start()
            for n in range(RIGHT_BLOCKS[k]):
                for copy in right_copies(b, source.at[:, pl.ds(n * wide, wide)]):
                    copy.start()
                b += 1

    def y_copy(i):
        return pltpu.make_async_remote_copy(
            src_ref=total.at[lax.rem(i, ring), :, :, :, pl.ds(pl.multiple_of((1 - y) * kept, quarter), quarter)],
            dst_ref=y_in.at[lax.rem(i, SLOTS)],
            send_sem=y_sem.at[0, i],
            recv_sem=y_sem.at[1, i],
            device_id=to_y,
            device_id_type=MESH,
        )

    def f_copy(i):
        return pltpu.make_async_remote_copy(
            src_ref=total.at[lax.rem(i, ring), x, z, :, pl.ds(kept_at, kept)],
            dst_ref=f_in.at[lax.rem(i, SLOTS)],
            send_sem=f_sem.at[0, i],
            recv_sem=f_sem.at[1, i],
            device_id=to_y,
            device_id_type=MESH,
        )

    def use(flow):
        pl.semaphore_wait(credit.at[flow], 1)

    def give(i, flow, device):
        @pl.when(i + SLOTS < pieces)
        def _():
            pl.semaphore_signal(credit.at[flow], inc=1, device_id=device, device_id_type=MESH)

    def spend(i, flow):
        @pl.when(i >= SLOTS)
        def _():
            use(flow)

    def product(i):
        layer, j, sub, rb = blocks(i)
        for k, first in enumerate(LEFT_FIRST):

            @pl.when(j == first)
            def _():
                for copy in left_copies(k, layer, lefts[0][k]):
                    copy.wait()

                for who in range(2):
                    for xs in range(nx):
                        flipped = left_at[k][who, layer, xs].T.reshape(nz, LEFT_BLOCKS[k], rows, tokens)
                        for n in range(LEFT_BLOCKS[k]):
                            turned[who, n, xs] = flipped[:, n]

        @pl.when(first_right(j))
        def _():
            for copy in right_copies(rb, rights[0][1]):
                copy.wait()

        slot = lax.rem(i, ring)

        def tile(c, carry):
            at = pl.ds(pl.multiple_of(c * quarter, quarter), quarter)
            acc = None
            for who in range(2):
                left = turned[who, sub].reshape(nx * nz * rows, tokens)
                part = jnp.dot(left, right_at[who, rb, :, at], preferred_element_type=jnp.float32)
                acc = part if acc is None else acc + part
            total[slot, :, :, :, at] = acc.reshape(nx, nz, rows, quarter).astype(total.dtype)
            return carry

        lax.fori_loop(0, 4, tile, 0)
        spend(i, 0)
        y_copy(i).start()

    def add(slot, xs, zs, at, width, value):
        where = (slot, xs, zs, slice(None), pl.ds(at, width))
        total[where] = (total[where].astype(jnp.float32) + value.astype(jnp.float32)).astype(total.dtype)

    def take_y(i):
        slot, small = lax.rem(i, ring), lax.rem(i, SLOTS)
        y_copy(i).wait_recv()

        def body(n, carry):
            xs, zs = lax.div(n, nz), lax.rem(n, nz)
            add(slot, xs, zs, pl.multiple_of(y * kept, quarter), quarter, y_in[small, xs, zs])
            return carry

        lax.fori_loop(0, nx * nz, body, 0)
        give(i, 0, to_y)

    def x_copy(i, up, here):
        low, high = (here + 1, nx) if up else (0, here)
        side = 0 if (up or nx == 2) else 1
        return pltpu.make_async_remote_copy(
            src_ref=total.at[lax.rem(i, ring), pl.ds(low, high - low), :, :, pl.ds(kept_at, kept)],
            dst_ref=x_in.at[lax.rem(i, SLOTS), side, pl.ds(low - (1 if up else 0), high - low)],
            send_sem=x_sem.at[0 if up else 1, i],
            recv_sem=x_sem.at[2 if up else 3, i],
            device_id=to_x(1 if up else -1),
            device_id_type=MESH,
        )

    def z_copy(i, up, here):
        low, high = (here + 1, nz) if up else (0, here)
        into = zup_in if up else zdown_in
        sems = zup_sem if up else zdown_sem
        return pltpu.make_async_remote_copy(
            src_ref=total.at[lax.rem(i, ring), x, pl.ds(low, high - low), :, pl.ds(kept_at, kept)],
            dst_ref=into.at[lax.rem(i, SLOTS), pl.ds(low - (1 if up else 0), high - low)],
            send_sem=sems.at[0, i],
            recv_sem=sems.at[1, i],
            device_id=to_z(1 if up else -1),
            device_id_type=MESH,
        )

    def x_hop(i, h):
        slot, small = lax.rem(i, ring), lax.rem(i, SLOTS)
        for up in (True, False):
            here = h if up else nx - 1 - h
            side = 0 if (up or nx == 2) else 1

            @pl.when(x == here)
            def _():
                if h > 0:
                    x_copy(i, up, here - 1 if up else here + 1).wait_recv()
                    for target in range(here, nx) if up else range(here + 1):

                        def body(zs, carry):
                            add(slot, target, zs, kept_at, kept, x_in[small, side, target - (1 if up else 0), zs])
                            return carry

                        lax.fori_loop(0, nz, body, 0)
                    give(i, 1 if up else 2, to_x(-1 if up else 1))
                if h < nx - 1:
                    spend(i, 1 if up else 2)
                    x_copy(i, up, here).start()

    def z_hop(i, h):
        slot, small = lax.rem(i, ring), lax.rem(i, SLOTS)
        for up in (True, False):
            here = h if up else nz - 1 - h

            @pl.when(z == here)
            def _():
                if h > 0:
                    z_copy(i, up, here - 1 if up else here + 1).wait_recv()
                    into = zup_in if up else zdown_in

                    def body(target, carry):
                        add(slot, x, target, kept_at, kept, into[small, target - (1 if up else 0)])
                        return carry

                    lax.fori_loop(here if up else 0, nz if up else here + 1, body, 0)
                    give(i, 3 if up else 4, to_z(-1 if up else 1))
                if h < nz - 1:
                    spend(i, 3 if up else 4)
                    z_copy(i, up, here).start()

    def send_f(i):
        spend(i, 5)
        f_copy(i).start()

    def result_copy(i, into):
        return pltpu.make_async_copy(result.at[lax.rem(i, 2)], into, result_sem.at[lax.rem(i, 2)])

    def keep_result(i):
        layer, j = lax.div(i, PIECES), lax.rem(i, PIECES)
        for into, (first, across, below) in zip(outs, WEIGHTS):
            for n in range(across * below):

                @pl.when(j == first + n)
                def _():
                    place = (pl.ds(0, rows), pl.ds(n * wide, wide)) if below == 1 else (pl.ds(n * rows, rows), pl.ds(0, wide))
                    result_copy(i, into.at[(layer, *place)]).start()

    def result_kept(i):
        result_copy(i, outs[1].at[0]).wait()

    def gain_copy(n, source, device):
        return pltpu.make_async_remote_copy(
            src_ref=source,
            dst_ref=gain_in.at[n],
            send_sem=gain_sem.at[0, n],
            recv_sem=gain_sem.at[1, n],
            device_id=device,
            device_id_type=MESH,
        )

    def gain_start():
        copy = pltpu.make_async_copy(gains, gain_in.at[0], gain_sem.at[0, 0])
        copy.start()
        copy.wait()
        gain_copy(1, gain_in.at[0], to_core).start()

    def gain_pair():
        gain_copy(1, gain_in.at[0], to_core).wait()
        gain_up[0] = gain_in[0] + gain_in[1]
        gain_copy(2, gain_up.at[0], to_y).start()

    def gain_y():
        gain_copy(2, gain_up.at[0], to_y).wait()
        gain_in[0] = gain_up[0] + gain_in[2]

    def gain_hop(h, n, here, to, first, level):
        for up in (True, False):
            buffer = (gain_up if up else gain_down).at[level]
            slot = first if up else first + 1

            @pl.when(here == (h if up else n - 1 - h))
            def _():
                buffer[...] = gain_in[0]
                if h > 0:
                    gain_copy(slot, buffer, to(1 if up else -1)).wait_recv()
                    buffer[...] = gain_in[0] + gain_in[slot]
                if h < n - 1:
                    gain_copy(slot, buffer, to(1 if up else -1)).start()

    def gain_line(n, here, to, first, level):
        @pl.when(here < n - 1)
        def _():
            gain_copy(first, gain_up.at[level], to(1)).wait_send()

        @pl.when(here > 0)
        def _():
            gain_copy(first + 1, gain_down.at[level], to(-1)).wait_send()

        gain_in[0] = gain_up[level] + gain_down[level] - gain_in[0]

    def gain_end():
        copy = pltpu.make_async_copy(gain_in.at[0], gains_out, gain_sem.at[0, 0])
        copy.start()
        copy.wait()

    def finish(i):
        slot, small, two = lax.rem(i, ring), lax.rem(i, SLOTS), lax.rem(i, 2)
        f_copy(i).wait_recv()

        @pl.when(i >= 2)
        def _():
            result_kept(i - 2)

        mine = total[slot, x, z].astype(jnp.float32)
        got = f_in[small].astype(jnp.float32)

        @pl.when(y == 0)
        def _():
            result[two, :, :quarter] = mine[:, :quarter]
            result[two, :, quarter:kept] = mine[:, quarter:kept] + got[:, : 2 * quarter]
            result[two, :, kept:] = got[:, 2 * quarter :]

        @pl.when(y == 1)
        def _():
            result[two, :, :quarter] = got[:, :quarter]
            result[two, :, quarter:kept] = mine[:, quarter:kept] + got[:, quarter:]
            result[two, :, kept:] = mine[:, kept:]

        give(i, 5, to_y)
        keep_result(i)
        y_copy(i).wait_send()
        f_copy(i).wait_send()
        for here in range(nx):

            @pl.when(x == here)
            def _():
                if here < nx - 1:
                    x_copy(i, True, here).wait_send()
                if here > 0:
                    x_copy(i, False, here).wait_send()

        for here in range(nz):

            @pl.when(z == here)
            def _():
                if here < nz - 1:
                    z_copy(i, True, here).wait_send()
                if here > 0:
                    z_copy(i, False, here).wait_send()

    plan = [[("product",)]]
    plan.append([("y",), ("x", 0)])
    for h in range(1, nx):
        plan.append([("x", h)])
    plan[-1].append(("z", 0))
    for h in range(1, nz):
        plan.append([("z", h)])
    plan[-1].append(("f",))
    plan.append([("end",)])
    does = {
        "product": product,
        "y": take_y,
        "x": x_hop,
        "z": z_hop,
        "f": send_f,
        "end": finish,
    }

    steps = [gain_start, gain_pair, gain_y]
    for h in range(nx):
        steps.append(functools.partial(gain_hop, h, nx, x, to_x, 3, 1))
    steps.append(functools.partial(gain_line, nx, x, to_x, 3, 1))
    for h in range(nz):
        steps.append(functools.partial(gain_hop, h, nz, z, to_z, 5, 2))
    steps.append(functools.partial(gain_line, nz, z, to_z, 5, 2))
    steps.append(gain_end)

    def tick(t, carry):
        for n, step in enumerate(steps):
            pl.when(t == n)(step)

        for depth in [*range(1, len(plan)), 0]:
            i = t - depth

            @pl.when((i >= 0) & (i < pieces))
            def _():
                for name, *more in plan[depth]:
                    does[name](i, *more)

        return carry

    lax.fori_loop(0, pieces + len(plan) - 1, tick, 0)
    result_kept(pieces - 2)
    result_kept(pieces - 1)


def reduce_weights(operands, gains, nx, nz, collective_id):
    layers = len(operands)
    flat = [a for layer in operands for a in layer]
    tokens, wide = flat[0].shape
    rows = wide // (2 * nx * nz)
    pieces = layers * PIECES
    kept = 3 * wide // 4
    ring = nx + nz + 2
    sides = 1 if nx == 2 else 2
    low = jnp.bfloat16
    dma = pltpu.SemaphoreType.DMA
    anywhere = pl.BlockSpec(memory_space=pl.ANY)
    return pl.pallas_call(
        functools.partial(reduce_kernel, nx, nz, layers),
        out_shape=[
            jax.ShapeDtypeStruct((layers, rows * below, wide * across), jnp.float32) for _, across, below in WEIGHTS
        ]
        + [jax.ShapeDtypeStruct(gains.shape, gains.dtype)],
        in_specs=[anywhere] * (len(flat) + 1),
        out_specs=[anywhere] * (len(WEIGHTS) + 1),
        scratch_shapes=[pltpu.VMEM((2, layers, nx, tokens, nz * n * rows), low) for n in LEFT_BLOCKS]
        + [
            pltpu.VMEM((2, layers * RIGHTS, tokens, wide), low),
            pltpu.VMEM((2, max(LEFT_BLOCKS), nx, nz, rows, tokens), low),
            pltpu.VMEM((ring, nx, nz, rows, wide), low),
            pltpu.VMEM((SLOTS, nx, nz, rows, wide // 4), low),
            pltpu.VMEM((SLOTS, sides, nx - 1, nz, rows, kept), low),
            pltpu.VMEM((SLOTS, nz - 1, rows, kept), low),
            pltpu.VMEM((SLOTS, nz - 1, rows, kept), low),
            pltpu.VMEM((SLOTS, rows, kept), low),
            pltpu.VMEM((2, rows, wide), jnp.float32),
            pltpu.VMEM((7, *gains.shape), gains.dtype),
            pltpu.VMEM((3, *gains.shape), gains.dtype),
            pltpu.VMEM((3, *gains.shape), gains.dtype),
            dma((3, layers * len(LEFT_BLOCKS), nx)),
            dma((3, layers * RIGHTS)),
            dma((2, pieces)),
            dma((4, pieces)),
            dma((2, pieces)),
            dma((2, pieces)),
            dma((2, pieces)),
            dma((2,)),
            dma((2, 7)),
            pltpu.SemaphoreType.REGULAR((6,)),
        ],
        compiler_params=pltpu.CompilerParams(
            collective_id=collective_id, has_side_effects=True, vmem_limit_bytes=56 * 1024 * 1024
        ),
    )(*flat, gains)


CHUNK_HEADS = 2
CHUNKS = KEYVALUE_HEADS // CHUNK_HEADS
CHUNK = CHUNK_HEADS * HEAD_SIZE
GROUP = QUERY_HEADS // KEYVALUE_HEADS
SCORE_SCALE = 1.0 / math.sqrt(HEAD_SIZE)


def group_place(m):
    y, shard, z = lax.axis_index("rep"), lax.axis_index("shard"), lax.axis_index("ctx")
    core, zz = lax.rem(shard, 2), lax.rem(z, m)
    to_core = (y, shard + 1 - 2 * core, z)

    def to_line(step):
        return (y, shard, z + step)

    return core, zz, to_core, to_line


def greet(m, zz, to_core, to_line):
    barrier = pltpu.get_barrier_semaphore()
    pl.semaphore_signal(barrier, inc=1, device_id=to_core, device_id_type=MESH)
    for here, there in ((zz > 0, to_line(-1)), (zz < m - 1, to_line(1))):

        @pl.when(here)
        def _():
            pl.semaphore_signal(barrier, inc=1, device_id=there, device_id_type=MESH)

    pl.semaphore_wait(barrier, 1 + (zz > 0).astype(jnp.int32) + (zz < m - 1).astype(jnp.int32))


def remote(src, dst, send_sem, recv_sem, device):
    return pltpu.make_async_remote_copy(
        src_ref=src, dst_ref=dst, send_sem=send_sem, recv_sem=recv_sem, device_id=device, device_id_type=MESH
    )


def head_prepare(v, gain, cosine, sine):
    v = v * lax.rsqrt(jnp.mean(v * v, axis=-1, keepdims=True) + NORM_EPS) * gain
    return v * cosine + pltpu.roll(v, HEAD_SIZE // 2, 1) * sine


def head_prepare_back(grad, v, gain, cosine, sine):
    grad = grad * cosine + pltpu.roll(grad * sine, HEAD_SIZE // 2, 1)
    r = lax.rsqrt(jnp.mean(v * v, axis=-1, keepdims=True) + NORM_EPS)
    unit = v * r
    by_gain = jnp.sum(grad * unit, axis=0, keepdims=True)
    grad = grad * gain
    return r * (grad - unit * jnp.mean(grad * unit, axis=-1, keepdims=True)), by_gain


def attend_kernel(m, qp, kp, v, q_gain, k_gain, cosine, sine, place_q, segment_k, q_out, kv, att, att_low, lse, core_sem, line_sem, core_out, line_out):
    tokens, length = qp.shape[0], kv.shape[0]
    core, zz, to_core, to_line = group_place(m)
    greet(m, zz, to_core, to_line)
    cos, sin = cosine[...], sine[...]

    def part(j, source_zz, of_core=core):
        rows = pl.multiple_of((source_zz + of_core * m) * tokens, 16)
        return kv.at[pl.ds(rows, tokens), pl.ds(pl.multiple_of(j * 2 * CHUNK, 128), 2 * CHUNK)]

    def core_copy(j, source_zz, of_core=core):
        ref = part(j, source_zz, of_core)
        return remote(ref, ref, core_out.at[j, source_zz], core_sem.at[j, source_zz], to_core)

    def line_copy(j, source_zz, step):
        ref = part(j, source_zz)
        return remote(ref, ref, line_out.at[0 if step > 0 else 1, j, source_zz], line_sem.at[j, source_zz], to_line(step))

    def onward(j, source_zz, step, do):
        @pl.when((zz + step >= 0) & (zz + step < m))
        def _():
            do(line_copy(j, source_zz, step))

    begin, ended = lambda copy: copy.start(), lambda copy: copy.wait_send()
    own_rows = pl.ds(pl.multiple_of((zz + core * m) * tokens, 16), tokens)
    for j in range(CHUNKS):
        for n in range(CHUNK_HEADS):
            h = j * CHUNK_HEADS + n
            ready = head_prepare(kp[:, h * HEAD_SIZE : (h + 1) * HEAD_SIZE], k_gain[...], cos, sin)
            kv[own_rows, j * 2 * CHUNK + n * HEAD_SIZE : j * 2 * CHUNK + (n + 1) * HEAD_SIZE] = ready.astype(kv.dtype)
        kv[own_rows, j * 2 * CHUNK + CHUNK : (j + 1) * 2 * CHUNK] = v[:, j * CHUNK : (j + 1) * CHUNK]
        for step in (1, -1):
            onward(j, zz, step, begin)
        core_copy(j, zz).start()
    for h in range(QUERY_HEADS):
        at = slice(h * HEAD_SIZE, (h + 1) * HEAD_SIZE)
        q_out[:, at] = head_prepare(qp[:, at], q_gain[...], cos, sin).astype(q_out.dtype)

    def arrivals(j):
        for d in range(1, m):
            for step in (1, -1):
                source = zz - step * d

                @pl.when((source >= 0) & (source < m))
                def _():
                    line_copy(j, source, step).wait_recv()
                    onward(j, source, step, begin)
                    core_copy(j, source).start()

    segment_q = place_q[:, 0:1]
    index_q = place_q[:, 1:2]
    index_k = lax.broadcasted_iota(jnp.int32, (tokens, length), 1)
    allowed = (segment_q == segment_k[...]) & (index_q >= index_k)
    lane = lax.broadcasted_iota(jnp.int32, (tokens, HEAD_SIZE), 1)

    def attend(j):
        for source in range(m):
            core_copy(j, source, 1 - core).wait_recv()
        for n in range(CHUNK_HEADS):
            keys = kv[:, pl.ds(pl.multiple_of(j * 2 * CHUNK + n * HEAD_SIZE, 128), HEAD_SIZE)]
            values = kv[:, pl.ds(pl.multiple_of(j * 2 * CHUNK + CHUNK + n * HEAD_SIZE, 128), HEAD_SIZE)]
            for g in range(GROUP):
                h = (j * CHUNK_HEADS + n) * GROUP + g
                at = pl.ds(pl.multiple_of(h * HEAD_SIZE, 128), HEAD_SIZE)
                s = lax.dot_general(q_out[:, at], keys, (((1,), (1,)), ((), ())), preferred_element_type=jnp.float32)
                s = jnp.where(allowed, s * SCORE_SCALE, VERY_NEGATIVE)
                top = jnp.max(s, axis=-1, keepdims=True)
                p = jnp.exp(s - top)
                norm = jnp.sum(p, axis=-1, keepdims=True)
                o = jnp.dot(p.astype(values.dtype), values, preferred_element_type=jnp.float32) / norm
                att[:, at] = o
                att_low[:, at] = o.astype(att_low.dtype)
                lse[...] = jnp.where(lane == h, top + jnp.log(norm), lse[...])

    lse[...] = jnp.zeros_like(lse)

    def tick(t, carry):
        @pl.when(t < CHUNKS)
        def _():
            arrivals(t)

        @pl.when(t > 0)
        def _():
            attend(t - 1)

        return carry

    lax.fori_loop(0, CHUNKS + 1, tick, 0)

    def leave(j, carry):
        for source in range(m):
            core_copy(j, source).wait_send()
        for d in range(m):
            for step in (1, -1):
                source = zz - step * d

                @pl.when((source >= 0) & (source < m))
                def _():
                    onward(j, source, step, ended)

        return carry

    lax.fori_loop(0, CHUNKS, leave, 0)


def attend(m, qp, kp, v, q_gain, k_gain, cosine, sine, place_q, segment_k, collective_id):
    tokens = qp.shape[0]
    length = 2 * m * tokens
    low = jnp.bfloat16
    dma = pltpu.SemaphoreType.DMA
    vmem = pl.BlockSpec(memory_space=pltpu.VMEM)
    return pl.pallas_call(
        functools.partial(attend_kernel, m),
        out_shape=[
            jax.ShapeDtypeStruct((tokens, QD), low),
            jax.ShapeDtypeStruct((length, 2 * KEY_FEATURES), low),
            jax.ShapeDtypeStruct((tokens, QD), jnp.float32),
            jax.ShapeDtypeStruct((tokens, QD), low),
            jax.ShapeDtypeStruct((tokens, HEAD_SIZE), jnp.float32),
        ],
        in_specs=[vmem] * 9,
        out_specs=[vmem] * 5,
        scratch_shapes=[dma((CHUNKS, m)), dma((CHUNKS, m)), dma((CHUNKS, m)), dma((2, CHUNKS, m))],
        compiler_params=pltpu.CompilerParams(
            collective_id=collective_id, has_side_effects=True, vmem_limit_bytes=48 * 1024 * 1024
        ),
    )(qp, kp, v, q_gain, k_gain, cosine, sine, place_q, segment_k)


def attend_back_kernel(m, q, kv, d_att, att, lse, qp, kp, q_gain, k_gain, cosine, sine, place_q, segment_k, dq_low, dk_low, dv_low, gains, partial, core_in, up_in, down_in, core_sem, up_sem, down_sem):
    tokens, length = q.shape[0], kv.shape[0]
    core, zz, to_core, to_line = group_place(m)
    greet(m, zz, to_core, to_line)
    cos, sin = cosine[...], sine[...]
    segment_q = place_q[:, 0:1]
    index_q = place_q[:, 1:2]
    index_k = lax.broadcasted_iota(jnp.int32, (tokens, length), 1)
    allowed = (segment_q == segment_k[...]) & (index_q >= index_k)
    lane = lax.broadcasted_iota(jnp.int32, (tokens, HEAD_SIZE), 1)
    gains[...] = jnp.zeros_like(gains)
    over_rows = (((0,), (0,)), ((), ()))
    over_columns = (((1,), (1,)), ((), ()))

    def core_copy(j):
        return remote(partial.at[j, 1 - core], core_in.at[j], core_sem.at[0, j], core_sem.at[1, j], to_core)

    def line_copy(j, up, here):
        low, high = (here + 1, m) if up else (0, here)
        into, sems = (up_in, up_sem) if up else (down_in, down_sem)
        return remote(
            partial.at[j, core, pl.ds(low, high - low)],
            into.at[j, pl.ds(low - (1 if up else 0), high - low)],
            sems.at[0, j],
            sems.at[1, j],
            to_line(1 if up else -1),
        )

    def add(j, place, value):
        partial[j, core, place] = (partial[j, core, place].astype(jnp.float32) + value.astype(jnp.float32)).astype(partial.dtype)

    def compute(j):
        for n in range(CHUNK_HEADS):
            keys = kv[:, pl.ds(pl.multiple_of(j * 2 * CHUNK + n * HEAD_SIZE, 128), HEAD_SIZE)]
            values = kv[:, pl.ds(pl.multiple_of(j * 2 * CHUNK + CHUNK + n * HEAD_SIZE, 128), HEAD_SIZE)]
            dk = dv = None
            for g in range(GROUP):
                h = (j * CHUNK_HEADS + n) * GROUP + g
                at = pl.ds(pl.multiple_of(h * HEAD_SIZE, 128), HEAD_SIZE)
                queries, grad = q[:, at], d_att[:, at]
                total = jnp.sum(jnp.where(lane == h, lse[...], 0.0), axis=-1, keepdims=True)
                delta = jnp.sum(grad.astype(jnp.float32) * att[:, at], axis=-1, keepdims=True)
                s = lax.dot_general(queries, keys, over_columns, preferred_element_type=jnp.float32)
                p = jnp.exp(jnp.where(allowed, s * SCORE_SCALE, VERY_NEGATIVE) - total)
                dp = lax.dot_general(grad, values, over_columns, preferred_element_type=jnp.float32)
                ds = (p * (dp - delta)).astype(queries.dtype)
                dq = jnp.dot(ds, keys, preferred_element_type=jnp.float32) * SCORE_SCALE
                here_k = lax.dot_general(ds, queries, over_rows, preferred_element_type=jnp.float32)
                here_v = lax.dot_general(p.astype(grad.dtype), grad, over_rows, preferred_element_type=jnp.float32)
                dk = here_k if dk is None else dk + here_k
                dv = here_v if dv is None else dv + here_v
                by_head, by_gain = head_prepare_back(dq, qp[:, at], q_gain[...], cos, sin)
                dq_low[:, at] = by_head.astype(dq_low.dtype)
                gains[0:1] += by_gain
            first = n * HEAD_SIZE
            partial[j, :, :, :, first : first + HEAD_SIZE] = (dk * SCORE_SCALE).astype(partial.dtype).reshape(2, m, tokens, HEAD_SIZE)
            first += CHUNK
            partial[j, :, :, :, first : first + HEAD_SIZE] = dv.astype(partial.dtype).reshape(2, m, tokens, HEAD_SIZE)
        core_copy(j).start()

    def take_core(j):
        core_copy(j).wait_recv()
        for place in range(m):
            add(j, place, core_in[j, place])

    def hop(j, h):
        for up in (True, False):
            here = h if up else m - 1 - h

            @pl.when(zz == here)
            def _():
                if h > 0:
                    line_copy(j, up, here - 1 if up else here + 1).wait_recv()
                    into = up_in if up else down_in
                    for place in range(here, m) if up else range(here + 1):
                        add(j, place, into[j, place - (1 if up else 0)])
                if h < m - 1:
                    line_copy(j, up, here).start()

    def finish(j):
        for n in range(CHUNK_HEADS):
            at = pl.ds(pl.multiple_of((j * CHUNK_HEADS + n) * HEAD_SIZE, 128), HEAD_SIZE)
            grad = partial[j, core, zz, :, n * HEAD_SIZE : (n + 1) * HEAD_SIZE].astype(jnp.float32)
            by_head, by_gain = head_prepare_back(grad, kp[:, at], k_gain[...], cos, sin)
            dk_low[:, at] = by_head.astype(dk_low.dtype)
            gains[1:2] += by_gain
        at = pl.ds(pl.multiple_of(j * CHUNK, 128), CHUNK)
        dv_low[:, at] = partial[j, core, zz, :, CHUNK:]
        core_copy(j).wait_send()
        for here in range(m):

            @pl.when(zz == here)
            def _():
                if here < m - 1:
                    line_copy(j, True, here).wait_send()
                if here > 0:
                    line_copy(j, False, here).wait_send()

    plan = [[compute], [take_core, functools.partial(hop, h=0)]]
    for h in range(1, m):
        plan.append([functools.partial(hop, h=h)])
    plan[-1].append(finish)

    def tick(t, carry):
        for depth in [*range(1, len(plan)), 0]:
            j = t - depth

            @pl.when((j >= 0) & (j < CHUNKS))
            def _():
                for stage in plan[depth]:
                    stage(j)

        return carry

    lax.fori_loop(0, CHUNKS + len(plan) - 1, tick, 0)


def attend_back(m, q, kv, d_att, att, lse, qp, kp, q_gain, k_gain, cosine, sine, place_q, segment_k, collective_id):
    tokens = q.shape[0]
    low = jnp.bfloat16
    dma = pltpu.SemaphoreType.DMA
    vmem = pl.BlockSpec(memory_space=pltpu.VMEM)
    return pl.pallas_call(
        functools.partial(attend_back_kernel, m),
        out_shape=[
            jax.ShapeDtypeStruct((tokens, QD), low),
            jax.ShapeDtypeStruct((tokens, KEY_FEATURES), low),
            jax.ShapeDtypeStruct((tokens, KEY_FEATURES), low),
            jax.ShapeDtypeStruct((8, HEAD_SIZE), jnp.float32),
        ],
        in_specs=[vmem] * 13,
        out_specs=[vmem] * 4,
        scratch_shapes=[
            pltpu.VMEM((CHUNKS, 2, m, tokens, 2 * CHUNK), low),
            pltpu.VMEM((CHUNKS, m, tokens, 2 * CHUNK), low),
            pltpu.VMEM((CHUNKS, max(m - 1, 1), tokens, 2 * CHUNK), low),
            pltpu.VMEM((CHUNKS, max(m - 1, 1), tokens, 2 * CHUNK), low),
            dma((2, CHUNKS)),
            dma((2, CHUNKS)),
            dma((2, CHUNKS)),
        ],
        compiler_params=pltpu.CompilerParams(
            collective_id=collective_id, has_side_effects=True, vmem_limit_bytes=48 * 1024 * 1024
        ),
    )(q, kv, d_att, att, lse, qp, kp, q_gain, k_gain, cosine, sine, place_q, segment_k)


def segment_of(doc_ends, token_index):
    return jnp.sum((token_index[:, None] >= doc_ends[None, :]).astype(jnp.int32), axis=1)


def doc_layout(doc_ends, token_index):
    token_segment = segment_of(doc_ends, token_index)
    starts = jnp.concatenate([jnp.zeros((1,), jnp.int32), doc_ends])
    labels = jnp.arange(starts.shape[0], dtype=jnp.int32)
    doc_begin = jnp.sum(
        jnp.where(token_segment[:, None] == labels[None, :], starts[None, :], 0), axis=1
    )
    return (token_segment, token_index - doc_begin)


def rotary(positions, head_width):
    middle = head_width // 2
    inv_rates = jnp.exp(
        jnp.arange(middle, dtype=jnp.float32) * jnp.float32(-2.0 * math.log(ROPE_BASE) / head_width)
    )
    angles = positions.astype(jnp.float32)[:, None] * inv_rates[None, :]
    cosine = jnp.cos(angles)
    sine = jnp.sin(angles)
    return (jnp.concatenate([cosine, cosine], axis=1), jnp.concatenate([-sine, sine], axis=1))


def rms_scale(values, gain_vec):
    return (
        values * lax.rsqrt(jnp.mean(values * values, axis=-1, keepdims=True) + NORM_EPS) * gain_vec
    )


def swiglu(gate_pre, upward):
    return jax.nn.silu(gate_pre) * upward


def product(left, right):
    return jnp.dot(left, right, preferred_element_type=jnp.float32)


def product_back(grad, right):
    return lax.dot_general(grad, right, (((1,), (1,)), ((), ())), preferred_element_type=jnp.float32)


def head_gain(gain):
    return gain.astype(jnp.float32)[None, :]


def layer_ahead(hidden, weights, tables, m):
    (
        gain_first,
        query_weight,
        key_matrix,
        value_matrix,
        gain_query,
        gain_key,
        output_weight,
        gain_second,
        gate_weight,
        up_weight,
        down_weight,
    ) = weights
    normalized_rows = rms_scale(hidden, gain_first.astype(jnp.float32)).astype(jnp.bfloat16)
    key_projection = product(normalized_rows, key_matrix)
    rows_of_values = product(normalized_rows, value_matrix).astype(jnp.bfloat16)
    query_proj = product(normalized_rows, query_weight)
    query_rows, keys_values, attended_rows, attended_low, log_sum = attend(
        m, query_proj, key_projection, rows_of_values, head_gain(gain_query), head_gain(gain_key), *tables, 2
    )
    hidden_mid = hidden + product(attended_low, output_weight)
    normed_two = rms_scale(hidden_mid, gain_second.astype(jnp.float32)).astype(jnp.bfloat16)
    gate_pre = product(normed_two, gate_weight)
    upward = product(normed_two, up_weight)
    activated = swiglu(gate_pre, upward).astype(jnp.bfloat16)
    hidden_out = hidden_mid + product(activated, down_weight)
    saved = (
        hidden,
        normalized_rows,
        query_proj,
        key_projection,
        query_rows,
        keys_values,
        attended_rows,
        attended_low,
        log_sum,
        hidden_mid,
        normed_two,
        gate_pre,
        upward,
        activated,
    )
    return (hidden_out, saved)


def layer_back(upstream, weights, saved, tables, m):
    (
        gain_first,
        query_weight,
        key_matrix,
        value_matrix,
        gain_query,
        gain_key,
        output_weight,
        gain_second,
        gate_weight,
        up_weight,
        down_weight,
    ) = weights
    (
        hidden,
        normalized_rows,
        query_proj,
        key_projection,
        query_rows,
        keys_values,
        attended_rows,
        attended_low,
        log_sum,
        hidden_mid,
        normed_two,
        gate_pre,
        upward,
        activated,
    ) = saved
    branch_low = upstream.astype(jnp.bfloat16)
    grad_act = product_back(branch_low, down_weight)
    ignored, swiglu_back = jax.vjp(swiglu, gate_pre, upward)
    grad_gate_pre, grad_upward = swiglu_back(grad_act)
    gate_low = grad_gate_pre.astype(jnp.bfloat16)
    up_low = grad_upward.astype(jnp.bfloat16)
    grad_normed_two = product_back(gate_low, gate_weight) + product_back(up_low, up_weight)
    ignored, second_back = jax.vjp(rms_scale, hidden_mid, gain_second.astype(jnp.float32))
    grad_mid, grad_gain_second = second_back(grad_normed_two)
    upstream_mid = upstream + grad_mid
    attn_low = upstream_mid.astype(jnp.bfloat16)
    grad_attended = product_back(attn_low, output_weight).astype(jnp.bfloat16)
    query_low, key_low, value_low, head_gains = attend_back(
        m,
        query_rows,
        keys_values,
        grad_attended,
        attended_rows,
        log_sum,
        query_proj,
        key_projection,
        head_gain(gain_query),
        head_gain(gain_key),
        *tables,
        3,
    )
    grad_normed = product_back(query_low, query_weight)
    grad_normed = grad_normed + product_back(key_low, key_matrix)
    grad_normed = grad_normed + product_back(value_low, value_matrix)
    ignored, first_back = jax.vjp(rms_scale, hidden, gain_first.astype(jnp.float32))
    grad_hidden, grad_gain_first = first_back(grad_normed)
    lefts = (normalized_rows, normed_two, attended_low, activated)
    rights = (query_low, key_low, value_low, gate_low, up_low, attn_low, branch_low)
    gains = (grad_gain_first, head_gains[0], head_gains[1], grad_gain_second)
    return (upstream_mid + grad_hidden, (lefts + rights, gains))


def near_rows(rows, share):
    return min(rows, -(-int(rows * share) // 16) * 16)


def gather_all(parts):
    nx, nz = lax.axis_size("shard") // 2, lax.axis_size("ctx")
    gains = (parts[0], parts[4], parts[5], parts[7])
    flat = jnp.concatenate([g.reshape(-1) for g in gains])
    small = jnp.zeros((16 * 128,), flat.dtype).at[: flat.shape[0]].set(flat).reshape(16, 128)
    big = (1, 2, 3, 6, 8, 9, 10)
    shares = (0.75, 0.75, 0.75, 0.6, 0.5, 0.75, 0.55)
    shards, nears = [small], [16]
    for which_layer in range(LAYERS):
        for member, share in zip(big, shares):
            shards.append(parts[member][which_layer])
            nears.append(near_rows(parts[member].shape[1], share))
    wholes = gather_weights(shards, nears, nx, nz, 0)
    every = wholes[0].reshape(2 * nx * nz, 16 * 128)[:, : flat.shape[0]]
    out, used = [[None] * 11 for _ in range(LAYERS)], 0
    for member, g in zip((0, 4, 5, 7), gains):
        here = every[:, used : used + g.size].reshape(-1, LAYERS, g.shape[1])
        used += g.size
        for which_layer in range(LAYERS):
            out[which_layer][member] = here[:, which_layer].reshape(-1)
    for which_layer in range(LAYERS):
        for i, member in enumerate(big):
            out[which_layer][member] = wholes[1 + which_layer * 7 + i]
    return out


def weight_gradients(operands):
    nx, nz = lax.axis_size("shard") // 2, lax.axis_size("ctx")
    shards = 2 * nx * nz
    flat = jnp.concatenate([g for _, gains in operands for g in gains])
    size = -(-flat.shape[0] // 1024) * 1024
    padded = jnp.zeros((size,), flat.dtype).at[: flat.shape[0]].set(flat).reshape(-1, 128)
    *grads, summed = reduce_weights([members for members, _ in operands], padded, nx, nz, 1)
    summed = summed.reshape(-1)[: flat.shape[0]].reshape(LAYERS, -1)
    here = lax.axis_index("shard") * nz + lax.axis_index("ctx")
    small, used = [], 0
    for size in (D, HEAD_SIZE, HEAD_SIZE, D):
        own = size // shards
        small.append(lax.dynamic_slice_in_dim(summed, used + here * own, own, axis=1))
        used += size
    query, key, value, output, gate, up, down = grads
    return (small[0], query, key, value, small[1], small[2], output, small[3], gate, up, down)


def local(
    tokens,
    lengths,
    norm_one,
    w_query,
    w_key,
    w_value,
    query_gain,
    key_gain,
    w_output,
    norm_two,
    w_gate,
    w_up,
    w_down,
    cotangent,
):
    token_rows = tokens.shape[1]
    nx, nz = lax.axis_size("shard") // 2, lax.axis_size("ctx")
    m = nz // 2
    pairs = []
    for x in range(nx):
        for z in range(m):
            low, high = (2 * x + 1) * nz + z, 2 * x * nz + z + m
            same = (2 * x * nz + z, (2 * x + 1) * nz + z + m)
            pairs += [(low, high), (high, low)] + [(s, s) for s in same]

    def swap(values):
        return lax.ppermute(values, ("shard", "ctx"), pairs)

    tokens, lengths, cotangent = swap(tokens), swap(lengths), swap(cotangent)
    block = lax.axis_index("ctx") % m + (lax.axis_index("shard") % 2) * m
    token_index = block * token_rows + jnp.arange(token_rows, dtype=jnp.int32)
    doc_lengths = lengths[0]
    upto = jnp.arange(doc_lengths.shape[0])
    doc_ends = jnp.sum(jnp.where(upto[:, None] >= upto[None, :], doc_lengths[None, :], 0), axis=1)
    token_segment, positions = doc_layout(doc_ends, token_index)
    cosine, sine = rotary(positions, HEAD_SIZE)
    key_segment = segment_of(doc_ends, jnp.arange(token_rows * nz, dtype=jnp.int32))
    tables = (cosine, sine, jnp.stack([token_segment, token_index], axis=1), key_segment[None, :])
    gathered = gather_all(
        (norm_one, w_query, w_key, w_value, query_gain, key_gain, w_output, norm_two, w_gate, w_up, w_down)
    )
    hidden = tokens[0].astype(jnp.float32)
    stored = []
    for which_layer in range(LAYERS):
        hidden, saved = layer_ahead(hidden, gathered[which_layer], tables, m)
        stored.append(saved)
    output = swap(hidden.astype(jnp.bfloat16))[None]
    live_mask = (token_segment < doc_lengths.shape[0]).astype(jnp.float32)
    upstream = cotangent[0].astype(jnp.float32) * live_mask[:, None]
    operands = [None] * LAYERS
    for which_layer in reversed(range(LAYERS)):
        upstream, operands[which_layer] = layer_back(
            upstream, gathered[which_layer], stored[which_layer], tables, m
        )
    grad_tokens = swap(upstream.astype(jnp.bfloat16))[None]
    return (output, grad_tokens) + weight_gradients(operands)


def solution(mesh):
    return jax.shard_map(
        local,
        mesh=mesh,
        in_specs=(
            P(("rep", "shard"), "ctx", None),
            P(("rep", "shard"), None),
            P(None, ("shard", "ctx")),
            P(None, ("shard", "ctx"), None),
            P(None, ("shard", "ctx"), None),
            P(None, ("shard", "ctx"), None),
            P(None, ("shard", "ctx")),
            P(None, ("shard", "ctx")),
            P(None, ("shard", "ctx"), None),
            P(None, ("shard", "ctx")),
            P(None, ("shard", "ctx"), None),
            P(None, ("shard", "ctx"), None),
            P(None, ("shard", "ctx"), None),
            P(("rep", "shard"), "ctx", None),
        ),
        out_specs=(
            P(("rep", "shard"), "ctx", None),
            P(("rep", "shard"), "ctx", None),
            P(None, ("shard", "ctx")),
            P(None, ("shard", "ctx"), None),
            P(None, ("shard", "ctx"), None),
            P(None, ("shard", "ctx"), None),
            P(None, ("shard", "ctx")),
            P(None, ("shard", "ctx")),
            P(None, ("shard", "ctx"), None),
            P(None, ("shard", "ctx")),
            P(None, ("shard", "ctx"), None),
            P(None, ("shard", "ctx"), None),
            P(None, ("shard", "ctx"), None),
        ),
        check_vma=False,
    )
```

```python
import functools
import math

import jax
import jax.numpy as jnp
from jax import lax
from jax.experimental import pallas as pl
from jax.experimental.pallas import tpu as pltpu
from jax.sharding import PartitionSpec as P

D = 1024
QUERY_HEADS = 16
KEYVALUE_HEADS = 8
HEAD_SIZE = 128
LAYERS = 2
QD = 2048
KEY_FEATURES = 1024


NORM_EPS = 1e-06
ROPE_BASE = 1000000.0
VERY_NEGATIVE = -1e30
MESH = pl.DeviceIdType.MESH


def gather_kernel(shapes, nx, nz, *refs):
    count = len(shapes)
    shards, wholes = refs[:count], refs[count : 2 * count]
    own_sem, z_sem, x_sem, y_sem, core_sem, out_sem = refs[2 * count :]
    y = lax.axis_index("rep")
    shard = lax.axis_index("shard")
    z = lax.axis_index("ctx")
    core, x = lax.rem(shard, 2), lax.div(shard, 2)
    to_core = (y, x * 2 + 1 - core, z)
    to_y = (1 - y, shard, z)

    def to_x(step):
        return (y, shard + 2 * step, z)

    def to_z(step):
        return (y, shard, z + step)

    def rows_of(k, xs, zs, start, size, of_core=core):
        rows = shapes[k][0]
        first = ((xs * 2 + of_core) * nz + zs) * rows + start
        return wholes[k].at[pl.ds(pl.multiple_of(first, 16), size)]

    def inplane(k):
        rows, _, near = shapes[k]
        return y * (rows - near), near

    def send(src, dst, send_sem, recv_sem, device):
        pltpu.make_async_remote_copy(
            src_ref=src,
            dst_ref=dst,
            send_sem=send_sem,
            recv_sem=recv_sem,
            device_id=device,
            device_id_type=MESH,
        ).start()

    def arrived(ref, sem):
        pltpu.make_async_copy(ref, ref, sem).wait()

    def pass_z(k, src, zs, step, kind):
        start, size = inplane(k)
        send(src, rows_of(k, x, zs, start, size), out_sem.at[k, kind], z_sem.at[k, zs], to_z(step))

    def pass_x(k, src, xs, zs, step, kind):
        start, size = inplane(k)
        send(src, rows_of(k, xs, zs, start, size), out_sem.at[k, kind], x_sem.at[k, xs * nz + zs], to_x(step))

    def pass_y(k, xs, zs):
        rows, _, near = shapes[k]
        if rows > near:
            part = rows_of(k, xs, zs, y * near, rows - near)
            send(part, part, out_sem.at[k, 4], y_sem.at[k, xs * nz + zs], to_y)

    def pass_core(k, xs, zs, start, size):
        part = rows_of(k, xs, zs, start, size)
        send(part, part, out_sem.at[k, 5], core_sem.at[k], to_core)

    def stage_own(k):
        rows, _, near = shapes[k]
        start, size = inplane(k)
        part = shards[k].at[pl.ds(pl.multiple_of(start, 16), size)]

        @pl.when(z < nz - 1)
        def _():
            pass_z(k, part, z, 1, 0)

        @pl.when(z > 0)
        def _():
            pass_z(k, part, z, -1, 1)

        @pl.when(x < nx - 1)
        def _():
            pass_x(k, part, x, z, 1, 2)

        @pl.when(x > 0)
        def _():
            pass_x(k, part, x, z, -1, 3)

        send(shards[k], rows_of(k, x, z, 0, rows), out_sem.at[k, 5], core_sem.at[k], to_core)
        pltpu.make_async_copy(shards[k], rows_of(k, x, z, 0, rows), own_sem.at[k]).start()

    def stage_z(k, d):
        start, size = inplane(k)
        for step, kind in ((1, 0), (-1, 1)):
            zs = z - step * d

            @pl.when((zs >= 0) & (zs < nz))
            def _():
                part = rows_of(k, x, zs, start, size)
                arrived(part, z_sem.at[k, zs])

                @pl.when((z + step >= 0) & (z + step < nz))
                def _():
                    pass_z(k, part, zs, step, kind)

                @pl.when(x < nx - 1)
                def _():
                    pass_x(k, part, x, zs, 1, 2)

                @pl.when(x > 0)
                def _():
                    pass_x(k, part, x, zs, -1, 3)

                pass_y(k, x, zs)
                pass_core(k, x, zs, start, size)

    def stage_x(k, d):
        start, size = inplane(k)
        for step, kind in ((1, 2), (-1, 3)):
            xs = x - step * d

            @pl.when((xs >= 0) & (xs < nx))
            def _():
                def body(zs, carry):
                    part = rows_of(k, xs, zs, start, size)
                    arrived(part, x_sem.at[k, xs * nz + zs])
                    if nx > 2:

                        @pl.when((x + step >= 0) & (x + step < nx))
                        def _():
                            pass_x(k, part, xs, zs, step, kind)

                    pass_y(k, xs, zs)
                    pass_core(k, xs, zs, start, size)
                    return carry

                lax.fori_loop(0, nz, body, 0)

    def stage_y(k):
        rows, _, near = shapes[k]
        if rows > near:

            def body(i, carry):
                xs, zs = lax.div(i, nz), lax.rem(i, nz)

                @pl.when((xs != x) | (zs != z))
                def _():
                    start = (1 - y) * near
                    arrived(rows_of(k, xs, zs, start, rows - near), y_sem.at[k, i])
                    pass_core(k, xs, zs, start, rows - near)

                return carry

            lax.fori_loop(0, nx * nz, body, 0)

    def first_rows(k, size):
        return wholes[k].at[pl.ds(0, size)]

    def stage_end(k):
        rows, _, near = shapes[k]
        arrived(first_rows(k, nx * nz * rows), core_sem.at[k])
        arrived(first_rows(k, rows), own_sem.at[k])
        for zz in range(nz):

            @pl.when(z == zz)
            def _():
                if zz < nz - 1:
                    arrived(first_rows(k, (zz + 1) * near), out_sem.at[k, 0])
                if zz > 0:
                    arrived(first_rows(k, (nz - zz) * near), out_sem.at[k, 1])

        for xx in range(nx):

            @pl.when(x == xx)
            def _():
                if xx < nx - 1:
                    arrived(first_rows(k, (xx + 1) * nz * near), out_sem.at[k, 2])
                if xx > 0:
                    arrived(first_rows(k, (nx - xx) * nz * near), out_sem.at[k, 3])

        if rows > near:
            arrived(first_rows(k, (nx * nz - 1) * (rows - near)), out_sem.at[k, 4])
            arrived(
                first_rows(k, nx * nz * rows), out_sem.at[k, 5]
            )
        else:
            arrived(first_rows(k, nx * nz * rows), out_sem.at[k, 5])

    barrier = pltpu.get_barrier_semaphore()
    pl.semaphore_signal(barrier, inc=1, device_id=to_core, device_id_type=MESH)
    pl.semaphore_signal(barrier, inc=1, device_id=to_y, device_id_type=MESH)
    for here, there in ((z > 0, to_z(-1)), (z < nz - 1, to_z(1)), (x > 0, to_x(-1)), (x < nx - 1, to_x(1))):

        @pl.when(here)
        def _():
            pl.semaphore_signal(barrier, inc=1, device_id=there, device_id_type=MESH)

    greeted = 2 + (z > 0).astype(jnp.int32) + (z < nz - 1).astype(jnp.int32)
    greeted = greeted + (x > 0).astype(jnp.int32) + (x < nx - 1).astype(jnp.int32)
    pl.semaphore_wait(barrier, greeted)

    stages = [stage_own]
    stages += [functools.partial(stage_z, d=d) for d in range(1, nz)]
    stages += [functools.partial(stage_x, d=d) for d in range(1, nx)]
    stages += [stage_y]
    for tick in range(count + len(stages) - 1):
        for depth, stage in enumerate(stages):
            k = tick - depth
            if 0 <= k < count:
                stage(k)
    for k in range(count):
        stage_end(k)


def gather_weights(shards, nears, nx, nz, collective_id):
    count = len(shards)
    shapes = tuple((a.shape[0], a.shape[1], near) for a, near in zip(shards, nears))
    return pl.pallas_call(
        functools.partial(gather_kernel, shapes, nx, nz),
        out_shape=[
            jax.ShapeDtypeStruct((a.shape[0] * 2 * nx * nz, a.shape[1]), a.dtype) for a in shards
        ],
        in_specs=[pl.BlockSpec(memory_space=pl.ANY)] * count,
        out_specs=[pl.BlockSpec(memory_space=pl.ANY)] * count,
        scratch_shapes=[
            pltpu.SemaphoreType.DMA((count,)),
            pltpu.SemaphoreType.DMA((count, nz)),
            pltpu.SemaphoreType.DMA((count, nx * nz)),
            pltpu.SemaphoreType.DMA((count, nx * nz)),
            pltpu.SemaphoreType.DMA((count,)),
            pltpu.SemaphoreType.DMA((count, 6)),
        ],
        compiler_params=pltpu.CompilerParams(collective_id=collective_id, has_side_effects=True),
    )(*shards)


SLOTS = 4
PIECES = 15
LEFT_BLOCKS = (3, 2, 1, 1)
LEFT_FIRST = (0, 3, 5, 11)
RIGHTS = 7
RIGHT_FIRST = (0, 3, 5, 7, 9, 11, 13)
WEIGHT_BLOCKS = ((1, 3), (1, 2), (3, 1), (3, 1), (2, 1), (1, 1), (1, 1))


def piece_place(j, replica):
    if j < 2:
        return 0, replica, j
    if j == 2:
        return 0, 2, replica
    if j < 5:
        return 1, replica, j - 3
    if j < 11:
        return 2 + replica, 0, j - 5
    if replica == 0:
        return 4, 0, j - 11
    return (5, 0, j - 11) if j < 13 else (6, 0, j - 13)


def reduce_kernel(nx, nz, layers, *refs):
    per = 4 + 4 + 7 + 1
    operands, refs = refs[: layers * per], refs[layers * per :]
    gains, refs = refs[0], refs[1:]
    outs, refs = refs[: len(WEIGHT_BLOCKS)], refs[len(WEIGHT_BLOCKS) :]
    gains_out, left_at, refs = refs[0], refs[1:5], refs[5:]
    right_at, turned, total, x_in, zup_in, zdown_in, f_in, result, refs = *refs[:8], refs[8:]
    gain_in, gain_up, gain_down, refs = *refs[:3], refs[3:]
    left_sem, right_sem, x_sem, zup_sem, zdown_sem, f_sem, result_sem, gain_sem, credit = refs
    rows, width = total.shape[3:]
    tokens, wide = right_at.shape[2:]
    pieces = layers * PIECES
    ring = total.shape[0]
    y = lax.axis_index("rep")
    shard = lax.axis_index("shard")
    z = lax.axis_index("ctx")
    core, x = lax.rem(shard, 2), lax.div(shard, 2)
    to_core = (y, x * 2 + 1 - core, z)
    to_y = (1 - y, shard, z)

    def to_x(step):
        return (y, shard + 2 * step, z)

    def to_z(step):
        return (y, shard, z + step)

    barrier = pltpu.get_barrier_semaphore()
    pl.semaphore_signal(barrier, inc=1, device_id=to_core, device_id_type=MESH)
    pl.semaphore_signal(barrier, inc=1, device_id=to_y, device_id_type=MESH)
    for here, there in ((z > 0, to_z(-1)), (z < nz - 1, to_z(1)), (x > 0, to_x(-1)), (x < nx - 1, to_x(1))):

        @pl.when(here)
        def _():
            pl.semaphore_signal(barrier, inc=1, device_id=there, device_id_type=MESH)

    greeted = 2 + (z > 0).astype(jnp.int32) + (z < nz - 1).astype(jnp.int32)
    greeted = greeted + (x > 0).astype(jnp.int32) + (x < nx - 1).astype(jnp.int32)
    pl.semaphore_wait(barrier, greeted)

    def left_copies(k, layer, sources):
        span = nz * LEFT_BLOCKS[k] * rows
        sems = layer * 4 + k
        for whose, source in zip((0, 2), sources):

            def columns(xs, of_core):
                return source.at[:, pl.ds(pl.multiple_of((xs * 2 + of_core) * span, 128), span)]

            for xs in range(nx):
                yield pltpu.make_async_copy(
                    columns(xs, core), left_at[k].at[whose, layer, xs], left_sem.at[whose, sems, xs]
                )
                yield remote(
                    columns(xs, 1 - core),
                    left_at[k].at[whose + 1, layer, xs],
                    left_sem.at[4 + whose, sems, xs],
                    left_sem.at[whose + 1, sems, xs],
                    to_core,
                )

    def own_right(b, source):
        return pltpu.make_async_copy(source, right_at.at[0, b], right_sem.at[0, b])

    def pair_right(b, source):
        return remote(source, right_at.at[1, b], right_sem.at[4, b], right_sem.at[1, b], to_core)

    def held_right(b, source):
        return pltpu.make_async_copy(source, right_at.at[2, b], right_sem.at[2, b])

    def replica_right(b, source):
        return remote(source, right_at.at[2, b], right_sem.at[5, b], right_sem.at[2, b], to_y)

    def passed_right(b, source):
        return remote(source, right_at.at[3, b], right_sem.at[6, b], right_sem.at[3, b], to_core)

    def fetch(i):
        for layer in range(layers):
            mine = operands[layer * per : (layer + 1) * per]
            lefts, their_lefts = mine[:4], mine[4:8]
            down, output, gate, up, query, key, value, their_down = mine[8:]
            blocks = [((down, 0), (down, 0)), ((output, 0), (output, 0))]
            blocks += [((gate, n), (up, n)) for n in range(3)]
            blocks += [((query, 0), (key, 0)), ((query, 1), (value, 0))]
            for n in range(RIGHTS):

                @pl.when(i == layer * PIECES + RIGHT_FIRST[n])
                def _():
                    fetch_block(layer, n, lefts, their_lefts, blocks[n], their_down)

    def fetch_block(layer, n, lefts, their_lefts, block, their_down):
        b = layer * RIGHTS + n
        for replica in range(2):

            @pl.when(y == replica)
            def _():
                here, there = (
                    source.at[:, pl.ds(at * wide, wide)] for source, at in (block[replica], block[1 - replica])
                )
                if n > 0:
                    replica_right(b, there).start()
                own_right(b, here).start()
                pair_right(b, here).start()

        if n == 0:
            held_right(b, their_down).start()
            passed_right(b, their_down).start()
        for k, first in enumerate(LEFT_FIRST):
            if first == RIGHT_FIRST[n]:
                for copy in left_copies(k, layer, (lefts[k], their_lefts[k])):
                    copy.start()

    def place(i):
        return lax.div(i, PIECES), lax.rem(i, PIECES)

    def right_block(j):
        return jnp.where(j < 3, 0, jnp.where(j < 5, 1, lax.div(j - 1, 2)))

    def any_of(j, values):
        hit = j == values[0]
        for value in values[1:]:
            hit = hit | (j == value)
        return hit

    some_right = operands[8]

    def forward(i):
        layer, j = place(i)

        @pl.when(any_of(j, RIGHT_FIRST[1:]))
        def _():
            b = layer * RIGHTS + right_block(j)
            replica_right(b, some_right).wait_recv()
            passed_right(b, right_at.at[2, b]).start()

    def product(i):
        layer, j = place(i)
        b = layer * RIGHTS + right_block(j)
        for k, first in enumerate(LEFT_FIRST):

            @pl.when(j == first)
            def _():
                for copy in left_copies(k, layer, (operands[k], operands[k])):
                    copy.wait()

                for who in range(4):
                    for xs in range(nx):
                        flipped = left_at[k][who, layer, xs].T.reshape(nz, LEFT_BLOCKS[k], rows, tokens)
                        for n in range(LEFT_BLOCKS[k]):
                            turned[who, n, xs] = flipped[:, n]

        @pl.when(any_of(j, RIGHT_FIRST))
        def _():
            own_right(b, some_right).wait()
            pair_right(b, some_right).wait()
            passed_right(b, some_right).wait()

        @pl.when(j == 0)
        def _():
            held_right(b, some_right).wait()

        @pl.when(any_of(j, RIGHT_FIRST[1:]))
        def _():
            replica_right(b, some_right).wait_send()

        slot = lax.rem(i, ring)
        part = jnp.where(j == 2, 2, jnp.where(j < 5, y, 0))
        half = jnp.where(j < 2, j, jnp.where(j == 2, y, lax.rem(j + 1, 2)))
        tile = width // 2

        def columns(c, carry):
            source = pl.ds(pl.multiple_of(half * width + c * tile, tile), tile)
            acc = None
            for who in range(4):
                left = turned[who, part].reshape(nx * nz * rows, tokens)
                term = jnp.dot(left, right_at[who, b, :, source], preferred_element_type=jnp.float32)
                acc = term if acc is None else acc + term
            into = pl.ds(pl.multiple_of(c * tile, tile), tile)
            total[slot, :, :, :, into] = acc.reshape(nx, nz, rows, tile).astype(total.dtype)
            return carry

        lax.fori_loop(0, 2, columns, 0)

    def give(i, flow, device):
        @pl.when(i + SLOTS < pieces)
        def _():
            pl.semaphore_signal(credit.at[flow], inc=1, device_id=device, device_id_type=MESH)

    def spend(i, flow):
        @pl.when(i >= SLOTS)
        def _():
            pl.semaphore_wait(credit.at[flow], 1)

    def add(slot, xs, zs, value):
        where = (slot, xs, zs)
        total[where] = (total[where].astype(jnp.float32) + value.astype(jnp.float32)).astype(total.dtype)

    def x_copy(i, up, here):
        low, high = (here + 1, nx) if up else (0, here)
        side = 0 if (up or nx == 2) else 1
        return remote(
            total.at[lax.rem(i, ring), pl.ds(low, high - low)],
            x_in.at[lax.rem(i, SLOTS), side, pl.ds(low - (1 if up else 0), high - low)],
            x_sem.at[0 if up else 1, i],
            x_sem.at[2 if up else 3, i],
            to_x(1 if up else -1),
        )

    def z_copy(i, up, here):
        low, high = (here + 1, nz) if up else (0, here)
        into = zup_in if up else zdown_in
        sems = zup_sem if up else zdown_sem
        return remote(
            total.at[lax.rem(i, ring), x, pl.ds(low, high - low)],
            into.at[lax.rem(i, SLOTS), pl.ds(low - (1 if up else 0), high - low)],
            sems.at[0, i],
            sems.at[1, i],
            to_z(1 if up else -1),
        )

    def x_hop(i, h):
        slot, small = lax.rem(i, ring), lax.rem(i, SLOTS)
        for up in (True, False):
            here = h if up else nx - 1 - h
            side = 0 if (up or nx == 2) else 1

            @pl.when(x == here)
            def _():
                if h > 0:
                    x_copy(i, up, here - 1 if up else here + 1).wait_recv()
                    for target in range(here, nx) if up else range(here + 1):

                        def body(zs, carry):
                            add(slot, target, zs, x_in[small, side, target - (1 if up else 0), zs])
                            return carry

                        lax.fori_loop(0, nz, body, 0)
                    give(i, 0 if up else 1, to_x(-1 if up else 1))
                if h < nx - 1:
                    spend(i, 0 if up else 1)
                    x_copy(i, up, here).start()

    def z_hop(i, h):
        slot, small = lax.rem(i, ring), lax.rem(i, SLOTS)
        for up in (True, False):
            here = h if up else nz - 1 - h

            @pl.when(z == here)
            def _():
                if h > 0:
                    z_copy(i, up, here - 1 if up else here + 1).wait_recv()
                    into = zup_in if up else zdown_in

                    def body(target, carry):
                        add(slot, x, target, into[small, target - (1 if up else 0)])
                        return carry

                    lax.fori_loop(here if up else 0, nz if up else here + 1, body, 0)
                    give(i, 2 if up else 3, to_z(-1 if up else 1))
                if h < nz - 1:
                    spend(i, 2 if up else 3)
                    z_copy(i, up, here).start()

    def f_copy(i):
        return remote(
            total.at[lax.rem(i, ring), x, z], f_in.at[lax.rem(i, SLOTS)], f_sem.at[0, i], f_sem.at[1, i], to_y
        )

    def send_f(i):
        spend(i, 4)
        f_copy(i).start()

    def result_copy(i, replica, into):
        two = lax.rem(i, 2)
        return pltpu.make_async_copy(result.at[two, replica], into, result_sem.at[two, replica])

    def keep_result(i, replica):
        layer, j = place(i)
        for n in range(PIECES):
            for r in range(2):

                @pl.when((j == n) & (replica == r))
                def _():
                    which, part, column = piece_place(n, r)
                    into = outs[which].at[layer, pl.ds(part * rows, rows), pl.ds(column * width, width)]
                    result_copy(i, r, into).start()

    def result_kept(i):
        for r in range(2):
            result_copy(i, r, outs[5].at[0, :, pl.ds(0, width)]).wait()

    def finish(i):
        slot, small, two = lax.rem(i, ring), lax.rem(i, SLOTS), lax.rem(i, 2)
        f_copy(i).wait_recv()

        @pl.when(i >= 2)
        def _():
            result_kept(i - 2)

        result[two, y] = total[slot, x, z].astype(jnp.float32)
        result[two, 1 - y] = f_in[small].astype(jnp.float32)
        give(i, 4, to_y)
        keep_result(i, 0)
        keep_result(i, 1)
        f_copy(i).wait_send()
        for here in range(nx):

            @pl.when(x == here)
            def _():
                if here < nx - 1:
                    x_copy(i, True, here).wait_send()
                if here > 0:
                    x_copy(i, False, here).wait_send()

        for here in range(nz):

            @pl.when(z == here)
            def _():
                if here < nz - 1:
                    z_copy(i, True, here).wait_send()
                if here > 0:
                    z_copy(i, False, here).wait_send()

    def gain_copy(n, source, device):
        return remote(source, gain_in.at[n], gain_sem.at[0, n], gain_sem.at[1, n], device)

    def gain_start():
        copy = pltpu.make_async_copy(gains, gain_in.at[0], gain_sem.at[0, 0])
        copy.start()
        copy.wait()
        gain_copy(1, gain_in.at[0], to_core).start()

    def gain_pair():
        gain_copy(1, gain_in.at[0], to_core).wait()
        gain_up[0] = gain_in[0] + gain_in[1]
        gain_copy(2, gain_up.at[0], to_y).start()

    def gain_y():
        gain_copy(2, gain_up.at[0], to_y).wait()
        gain_in[0] = gain_up[0] + gain_in[2]

    def gain_hop(h, n, here, to, first, level):
        for up in (True, False):
            buffer = (gain_up if up else gain_down).at[level]
            slot = first if up else first + 1

            @pl.when(here == (h if up else n - 1 - h))
            def _():
                buffer[...] = gain_in[0]
                if h > 0:
                    gain_copy(slot, buffer, to(1 if up else -1)).wait_recv()
                    buffer[...] = gain_in[0] + gain_in[slot]
                if h < n - 1:
                    gain_copy(slot, buffer, to(1 if up else -1)).start()

    def gain_line(n, here, to, first, level):
        @pl.when(here < n - 1)
        def _():
            gain_copy(first, gain_up.at[level], to(1)).wait_send()

        @pl.when(here > 0)
        def _():
            gain_copy(first + 1, gain_down.at[level], to(-1)).wait_send()

        gain_in[0] = gain_up[level] + gain_down[level] - gain_in[0]

    def gain_end():
        copy = pltpu.make_async_copy(gain_in.at[0], gains_out, gain_sem.at[0, 0])
        copy.start()
        copy.wait()

    steps = [gain_start, gain_pair, gain_y]
    for h in range(nx):
        steps.append(functools.partial(gain_hop, h, nx, x, to_x, 3, 1))
    steps.append(functools.partial(gain_line, nx, x, to_x, 3, 1))
    for h in range(nz):
        steps.append(functools.partial(gain_hop, h, nz, z, to_z, 5, 2))
    steps.append(functools.partial(gain_line, nz, z, to_z, 5, 2))
    steps.append(gain_end)

    plan = [[fetch], [], [], [forward], [], [product], [functools.partial(x_hop, h=0)]]
    for h in range(1, nx):
        plan += [[], [functools.partial(x_hop, h=h)]]
    plan[-1].append(functools.partial(z_hop, h=0))
    for h in range(1, nz):
        plan.append([functools.partial(z_hop, h=h)])
    plan[-1].append(send_f)
    plan.append([finish])

    def tick(t, carry):
        for depth in [*range(6, len(plan)), 0, 3, 5]:
            if not plan[depth]:
                continue
            i = t - depth

            @pl.when((i >= 0) & (i < pieces))
            def _():
                for stage in plan[depth]:
                    stage(i)

        for n, step in enumerate(steps):
            pl.when(t == n)(step)
        return carry

    lax.fori_loop(0, pieces + len(plan) - 1, tick, 0)
    result_kept(pieces - 2)
    result_kept(pieces - 1)


def reduce_weights(operands, gains, nx, nz, collective_id):
    layers = len(operands)
    flat = [a for layer in operands for a in layer]
    tokens, wide = operands[0][8].shape
    rows, width = wide // (2 * nx * nz), wide // 2
    pieces = layers * PIECES
    ring = 2 * nx + nz + 1
    sides = 1 if nx == 2 else 2
    low = jnp.bfloat16
    dma = pltpu.SemaphoreType.DMA
    anywhere = pl.BlockSpec(memory_space=pl.ANY)
    return pl.pallas_call(
        functools.partial(reduce_kernel, nx, nz, layers),
        out_shape=[
            jax.ShapeDtypeStruct((layers, rows * below, wide * across), jnp.float32) for across, below in WEIGHT_BLOCKS
        ]
        + [jax.ShapeDtypeStruct(gains.shape, gains.dtype)],
        in_specs=[anywhere] * (len(flat) + 1),
        out_specs=[anywhere] * (len(WEIGHT_BLOCKS) + 1),
        scratch_shapes=[pltpu.VMEM((4, layers, nx, tokens, nz * n * rows), low) for n in LEFT_BLOCKS]
        + [
            pltpu.VMEM((4, layers * RIGHTS, tokens, wide), low),
            pltpu.VMEM((4, max(LEFT_BLOCKS), nx, nz, rows, tokens), low),
            pltpu.VMEM((ring, nx, nz, rows, width), low),
            pltpu.VMEM((SLOTS, sides, nx - 1, nz, rows, width), low),
            pltpu.VMEM((SLOTS, nz - 1, rows, width), low),
            pltpu.VMEM((SLOTS, nz - 1, rows, width), low),
            pltpu.VMEM((SLOTS, rows, width), low),
            pltpu.VMEM((2, 2, rows, width), jnp.float32),
            pltpu.VMEM((7, *gains.shape), gains.dtype),
            pltpu.VMEM((3, *gains.shape), gains.dtype),
            pltpu.VMEM((3, *gains.shape), gains.dtype),
            dma((7, layers * 4, nx)),
            dma((7, layers * RIGHTS)),
            dma((4, pieces)),
            dma((2, pieces)),
            dma((2, pieces)),
            dma((2, pieces)),
            dma((2, 2)),
            dma((2, 7)),
            pltpu.SemaphoreType.REGULAR((5,)),
        ],
        compiler_params=pltpu.CompilerParams(
            collective_id=collective_id, has_side_effects=True, vmem_limit_bytes=56 * 1024 * 1024
        ),
    )(*flat, gains)


CHUNK_HEADS = 2
CHUNKS = KEYVALUE_HEADS // CHUNK_HEADS
CHUNK = CHUNK_HEADS * HEAD_SIZE
GROUP = QUERY_HEADS // KEYVALUE_HEADS
SCORE_SCALE = 1.0 / math.sqrt(HEAD_SIZE)


def group_place(m):
    y, shard, z = lax.axis_index("rep"), lax.axis_index("shard"), lax.axis_index("ctx")
    core, zz = lax.rem(shard, 2), lax.rem(z, m)
    to_core = (y, shard + 1 - 2 * core, z)

    def to_line(step):
        return (y, shard, z + step)

    return core, zz, to_core, to_line


def greet(m, zz, to_core, to_line):
    barrier = pltpu.get_barrier_semaphore()
    pl.semaphore_signal(barrier, inc=1, device_id=to_core, device_id_type=MESH)
    for here, there in ((zz > 0, to_line(-1)), (zz < m - 1, to_line(1))):

        @pl.when(here)
        def _():
            pl.semaphore_signal(barrier, inc=1, device_id=there, device_id_type=MESH)

    pl.semaphore_wait(barrier, 1 + (zz > 0).astype(jnp.int32) + (zz < m - 1).astype(jnp.int32))


def remote(src, dst, send_sem, recv_sem, device):
    return pltpu.make_async_remote_copy(
        src_ref=src, dst_ref=dst, send_sem=send_sem, recv_sem=recv_sem, device_id=device, device_id_type=MESH
    )


def head_prepare(v, gain, cosine, sine):
    v = v * lax.rsqrt(jnp.mean(v * v, axis=-1, keepdims=True) + NORM_EPS) * gain
    return v * cosine + pltpu.roll(v, HEAD_SIZE // 2, 1) * sine


def head_prepare_back(grad, v, gain, cosine, sine):
    grad = grad * cosine + pltpu.roll(grad * sine, HEAD_SIZE // 2, 1)
    r = lax.rsqrt(jnp.mean(v * v, axis=-1, keepdims=True) + NORM_EPS)
    unit = v * r
    by_gain = jnp.sum(grad * unit, axis=0, keepdims=True)
    grad = grad * gain
    return r * (grad - unit * jnp.mean(grad * unit, axis=-1, keepdims=True)), by_gain


def attend_kernel(m, qp, kp, v, q_gain, k_gain, cosine, sine, place_q, segment_k, q_out, kv, att, att_low, lse, core_sem, line_sem, core_out, line_out):
    tokens, length = qp.shape[0], kv.shape[0]
    core, zz, to_core, to_line = group_place(m)
    greet(m, zz, to_core, to_line)
    cos, sin = cosine[...], sine[...]

    def part(j, source_zz, of_core=core):
        rows = pl.multiple_of((source_zz + of_core * m) * tokens, 16)
        return kv.at[pl.ds(rows, tokens), pl.ds(pl.multiple_of(j * 2 * CHUNK, 128), 2 * CHUNK)]

    def core_copy(j, source_zz, of_core=core):
        ref = part(j, source_zz, of_core)
        return remote(ref, ref, core_out.at[j, source_zz], core_sem.at[j, source_zz], to_core)

    def line_copy(j, source_zz, step):
        ref = part(j, source_zz)
        return remote(ref, ref, line_out.at[0 if step > 0 else 1, j, source_zz], line_sem.at[j, source_zz], to_line(step))

    def onward(j, source_zz, step, do):
        @pl.when((zz + step >= 0) & (zz + step < m))
        def _():
            do(line_copy(j, source_zz, step))

    begin, ended = lambda copy: copy.start(), lambda copy: copy.wait_send()
    own_rows = pl.ds(pl.multiple_of((zz + core * m) * tokens, 16), tokens)
    for j in range(CHUNKS):
        for n in range(CHUNK_HEADS):
            h = j * CHUNK_HEADS + n
            ready = head_prepare(kp[:, h * HEAD_SIZE : (h + 1) * HEAD_SIZE], k_gain[...], cos, sin)
            kv[own_rows, j * 2 * CHUNK + n * HEAD_SIZE : j * 2 * CHUNK + (n + 1) * HEAD_SIZE] = ready.astype(kv.dtype)
        kv[own_rows, j * 2 * CHUNK + CHUNK : (j + 1) * 2 * CHUNK] = v[:, j * CHUNK : (j + 1) * CHUNK]
        for step in (1, -1):
            onward(j, zz, step, begin)
        core_copy(j, zz).start()
    for h in range(QUERY_HEADS):
        at = slice(h * HEAD_SIZE, (h + 1) * HEAD_SIZE)
        q_out[:, at] = head_prepare(qp[:, at], q_gain[...], cos, sin).astype(q_out.dtype)

    def arrivals(j):
        for d in range(1, m):
            for step in (1, -1):
                source = zz - step * d

                @pl.when((source >= 0) & (source < m))
                def _():
                    line_copy(j, source, step).wait_recv()
                    onward(j, source, step, begin)
                    core_copy(j, source).start()

    segment_q = place_q[:, 0:1]
    index_q = place_q[:, 1:2]
    index_k = lax.broadcasted_iota(jnp.int32, (tokens, length), 1)
    allowed = (segment_q == segment_k[...]) & (index_q >= index_k)
    lane = lax.broadcasted_iota(jnp.int32, (tokens, HEAD_SIZE), 1)

    def attend(j):
        for source in range(m):
            core_copy(j, source, 1 - core).wait_recv()
        for n in range(CHUNK_HEADS):
            keys = kv[:, pl.ds(pl.multiple_of(j * 2 * CHUNK + n * HEAD_SIZE, 128), HEAD_SIZE)]
            values = kv[:, pl.ds(pl.multiple_of(j * 2 * CHUNK + CHUNK + n * HEAD_SIZE, 128), HEAD_SIZE)]
            for g in range(GROUP):
                h = (j * CHUNK_HEADS + n) * GROUP + g
                at = pl.ds(pl.multiple_of(h * HEAD_SIZE, 128), HEAD_SIZE)
                s = lax.dot_general(q_out[:, at], keys, (((1,), (1,)), ((), ())), preferred_element_type=jnp.float32)
                s = jnp.where(allowed, s * SCORE_SCALE, VERY_NEGATIVE)
                top = jnp.max(s, axis=-1, keepdims=True)
                p = jnp.exp(s - top)
                norm = jnp.sum(p, axis=-1, keepdims=True)
                o = jnp.dot(p.astype(values.dtype), values, preferred_element_type=jnp.float32) / norm
                att[:, at] = o
                att_low[:, at] = o.astype(att_low.dtype)
                lse[...] = jnp.where(lane == h, top + jnp.log(norm), lse[...])

    lse[...] = jnp.zeros_like(lse)

    def tick(t, carry):
        @pl.when(t < CHUNKS)
        def _():
            arrivals(t)

        @pl.when(t > 0)
        def _():
            attend(t - 1)

        return carry

    lax.fori_loop(0, CHUNKS + 1, tick, 0)

    def leave(j, carry):
        for source in range(m):
            core_copy(j, source).wait_send()
        for d in range(m):
            for step in (1, -1):
                source = zz - step * d

                @pl.when((source >= 0) & (source < m))
                def _():
                    onward(j, source, step, ended)

        return carry

    lax.fori_loop(0, CHUNKS, leave, 0)


def attend(m, qp, kp, v, q_gain, k_gain, cosine, sine, place_q, segment_k, collective_id):
    tokens = qp.shape[0]
    length = 2 * m * tokens
    low = jnp.bfloat16
    dma = pltpu.SemaphoreType.DMA
    vmem = pl.BlockSpec(memory_space=pltpu.VMEM)
    return pl.pallas_call(
        functools.partial(attend_kernel, m),
        out_shape=[
            jax.ShapeDtypeStruct((tokens, QD), low),
            jax.ShapeDtypeStruct((length, 2 * KEY_FEATURES), low),
            jax.ShapeDtypeStruct((tokens, QD), jnp.float32),
            jax.ShapeDtypeStruct((tokens, QD), low),
            jax.ShapeDtypeStruct((tokens, HEAD_SIZE), jnp.float32),
        ],
        in_specs=[vmem] * 9,
        out_specs=[vmem] * 5,
        scratch_shapes=[dma((CHUNKS, m)), dma((CHUNKS, m)), dma((CHUNKS, m)), dma((2, CHUNKS, m))],
        compiler_params=pltpu.CompilerParams(
            collective_id=collective_id, has_side_effects=True, vmem_limit_bytes=48 * 1024 * 1024
        ),
    )(qp, kp, v, q_gain, k_gain, cosine, sine, place_q, segment_k)


def attend_back_kernel(m, q, kv, d_att, att, lse, qp, kp, q_gain, k_gain, cosine, sine, place_q, segment_k, dq_low, dk_low, dv_low, gains, partial, core_in, up_in, down_in, core_sem, up_sem, down_sem):
    tokens, length = q.shape[0], kv.shape[0]
    core, zz, to_core, to_line = group_place(m)
    greet(m, zz, to_core, to_line)
    cos, sin = cosine[...], sine[...]
    segment_q = place_q[:, 0:1]
    index_q = place_q[:, 1:2]
    index_k = lax.broadcasted_iota(jnp.int32, (tokens, length), 1)
    allowed = (segment_q == segment_k[...]) & (index_q >= index_k)
    lane = lax.broadcasted_iota(jnp.int32, (tokens, HEAD_SIZE), 1)
    gains[...] = jnp.zeros_like(gains)
    over_rows = (((0,), (0,)), ((), ()))
    over_columns = (((1,), (1,)), ((), ()))

    def core_copy(j):
        return remote(partial.at[j, 1 - core], core_in.at[j], core_sem.at[0, j], core_sem.at[1, j], to_core)

    def line_copy(j, up, here):
        low, high = (here + 1, m) if up else (0, here)
        into, sems = (up_in, up_sem) if up else (down_in, down_sem)
        return remote(
            partial.at[j, core, pl.ds(low, high - low)],
            into.at[j, pl.ds(low - (1 if up else 0), high - low)],
            sems.at[0, j],
            sems.at[1, j],
            to_line(1 if up else -1),
        )

    def add(j, place, value):
        partial[j, core, place] = (partial[j, core, place].astype(jnp.float32) + value.astype(jnp.float32)).astype(partial.dtype)

    def compute(j):
        for n in range(CHUNK_HEADS):
            keys = kv[:, pl.ds(pl.multiple_of(j * 2 * CHUNK + n * HEAD_SIZE, 128), HEAD_SIZE)]
            values = kv[:, pl.ds(pl.multiple_of(j * 2 * CHUNK + CHUNK + n * HEAD_SIZE, 128), HEAD_SIZE)]
            dk = dv = None
            for g in range(GROUP):
                h = (j * CHUNK_HEADS + n) * GROUP + g
                at = pl.ds(pl.multiple_of(h * HEAD_SIZE, 128), HEAD_SIZE)
                queries, grad = q[:, at], d_att[:, at]
                total = jnp.sum(jnp.where(lane == h, lse[...], 0.0), axis=-1, keepdims=True)
                delta = jnp.sum(grad.astype(jnp.float32) * att[:, at], axis=-1, keepdims=True)
                s = lax.dot_general(queries, keys, over_columns, preferred_element_type=jnp.float32)
                p = jnp.exp(jnp.where(allowed, s * SCORE_SCALE, VERY_NEGATIVE) - total)
                dp = lax.dot_general(grad, values, over_columns, preferred_element_type=jnp.float32)
                ds = (p * (dp - delta)).astype(queries.dtype)
                dq = jnp.dot(ds, keys, preferred_element_type=jnp.float32) * SCORE_SCALE
                here_k = lax.dot_general(ds, queries, over_rows, preferred_element_type=jnp.float32)
                here_v = lax.dot_general(p.astype(grad.dtype), grad, over_rows, preferred_element_type=jnp.float32)
                dk = here_k if dk is None else dk + here_k
                dv = here_v if dv is None else dv + here_v
                by_head, by_gain = head_prepare_back(dq, qp[:, at], q_gain[...], cos, sin)
                dq_low[:, at] = by_head.astype(dq_low.dtype)
                gains[0:1] += by_gain
            first = n * HEAD_SIZE
            partial[j, :, :, :, first : first + HEAD_SIZE] = (dk * SCORE_SCALE).astype(partial.dtype).reshape(2, m, tokens, HEAD_SIZE)
            first += CHUNK
            partial[j, :, :, :, first : first + HEAD_SIZE] = dv.astype(partial.dtype).reshape(2, m, tokens, HEAD_SIZE)
        core_copy(j).start()

    def take_core(j):
        core_copy(j).wait_recv()
        for place in range(m):
            add(j, place, core_in[j, place])

    def hop(j, h):
        for up in (True, False):
            here = h if up else m - 1 - h

            @pl.when(zz == here)
            def _():
                if h > 0:
                    line_copy(j, up, here - 1 if up else here + 1).wait_recv()
                    into = up_in if up else down_in
                    for place in range(here, m) if up else range(here + 1):
                        add(j, place, into[j, place - (1 if up else 0)])
                if h < m - 1:
                    line_copy(j, up, here).start()

    def finish(j):
        for n in range(CHUNK_HEADS):
            at = pl.ds(pl.multiple_of((j * CHUNK_HEADS + n) * HEAD_SIZE, 128), HEAD_SIZE)
            grad = partial[j, core, zz, :, n * HEAD_SIZE : (n + 1) * HEAD_SIZE].astype(jnp.float32)
            by_head, by_gain = head_prepare_back(grad, kp[:, at], k_gain[...], cos, sin)
            dk_low[:, at] = by_head.astype(dk_low.dtype)
            gains[1:2] += by_gain
        at = pl.ds(pl.multiple_of(j * CHUNK, 128), CHUNK)
        dv_low[:, at] = partial[j, core, zz, :, CHUNK:]
        core_copy(j).wait_send()
        for here in range(m):

            @pl.when(zz == here)
            def _():
                if here < m - 1:
                    line_copy(j, True, here).wait_send()
                if here > 0:
                    line_copy(j, False, here).wait_send()

    plan = [[compute], [take_core, functools.partial(hop, h=0)]]
    for h in range(1, m):
        plan.append([functools.partial(hop, h=h)])
    plan[-1].append(finish)

    def tick(t, carry):
        for depth in [*range(1, len(plan)), 0]:
            j = t - depth

            @pl.when((j >= 0) & (j < CHUNKS))
            def _():
                for stage in plan[depth]:
                    stage(j)

        return carry

    lax.fori_loop(0, CHUNKS + len(plan) - 1, tick, 0)


def attend_back(m, q, kv, d_att, att, lse, qp, kp, q_gain, k_gain, cosine, sine, place_q, segment_k, collective_id):
    tokens = q.shape[0]
    low = jnp.bfloat16
    dma = pltpu.SemaphoreType.DMA
    vmem = pl.BlockSpec(memory_space=pltpu.VMEM)
    return pl.pallas_call(
        functools.partial(attend_back_kernel, m),
        out_shape=[
            jax.ShapeDtypeStruct((tokens, QD), low),
            jax.ShapeDtypeStruct((tokens, KEY_FEATURES), low),
            jax.ShapeDtypeStruct((tokens, KEY_FEATURES), low),
            jax.ShapeDtypeStruct((8, HEAD_SIZE), jnp.float32),
        ],
        in_specs=[vmem] * 13,
        out_specs=[vmem] * 4,
        scratch_shapes=[
            pltpu.VMEM((CHUNKS, 2, m, tokens, 2 * CHUNK), low),
            pltpu.VMEM((CHUNKS, m, tokens, 2 * CHUNK), low),
            pltpu.VMEM((CHUNKS, max(m - 1, 1), tokens, 2 * CHUNK), low),
            pltpu.VMEM((CHUNKS, max(m - 1, 1), tokens, 2 * CHUNK), low),
            dma((2, CHUNKS)),
            dma((2, CHUNKS)),
            dma((2, CHUNKS)),
        ],
        compiler_params=pltpu.CompilerParams(
            collective_id=collective_id, has_side_effects=True, vmem_limit_bytes=48 * 1024 * 1024
        ),
    )(q, kv, d_att, att, lse, qp, kp, q_gain, k_gain, cosine, sine, place_q, segment_k)


def segment_of(doc_ends, token_index):
    return jnp.sum((token_index[:, None] >= doc_ends[None, :]).astype(jnp.int32), axis=1)


def doc_layout(doc_ends, token_index):
    token_segment = segment_of(doc_ends, token_index)
    starts = jnp.concatenate([jnp.zeros((1,), jnp.int32), doc_ends])
    labels = jnp.arange(starts.shape[0], dtype=jnp.int32)
    doc_begin = jnp.sum(
        jnp.where(token_segment[:, None] == labels[None, :], starts[None, :], 0), axis=1
    )
    return (token_segment, token_index - doc_begin)


def rotary(positions, head_width):
    middle = head_width // 2
    inv_rates = jnp.exp(
        jnp.arange(middle, dtype=jnp.float32) * jnp.float32(-2.0 * math.log(ROPE_BASE) / head_width)
    )
    angles = positions.astype(jnp.float32)[:, None] * inv_rates[None, :]
    cosine = jnp.cos(angles)
    sine = jnp.sin(angles)
    return (jnp.concatenate([cosine, cosine], axis=1), jnp.concatenate([-sine, sine], axis=1))


def rms_scale(values, gain_vec):
    return (
        values * lax.rsqrt(jnp.mean(values * values, axis=-1, keepdims=True) + NORM_EPS) * gain_vec
    )


def swiglu(gate_pre, upward):
    return jax.nn.silu(gate_pre) * upward


def product(left, right):
    return jnp.dot(left, right, preferred_element_type=jnp.float32)


def product_back(grad, right):
    return lax.dot_general(grad, right, (((1,), (1,)), ((), ())), preferred_element_type=jnp.float32)


def over_replica(values):
    return lax.ppermute(values, "rep", [(0, 1), (1, 0)])


def after(value, others):
    value, *others = lax.optimization_barrier((value, *others))
    return value, others


def head_gain(gain):
    return gain.astype(jnp.float32)[None, :]


def layer_ahead(hidden, weights, tables, m, which_layer, waiting):
    (
        gain_first,
        query_weight,
        key_matrix,
        value_matrix,
        gain_query,
        gain_key,
        output_weight,
        gain_second,
        gate_weight,
        up_weight,
        down_weight,
    ) = weights
    normalized_rows = rms_scale(hidden, gain_first.astype(jnp.float32)).astype(jnp.bfloat16)
    key_projection = product(normalized_rows, key_matrix)
    rows_of_values = product(normalized_rows, value_matrix).astype(jnp.bfloat16)
    query_proj = product(normalized_rows, query_weight)
    waiting.append(over_replica(normalized_rows))
    query_rows, keys_values, attended_rows, attended_low, log_sum = attend(
        m, query_proj, key_projection, rows_of_values, head_gain(gain_query), head_gain(gain_key), *tables, 2
    )
    attended_low, before = after(attended_low, waiting if which_layer == 0 else waiting[:3])
    waiting[: len(before)] = before
    waiting.append(over_replica(attended_low))
    hidden_mid = hidden + product(attended_low, output_weight)
    normed_two = rms_scale(hidden_mid, gain_second.astype(jnp.float32)).astype(jnp.bfloat16)
    waiting.append(over_replica(normed_two))
    gate_pre = product(normed_two, gate_weight)
    upward = product(normed_two, up_weight)
    activated = swiglu(gate_pre, upward).astype(jnp.bfloat16)
    waiting.append(over_replica(activated))
    hidden_out = hidden_mid + product(activated, down_weight)
    saved = (
        hidden,
        normalized_rows,
        query_proj,
        key_projection,
        query_rows,
        keys_values,
        attended_rows,
        attended_low,
        log_sum,
        hidden_mid,
        normed_two,
        gate_pre,
        upward,
        activated,
    )
    return (hidden_out, saved)


def layer_back(upstream, weights, saved, tables, m, which_layer, waiting):
    (
        gain_first,
        query_weight,
        key_matrix,
        value_matrix,
        gain_query,
        gain_key,
        output_weight,
        gain_second,
        gate_weight,
        up_weight,
        down_weight,
    ) = weights
    (
        hidden,
        normalized_rows,
        query_proj,
        key_projection,
        query_rows,
        keys_values,
        attended_rows,
        attended_low,
        log_sum,
        hidden_mid,
        normed_two,
        gate_pre,
        upward,
        activated,
    ) = saved
    branch_low = upstream.astype(jnp.bfloat16)
    waiting.append(over_replica(branch_low))
    grad_act = product_back(branch_low, down_weight)
    ignored, swiglu_back = jax.vjp(swiglu, gate_pre, upward)
    grad_gate_pre, grad_upward = swiglu_back(grad_act)
    gate_low = grad_gate_pre.astype(jnp.bfloat16)
    up_low = grad_upward.astype(jnp.bfloat16)
    grad_normed_two = product_back(gate_low, gate_weight) + product_back(up_low, up_weight)
    ignored, second_back = jax.vjp(rms_scale, hidden_mid, gain_second.astype(jnp.float32))
    grad_mid, grad_gain_second = second_back(grad_normed_two)
    upstream_mid = upstream + grad_mid
    attn_low = upstream_mid.astype(jnp.bfloat16)
    grad_attended = product_back(attn_low, output_weight).astype(jnp.bfloat16)
    ready = 5 if which_layer == 1 else 8
    grad_attended, waiting[:ready] = after(grad_attended, waiting[:ready])
    query_low, key_low, value_low, head_gains = attend_back(
        m,
        query_rows,
        keys_values,
        grad_attended,
        attended_rows,
        log_sum,
        query_proj,
        key_projection,
        head_gain(gain_query),
        head_gain(gain_key),
        *tables,
        3,
    )
    ready = 7 if which_layer == 1 else 10
    query_low, waiting[:ready] = after(query_low, waiting[:ready])
    grad_normed = product_back(query_low, query_weight)
    grad_normed = grad_normed + product_back(key_low, key_matrix)
    grad_normed = grad_normed + product_back(value_low, value_matrix)
    ignored, first_back = jax.vjp(rms_scale, hidden, gain_first.astype(jnp.float32))
    grad_hidden, grad_gain_first = first_back(grad_normed)
    lefts = (activated, attended_low, normed_two, normalized_rows)
    rights = (branch_low, attn_low, gate_low, up_low, query_low, key_low, value_low)
    gains = (grad_gain_first, head_gains[0], head_gains[1], grad_gain_second)
    return (upstream_mid + grad_hidden, (lefts, rights, gains))


def near_rows(rows, share):
    return min(rows, -(-int(rows * share) // 16) * 16)


def gather_all(parts):
    nx, nz = lax.axis_size("shard") // 2, lax.axis_size("ctx")
    gains = (parts[0], parts[4], parts[5], parts[7])
    flat = jnp.concatenate([g.reshape(-1) for g in gains])
    small = jnp.zeros((16 * 128,), flat.dtype).at[: flat.shape[0]].set(flat).reshape(16, 128)
    big = (1, 2, 3, 6, 8, 9, 10)
    shares = (0.75, 0.75, 0.75, 0.6, 0.5, 0.75, 0.55)
    shards, nears = [small], [16]
    for which_layer in range(LAYERS):
        for member, share in zip(big, shares):
            shards.append(parts[member][which_layer])
            nears.append(near_rows(parts[member].shape[1], share))
    wholes = gather_weights(shards, nears, nx, nz, 0)
    every = wholes[0].reshape(2 * nx * nz, 16 * 128)[:, : flat.shape[0]]
    out, used = [[None] * 11 for _ in range(LAYERS)], 0
    for member, g in zip((0, 4, 5, 7), gains):
        here = every[:, used : used + g.size].reshape(-1, LAYERS, g.shape[1])
        used += g.size
        for which_layer in range(LAYERS):
            out[which_layer][member] = here[:, which_layer].reshape(-1)
    for which_layer in range(LAYERS):
        for i, member in enumerate(big):
            out[which_layer][member] = wholes[1 + which_layer * 7 + i]
    return out


def weight_gradients(operands):
    nx, nz = lax.axis_size("shard") // 2, lax.axis_size("ctx")
    shards = 2 * nx * nz
    flat = jnp.concatenate([g for _, gains in operands for g in gains])
    size = -(-flat.shape[0] // 1024) * 1024
    padded = jnp.zeros((size,), flat.dtype).at[: flat.shape[0]].set(flat).reshape(-1, 128)
    *grads, summed = reduce_weights([members for members, _ in operands], padded, nx, nz, 1)
    summed = summed.reshape(-1)[: flat.shape[0]].reshape(LAYERS, -1)
    here = lax.axis_index("shard") * nz + lax.axis_index("ctx")
    small, used = [], 0
    for size in (D, HEAD_SIZE, HEAD_SIZE, D):
        own = size // shards
        small.append(lax.dynamic_slice_in_dim(summed, used + here * own, own, axis=1))
        used += size
    down, output, gate, up, query, key, value = grads
    return (small[0], query, key, value, small[1], small[2], output, small[3], gate, up, down)


def local(
    tokens,
    lengths,
    norm_one,
    w_query,
    w_key,
    w_value,
    query_gain,
    key_gain,
    w_output,
    norm_two,
    w_gate,
    w_up,
    w_down,
    cotangent,
):
    token_rows = tokens.shape[1]
    nx, nz = lax.axis_size("shard") // 2, lax.axis_size("ctx")
    m = nz // 2
    pairs = []
    for x in range(nx):
        for z in range(m):
            low, high = (2 * x + 1) * nz + z, 2 * x * nz + z + m
            same = (2 * x * nz + z, (2 * x + 1) * nz + z + m)
            pairs += [(low, high), (high, low)] + [(s, s) for s in same]

    def swap(values):
        return lax.ppermute(values, ("shard", "ctx"), pairs)

    tokens, lengths, cotangent = swap(tokens), swap(lengths), swap(cotangent)
    block = lax.axis_index("ctx") % m + (lax.axis_index("shard") % 2) * m
    token_index = block * token_rows + jnp.arange(token_rows, dtype=jnp.int32)
    doc_lengths = lengths[0]
    upto = jnp.arange(doc_lengths.shape[0])
    doc_ends = jnp.sum(jnp.where(upto[:, None] >= upto[None, :], doc_lengths[None, :], 0), axis=1)
    token_segment, positions = doc_layout(doc_ends, token_index)
    cosine, sine = rotary(positions, HEAD_SIZE)
    key_segment = segment_of(doc_ends, jnp.arange(token_rows * nz, dtype=jnp.int32))
    tables = (cosine, sine, jnp.stack([token_segment, token_index], axis=1), key_segment[None, :])
    gathered = gather_all(
        (norm_one, w_query, w_key, w_value, query_gain, key_gain, w_output, norm_two, w_gate, w_up, w_down)
    )
    hidden = tokens[0].astype(jnp.float32)
    stored, waiting = [], []
    for which_layer in range(LAYERS):
        hidden, saved = layer_ahead(hidden, gathered[which_layer], tables, m, which_layer, waiting)
        stored.append(saved)
    output = swap(hidden.astype(jnp.bfloat16))[None]
    live_mask = (token_segment < doc_lengths.shape[0]).astype(jnp.float32)
    upstream = cotangent[0].astype(jnp.float32) * live_mask[:, None]
    operands = [None] * LAYERS
    for which_layer in reversed(range(LAYERS)):
        upstream, operands[which_layer] = layer_back(
            upstream, gathered[which_layer], stored[which_layer], tables, m, which_layer, waiting
        )
    grad_tokens = swap(upstream.astype(jnp.bfloat16))[None]
    for which_layer, (lefts, rights, gains) in enumerate(operands):
        normed, attended, normed_two, activated = waiting[which_layer * 4 : which_layer * 4 + 4]
        theirs = (activated, attended, normed_two, normed)
        operands[which_layer] = (lefts + theirs + rights + (waiting[9 - which_layer],), gains)
    return (output, grad_tokens) + weight_gradients(operands)


def solution(mesh):
    return jax.shard_map(
        local,
        mesh=mesh,
        in_specs=(
            P(("rep", "shard"), "ctx", None),
            P(("rep", "shard"), None),
            P(None, ("shard", "ctx")),
            P(None, ("shard", "ctx"), None),
            P(None, ("shard", "ctx"), None),
            P(None, ("shard", "ctx"), None),
            P(None, ("shard", "ctx")),
            P(None, ("shard", "ctx")),
            P(None, ("shard", "ctx"), None),
            P(None, ("shard", "ctx")),
            P(None, ("shard", "ctx"), None),
            P(None, ("shard", "ctx"), None),
            P(None, ("shard", "ctx"), None),
            P(("rep", "shard"), "ctx", None),
        ),
        out_specs=(
            P(("rep", "shard"), "ctx", None),
            P(("rep", "shard"), "ctx", None),
            P(None, ("shard", "ctx")),
            P(None, ("shard", "ctx"), None),
            P(None, ("shard", "ctx"), None),
            P(None, ("shard", "ctx"), None),
            P(None, ("shard", "ctx")),
            P(None, ("shard", "ctx")),
            P(None, ("shard", "ctx"), None),
            P(None, ("shard", "ctx")),
            P(None, ("shard", "ctx"), None),
            P(None, ("shard", "ctx"), None),
            P(None, ("shard", "ctx"), None),
        ),
        check_vma=False,
    )
```

```python
import functools
import math

import jax
import jax.numpy as jnp
from jax import lax
from jax.experimental import pallas as pl
from jax.experimental.pallas import tpu as pltpu
from jax.sharding import PartitionSpec as P

D = 1024
QUERY_HEADS = 16
KEYVALUE_HEADS = 8
HEAD_SIZE = 128
LAYERS = 2
QD = 2048
KEY_FEATURES = 1024


NORM_EPS = 1e-06
ROPE_BASE = 1000000.0
VERY_NEGATIVE = -1e30
MESH = pl.DeviceIdType.MESH


CHUNK_HEADS = 2
CHUNKS = KEYVALUE_HEADS // CHUNK_HEADS
CHUNK = CHUNK_HEADS * HEAD_SIZE
GROUP = QUERY_HEADS // KEYVALUE_HEADS
SCORE_SCALE = 1.0 / math.sqrt(HEAD_SIZE)


def group_place(m):
    y, shard, z = lax.axis_index("rep"), lax.axis_index("shard"), lax.axis_index("ctx")
    core, zz = lax.rem(shard, 2), lax.rem(z, m)
    to_core = (y, shard + 1 - 2 * core, z)

    def to_line(step):
        return (y, shard, z + step)

    return core, zz, to_core, to_line


def greet(m, zz, to_core, to_line):
    barrier = pltpu.get_barrier_semaphore()
    pl.semaphore_signal(barrier, inc=1, device_id=to_core, device_id_type=MESH)
    for here, there in ((zz > 0, to_line(-1)), (zz < m - 1, to_line(1))):

        @pl.when(here)
        def _():
            pl.semaphore_signal(barrier, inc=1, device_id=there, device_id_type=MESH)

    pl.semaphore_wait(barrier, 1 + (zz > 0).astype(jnp.int32) + (zz < m - 1).astype(jnp.int32))


def remote(src, dst, send_sem, recv_sem, device):
    return pltpu.make_async_remote_copy(
        src_ref=src, dst_ref=dst, send_sem=send_sem, recv_sem=recv_sem, device_id=device, device_id_type=MESH
    )


def head_prepare(v, gain, cosine, sine):
    v = v * lax.rsqrt(jnp.mean(v * v, axis=-1, keepdims=True) + NORM_EPS) * gain
    return v * cosine + pltpu.roll(v, HEAD_SIZE // 2, 1) * sine


def head_prepare_back(grad, v, gain, cosine, sine):
    grad = grad * cosine + pltpu.roll(grad * sine, HEAD_SIZE // 2, 1)
    r = lax.rsqrt(jnp.mean(v * v, axis=-1, keepdims=True) + NORM_EPS)
    unit = v * r
    by_gain = jnp.sum(grad * unit, axis=0, keepdims=True)
    grad = grad * gain
    return r * (grad - unit * jnp.mean(grad * unit, axis=-1, keepdims=True)), by_gain


def attend_back_kernel(m, q, kv, d_att, att, lse, qp, kp, q_gain, k_gain, cosine, sine, place_q, segment_k, dq_low, dk_low, dv_low, gains, partial, core_in, up_in, down_in, core_sem, up_sem, down_sem):
    tokens, length = q.shape[0], kv.shape[0]
    core, zz, to_core, to_line = group_place(m)
    greet(m, zz, to_core, to_line)
    cos, sin = cosine[...], sine[...]
    segment_q = place_q[:, 0:1]
    index_q = place_q[:, 1:2]
    index_k = lax.broadcasted_iota(jnp.int32, (tokens, length), 1)
    allowed = (segment_q == segment_k[...]) & (index_q >= index_k)
    lane = lax.broadcasted_iota(jnp.int32, (tokens, HEAD_SIZE), 1)
    gains[...] = jnp.zeros_like(gains)
    over_rows = (((0,), (0,)), ((), ()))
    over_columns = (((1,), (1,)), ((), ()))

    def core_copy(j):
        return remote(partial.at[j, 1 - core], core_in.at[j], core_sem.at[0, j], core_sem.at[1, j], to_core)

    def line_copy(j, up, here):
        low, high = (here + 1, m) if up else (0, here)
        into, sems = (up_in, up_sem) if up else (down_in, down_sem)
        return remote(
            partial.at[j, core, pl.ds(low, high - low)],
            into.at[j, pl.ds(low - (1 if up else 0), high - low)],
            sems.at[0, j],
            sems.at[1, j],
            to_line(1 if up else -1),
        )

    def add(j, place, value):
        partial[j, core, place] = (partial[j, core, place].astype(jnp.float32) + value.astype(jnp.float32)).astype(partial.dtype)

    def compute(j):
        for n in range(CHUNK_HEADS):
            keys = kv[:, pl.ds(pl.multiple_of(j * 2 * CHUNK + n * HEAD_SIZE, 128), HEAD_SIZE)]
            values = kv[:, pl.ds(pl.multiple_of(j * 2 * CHUNK + CHUNK + n * HEAD_SIZE, 128), HEAD_SIZE)]
            dk = dv = None
            for g in range(GROUP):
                h = (j * CHUNK_HEADS + n) * GROUP + g
                at = pl.ds(pl.multiple_of(h * HEAD_SIZE, 128), HEAD_SIZE)
                queries, grad = q[:, at], d_att[:, at]
                total = jnp.sum(jnp.where(lane == h, lse[...], 0.0), axis=-1, keepdims=True)
                delta = jnp.sum(grad.astype(jnp.float32) * att[:, at], axis=-1, keepdims=True)
                s = lax.dot_general(queries, keys, over_columns, preferred_element_type=jnp.float32)
                p = jnp.exp(jnp.where(allowed, s * SCORE_SCALE, VERY_NEGATIVE) - total)
                dp = lax.dot_general(grad, values, over_columns, preferred_element_type=jnp.float32)
                ds = (p * (dp - delta)).astype(queries.dtype)
                dq = jnp.dot(ds, keys, preferred_element_type=jnp.float32) * SCORE_SCALE
                here_k = lax.dot_general(ds, queries, over_rows, preferred_element_type=jnp.float32)
                here_v = lax.dot_general(p.astype(grad.dtype), grad, over_rows, preferred_element_type=jnp.float32)
                dk = here_k if dk is None else dk + here_k
                dv = here_v if dv is None else dv + here_v
                by_head, by_gain = head_prepare_back(dq, qp[:, at], q_gain[...], cos, sin)
                dq_low[:, at] = by_head.astype(dq_low.dtype)
                gains[0:1] += by_gain
            first = n * HEAD_SIZE
            partial[j, :, :, :, first : first + HEAD_SIZE] = (dk * SCORE_SCALE).astype(partial.dtype).reshape(2, m, tokens, HEAD_SIZE)
            first += CHUNK
            partial[j, :, :, :, first : first + HEAD_SIZE] = dv.astype(partial.dtype).reshape(2, m, tokens, HEAD_SIZE)
        core_copy(j).start()

    def take_core(j):
        core_copy(j).wait_recv()
        for place in range(m):
            add(j, place, core_in[j, place])

    def hop(j, h):
        for up in (True, False):
            here = h if up else m - 1 - h

            @pl.when(zz == here)
            def _():
                if h > 0:
                    line_copy(j, up, here - 1 if up else here + 1).wait_recv()
                    into = up_in if up else down_in
                    for place in range(here, m) if up else range(here + 1):
                        add(j, place, into[j, place - (1 if up else 0)])
                if h < m - 1:
                    line_copy(j, up, here).start()

    def finish(j):
        for n in range(CHUNK_HEADS):
            at = pl.ds(pl.multiple_of((j * CHUNK_HEADS + n) * HEAD_SIZE, 128), HEAD_SIZE)
            grad = partial[j, core, zz, :, n * HEAD_SIZE : (n + 1) * HEAD_SIZE].astype(jnp.float32)
            by_head, by_gain = head_prepare_back(grad, kp[:, at], k_gain[...], cos, sin)
            dk_low[:, at] = by_head.astype(dk_low.dtype)
            gains[1:2] += by_gain
        at = pl.ds(pl.multiple_of(j * CHUNK, 128), CHUNK)
        dv_low[:, at] = partial[j, core, zz, :, CHUNK:]
        core_copy(j).wait_send()
        for here in range(m):

            @pl.when(zz == here)
            def _():
                if here < m - 1:
                    line_copy(j, True, here).wait_send()
                if here > 0:
                    line_copy(j, False, here).wait_send()

    plan = [[compute], [take_core, functools.partial(hop, h=0)]]
    for h in range(1, m):
        plan.append([functools.partial(hop, h=h)])
    plan[-1].append(finish)

    def tick(t, carry):
        for depth in [*range(1, len(plan)), 0]:
            j = t - depth

            @pl.when((j >= 0) & (j < CHUNKS))
            def _():
                for stage in plan[depth]:
                    stage(j)

        return carry

    lax.fori_loop(0, CHUNKS + len(plan) - 1, tick, 0)


def attend_back(m, q, kv, d_att, att, lse, qp, kp, q_gain, k_gain, cosine, sine, place_q, segment_k, collective_id):
    tokens = q.shape[0]
    low = jnp.bfloat16
    dma = pltpu.SemaphoreType.DMA
    vmem = pl.BlockSpec(memory_space=pltpu.VMEM)
    return pl.pallas_call(
        functools.partial(attend_back_kernel, m),
        out_shape=[
            jax.ShapeDtypeStruct((tokens, QD), low),
            jax.ShapeDtypeStruct((tokens, KEY_FEATURES), low),
            jax.ShapeDtypeStruct((tokens, KEY_FEATURES), low),
            jax.ShapeDtypeStruct((8, HEAD_SIZE), jnp.float32),
        ],
        in_specs=[vmem] * 13,
        out_specs=[vmem] * 4,
        scratch_shapes=[
            pltpu.VMEM((CHUNKS, 2, m, tokens, 2 * CHUNK), low),
            pltpu.VMEM((CHUNKS, m, tokens, 2 * CHUNK), low),
            pltpu.VMEM((CHUNKS, max(m - 1, 1), tokens, 2 * CHUNK), low),
            pltpu.VMEM((CHUNKS, max(m - 1, 1), tokens, 2 * CHUNK), low),
            dma((2, CHUNKS)),
            dma((2, CHUNKS)),
            dma((2, CHUNKS)),
        ],
        compiler_params=pltpu.CompilerParams(
            collective_id=collective_id, has_side_effects=True, vmem_limit_bytes=48 * 1024 * 1024
        ),
    )(q, kv, d_att, att, lse, qp, kp, q_gain, k_gain, cosine, sine, place_q, segment_k)


WIDE_TILE, NARROW_TILE = 512, 256


def unit_rms(values):
    return values * lax.rsqrt(jnp.mean(values * values, axis=-1, keepdims=True) + NORM_EPS)


def forward_kernel(chunks, nx, nz, *refs):
    count = len(chunks)
    weights = 7
    gain_shard, shards, refs = refs[0], refs[1 : 1 + weights], refs[1 + weights :]
    tokens_here, cosine, sine, place_q, segment_k, refs = *refs[:5], refs[5:]
    wholes, refs = refs[:count], refs[count:]
    gains_out, tokens_out, hidden_out, last_out, refs = *refs[:4], refs[4:]
    saved_out, refs = [refs[n * SAVED : (n + 1) * SAVED] for n in range(LAYERS)], refs[LAYERS * SAVED :]
    own_sem, z_sem, x_sem, y_sem, core_sem, out_sem, refs = *refs[:6], refs[6:]
    gain_all, gains, low_tokens, h, normed, qp, kp, v, q, kv, att, att_low, lse, h_mid, n2, gate, up, act, last, refs = (
        *refs[:19],
        refs[19:],
    )
    wide_buf, output_buf, down_buf, refs = *refs[:3], refs[3:]
    tile_sem, save_sem, misc_sem, kv_core_sem, kv_line_sem, kv_core_out, kv_line_out = refs
    tokens, length = q.shape[0], kv.shape[1]
    m = nz // 2
    y = lax.axis_index("rep")
    shard = lax.axis_index("shard")
    z = lax.axis_index("ctx")
    core, x = lax.rem(shard, 2), lax.div(shard, 2)
    to_core = (y, x * 2 + 1 - core, z)
    to_y = (1 - y, shard, z)
    upper = z >= m
    moves = ((core == 0) & upper) | ((core == 1) & (z < m))
    to_swap = (y, x * 2 + 1 - core, jnp.where(upper, z - m, z + m))

    def to_x(step):
        return (y, shard + 2 * step, z)

    def to_z(step):
        return (y, shard, z + step)

    def own_shard(k):
        weight, layer = chunks[k][:2]
        return gain_shard if weight < 0 else shards[weight].at[layer]

    def rows_of(k, xs, zs, start, size, of_core=core):
        rows = chunks[k][2]
        first = ((xs * 2 + of_core) * nz + zs) * rows + start
        return wholes[k].at[pl.ds(pl.multiple_of(first, 16), size)]

    def inplane(k):
        rows, near = chunks[k][2:]
        return y * (rows - near), near

    def arrived(ref, sem):
        pltpu.make_async_copy(ref, ref, sem).wait()

    def pass_z(k, src, zs, step, kind):
        start, size = inplane(k)
        remote(src, rows_of(k, x, zs, start, size), out_sem.at[k, kind], z_sem.at[k, zs], to_z(step)).start()

    def pass_x(k, src, xs, zs, step, kind):
        start, size = inplane(k)
        into = rows_of(k, xs, zs, start, size)
        remote(src, into, out_sem.at[k, kind], x_sem.at[k, xs * nz + zs], to_x(step)).start()

    def pass_y(k, xs, zs):
        rows, near = chunks[k][2:]
        if rows > near:
            part = rows_of(k, xs, zs, y * near, rows - near)
            remote(part, part, out_sem.at[k, 4], y_sem.at[k, xs * nz + zs], to_y).start()

    def pass_core(k, xs, zs, start, size):
        part = rows_of(k, xs, zs, start, size)
        remote(part, part, out_sem.at[k, 5], core_sem.at[k], to_core).start()

    def stage_own(k):
        rows = chunks[k][2]
        start, size = inplane(k)
        part = own_shard(k).at[pl.ds(pl.multiple_of(start, 16), size)]

        @pl.when(z < nz - 1)
        def _():
            pass_z(k, part, z, 1, 0)

        @pl.when(z > 0)
        def _():
            pass_z(k, part, z, -1, 1)

        @pl.when(x < nx - 1)
        def _():
            pass_x(k, part, x, z, 1, 2)

        @pl.when(x > 0)
        def _():
            pass_x(k, part, x, z, -1, 3)

        remote(own_shard(k), rows_of(k, x, z, 0, rows), out_sem.at[k, 5], core_sem.at[k], to_core).start()
        pltpu.make_async_copy(own_shard(k), rows_of(k, x, z, 0, rows), own_sem.at[k]).start()

    def stage_z(k, d):
        start, size = inplane(k)
        for step, kind in ((1, 0), (-1, 1)):
            zs = z - step * d

            @pl.when((zs >= 0) & (zs < nz))
            def _():
                part = rows_of(k, x, zs, start, size)
                arrived(part, z_sem.at[k, zs])

                @pl.when((z + step >= 0) & (z + step < nz))
                def _():
                    pass_z(k, part, zs, step, kind)

                @pl.when(x < nx - 1)
                def _():
                    pass_x(k, part, x, zs, 1, 2)

                @pl.when(x > 0)
                def _():
                    pass_x(k, part, x, zs, -1, 3)

                pass_y(k, x, zs)
                pass_core(k, x, zs, start, size)

    def stage_x(k, d):
        start, size = inplane(k)
        for step, kind in ((1, 2), (-1, 3)):
            xs = x - step * d

            @pl.when((xs >= 0) & (xs < nx))
            def _():
                def body(zs, carry):
                    part = rows_of(k, xs, zs, start, size)
                    arrived(part, x_sem.at[k, xs * nz + zs])
                    if nx > 2:

                        @pl.when((x + step >= 0) & (x + step < nx))
                        def _():
                            pass_x(k, part, xs, zs, step, kind)

                    pass_y(k, xs, zs)
                    pass_core(k, xs, zs, start, size)
                    return carry

                lax.fori_loop(0, nz, body, 0)

    def stage_y(k):
        rows, near = chunks[k][2:]
        if rows > near:

            def body(i, carry):
                xs, zs = lax.div(i, nz), lax.rem(i, nz)

                @pl.when((xs != x) | (zs != z))
                def _():
                    start = (1 - y) * near
                    arrived(rows_of(k, xs, zs, start, rows - near), y_sem.at[k, i])
                    pass_core(k, xs, zs, start, rows - near)

                return carry

            lax.fori_loop(0, nx * nz, body, 0)

    def first_rows(k, size):
        return wholes[k].at[pl.ds(0, size)]

    def complete(k):
        rows = chunks[k][2]
        arrived(first_rows(k, nx * nz * rows), core_sem.at[k])
        arrived(first_rows(k, rows), own_sem.at[k])

    def sent(k):
        rows, near = chunks[k][2:]
        for zz in range(nz):

            @pl.when(z == zz)
            def _():
                if zz < nz - 1:
                    arrived(first_rows(k, (zz + 1) * near), out_sem.at[k, 0])
                if zz > 0:
                    arrived(first_rows(k, (nz - zz) * near), out_sem.at[k, 1])

        for xx in range(nx):

            @pl.when(x == xx)
            def _():
                if xx < nx - 1:
                    arrived(first_rows(k, (xx + 1) * nz * near), out_sem.at[k, 2])
                if xx > 0:
                    arrived(first_rows(k, (nx - xx) * nz * near), out_sem.at[k, 3])

        if rows > near:
            arrived(first_rows(k, (nx * nz - 1) * (rows - near)), out_sem.at[k, 4])
        arrived(first_rows(k, nx * nz * rows), out_sem.at[k, 5])

    barrier = pltpu.get_barrier_semaphore()
    pl.semaphore_signal(barrier, inc=1, device_id=to_core, device_id_type=MESH)
    pl.semaphore_signal(barrier, inc=1, device_id=to_y, device_id_type=MESH)
    meets = ((z > 0, to_z(-1)), (z < nz - 1, to_z(1)), (x > 0, to_x(-1)), (x < nx - 1, to_x(1)), (moves, to_swap))
    greeted = 2
    for here, there in meets:

        @pl.when(here)
        def _():
            pl.semaphore_signal(barrier, inc=1, device_id=there, device_id_type=MESH)

        greeted = greeted + here.astype(jnp.int32)
    pl.semaphore_wait(barrier, greeted)

    def swap_copy():
        return remote(tokens_here, low_tokens, misc_sem.at[0], misc_sem.at[1], to_swap)

    def stay_copy():
        return pltpu.make_async_copy(tokens_here, low_tokens, misc_sem.at[1])

    @pl.when(moves)
    def _():
        swap_copy().start()

    @pl.when(~moves)
    def _():
        stay_copy().start()

    def begin():
        @pl.when(moves)
        def _():
            swap_copy().wait()

        @pl.when(~moves)
        def _():
            stay_copy().wait()

        h[...] = low_tokens[...].astype(jnp.float32)
        pltpu.make_async_copy(low_tokens, tokens_out, misc_sem.at[2]).start()

    def read_gains():
        complete(0)
        copy = pltpu.make_async_copy(wholes[0], gain_all, misc_sem.at[3])
        copy.start()
        copy.wait()
        gains[...] = jnp.zeros_like(gains)

        def body(n, carry):
            gains[...] += gain_all[pl.ds(pl.multiple_of(n * 16, 16), 16)].astype(jnp.float32)
            return carry

        lax.fori_loop(0, 2 * nx * nz, body, 0)
        pltpu.make_async_copy(gains, gains_out, misc_sem.at[4]).start()

    zz = lax.rem(z, m)

    def kv_part(layer, j, source, of_core=core):
        rows = pl.multiple_of((source + of_core * m) * tokens, 16)
        at = j * 2 * CHUNK if isinstance(j, int) else pl.multiple_of(j * 2 * CHUNK, 128)
        return kv.at[layer, pl.ds(rows, tokens), pl.ds(at, 2 * CHUNK)]

    def kv_core(layer, j, source, of_core=core):
        ref = kv_part(layer, j, source, of_core)
        return remote(ref, ref, kv_core_out.at[layer, j, source], kv_core_sem.at[layer, j, source], to_core)

    def kv_line(layer, j, source, step):
        ref = kv_part(layer, j, source)
        send_sem = kv_line_out.at[0 if step > 0 else 1, layer, j, source]
        return remote(ref, ref, send_sem, kv_line_sem.at[layer, j, source], to_z(step))

    def onward(layer, j, source, step, do):
        @pl.when((zz + step >= 0) & (zz + step < m))
        def _():
            do(kv_line(layer, j, source, step))

    start, ended = lambda copy: copy.start(), lambda copy: copy.wait_send()

    def kv_left(layer):
        for j in range(CHUNKS):
            for source in range(m):
                kv_core(layer, j, source).wait_send()
            for d in range(m):
                for step in (1, -1):
                    source = zz - step * d

                    @pl.when((source >= 0) & (source < m))
                    def _():
                        onward(layer, j, source, step, ended)

    saves = (normed, qp, kp, q, None, att, att_low, lse, h_mid, n2, gate, up, act)

    def save_copy(layer, n):
        source = kv.at[layer] if saves[n] is None else saves[n]
        return pltpu.make_async_copy(source, saved_out[layer][n], save_sem.at[layer, n])

    def save(layer, *which):
        for n in which:
            save_copy(layer, n).start()

    def reusable(layer, *which):
        if layer > 0:
            for n in which:
                save_copy(layer - 1, n).wait()

    def layer_tasks(layer):
        chunk = {c[0]: k for k, c in enumerate(chunks) if c[1] == layer and c[0] >= 0}
        row = lambda n, width=D: gains[n + layer : n + layer + 1, :width]
        tasks = []

        def streamed(weight, buf, base, sems, tile, use, tiles, lead=None):
            k = chunk[weight]

            def copy(i):
                slot = base + i % 2
                source = wholes[k].at[:, pl.ds(i * tile, tile)]
                return pltpu.make_async_copy(source, buf.at[slot], tile_sem.at[sems + i % 2])

            def first():
                complete(k)
                copy(0).start()

            def one(i):
                copy(i).wait()
                if i + 1 < tiles:
                    copy(i + 1).start()
                use(i, buf.at[base + i % 2])

            return first, [functools.partial(one, i) for i in range(tiles)], k

        def put(k, *steps):
            tasks.append((k, lambda: [step() for step in steps]))

        def norm_first():
            if layer == 0:
                begin()
                read_gains()
            reusable(layer, 0)
            normed[...] = (unit_rms(h[...]) * row(0)).astype(normed.dtype)
            save(layer, 0)
            if layer > 0:
                pltpu.make_async_copy(h, hidden_out, misc_sem.at[5]).start()

        def keys(i, w):
            if i == 0:
                reusable(layer, 2)
            kp[:, i * WIDE_TILE : (i + 1) * WIDE_TILE] = jnp.dot(normed[...], w[...], preferred_element_type=jnp.float32)
            if i == 1:
                save(layer, 2)

        def values(i, w):
            term = jnp.dot(normed[...], w[...], preferred_element_type=jnp.float32)
            v[:, i * WIDE_TILE : (i + 1) * WIDE_TILE] = term.astype(v.dtype)

        def queries(i, w):
            if i == 0:
                reusable(layer, 1)
            qp[:, i * WIDE_TILE : (i + 1) * WIDE_TILE] = jnp.dot(normed[...], w[...], preferred_element_type=jnp.float32)
            if i == 3:
                save(layer, 1)

        cos = lambda: cosine[...]
        sin = lambda: sine[...]
        own_rows = pl.ds(pl.multiple_of((zz + core * m) * tokens, 16), tokens)

        def send_keys(j):
            for n in range(CHUNK_HEADS):
                hd = j * CHUNK_HEADS + n
                ready = head_prepare(kp[:, hd * HEAD_SIZE : (hd + 1) * HEAD_SIZE], row(6, HEAD_SIZE), cos(), sin())
                first = j * 2 * CHUNK + n * HEAD_SIZE
                kv[layer, own_rows, first : first + HEAD_SIZE] = ready.astype(kv.dtype)
            kv[layer, own_rows, j * 2 * CHUNK + CHUNK : (j + 1) * 2 * CHUNK] = v[:, j * CHUNK : (j + 1) * CHUNK]
            for step in (1, -1):
                onward(layer, j, zz, step, start)
            kv_core(layer, j, zz).start()

        def prepare_queries(part):
            if part == 0:
                reusable(layer, 3)
            for hd in range(part * 4, part * 4 + 4):
                at = slice(hd * HEAD_SIZE, (hd + 1) * HEAD_SIZE)
                q[:, at] = head_prepare(qp[:, at], row(4, HEAD_SIZE), cos(), sin()).astype(q.dtype)
            if part == 3:
                save(layer, 3)

        def arrivals(j):
            for d in range(1, m):
                for step in (1, -1):
                    source = zz - step * d

                    @pl.when((source >= 0) & (source < m))
                    def _():
                        kv_line(layer, j, source, step).wait_recv()
                        onward(layer, j, source, step, start)
                        kv_core(layer, j, source).start()

        def attend(j):
            if j == 0:
                reusable(layer, 5, 6, 7)
                lse[...] = jnp.zeros_like(lse)
            for source in range(m):
                kv_core(layer, j, source, 1 - core).wait_recv()
            index_k = lax.broadcasted_iota(jnp.int32, (tokens, length), 1)
            allowed = (place_q[:, 0:1] == segment_k[...]) & (place_q[:, 1:2] >= index_k)
            lane = lax.broadcasted_iota(jnp.int32, (tokens, HEAD_SIZE), 1)

            def head(n, carry):
                first = j * 2 * CHUNK + lax.div(n, GROUP) * HEAD_SIZE
                their_keys = kv[layer, :, pl.ds(pl.multiple_of(first, 128), HEAD_SIZE)]
                their_values = kv[layer, :, pl.ds(pl.multiple_of(first + CHUNK, 128), HEAD_SIZE)]
                hd = j * CHUNK_HEADS * GROUP + n
                at = pl.ds(pl.multiple_of(hd * HEAD_SIZE, 128), HEAD_SIZE)
                s = lax.dot_general(q[:, at], their_keys, (((1,), (1,)), ((), ())), preferred_element_type=jnp.float32)
                s = jnp.where(allowed, s * SCORE_SCALE, VERY_NEGATIVE)
                top = jnp.max(s, axis=-1, keepdims=True)
                p = jnp.exp(s - top)
                total = jnp.sum(p, axis=-1, keepdims=True)
                o = jnp.dot(p.astype(jnp.bfloat16), their_values, preferred_element_type=jnp.float32) / total
                att[:, at] = o
                att_low[:, at] = o.astype(att_low.dtype)
                lse[...] = jnp.where(lane == hd, top + jnp.log(total), lse[...])
                return carry

            lax.fori_loop(0, CHUNK_HEADS * GROUP, head, 0)
            if j == CHUNKS - 1:
                save(layer, 4, 5, 6, 7)

        def outputs(i, w):
            if i == 0:
                reusable(layer, 8)
            at = slice(i * NARROW_TILE, (i + 1) * NARROW_TILE)
            h_mid[:, at] = h[:, at] + jnp.dot(att_low[...], w[...], preferred_element_type=jnp.float32)
            if i == 3:
                save(layer, 8)

        def norm_second():
            reusable(layer, 9)
            n2[...] = (unit_rms(h_mid[...]) * row(2)).astype(n2.dtype)
            save(layer, 9)

        def gates(i, w):
            if i == 0:
                reusable(layer, 10, 12)
            gate[:, i * WIDE_TILE : (i + 1) * WIDE_TILE] = jnp.dot(n2[...], w[...], preferred_element_type=jnp.float32)

        def ups(i, w):
            if i == 0:
                reusable(layer, 11)
            at = slice(i * WIDE_TILE, (i + 1) * WIDE_TILE)
            term = jnp.dot(n2[...], w[...], preferred_element_type=jnp.float32)
            up[:, at] = term
            opened = gate[:, at]
            act[:, at] = (opened / (1.0 + jnp.exp(-opened)) * term).astype(act.dtype)
            if i == 5:
                save(layer, 10, 11, 12)

        def downs(i, w):
            if layer > 0 and i == 0:
                pltpu.make_async_copy(h, hidden_out, misc_sem.at[5]).wait()
            at = slice(i * NARROW_TILE, (i + 1) * NARROW_TILE)
            h[:, at] = h_mid[:, at] + jnp.dot(act[...], w[...], preferred_element_type=jnp.float32)

        first_k, key_tiles, kk = streamed(1, wide_buf, 0, 0, WIDE_TILE, keys, 2)
        first_v, value_tiles, kv_chunk = streamed(2, wide_buf, 2, 2, WIDE_TILE, values, 2)
        first_q, query_tiles, kq = streamed(0, wide_buf, 0, 0, WIDE_TILE, queries, 4)
        first_o, output_tiles, ko = streamed(3, output_buf, 0, 4, NARROW_TILE, outputs, 4)
        first_g, gate_tiles, kg = streamed(4, wide_buf, 0, 0, WIDE_TILE, gates, 6)
        first_u, up_tiles, ku = streamed(5, wide_buf, 2, 2, WIDE_TILE, ups, 6)
        first_d, down_tiles, kd = streamed(6, down_buf, 0, 6, NARROW_TILE, downs, 4)
        kqkv = max(kk, kv_chunk, kq)
        put(kqkv, norm_first, first_k, first_v)
        put(kqkv, *key_tiles)
        put(kqkv, first_q, *value_tiles)
        put(kqkv, functools.partial(send_keys, 0), functools.partial(send_keys, 1))
        put(kqkv, functools.partial(send_keys, 2), functools.partial(send_keys, 3))
        put(kqkv, *query_tiles[:2])
        put(kqkv, *query_tiles[2:])
        for part in range(4):
            put(kqkv, functools.partial(prepare_queries, part))
        put(kqkv, functools.partial(arrivals, 0))
        for j in range(CHUNKS):
            if j + 1 < CHUNKS:
                put(kqkv, functools.partial(arrivals, j + 1))
            if j + 1 == CHUNKS:
                put(kqkv)
            put(kqkv, functools.partial(attend, j))
        put(ko, first_o)
        put(ko, *output_tiles[:2])
        put(ko, *output_tiles[2:])
        put(kg, norm_second, first_g)
        for n in range(3):
            put(kg, *gate_tiles[2 * n : 2 * n + 2])
        put(ku, first_u)
        for n in range(3):
            put(ku, *up_tiles[2 * n : 2 * n + 2])
        put(kd, first_d)
        put(kd, *down_tiles[:2])
        put(kd, *down_tiles[2:])
        return tasks

    stages = [stage_own]
    stages += [functools.partial(stage_z, d=d) for d in range(1, nz)]
    stages += [functools.partial(stage_x, d=d) for d in range(1, nx)]
    stages += [stage_y]
    tasks = [task for layer in range(LAYERS) for task in layer_tasks(layer)]
    for tick in range(count + len(stages) - 1):
        for depth, stage in enumerate(stages):
            k = tick - depth
            if 0 <= k < count:
                stage(k)
            if tasks and tasks[0][0] + len(stages) <= tick:
                tasks.pop(0)[1]()
    for _, task in tasks:
        task()
    last[...] = h[...].astype(last.dtype)
    pltpu.make_async_copy(last, last_out, misc_sem.at[6]).start()
    for k in range(count):
        sent(k)
    for layer in range(LAYERS):
        kv_left(layer)
    for n in range(SAVED):
        save_copy(LAYERS - 1, n).wait()
    save_copy(0, 4).wait()
    pltpu.make_async_copy(low_tokens, tokens_out, misc_sem.at[2]).wait()
    pltpu.make_async_copy(gains, gains_out, misc_sem.at[4]).wait()
    pltpu.make_async_copy(last, last_out, misc_sem.at[6]).wait()


SAVED = 13


def forward(gain_shard, shards, tokens, tables, chunks, nx, nz, collective_id):
    count, m = len(chunks), nz // 2
    rows = tokens.shape[0]
    low, wide = jnp.bfloat16, jnp.float32
    dma, vmem = pltpu.SemaphoreType.DMA, pltpu.VMEM
    anywhere = pl.BlockSpec(memory_space=pl.ANY)
    arrays = [gain_shard if c[0] < 0 else shards[c[0]] for c in chunks]
    ff = shards[4].shape[-1]
    kept = [((rows, D), low), ((rows, QD), wide), ((rows, KEY_FEATURES), wide), ((rows, QD), low)]
    kept += [((2 * m * rows, 2 * KEY_FEATURES), low), ((rows, QD), wide), ((rows, QD), low), ((rows, HEAD_SIZE), wide)]
    kept += [((rows, D), wide), ((rows, D), low), ((rows, ff), wide), ((rows, ff), wide), ((rows, ff), low)]
    shape = jax.ShapeDtypeStruct
    outs = pl.pallas_call(
        functools.partial(forward_kernel, chunks, nx, nz),
        out_shape=[shape((a.shape[-2] * 2 * nx * nz, a.shape[-1]), low) for a in arrays]
        + [shape((16, D), wide), shape((rows, D), low), shape((rows, D), wide), shape((rows, D), low)]
        + [shape(*k) for k in kept] * LAYERS,
        in_specs=[anywhere] * (2 + len(shards)) + [pl.BlockSpec(memory_space=pltpu.VMEM)] * 4,
        out_specs=[anywhere] * (count + 4 + SAVED * LAYERS),
        scratch_shapes=[
            dma((count,)),
            dma((count, nz)),
            dma((count, nx * nz)),
            dma((count, nx * nz)),
            dma((count,)),
            dma((count, 6)),
            vmem((16 * 2 * nx * nz, D), low),
            vmem((16, D), wide),
            vmem((rows, D), low),
            vmem((rows, D), wide),
            vmem(*kept[0]),
            vmem(*kept[1]),
            vmem(*kept[2]),
            vmem((rows, KEY_FEATURES), low),
            vmem(*kept[3]),
            vmem((LAYERS, *kept[4][0]), low),
            *[vmem(*k) for k in kept[5:]],
            vmem((rows, D), low),
            vmem((4, D, WIDE_TILE), low),
            vmem((2, QD, NARROW_TILE), low),
            vmem((2, ff, NARROW_TILE), low),
            dma((8,)),
            dma((LAYERS, SAVED)),
            dma((7,)),
            dma((LAYERS, CHUNKS, m)),
            dma((LAYERS, CHUNKS, m)),
            dma((LAYERS, CHUNKS, m)),
            dma((2, LAYERS, CHUNKS, m)),
        ],
        compiler_params=pltpu.CompilerParams(
            collective_id=collective_id, has_side_effects=True, vmem_limit_bytes=56 * 1024 * 1024
        ),
    )(gain_shard, *shards, tokens, *tables)
    wholes, outs = outs[:count], outs[count:]
    return wholes, outs[:4], [outs[4 + n * SAVED : 4 + (n + 1) * SAVED] for n in range(LAYERS)]


SLOTS = 4
PIECES = 15
LEFT_BLOCKS = (3, 2, 1, 1)
LEFT_FIRST = (0, 3, 5, 11)
RIGHTS = 7
RIGHT_FIRST = (0, 3, 5, 7, 9, 11, 13)
WEIGHT_BLOCKS = ((1, 3), (1, 2), (3, 1), (3, 1), (2, 1), (1, 1), (1, 1))


def piece_place(j, replica):
    if j < 2:
        return 0, replica, j
    if j == 2:
        return 0, 2, replica
    if j < 5:
        return 1, replica, j - 3
    if j < 11:
        return 2 + replica, 0, j - 5
    if replica == 0:
        return 4, 0, j - 11
    return (5, 0, j - 11) if j < 13 else (6, 0, j - 13)


def reduce_kernel(nx, nz, layers, *refs):
    per = 4 + 4 + 7 + 1
    operands, refs = refs[: layers * per], refs[layers * per :]
    gains, refs = refs[0], refs[1:]
    outs, refs = refs[: len(WEIGHT_BLOCKS)], refs[len(WEIGHT_BLOCKS) :]
    gains_out, left_at, refs = refs[0], refs[1:5], refs[5:]
    right_at, turned, total, x_in, zup_in, zdown_in, f_in, result, refs = *refs[:8], refs[8:]
    gain_in, gain_up, gain_down, refs = *refs[:3], refs[3:]
    left_sem, right_sem, x_sem, zup_sem, zdown_sem, f_sem, result_sem, gain_sem, credit = refs
    rows, width = total.shape[3:]
    tokens, wide = right_at.shape[2:]
    pieces = layers * PIECES
    ring = total.shape[0]
    y = lax.axis_index("rep")
    shard = lax.axis_index("shard")
    z = lax.axis_index("ctx")
    core, x = lax.rem(shard, 2), lax.div(shard, 2)
    to_core = (y, x * 2 + 1 - core, z)
    to_y = (1 - y, shard, z)

    def to_x(step):
        return (y, shard + 2 * step, z)

    def to_z(step):
        return (y, shard, z + step)

    barrier = pltpu.get_barrier_semaphore()
    pl.semaphore_signal(barrier, inc=1, device_id=to_core, device_id_type=MESH)
    pl.semaphore_signal(barrier, inc=1, device_id=to_y, device_id_type=MESH)
    for here, there in ((z > 0, to_z(-1)), (z < nz - 1, to_z(1)), (x > 0, to_x(-1)), (x < nx - 1, to_x(1))):

        @pl.when(here)
        def _():
            pl.semaphore_signal(barrier, inc=1, device_id=there, device_id_type=MESH)

    greeted = 2 + (z > 0).astype(jnp.int32) + (z < nz - 1).astype(jnp.int32)
    greeted = greeted + (x > 0).astype(jnp.int32) + (x < nx - 1).astype(jnp.int32)
    pl.semaphore_wait(barrier, greeted)

    def left_copies(k, layer, sources):
        span = nz * LEFT_BLOCKS[k] * rows
        sems = layer * 4 + k
        for whose, source in zip((0, 2), sources):

            def columns(xs, of_core):
                return source.at[:, pl.ds(pl.multiple_of((xs * 2 + of_core) * span, 128), span)]

            for xs in range(nx):
                yield pltpu.make_async_copy(
                    columns(xs, core), left_at[k].at[whose, layer, xs], left_sem.at[whose, sems, xs]
                )
                yield remote(
                    columns(xs, 1 - core),
                    left_at[k].at[whose + 1, layer, xs],
                    left_sem.at[4 + whose, sems, xs],
                    left_sem.at[whose + 1, sems, xs],
                    to_core,
                )

    def own_right(b, source):
        return pltpu.make_async_copy(source, right_at.at[0, b], right_sem.at[0, b])

    def pair_right(b, source):
        return remote(source, right_at.at[1, b], right_sem.at[4, b], right_sem.at[1, b], to_core)

    def held_right(b, source):
        return pltpu.make_async_copy(source, right_at.at[2, b], right_sem.at[2, b])

    def replica_right(b, source):
        return remote(source, right_at.at[2, b], right_sem.at[5, b], right_sem.at[2, b], to_y)

    def passed_right(b, source):
        return remote(source, right_at.at[3, b], right_sem.at[6, b], right_sem.at[3, b], to_core)

    def fetch(i):
        for layer in range(layers):
            mine = operands[layer * per : (layer + 1) * per]
            lefts, their_lefts = mine[:4], mine[4:8]
            down, output, gate, up, query, key, value, their_down = mine[8:]
            blocks = [((down, 0), (down, 0)), ((output, 0), (output, 0))]
            blocks += [((gate, n), (up, n)) for n in range(3)]
            blocks += [((query, 0), (key, 0)), ((query, 1), (value, 0))]
            for n in range(RIGHTS):

                @pl.when(i == layer * PIECES + RIGHT_FIRST[n])
                def _():
                    fetch_block(layer, n, lefts, their_lefts, blocks[n], their_down)

    def fetch_block(layer, n, lefts, their_lefts, block, their_down):
        b = layer * RIGHTS + n
        for replica in range(2):

            @pl.when(y == replica)
            def _():
                here, there = (
                    source.at[:, pl.ds(at * wide, wide)] for source, at in (block[replica], block[1 - replica])
                )
                if n > 0:
                    replica_right(b, there).start()
                own_right(b, here).start()
                pair_right(b, here).start()

        if n == 0:
            held_right(b, their_down).start()
            passed_right(b, their_down).start()
        for k, first in enumerate(LEFT_FIRST):
            if first == RIGHT_FIRST[n]:
                for copy in left_copies(k, layer, (lefts[k], their_lefts[k])):
                    copy.start()

    def place(i):
        return lax.div(i, PIECES), lax.rem(i, PIECES)

    def right_block(j):
        return jnp.where(j < 3, 0, jnp.where(j < 5, 1, lax.div(j - 1, 2)))

    def any_of(j, values):
        hit = j == values[0]
        for value in values[1:]:
            hit = hit | (j == value)
        return hit

    some_right = operands[8]

    def forward(i):
        layer, j = place(i)

        @pl.when(any_of(j, RIGHT_FIRST[1:]))
        def _():
            b = layer * RIGHTS + right_block(j)
            replica_right(b, some_right).wait_recv()
            passed_right(b, right_at.at[2, b]).start()

    def product(i):
        layer, j = place(i)
        b = layer * RIGHTS + right_block(j)
        for k, first in enumerate(LEFT_FIRST):

            @pl.when(j == first)
            def _():
                for copy in left_copies(k, layer, (operands[k], operands[k])):
                    copy.wait()

                for who in range(4):
                    for xs in range(nx):
                        flipped = left_at[k][who, layer, xs].T.reshape(nz, LEFT_BLOCKS[k], rows, tokens)
                        for n in range(LEFT_BLOCKS[k]):
                            turned[who, n, xs] = flipped[:, n]

        @pl.when(any_of(j, RIGHT_FIRST))
        def _():
            own_right(b, some_right).wait()
            pair_right(b, some_right).wait()
            passed_right(b, some_right).wait()

        @pl.when(j == 0)
        def _():
            held_right(b, some_right).wait()

        @pl.when(any_of(j, RIGHT_FIRST[1:]))
        def _():
            replica_right(b, some_right).wait_send()

        slot = lax.rem(i, ring)
        part = jnp.where(j == 2, 2, jnp.where(j < 5, y, 0))
        half = jnp.where(j < 2, j, jnp.where(j == 2, y, lax.rem(j + 1, 2)))
        tile = width // 2

        def columns(c, carry):
            source = pl.ds(pl.multiple_of(half * width + c * tile, tile), tile)
            acc = None
            for who in range(4):
                left = turned[who, part].reshape(nx * nz * rows, tokens)
                term = jnp.dot(left, right_at[who, b, :, source], preferred_element_type=jnp.float32)
                acc = term if acc is None else acc + term
            into = pl.ds(pl.multiple_of(c * tile, tile), tile)
            total[slot, :, :, :, into] = acc.reshape(nx, nz, rows, tile).astype(total.dtype)
            return carry

        lax.fori_loop(0, 2, columns, 0)

    def give(i, flow, device):
        @pl.when(i + SLOTS < pieces)
        def _():
            pl.semaphore_signal(credit.at[flow], inc=1, device_id=device, device_id_type=MESH)

    def spend(i, flow):
        @pl.when(i >= SLOTS)
        def _():
            pl.semaphore_wait(credit.at[flow], 1)

    def add(slot, xs, zs, value):
        where = (slot, xs, zs)
        total[where] = (total[where].astype(jnp.float32) + value.astype(jnp.float32)).astype(total.dtype)

    def x_copy(i, up, here):
        low, high = (here + 1, nx) if up else (0, here)
        side = 0 if (up or nx == 2) else 1
        return remote(
            total.at[lax.rem(i, ring), pl.ds(low, high - low)],
            x_in.at[lax.rem(i, SLOTS), side, pl.ds(low - (1 if up else 0), high - low)],
            x_sem.at[0 if up else 1, i],
            x_sem.at[2 if up else 3, i],
            to_x(1 if up else -1),
        )

    def z_copy(i, up, here):
        low, high = (here + 1, nz) if up else (0, here)
        into = zup_in if up else zdown_in
        sems = zup_sem if up else zdown_sem
        return remote(
            total.at[lax.rem(i, ring), x, pl.ds(low, high - low)],
            into.at[lax.rem(i, SLOTS), pl.ds(low - (1 if up else 0), high - low)],
            sems.at[0, i],
            sems.at[1, i],
            to_z(1 if up else -1),
        )

    def x_hop(i, h):
        slot, small = lax.rem(i, ring), lax.rem(i, SLOTS)
        for up in (True, False):
            here = h if up else nx - 1 - h
            side = 0 if (up or nx == 2) else 1

            @pl.when(x == here)
            def _():
                if h > 0:
                    x_copy(i, up, here - 1 if up else here + 1).wait_recv()
                    for target in range(here, nx) if up else range(here + 1):

                        def body(zs, carry):
                            add(slot, target, zs, x_in[small, side, target - (1 if up else 0), zs])
                            return carry

                        lax.fori_loop(0, nz, body, 0)
                    give(i, 0 if up else 1, to_x(-1 if up else 1))
                if h < nx - 1:
                    spend(i, 0 if up else 1)
                    x_copy(i, up, here).start()

    def z_hop(i, h):
        slot, small = lax.rem(i, ring), lax.rem(i, SLOTS)
        for up in (True, False):
            here = h if up else nz - 1 - h

            @pl.when(z == here)
            def _():
                if h > 0:
                    z_copy(i, up, here - 1 if up else here + 1).wait_recv()
                    into = zup_in if up else zdown_in

                    def body(target, carry):
                        add(slot, x, target, into[small, target - (1 if up else 0)])
                        return carry

                    lax.fori_loop(here if up else 0, nz if up else here + 1, body, 0)
                    give(i, 2 if up else 3, to_z(-1 if up else 1))
                if h < nz - 1:
                    spend(i, 2 if up else 3)
                    z_copy(i, up, here).start()

    def f_copy(i):
        return remote(
            total.at[lax.rem(i, ring), x, z], f_in.at[lax.rem(i, SLOTS)], f_sem.at[0, i], f_sem.at[1, i], to_y
        )

    def send_f(i):
        spend(i, 4)
        f_copy(i).start()

    def result_copy(i, replica, into):
        two = lax.rem(i, 2)
        return pltpu.make_async_copy(result.at[two, replica], into, result_sem.at[two, replica])

    def keep_result(i, replica):
        layer, j = place(i)
        for n in range(PIECES):
            for r in range(2):

                @pl.when((j == n) & (replica == r))
                def _():
                    which, part, column = piece_place(n, r)
                    into = outs[which].at[layer, pl.ds(part * rows, rows), pl.ds(column * width, width)]
                    result_copy(i, r, into).start()

    def result_kept(i):
        for r in range(2):
            result_copy(i, r, outs[5].at[0, :, pl.ds(0, width)]).wait()

    def finish(i):
        slot, small, two = lax.rem(i, ring), lax.rem(i, SLOTS), lax.rem(i, 2)
        f_copy(i).wait_recv()

        @pl.when(i >= 2)
        def _():
            result_kept(i - 2)

        result[two, y] = total[slot, x, z].astype(jnp.float32)
        result[two, 1 - y] = f_in[small].astype(jnp.float32)
        give(i, 4, to_y)
        keep_result(i, 0)
        keep_result(i, 1)
        f_copy(i).wait_send()
        for here in range(nx):

            @pl.when(x == here)
            def _():
                if here < nx - 1:
                    x_copy(i, True, here).wait_send()
                if here > 0:
                    x_copy(i, False, here).wait_send()

        for here in range(nz):

            @pl.when(z == here)
            def _():
                if here < nz - 1:
                    z_copy(i, True, here).wait_send()
                if here > 0:
                    z_copy(i, False, here).wait_send()

    def gain_copy(n, source, device):
        return remote(source, gain_in.at[n], gain_sem.at[0, n], gain_sem.at[1, n], device)

    def gain_start():
        copy = pltpu.make_async_copy(gains, gain_in.at[0], gain_sem.at[0, 0])
        copy.start()
        copy.wait()
        gain_copy(1, gain_in.at[0], to_core).start()

    def gain_pair():
        gain_copy(1, gain_in.at[0], to_core).wait()
        gain_up[0] = gain_in[0] + gain_in[1]
        gain_copy(2, gain_up.at[0], to_y).start()

    def gain_y():
        gain_copy(2, gain_up.at[0], to_y).wait()
        gain_in[0] = gain_up[0] + gain_in[2]

    def gain_hop(h, n, here, to, first, level):
        for up in (True, False):
            buffer = (gain_up if up else gain_down).at[level]
            slot = first if up else first + 1

            @pl.when(here == (h if up else n - 1 - h))
            def _():
                buffer[...] = gain_in[0]
                if h > 0:
                    gain_copy(slot, buffer, to(1 if up else -1)).wait_recv()
                    buffer[...] = gain_in[0] + gain_in[slot]
                if h < n - 1:
                    gain_copy(slot, buffer, to(1 if up else -1)).start()

    def gain_line(n, here, to, first, level):
        @pl.when(here < n - 1)
        def _():
            gain_copy(first, gain_up.at[level], to(1)).wait_send()

        @pl.when(here > 0)
        def _():
            gain_copy(first + 1, gain_down.at[level], to(-1)).wait_send()

        gain_in[0] = gain_up[level] + gain_down[level] - gain_in[0]

    def gain_end():
        copy = pltpu.make_async_copy(gain_in.at[0], gains_out, gain_sem.at[0, 0])
        copy.start()
        copy.wait()

    steps = [gain_start, gain_pair, gain_y]
    for h in range(nx):
        steps.append(functools.partial(gain_hop, h, nx, x, to_x, 3, 1))
    steps.append(functools.partial(gain_line, nx, x, to_x, 3, 1))
    for h in range(nz):
        steps.append(functools.partial(gain_hop, h, nz, z, to_z, 5, 2))
    steps.append(functools.partial(gain_line, nz, z, to_z, 5, 2))
    steps.append(gain_end)

    plan = [[fetch], [], [], [forward], [], [product], [functools.partial(x_hop, h=0)]]
    for h in range(1, nx):
        plan += [[], [functools.partial(x_hop, h=h)]]
    plan[-1].append(functools.partial(z_hop, h=0))
    for h in range(1, nz):
        plan.append([functools.partial(z_hop, h=h)])
    plan[-1].append(send_f)
    plan.append([finish])

    def tick(t, carry):
        for depth in [*range(6, len(plan)), 0, 3, 5]:
            if not plan[depth]:
                continue
            i = t - depth

            @pl.when((i >= 0) & (i < pieces))
            def _():
                for stage in plan[depth]:
                    stage(i)

        for n, step in enumerate(steps):
            pl.when(t == n)(step)
        return carry

    lax.fori_loop(0, pieces + len(plan) - 1, tick, 0)
    result_kept(pieces - 2)
    result_kept(pieces - 1)


def reduce_weights(operands, gains, nx, nz, collective_id):
    layers = len(operands)
    flat = [a for layer in operands for a in layer]
    tokens, wide = operands[0][8].shape
    rows, width = wide // (2 * nx * nz), wide // 2
    pieces = layers * PIECES
    ring = 2 * nx + nz + 1
    sides = 1 if nx == 2 else 2
    low = jnp.bfloat16
    dma = pltpu.SemaphoreType.DMA
    anywhere = pl.BlockSpec(memory_space=pl.ANY)
    return pl.pallas_call(
        functools.partial(reduce_kernel, nx, nz, layers),
        out_shape=[
            jax.ShapeDtypeStruct((layers, rows * below, wide * across), jnp.float32) for across, below in WEIGHT_BLOCKS
        ]
        + [jax.ShapeDtypeStruct(gains.shape, gains.dtype)],
        in_specs=[anywhere] * (len(flat) + 1),
        out_specs=[anywhere] * (len(WEIGHT_BLOCKS) + 1),
        scratch_shapes=[pltpu.VMEM((4, layers, nx, tokens, nz * n * rows), low) for n in LEFT_BLOCKS]
        + [
            pltpu.VMEM((4, layers * RIGHTS, tokens, wide), low),
            pltpu.VMEM((4, max(LEFT_BLOCKS), nx, nz, rows, tokens), low),
            pltpu.VMEM((ring, nx, nz, rows, width), low),
            pltpu.VMEM((SLOTS, sides, nx - 1, nz, rows, width), low),
            pltpu.VMEM((SLOTS, nz - 1, rows, width), low),
            pltpu.VMEM((SLOTS, nz - 1, rows, width), low),
            pltpu.VMEM((SLOTS, rows, width), low),
            pltpu.VMEM((2, 2, rows, width), jnp.float32),
            pltpu.VMEM((7, *gains.shape), gains.dtype),
            pltpu.VMEM((3, *gains.shape), gains.dtype),
            pltpu.VMEM((3, *gains.shape), gains.dtype),
            dma((7, layers * 4, nx)),
            dma((7, layers * RIGHTS)),
            dma((4, pieces)),
            dma((2, pieces)),
            dma((2, pieces)),
            dma((2, pieces)),
            dma((2, 2)),
            dma((2, 7)),
            pltpu.SemaphoreType.REGULAR((5,)),
        ],
        compiler_params=pltpu.CompilerParams(
            collective_id=collective_id, has_side_effects=True, vmem_limit_bytes=56 * 1024 * 1024
        ),
    )(*flat, gains)


def segment_of(doc_ends, token_index):
    return jnp.sum((token_index[:, None] >= doc_ends[None, :]).astype(jnp.int32), axis=1)


def doc_layout(doc_ends, token_index):
    token_segment = segment_of(doc_ends, token_index)
    starts = jnp.concatenate([jnp.zeros((1,), jnp.int32), doc_ends])
    labels = jnp.arange(starts.shape[0], dtype=jnp.int32)
    doc_begin = jnp.sum(
        jnp.where(token_segment[:, None] == labels[None, :], starts[None, :], 0), axis=1
    )
    return (token_segment, token_index - doc_begin)


def rotary(positions, head_width):
    middle = head_width // 2
    inv_rates = jnp.exp(
        jnp.arange(middle, dtype=jnp.float32) * jnp.float32(-2.0 * math.log(ROPE_BASE) / head_width)
    )
    angles = positions.astype(jnp.float32)[:, None] * inv_rates[None, :]
    cosine = jnp.cos(angles)
    sine = jnp.sin(angles)
    return (jnp.concatenate([cosine, cosine], axis=1), jnp.concatenate([-sine, sine], axis=1))


def rms_scale(values, gain_vec):
    return (
        values * lax.rsqrt(jnp.mean(values * values, axis=-1, keepdims=True) + NORM_EPS) * gain_vec
    )


def swiglu(gate_pre, upward):
    return jax.nn.silu(gate_pre) * upward


def product(left, right):
    return jnp.dot(left, right, preferred_element_type=jnp.float32)


def product_back(grad, right):
    return lax.dot_general(grad, right, (((1,), (1,)), ((), ())), preferred_element_type=jnp.float32)


def over_replica(values):
    return lax.ppermute(values, "rep", [(0, 1), (1, 0)])


def after(value, others):
    value, *others = lax.optimization_barrier((value, *others))
    return value, others


def layer_back(upstream, hidden, weights, gains, saved, tables, m, which_layer, waiting):
    (
        query_weight,
        key_matrix,
        value_matrix,
        output_weight,
        gate_weight,
        up_weight,
        down_weight,
    ) = weights
    gain_first, gain_second = gains[which_layer], gains[2 + which_layer]
    gain_query, gain_key = gains[4 + which_layer, :HEAD_SIZE], gains[6 + which_layer, :HEAD_SIZE]
    (
        normalized_rows,
        query_proj,
        key_projection,
        query_rows,
        keys_values,
        attended_rows,
        attended_low,
        log_sum,
        hidden_mid,
        normed_two,
        gate_pre,
        upward,
        activated,
    ) = saved
    branch_low = upstream.astype(jnp.bfloat16)
    waiting.append(over_replica(branch_low))
    grad_act = product_back(branch_low, down_weight)
    ignored, swiglu_back = jax.vjp(swiglu, gate_pre, upward)
    grad_gate_pre, grad_upward = swiglu_back(grad_act)
    gate_low = grad_gate_pre.astype(jnp.bfloat16)
    up_low = grad_upward.astype(jnp.bfloat16)
    grad_normed_two = product_back(gate_low, gate_weight) + product_back(up_low, up_weight)
    ignored, second_back = jax.vjp(rms_scale, hidden_mid, gain_second)
    grad_mid, grad_gain_second = second_back(grad_normed_two)
    upstream_mid = upstream + grad_mid
    attn_low = upstream_mid.astype(jnp.bfloat16)
    grad_attended = product_back(attn_low, output_weight).astype(jnp.bfloat16)
    ready = 0 if which_layer == 1 else 4
    grad_attended, waiting[:ready] = after(grad_attended, waiting[:ready])
    query_low, key_low, value_low, head_gains = attend_back(
        m,
        query_rows,
        keys_values,
        grad_attended,
        attended_rows,
        log_sum,
        query_proj,
        key_projection,
        gain_query[None],
        gain_key[None],
        *tables,
        3,
    )
    ready = 3 if which_layer == 1 else 8
    query_low, waiting[:ready] = after(query_low, waiting[:ready])
    grad_normed = product_back(query_low, query_weight)
    grad_normed = grad_normed + product_back(key_low, key_matrix)
    grad_normed = grad_normed + product_back(value_low, value_matrix)
    ignored, first_back = jax.vjp(rms_scale, hidden, gain_first)
    grad_hidden, grad_gain_first = first_back(grad_normed)
    lefts = (activated, attended_low, normed_two, normalized_rows)
    rights = (branch_low, attn_low, gate_low, up_low, query_low, key_low, value_low)
    gains = (grad_gain_first, head_gains[0], head_gains[1], grad_gain_second)
    return (upstream_mid + grad_hidden, (lefts, rights, gains))


def near_rows(rows, share):
    return min(rows, -(-int(rows * share) // 16) * 16)


NEAR_SHARES = (0.75, 0.75, 0.75, 0.6, 0.5, 0.75, 0.55)
ARRIVAL = [(weight, layer) for layer in range(LAYERS) for weight in range(7)]


def run_forward(tokens, tables, weights, gains):
    nx, nz = lax.axis_size("shard") // 2, lax.axis_size("ctx")
    here = lax.axis_index("shard") * nz + lax.axis_index("ctx")
    block = jnp.zeros((16, D), jnp.bfloat16)
    for row, parts in ((0, gains[:2]), (4, gains[2:])):
        part = jnp.concatenate(parts)
        block = lax.dynamic_update_slice(block, part, (row, here * part.shape[1]))
    chunks = [(-1, 0, 16, 16)]
    for weight, layer in ARRIVAL:
        rows = weights[weight].shape[1]
        chunks.append((weight, layer, rows, near_rows(rows, NEAR_SHARES[weight])))
    wholes, outs, saved = forward(block, weights, tokens, tables, tuple(chunks), nx, nz, 0)
    by_place = dict(zip(ARRIVAL, wholes[1:]))
    gathered = [[by_place[weight, layer] for weight in range(7)] for layer in range(LAYERS)]
    return gathered, outs, saved


def weight_gradients(operands):
    nx, nz = lax.axis_size("shard") // 2, lax.axis_size("ctx")
    shards = 2 * nx * nz
    flat = jnp.concatenate([g for _, gains in operands for g in gains])
    size = -(-flat.shape[0] // 1024) * 1024
    padded = jnp.zeros((size,), flat.dtype).at[: flat.shape[0]].set(flat).reshape(-1, 128)
    *grads, summed = reduce_weights([members for members, _ in operands], padded, nx, nz, 1)
    summed = summed.reshape(-1)[: flat.shape[0]].reshape(LAYERS, -1)
    here = lax.axis_index("shard") * nz + lax.axis_index("ctx")
    small, used = [], 0
    for size in (D, HEAD_SIZE, HEAD_SIZE, D):
        own = size // shards
        small.append(lax.dynamic_slice_in_dim(summed, used + here * own, own, axis=1))
        used += size
    down, output, gate, up, query, key, value = grads
    return (small[0], query, key, value, small[1], small[2], output, small[3], gate, up, down)


def local(
    tokens,
    lengths,
    norm_one,
    w_query,
    w_key,
    w_value,
    query_gain,
    key_gain,
    w_output,
    norm_two,
    w_gate,
    w_up,
    w_down,
    cotangent,
):
    token_rows = tokens.shape[1]
    nx, nz = lax.axis_size("shard") // 2, lax.axis_size("ctx")
    m = nz // 2
    pairs = []
    for x in range(nx):
        for z in range(m):
            low, high = (2 * x + 1) * nz + z, 2 * x * nz + z + m
            same = (2 * x * nz + z, (2 * x + 1) * nz + z + m)
            pairs += [(low, high), (high, low)] + [(s, s) for s in same]

    def swap(values):
        return lax.ppermute(values, ("shard", "ctx"), pairs)

    lengths = swap(lengths)
    block = lax.axis_index("ctx") % m + (lax.axis_index("shard") % 2) * m
    token_index = block * token_rows + jnp.arange(token_rows, dtype=jnp.int32)
    doc_lengths = lengths[0]
    upto = jnp.arange(doc_lengths.shape[0])
    doc_ends = jnp.sum(jnp.where(upto[:, None] >= upto[None, :], doc_lengths[None, :], 0), axis=1)
    token_segment, positions = doc_layout(doc_ends, token_index)
    cosine, sine = rotary(positions, HEAD_SIZE)
    key_segment = segment_of(doc_ends, jnp.arange(token_rows * nz, dtype=jnp.int32))
    tables = (cosine, sine, jnp.stack([token_segment, token_index], axis=1), key_segment[None, :])
    gathered, (gains, tokens, hidden, last), saved = run_forward(
        tokens[0],
        tables,
        (w_query, w_key, w_value, w_output, w_gate, w_up, w_down),
        (norm_one, norm_two, query_gain, key_gain),
    )
    cotangent = swap(cotangent)
    output = swap(last)[None]
    hiddens = (tokens.astype(jnp.float32), hidden)
    waiting = []
    for normed, _, _, _, _, _, attended, _, _, normed_two, _, _, activated in saved:
        waiting += [over_replica(a) for a in (normed, attended, normed_two, activated)]
    live_mask = (token_segment < doc_lengths.shape[0]).astype(jnp.float32)
    upstream = cotangent[0].astype(jnp.float32) * live_mask[:, None]
    operands = [None] * LAYERS
    for which_layer in reversed(range(LAYERS)):
        upstream, operands[which_layer] = layer_back(
            upstream,
            hiddens[which_layer],
            gathered[which_layer],
            gains,
            saved[which_layer],
            tables,
            m,
            which_layer,
            waiting,
        )
    grad_tokens = swap(upstream.astype(jnp.bfloat16))[None]
    for which_layer, (lefts, rights, gains) in enumerate(operands):
        normed, attended, normed_two, activated = waiting[which_layer * 4 : which_layer * 4 + 4]
        theirs = (activated, attended, normed_two, normed)
        operands[which_layer] = (lefts + theirs + rights + (waiting[9 - which_layer],), gains)
    return (output, grad_tokens) + weight_gradients(operands)


def solution(mesh):
    return jax.shard_map(
        local,
        mesh=mesh,
        in_specs=(
            P(("rep", "shard"), "ctx", None),
            P(("rep", "shard"), None),
            P(None, ("shard", "ctx")),
            P(None, ("shard", "ctx"), None),
            P(None, ("shard", "ctx"), None),
            P(None, ("shard", "ctx"), None),
            P(None, ("shard", "ctx")),
            P(None, ("shard", "ctx")),
            P(None, ("shard", "ctx"), None),
            P(None, ("shard", "ctx")),
            P(None, ("shard", "ctx"), None),
            P(None, ("shard", "ctx"), None),
            P(None, ("shard", "ctx"), None),
            P(("rep", "shard"), "ctx", None),
        ),
        out_specs=(
            P(("rep", "shard"), "ctx", None),
            P(("rep", "shard"), "ctx", None),
            P(None, ("shard", "ctx")),
            P(None, ("shard", "ctx"), None),
            P(None, ("shard", "ctx"), None),
            P(None, ("shard", "ctx"), None),
            P(None, ("shard", "ctx")),
            P(None, ("shard", "ctx")),
            P(None, ("shard", "ctx"), None),
            P(None, ("shard", "ctx")),
            P(None, ("shard", "ctx"), None),
            P(None, ("shard", "ctx"), None),
            P(None, ("shard", "ctx"), None),
        ),
        check_vma=False,
    )
```

```python
import functools
import math

import jax
import jax.numpy as jnp
from jax import lax
from jax.experimental import pallas as pl
from jax.experimental.pallas import tpu as pltpu
from jax.sharding import PartitionSpec as P

D = 1024
QUERY_HEADS = 16
KEYVALUE_HEADS = 8
HEAD_SIZE = 128
LAYERS = 2
QD = 2048
KEY_FEATURES = 1024


NORM_EPS = 1e-06
ROPE_BASE = 1000000.0
VERY_NEGATIVE = -1e30
MESH = pl.DeviceIdType.MESH


CHUNK_HEADS = 2
CHUNKS = KEYVALUE_HEADS // CHUNK_HEADS
CHUNK = CHUNK_HEADS * HEAD_SIZE
GROUP = QUERY_HEADS // KEYVALUE_HEADS
SCORE_SCALE = 1.0 / math.sqrt(HEAD_SIZE)


def group_place(m):
    y, shard, z = lax.axis_index("rep"), lax.axis_index("shard"), lax.axis_index("ctx")
    core, zz = lax.rem(shard, 2), lax.rem(z, m)
    to_core = (y, shard + 1 - 2 * core, z)

    def to_line(step):
        return (y, shard, z + step)

    return core, zz, to_core, to_line


def greet(m, zz, to_core, to_line):
    barrier = pltpu.get_barrier_semaphore()
    pl.semaphore_signal(barrier, inc=1, device_id=to_core, device_id_type=MESH)
    for here, there in ((zz > 0, to_line(-1)), (zz < m - 1, to_line(1))):

        @pl.when(here)
        def _():
            pl.semaphore_signal(barrier, inc=1, device_id=there, device_id_type=MESH)

    pl.semaphore_wait(barrier, 1 + (zz > 0).astype(jnp.int32) + (zz < m - 1).astype(jnp.int32))


def remote(src, dst, send_sem, recv_sem, device):
    return pltpu.make_async_remote_copy(
        src_ref=src, dst_ref=dst, send_sem=send_sem, recv_sem=recv_sem, device_id=device, device_id_type=MESH
    )


def head_prepare(v, gain, cosine, sine):
    v = v * lax.rsqrt(jnp.mean(v * v, axis=-1, keepdims=True) + NORM_EPS) * gain
    return v * cosine + pltpu.roll(v, HEAD_SIZE // 2, 1) * sine


def head_prepare_back(grad, v, gain, cosine, sine):
    grad = grad * cosine + pltpu.roll(grad * sine, HEAD_SIZE // 2, 1)
    r = lax.rsqrt(jnp.mean(v * v, axis=-1, keepdims=True) + NORM_EPS)
    unit = v * r
    by_gain = jnp.sum(grad * unit, axis=0, keepdims=True)
    grad = grad * gain
    return r * (grad - unit * jnp.mean(grad * unit, axis=-1, keepdims=True)), by_gain


def attend_back_kernel(m, q, kv, d_att, att, lse, qp, kp, q_gain, k_gain, cosine, sine, place_q, segment_k, dq_low, dk_low, dv_low, gains, partial, core_in, up_in, down_in, core_sem, up_sem, down_sem):
    tokens, length = q.shape[0], kv.shape[0]
    core, zz, to_core, to_line = group_place(m)
    greet(m, zz, to_core, to_line)
    cos, sin = cosine[...], sine[...]
    segment_q = place_q[:, 0:1]
    index_q = place_q[:, 1:2]
    index_k = lax.broadcasted_iota(jnp.int32, (tokens, length), 1)
    allowed = (segment_q == segment_k[...]) & (index_q >= index_k)
    lane = lax.broadcasted_iota(jnp.int32, (tokens, HEAD_SIZE), 1)
    gains[...] = jnp.zeros_like(gains)
    over_rows = (((0,), (0,)), ((), ()))
    over_columns = (((1,), (1,)), ((), ()))

    def core_copy(j):
        return remote(partial.at[j, 1 - core], core_in.at[j], core_sem.at[0, j], core_sem.at[1, j], to_core)

    def line_copy(j, up, here):
        low, high = (here + 1, m) if up else (0, here)
        into, sems = (up_in, up_sem) if up else (down_in, down_sem)
        return remote(
            partial.at[j, core, pl.ds(low, high - low)],
            into.at[j, pl.ds(low - (1 if up else 0), high - low)],
            sems.at[0, j],
            sems.at[1, j],
            to_line(1 if up else -1),
        )

    def add(j, place, value):
        partial[j, core, place] = (partial[j, core, place].astype(jnp.float32) + value.astype(jnp.float32)).astype(partial.dtype)

    def compute(j):
        for n in range(CHUNK_HEADS):
            keys = kv[:, pl.ds(pl.multiple_of(j * 2 * CHUNK + n * HEAD_SIZE, 128), HEAD_SIZE)]
            values = kv[:, pl.ds(pl.multiple_of(j * 2 * CHUNK + CHUNK + n * HEAD_SIZE, 128), HEAD_SIZE)]
            dk = dv = None
            for g in range(GROUP):
                h = (j * CHUNK_HEADS + n) * GROUP + g
                at = pl.ds(pl.multiple_of(h * HEAD_SIZE, 128), HEAD_SIZE)
                queries, grad = q[:, at], d_att[:, at]
                total = jnp.sum(jnp.where(lane == h, lse[...], 0.0), axis=-1, keepdims=True)
                delta = jnp.sum(grad.astype(jnp.float32) * att[:, at], axis=-1, keepdims=True)
                s = lax.dot_general(queries, keys, over_columns, preferred_element_type=jnp.float32)
                p = jnp.exp(jnp.where(allowed, s * SCORE_SCALE, VERY_NEGATIVE) - total)
                dp = lax.dot_general(grad, values, over_columns, preferred_element_type=jnp.float32)
                ds = (p * (dp - delta)).astype(queries.dtype)
                dq = jnp.dot(ds, keys, preferred_element_type=jnp.float32) * SCORE_SCALE
                here_k = lax.dot_general(ds, queries, over_rows, preferred_element_type=jnp.float32)
                here_v = lax.dot_general(p.astype(grad.dtype), grad, over_rows, preferred_element_type=jnp.float32)
                dk = here_k if dk is None else dk + here_k
                dv = here_v if dv is None else dv + here_v
                by_head, by_gain = head_prepare_back(dq, qp[:, at], q_gain[...], cos, sin)
                dq_low[:, at] = by_head.astype(dq_low.dtype)
                gains[0:1] += by_gain
            first = n * HEAD_SIZE
            partial[j, :, :, :, first : first + HEAD_SIZE] = (dk * SCORE_SCALE).astype(partial.dtype).reshape(2, m, tokens, HEAD_SIZE)
            first += CHUNK
            partial[j, :, :, :, first : first + HEAD_SIZE] = dv.astype(partial.dtype).reshape(2, m, tokens, HEAD_SIZE)
        core_copy(j).start()

    def take_core(j):
        core_copy(j).wait_recv()
        for place in range(m):
            add(j, place, core_in[j, place])

    def hop(j, h):
        for up in (True, False):
            here = h if up else m - 1 - h

            @pl.when(zz == here)
            def _():
                if h > 0:
                    line_copy(j, up, here - 1 if up else here + 1).wait_recv()
                    into = up_in if up else down_in
                    for place in range(here, m) if up else range(here + 1):
                        add(j, place, into[j, place - (1 if up else 0)])
                if h < m - 1:
                    line_copy(j, up, here).start()

    def finish(j):
        for n in range(CHUNK_HEADS):
            at = pl.ds(pl.multiple_of((j * CHUNK_HEADS + n) * HEAD_SIZE, 128), HEAD_SIZE)
            grad = partial[j, core, zz, :, n * HEAD_SIZE : (n + 1) * HEAD_SIZE].astype(jnp.float32)
            by_head, by_gain = head_prepare_back(grad, kp[:, at], k_gain[...], cos, sin)
            dk_low[:, at] = by_head.astype(dk_low.dtype)
            gains[1:2] += by_gain
        at = pl.ds(pl.multiple_of(j * CHUNK, 128), CHUNK)
        dv_low[:, at] = partial[j, core, zz, :, CHUNK:]
        core_copy(j).wait_send()
        for here in range(m):

            @pl.when(zz == here)
            def _():
                if here < m - 1:
                    line_copy(j, True, here).wait_send()
                if here > 0:
                    line_copy(j, False, here).wait_send()

    plan = [[compute], [take_core, functools.partial(hop, h=0)]]
    for h in range(1, m):
        plan.append([functools.partial(hop, h=h)])
    plan[-1].append(finish)

    def tick(t, carry):
        for depth in [*range(1, len(plan)), 0]:
            j = t - depth

            @pl.when((j >= 0) & (j < CHUNKS))
            def _():
                for stage in plan[depth]:
                    stage(j)

        return carry

    lax.fori_loop(0, CHUNKS + len(plan) - 1, tick, 0)


def attend_back(m, q, kv, d_att, att, lse, qp, kp, q_gain, k_gain, cosine, sine, place_q, segment_k, collective_id):
    tokens = q.shape[0]
    low = jnp.bfloat16
    dma = pltpu.SemaphoreType.DMA
    vmem = pl.BlockSpec(memory_space=pltpu.VMEM)
    return pl.pallas_call(
        functools.partial(attend_back_kernel, m),
        out_shape=[
            jax.ShapeDtypeStruct((tokens, QD), low),
            jax.ShapeDtypeStruct((tokens, KEY_FEATURES), low),
            jax.ShapeDtypeStruct((tokens, KEY_FEATURES), low),
            jax.ShapeDtypeStruct((8, HEAD_SIZE), jnp.float32),
        ],
        in_specs=[vmem] * 13,
        out_specs=[vmem] * 4,
        scratch_shapes=[
            pltpu.VMEM((CHUNKS, 2, m, tokens, 2 * CHUNK), low),
            pltpu.VMEM((CHUNKS, m, tokens, 2 * CHUNK), low),
            pltpu.VMEM((CHUNKS, max(m - 1, 1), tokens, 2 * CHUNK), low),
            pltpu.VMEM((CHUNKS, max(m - 1, 1), tokens, 2 * CHUNK), low),
            dma((2, CHUNKS)),
            dma((2, CHUNKS)),
            dma((2, CHUNKS)),
        ],
        compiler_params=pltpu.CompilerParams(
            collective_id=collective_id, has_side_effects=True, vmem_limit_bytes=48 * 1024 * 1024
        ),
    )(q, kv, d_att, att, lse, qp, kp, q_gain, k_gain, cosine, sine, place_q, segment_k)


WIDE_TILE, NARROW_TILE = 512, 256
IDLE = 2


def wholes_of(chunks):
    return list(dict.fromkeys(c[:2] for c in chunks))


def unit_rms(values):
    return values * lax.rsqrt(jnp.mean(values * values, axis=-1, keepdims=True) + NORM_EPS)


def forward_kernel(chunks, nx, nz, *refs):
    count = len(chunks)
    arrays = wholes_of(chunks)
    weights = 7
    gain_shard, shards, refs = refs[0], refs[1 : 1 + weights], refs[1 + weights :]
    tokens_here, cosine, sine, place_q, segment_k, refs = *refs[:5], refs[5:]
    wholes, refs = refs[: len(arrays)], refs[len(arrays) :]
    gains_out, tokens_out, hidden_out, last_out, refs = *refs[:4], refs[4:]
    saved_out, refs = [refs[n * SAVED : (n + 1) * SAVED] for n in range(LAYERS)], refs[LAYERS * SAVED :]
    own_sem, z_sem, x_sem, y_sem, core_sem, out_sem, refs = *refs[:6], refs[6:]
    gain_all, gains, low_tokens, h, normed, qp, kp, v, q, kv, att, att_low, lse, h_mid, n2, gate, up, act, last, refs = (
        *refs[:19],
        refs[19:],
    )
    wide_buf, output_buf, down_buf, refs = *refs[:3], refs[3:]
    tile_sem, save_sem, misc_sem, kv_core_sem, kv_line_sem, kv_core_out, kv_line_out = refs
    tokens, length = q.shape[0], kv.shape[1]
    m = nz // 2
    y = lax.axis_index("rep")
    shard = lax.axis_index("shard")
    z = lax.axis_index("ctx")
    core, x = lax.rem(shard, 2), lax.div(shard, 2)
    to_core = (y, x * 2 + 1 - core, z)
    to_y = (1 - y, shard, z)
    upper = z >= m
    moves = ((core == 0) & upper) | ((core == 1) & (z < m))
    to_swap = (y, x * 2 + 1 - core, jnp.where(upper, z - m, z + m))

    def to_x(step):
        return (y, shard + 2 * step, z)

    def to_z(step):
        return (y, shard, z + step)

    def own_part(k, start, size):
        weight, layer, column, width = chunks[k][:4]
        ref = gain_shard if weight < 0 else shards[weight].at[layer]
        return ref.at[pl.ds(start, size), pl.ds(column, width)]

    def whole_rows(k, first, size):
        weight, layer, column, width = chunks[k][:4]
        return wholes[arrays.index((weight, layer))].at[pl.ds(first, size), pl.ds(column, width)]

    def rows_of(k, xs, zs, start, size, of_core=core):
        first = ((xs * 2 + of_core) * nz + zs) * chunks[k][4] + start
        return whole_rows(k, pl.multiple_of(first, 16), size)

    def inplane(k):
        rows, near = chunks[k][4:]
        return y * (rows - near), near

    def arrived(ref, sem):
        pltpu.make_async_copy(ref, ref, sem).wait()

    def pass_z(k, src, zs, step, kind):
        start, size = inplane(k)
        remote(src, rows_of(k, x, zs, start, size), out_sem.at[k, kind], z_sem.at[k, zs], to_z(step)).start()

    def pass_x(k, src, xs, zs, step, kind):
        start, size = inplane(k)
        into = rows_of(k, xs, zs, start, size)
        remote(src, into, out_sem.at[k, kind], x_sem.at[k, xs * nz + zs], to_x(step)).start()

    def pass_y(k, xs, zs):
        rows, near = chunks[k][4:]
        if rows > near:
            part = rows_of(k, xs, zs, y * near, rows - near)
            remote(part, part, out_sem.at[k, 4], y_sem.at[k, xs * nz + zs], to_y).start()

    def pass_core(k, xs, zs, start, size):
        part = rows_of(k, xs, zs, start, size)
        remote(part, part, out_sem.at[k, 5], core_sem.at[k], to_core).start()

    def stage_own(k):
        rows = chunks[k][4]
        start, size = inplane(k)
        part = own_part(k, pl.multiple_of(start, 16), size)

        @pl.when(z < nz - 1)
        def _():
            pass_z(k, part, z, 1, 0)

        @pl.when(z > 0)
        def _():
            pass_z(k, part, z, -1, 1)

        @pl.when(x < nx - 1)
        def _():
            pass_x(k, part, x, z, 1, 2)

        @pl.when(x > 0)
        def _():
            pass_x(k, part, x, z, -1, 3)

        every = own_part(k, 0, rows)
        remote(every, rows_of(k, x, z, 0, rows), out_sem.at[k, 5], core_sem.at[k], to_core).start()
        pltpu.make_async_copy(every, rows_of(k, x, z, 0, rows), own_sem.at[k]).start()

    def stage_z(k, d):
        start, size = inplane(k)
        for step, kind in ((1, 0), (-1, 1)):
            zs = z - step * d

            @pl.when((zs >= 0) & (zs < nz))
            def _():
                part = rows_of(k, x, zs, start, size)
                arrived(part, z_sem.at[k, zs])

                @pl.when((z + step >= 0) & (z + step < nz))
                def _():
                    pass_z(k, part, zs, step, kind)

                @pl.when(x < nx - 1)
                def _():
                    pass_x(k, part, x, zs, 1, 2)

                @pl.when(x > 0)
                def _():
                    pass_x(k, part, x, zs, -1, 3)

                pass_y(k, x, zs)
                pass_core(k, x, zs, start, size)

    def stage_x(k, d):
        start, size = inplane(k)
        for step, kind in ((1, 2), (-1, 3)):
            xs = x - step * d

            @pl.when((xs >= 0) & (xs < nx))
            def _():
                def body(zs, carry):
                    part = rows_of(k, xs, zs, start, size)
                    arrived(part, x_sem.at[k, xs * nz + zs])
                    if nx > 2:

                        @pl.when((x + step >= 0) & (x + step < nx))
                        def _():
                            pass_x(k, part, xs, zs, step, kind)

                    pass_y(k, xs, zs)
                    pass_core(k, xs, zs, start, size)
                    return carry

                lax.fori_loop(0, nz, body, 0)

    def stage_y(k):
        rows, near = chunks[k][4:]
        if rows > near:

            def body(i, carry):
                xs, zs = lax.div(i, nz), lax.rem(i, nz)

                @pl.when((xs != x) | (zs != z))
                def _():
                    start = (1 - y) * near
                    arrived(rows_of(k, xs, zs, start, rows - near), y_sem.at[k, i])
                    pass_core(k, xs, zs, start, rows - near)

                return carry

            lax.fori_loop(0, nx * nz, body, 0)

    def first_rows(k, size):
        return whole_rows(k, 0, size)

    def complete(k):
        rows = chunks[k][4]
        arrived(first_rows(k, nx * nz * rows), core_sem.at[k])
        arrived(first_rows(k, rows), own_sem.at[k])

    def sent(k):
        rows, near = chunks[k][4:]
        for zz in range(nz):

            @pl.when(z == zz)
            def _():
                if zz < nz - 1:
                    arrived(first_rows(k, (zz + 1) * near), out_sem.at[k, 0])
                if zz > 0:
                    arrived(first_rows(k, (nz - zz) * near), out_sem.at[k, 1])

        for xx in range(nx):

            @pl.when(x == xx)
            def _():
                if xx < nx - 1:
                    arrived(first_rows(k, (xx + 1) * nz * near), out_sem.at[k, 2])
                if xx > 0:
                    arrived(first_rows(k, (nx - xx) * nz * near), out_sem.at[k, 3])

        if rows > near:
            arrived(first_rows(k, (nx * nz - 1) * (rows - near)), out_sem.at[k, 4])
        arrived(first_rows(k, nx * nz * rows), out_sem.at[k, 5])

    barrier = pltpu.get_barrier_semaphore()
    pl.semaphore_signal(barrier, inc=1, device_id=to_core, device_id_type=MESH)
    pl.semaphore_signal(barrier, inc=1, device_id=to_y, device_id_type=MESH)
    meets = ((z > 0, to_z(-1)), (z < nz - 1, to_z(1)), (x > 0, to_x(-1)), (x < nx - 1, to_x(1)), (moves, to_swap))
    greeted = 2
    for here, there in meets:

        @pl.when(here)
        def _():
            pl.semaphore_signal(barrier, inc=1, device_id=there, device_id_type=MESH)

        greeted = greeted + here.astype(jnp.int32)
    pl.semaphore_wait(barrier, greeted)

    def swap_copy():
        return remote(tokens_here, low_tokens, misc_sem.at[0], misc_sem.at[1], to_swap)

    def stay_copy():
        return pltpu.make_async_copy(tokens_here, low_tokens, misc_sem.at[1])

    @pl.when(moves)
    def _():
        swap_copy().start()

    @pl.when(~moves)
    def _():
        stay_copy().start()

    def begin():
        @pl.when(moves)
        def _():
            swap_copy().wait()

        @pl.when(~moves)
        def _():
            stay_copy().wait()

        h[...] = low_tokens[...].astype(jnp.float32)
        pltpu.make_async_copy(low_tokens, tokens_out, misc_sem.at[2]).start()

    def read_gains():
        complete(0)
        copy = pltpu.make_async_copy(wholes[0], gain_all, misc_sem.at[3])
        copy.start()
        copy.wait()
        gains[...] = jnp.zeros_like(gains)

        def body(n, carry):
            gains[...] += gain_all[pl.ds(pl.multiple_of(n * 16, 16), 16)].astype(jnp.float32)
            return carry

        lax.fori_loop(0, 2 * nx * nz, body, 0)
        pltpu.make_async_copy(gains, gains_out, misc_sem.at[4]).start()

    zz = lax.rem(z, m)

    def kv_part(layer, j, source, of_core=core):
        rows = pl.multiple_of((source + of_core * m) * tokens, 16)
        at = j * 2 * CHUNK if isinstance(j, int) else pl.multiple_of(j * 2 * CHUNK, 128)
        return kv.at[layer, pl.ds(rows, tokens), pl.ds(at, 2 * CHUNK)]

    def kv_core(layer, j, source, of_core=core):
        ref = kv_part(layer, j, source, of_core)
        return remote(ref, ref, kv_core_out.at[layer, j, source], kv_core_sem.at[layer, j, source], to_core)

    def kv_line(layer, j, source, step):
        ref = kv_part(layer, j, source)
        send_sem = kv_line_out.at[0 if step > 0 else 1, layer, j, source]
        return remote(ref, ref, send_sem, kv_line_sem.at[layer, j, source], to_z(step))

    def onward(layer, j, source, step, do):
        @pl.when((zz + step >= 0) & (zz + step < m))
        def _():
            do(kv_line(layer, j, source, step))

    start, ended = lambda copy: copy.start(), lambda copy: copy.wait_send()

    def kv_left(layer):
        for j in range(CHUNKS):
            for source in range(m):
                kv_core(layer, j, source).wait_send()
            for d in range(m):
                for step in (1, -1):
                    source = zz - step * d

                    @pl.when((source >= 0) & (source < m))
                    def _():
                        onward(layer, j, source, step, ended)

    saves = (normed, qp, kp, q, None, att, att_low, lse, h_mid, n2, gate, up, act)

    def save_copy(layer, n):
        source = kv.at[layer] if saves[n] is None else saves[n]
        into = saved_out[layer][SAVE_TO[n]]
        if n in LEFT_AT:
            into = into.at[:, pl.ds(LEFT_AT[n] * D, source.shape[1])]
        return pltpu.make_async_copy(source, into, save_sem.at[layer, n])

    def save(layer, *which):
        for n in which:
            save_copy(layer, n).start()

    def reusable(layer, *which):
        if layer > 0:
            for n in which:
                save_copy(layer - 1, n).wait()

    def layer_tasks(layer):
        parts = {w: [k for k, c in enumerate(chunks) if c[:2] == (w, layer)] for w in range(weights)}
        row = lambda n, width=D: gains[n + layer : n + layer + 1, :width]
        tasks = []

        def streamed(weight, buf, base, sems, tile, use, tiles):
            whole = wholes[arrays.index((weight, layer))]

            def copy(i):
                slot = base + i % 2
                source = whole.at[:, pl.ds(i * tile, tile)]
                return pltpu.make_async_copy(source, buf.at[slot], tile_sem.at[sems + i % 2])

            def first():
                for k in parts[weight]:
                    complete(k)
                copy(0).start()
                copy(1).start()

            def one(i):
                copy(i).wait()
                use(i, buf.at[base + i % 2])
                if i + 2 < tiles:
                    copy(i + 2).start()

            return first, [functools.partial(one, i) for i in range(tiles)], max(parts[weight])

        def put(k, *steps):
            tasks.append((k, lambda: [step() for step in steps]))

        def norm_first():
            if layer == 0:
                begin()
                read_gains()
            reusable(layer, 0)
            normed[...] = (unit_rms(h[...]) * row(0)).astype(normed.dtype)
            save(layer, 0)
            if layer > 0:
                pltpu.make_async_copy(h, hidden_out, misc_sem.at[5]).start()

        def keys(i, w):
            if i == 0:
                reusable(layer, 2)
            kp[:, i * WIDE_TILE : (i + 1) * WIDE_TILE] = jnp.dot(normed[...], w[...], preferred_element_type=jnp.float32)
            if i == 1:
                save(layer, 2)

        def values(i, w):
            term = jnp.dot(normed[...], w[...], preferred_element_type=jnp.float32)
            v[:, i * WIDE_TILE : (i + 1) * WIDE_TILE] = term.astype(v.dtype)

        def queries(i, w):
            if i == 0:
                reusable(layer, 1)
            qp[:, i * WIDE_TILE : (i + 1) * WIDE_TILE] = jnp.dot(normed[...], w[...], preferred_element_type=jnp.float32)
            if i == 3:
                save(layer, 1)

        cos = lambda: cosine[...]
        sin = lambda: sine[...]
        own_rows = pl.ds(pl.multiple_of((zz + core * m) * tokens, 16), tokens)

        def send_keys(j):
            for n in range(CHUNK_HEADS):
                hd = j * CHUNK_HEADS + n
                ready = head_prepare(kp[:, hd * HEAD_SIZE : (hd + 1) * HEAD_SIZE], row(6, HEAD_SIZE), cos(), sin())
                first = j * 2 * CHUNK + n * HEAD_SIZE
                kv[layer, own_rows, first : first + HEAD_SIZE] = ready.astype(kv.dtype)
            kv[layer, own_rows, j * 2 * CHUNK + CHUNK : (j + 1) * 2 * CHUNK] = v[:, j * CHUNK : (j + 1) * CHUNK]
            for step in (1, -1):
                onward(layer, j, zz, step, start)
            kv_core(layer, j, zz).start()

        def prepare_queries(part):
            if part == 0:
                reusable(layer, 3)
            for hd in range(part * 4, part * 4 + 4):
                at = slice(hd * HEAD_SIZE, (hd + 1) * HEAD_SIZE)
                q[:, at] = head_prepare(qp[:, at], row(4, HEAD_SIZE), cos(), sin()).astype(q.dtype)
            if part == 3:
                save(layer, 3)

        def arrivals(j):
            for d in range(1, m):
                for step in (1, -1):
                    source = zz - step * d

                    @pl.when((source >= 0) & (source < m))
                    def _():
                        kv_line(layer, j, source, step).wait_recv()
                        onward(layer, j, source, step, start)
                        kv_core(layer, j, source).start()

        def attend(j):
            if j == 0:
                reusable(layer, 5, 6, 7)
                lse[...] = jnp.zeros_like(lse)
            for source in range(m):
                kv_core(layer, j, source, 1 - core).wait_recv()
            index_k = lax.broadcasted_iota(jnp.int32, (tokens, length), 1)
            allowed = (place_q[:, 0:1] == segment_k[...]) & (place_q[:, 1:2] >= index_k)
            lane = lax.broadcasted_iota(jnp.int32, (tokens, HEAD_SIZE), 1)

            def head(n, carry):
                first = j * 2 * CHUNK + lax.div(n, GROUP) * HEAD_SIZE
                their_keys = kv[layer, :, pl.ds(pl.multiple_of(first, 128), HEAD_SIZE)]
                their_values = kv[layer, :, pl.ds(pl.multiple_of(first + CHUNK, 128), HEAD_SIZE)]
                hd = j * CHUNK_HEADS * GROUP + n
                at = pl.ds(pl.multiple_of(hd * HEAD_SIZE, 128), HEAD_SIZE)
                s = lax.dot_general(q[:, at], their_keys, (((1,), (1,)), ((), ())), preferred_element_type=jnp.float32)
                s = jnp.where(allowed, s * SCORE_SCALE, VERY_NEGATIVE)
                top = jnp.max(s, axis=-1, keepdims=True)
                p = jnp.exp(s - top)
                total = jnp.sum(p, axis=-1, keepdims=True)
                o = jnp.dot(p.astype(jnp.bfloat16), their_values, preferred_element_type=jnp.float32) / total
                att[:, at] = o
                att_low[:, at] = o.astype(att_low.dtype)
                lse[...] = jnp.where(lane == hd, top + jnp.log(total), lse[...])
                return carry

            lax.fori_loop(0, CHUNK_HEADS * GROUP, head, 0)
            if j == CHUNKS - 1:
                save(layer, 4, 5, 6, 7)

        def outputs(i, w):
            if i == 0:
                reusable(layer, 8)
            at = slice(i * NARROW_TILE, (i + 1) * NARROW_TILE)
            h_mid[:, at] = h[:, at] + jnp.dot(att_low[...], w[...], preferred_element_type=jnp.float32)
            if i == 3:
                save(layer, 8)

        def norm_second():
            reusable(layer, 9)
            n2[...] = (unit_rms(h_mid[...]) * row(2)).astype(n2.dtype)
            save(layer, 9)

        def gates(i, w):
            if i == 0:
                reusable(layer, 10, 12)
            gate[:, i * WIDE_TILE : (i + 1) * WIDE_TILE] = jnp.dot(n2[...], w[...], preferred_element_type=jnp.float32)

        def ups(i, w):
            if i == 0:
                reusable(layer, 11)
            at = slice(i * WIDE_TILE, (i + 1) * WIDE_TILE)
            term = jnp.dot(n2[...], w[...], preferred_element_type=jnp.float32)
            up[:, at] = term
            opened = gate[:, at]
            act[:, at] = (opened / (1.0 + jnp.exp(-opened)) * term).astype(act.dtype)
            if i == 5:
                save(layer, 10, 11, 12)

        def downs(i, w):
            if layer > 0 and i == 0:
                pltpu.make_async_copy(h, hidden_out, misc_sem.at[5]).wait()
            at = slice(i * NARROW_TILE, (i + 1) * NARROW_TILE)
            h[:, at] = h_mid[:, at] + jnp.dot(act[...], w[...], preferred_element_type=jnp.float32)

        first_k, key_tiles, kk = streamed(1, wide_buf, 0, 0, WIDE_TILE, keys, 2)
        first_v, value_tiles, kv_chunk = streamed(2, wide_buf, 2, 2, WIDE_TILE, values, 2)
        first_q, query_tiles, kq = streamed(0, wide_buf, 4, 8, WIDE_TILE, queries, 4)
        first_o, output_tiles, ko = streamed(3, output_buf, 0, 4, NARROW_TILE, outputs, 4)
        first_g, gate_tiles, kg = streamed(4, wide_buf, 0, 0, WIDE_TILE, gates, 6)
        first_u, up_tiles, ku = streamed(5, wide_buf, 2, 2, WIDE_TILE, ups, 6)
        first_d, down_tiles, kd = streamed(6, down_buf, 0, 6, NARROW_TILE, downs, 4)
        kqkv = max(kk, kv_chunk, kq)
        put(kqkv, first_k, first_v, first_q)
        put(kqkv, norm_first)
        put(kqkv, *key_tiles)
        put(kqkv, *value_tiles)
        put(kqkv, functools.partial(send_keys, 0), functools.partial(send_keys, 1))
        put(kqkv, functools.partial(send_keys, 2), functools.partial(send_keys, 3))
        put(kqkv, *query_tiles[:2])
        put(kqkv, *query_tiles[2:])
        for part in range(4):
            put(kqkv, functools.partial(prepare_queries, part))
        for j in range(CHUNKS):
            for _ in range(IDLE):
                put(kqkv)
            put(kqkv, functools.partial(arrivals, j))
            if j > 0:
                put(kqkv, functools.partial(attend, j - 1))
        for _ in range(IDLE // 2):
            put(kqkv)
        put(ko, first_o)
        put(kqkv, functools.partial(attend, CHUNKS - 1))
        put(ko, *output_tiles[:2])
        put(ko, *output_tiles[2:])
        put(kg, norm_second, first_g)
        for n in range(3):
            put(kg, *gate_tiles[2 * n : 2 * n + 2])
        put(ku, first_u)
        for n in range(3):
            put(ku, *up_tiles[2 * n : 2 * n + 2])
        put(kd, first_d)
        put(kd, *down_tiles[:2])
        put(kd, *down_tiles[2:])
        return tasks

    stages = [stage_own]
    stages += [functools.partial(stage_z, d=d) for d in range(1, nz)]
    stages += [functools.partial(stage_x, d=d) for d in range(1, nx)]
    stages += [stage_y]
    tasks = [task for layer in range(LAYERS) for task in layer_tasks(layer)]
    for tick in range(count + len(stages) - 1):
        for depth, stage in enumerate(stages):
            k = tick - depth
            if 0 <= k < count:
                stage(k)
            if tasks and tasks[0][0] + len(stages) <= tick:
                tasks.pop(0)[1]()
    for _, task in tasks:
        task()
    last[...] = h[...].astype(last.dtype)
    pltpu.make_async_copy(last, last_out, misc_sem.at[6]).start()
    for k in range(count):
        sent(k)
    for layer in range(LAYERS):
        kv_left(layer)
    for n in range(len(saves)):
        save_copy(LAYERS - 1, n).wait()
    save_copy(0, 4).wait()
    pltpu.make_async_copy(low_tokens, tokens_out, misc_sem.at[2]).wait()
    pltpu.make_async_copy(gains, gains_out, misc_sem.at[4]).wait()
    pltpu.make_async_copy(last, last_out, misc_sem.at[6]).wait()


LEFT_AT = {0: 6, 6: 3, 9: 5, 12: 0}
SAVE_TO = (0, 1, 2, 3, 4, 5, 0, 6, 7, 0, 8, 9, 0)
SAVED = 10


def forward(gain_shard, shards, tokens, tables, chunks, nx, nz, collective_id):
    count, m = len(chunks), nz // 2
    rows = tokens.shape[0]
    low, wide = jnp.bfloat16, jnp.float32
    dma, vmem = pltpu.SemaphoreType.DMA, pltpu.VMEM
    anywhere = pl.BlockSpec(memory_space=pl.ANY)
    arrays = [gain_shard if weight < 0 else shards[weight] for weight, _ in wholes_of(chunks)]
    ff = shards[4].shape[-1]
    left = ((rows, 7 * D), low)
    kept = [((rows, D), low), ((rows, QD), wide), ((rows, KEY_FEATURES), wide), ((rows, QD), low)]
    kept += [((2 * m * rows, 2 * KEY_FEATURES), low), ((rows, QD), wide), ((rows, QD), low), ((rows, HEAD_SIZE), wide)]
    kept += [((rows, D), wide), ((rows, D), low), ((rows, ff), wide), ((rows, ff), wide), ((rows, ff), low)]
    shape = jax.ShapeDtypeStruct
    outs = pl.pallas_call(
        functools.partial(forward_kernel, chunks, nx, nz),
        out_shape=[shape((a.shape[-2] * 2 * nx * nz, a.shape[-1]), low) for a in arrays]
        + [shape((16, D), wide), shape((rows, D), low), shape((rows, D), wide), shape((rows, D), low)]
        + [shape(*k) for k in [left, *kept[1:6], *kept[7:9], *kept[10:12]]] * LAYERS,
        in_specs=[anywhere] * (2 + len(shards)) + [pl.BlockSpec(memory_space=pltpu.VMEM)] * 4,
        out_specs=[anywhere] * (len(arrays) + 4 + SAVED * LAYERS),
        scratch_shapes=[
            dma((count,)),
            dma((count, nz)),
            dma((count, nx * nz)),
            dma((count, nx * nz)),
            dma((count,)),
            dma((count, 6)),
            vmem((16 * 2 * nx * nz, D), low),
            vmem((16, D), wide),
            vmem((rows, D), low),
            vmem((rows, D), wide),
            vmem(*kept[0]),
            vmem(*kept[1]),
            vmem(*kept[2]),
            vmem((rows, KEY_FEATURES), low),
            vmem(*kept[3]),
            vmem((LAYERS, *kept[4][0]), low),
            *[vmem(*k) for k in kept[5:]],
            vmem((rows, D), low),
            vmem((6, D, WIDE_TILE), low),
            vmem((2, QD, NARROW_TILE), low),
            vmem((2, ff, NARROW_TILE), low),
            dma((10,)),
            dma((LAYERS, len(SAVE_TO))),
            dma((7,)),
            dma((LAYERS, CHUNKS, m)),
            dma((LAYERS, CHUNKS, m)),
            dma((LAYERS, CHUNKS, m)),
            dma((2, LAYERS, CHUNKS, m)),
        ],
        compiler_params=pltpu.CompilerParams(
            collective_id=collective_id, has_side_effects=True, vmem_limit_bytes=56 * 1024 * 1024
        ),
    )(gain_shard, *shards, tokens, *tables)
    wholes, outs = outs[: len(arrays)], outs[len(arrays) :]
    return dict(zip(wholes_of(chunks), wholes)), outs[:4], [outs[4 + n * SAVED : 4 + (n + 1) * SAVED] for n in range(LAYERS)]


SLOTS = 4
PIECES = 15
LEFT_BLOCKS = (3, 2, 1, 1)
LEFT_FIRST = (0, 3, 5, 11)
RIGHTS = 7
RIGHT_FIRST = (0, 3, 5, 7, 9, 11, 13)
WEIGHT_BLOCKS = ((1, 3), (1, 2), (3, 1), (3, 1), (2, 1), (1, 1), (1, 1))


def piece_place(j, replica):
    if j < 2:
        return 0, replica, j
    if j == 2:
        return 0, 2, replica
    if j < 5:
        return 1, replica, j - 3
    if j < 11:
        return 2 + replica, 0, j - 5
    if replica == 0:
        return 4, 0, j - 11
    return (5, 0, j - 11) if j < 13 else (6, 0, j - 13)


def reduce_kernel(nx, nz, layers, *refs):
    per = 1 + 1 + 7
    held, refs = refs[0], refs[1:]
    operands, refs = refs[: layers * per], refs[layers * per :]
    gains, refs = refs[0], refs[1:]
    outs, refs = refs[: len(WEIGHT_BLOCKS)], refs[len(WEIGHT_BLOCKS) :]
    gains_out, left_at, refs = refs[0], refs[1:5], refs[5:]
    right_at, turned, total, x_in, zup_in, zdown_in, f_in, result, refs = *refs[:8], refs[8:]
    gain_in, gain_up, gain_down, refs = *refs[:3], refs[3:]
    left_sem, right_sem, x_sem, zup_sem, zdown_sem, f_sem, result_sem, gain_sem, credit = refs
    rows, width = total.shape[3:]
    tokens, wide = right_at.shape[2:]
    pieces = layers * PIECES
    ring = total.shape[0]
    y = lax.axis_index("rep")
    shard = lax.axis_index("shard")
    z = lax.axis_index("ctx")
    core, x = lax.rem(shard, 2), lax.div(shard, 2)
    to_core = (y, x * 2 + 1 - core, z)
    to_y = (1 - y, shard, z)

    def to_x(step):
        return (y, shard + 2 * step, z)

    def to_z(step):
        return (y, shard, z + step)

    barrier = pltpu.get_barrier_semaphore()
    pl.semaphore_signal(barrier, inc=1, device_id=to_core, device_id_type=MESH)
    pl.semaphore_signal(barrier, inc=1, device_id=to_y, device_id_type=MESH)
    for here, there in ((z > 0, to_z(-1)), (z < nz - 1, to_z(1)), (x > 0, to_x(-1)), (x < nx - 1, to_x(1))):

        @pl.when(here)
        def _():
            pl.semaphore_signal(barrier, inc=1, device_id=there, device_id_type=MESH)

    greeted = 2 + (z > 0).astype(jnp.int32) + (z < nz - 1).astype(jnp.int32)
    greeted = greeted + (x > 0).astype(jnp.int32) + (x < nx - 1).astype(jnp.int32)
    pl.semaphore_wait(barrier, greeted)

    def left_copies(k, layer, sources):
        span = nz * LEFT_BLOCKS[k] * rows
        base = sum(LEFT_BLOCKS[:k]) * wide
        sems = layer * 4 + k
        for whose, source in zip((0, 2), sources):

            def columns(xs, of_core):
                return source.at[:, pl.ds(pl.multiple_of(base + (xs * 2 + of_core) * span, 128), span)]

            for xs in range(nx):
                yield pltpu.make_async_copy(
                    columns(xs, core), left_at[k].at[whose, layer, xs], left_sem.at[whose, sems, xs]
                )
                yield remote(
                    columns(xs, 1 - core),
                    left_at[k].at[whose + 1, layer, xs],
                    left_sem.at[4 + whose, sems, xs],
                    left_sem.at[whose + 1, sems, xs],
                    to_core,
                )

    def own_right(b, source):
        return pltpu.make_async_copy(source, right_at.at[0, b], right_sem.at[0, b])

    def pair_right(b, source):
        return remote(source, right_at.at[1, b], right_sem.at[4, b], right_sem.at[1, b], to_core)

    def held_right(b, source):
        return pltpu.make_async_copy(source, right_at.at[2, b], right_sem.at[2, b])

    def replica_right(b, source):
        return remote(source, right_at.at[2, b], right_sem.at[5, b], right_sem.at[2, b], to_y)

    def passed_right(b, source):
        return remote(source, right_at.at[3, b], right_sem.at[6, b], right_sem.at[3, b], to_core)

    def fetch(i):
        for layer in range(layers):
            mine = operands[layer * per : (layer + 1) * per]
            lefts, their_lefts, down, output, gate, up, query, key, value = mine
            blocks = [((down, 0), (down, 0)), ((output, 0), (output, 0))]
            blocks += [((gate, n), (up, n)) for n in range(3)]
            blocks += [((query, 0), (key, 0)), ((query, 1), (value, 0))]
            for n in range(RIGHTS):

                @pl.when(i == layer * PIECES + RIGHT_FIRST[n])
                def _():
                    fetch_block(layer, n, lefts, their_lefts, blocks[n], held)

    def fetch_block(layer, n, lefts, their_lefts, block, their_down):
        b = layer * RIGHTS + n
        for replica in range(2):

            @pl.when(y == replica)
            def _():
                here, there = (
                    source.at[:, pl.ds(at * wide, wide)] for source, at in (block[replica], block[1 - replica])
                )
                if n > 0 or layer > 0:
                    replica_right(b, there).start()
                own_right(b, here).start()
                pair_right(b, here).start()

        if n == 0 and layer == 0:
            held_right(b, their_down).start()
            passed_right(b, their_down).start()
        for k, first in enumerate(LEFT_FIRST):
            if first == RIGHT_FIRST[n]:
                for copy in left_copies(k, layer, (lefts, their_lefts)):
                    copy.start()

    def place(i):
        return lax.div(i, PIECES), lax.rem(i, PIECES)

    def right_block(j):
        return jnp.where(j < 3, 0, jnp.where(j < 5, 1, lax.div(j - 1, 2)))

    def any_of(j, values):
        hit = j == values[0]
        for value in values[1:]:
            hit = hit | (j == value)
        return hit

    some_right = operands[2]

    def forward(i):
        layer, j = place(i)

        @pl.when(any_of(j, RIGHT_FIRST) & (i > 0))
        def _():
            b = layer * RIGHTS + right_block(j)
            replica_right(b, some_right).wait_recv()
            passed_right(b, right_at.at[2, b]).start()

    def product(i):
        layer, j = place(i)
        b = layer * RIGHTS + right_block(j)
        for k, first in enumerate(LEFT_FIRST):

            @pl.when(j == first)
            def _():
                for copy in left_copies(k, layer, operands[:2]):
                    copy.wait()

                for who in range(4):
                    for xs in range(nx):
                        flipped = left_at[k][who, layer, xs].T.reshape(nz, LEFT_BLOCKS[k], rows, tokens)
                        for n in range(LEFT_BLOCKS[k]):
                            turned[who, n, xs] = flipped[:, n]

        @pl.when(any_of(j, RIGHT_FIRST))
        def _():
            own_right(b, some_right).wait()
            pair_right(b, some_right).wait()
            passed_right(b, some_right).wait()

        @pl.when(i == 0)
        def _():
            held_right(b, some_right).wait()

        @pl.when(any_of(j, RIGHT_FIRST) & (i > 0))
        def _():
            replica_right(b, some_right).wait_send()

        slot = lax.rem(i, ring)
        part = jnp.where(j == 2, 2, jnp.where(j < 5, y, 0))
        half = jnp.where(j < 2, j, jnp.where(j == 2, y, lax.rem(j + 1, 2)))
        tile = width // 2

        def columns(c, carry):
            source = pl.ds(pl.multiple_of(half * width + c * tile, tile), tile)
            acc = None
            for who in range(4):
                left = turned[who, part].reshape(nx * nz * rows, tokens)
                term = jnp.dot(left, right_at[who, b, :, source], preferred_element_type=jnp.float32)
                acc = term if acc is None else acc + term
            into = pl.ds(pl.multiple_of(c * tile, tile), tile)
            total[slot, :, :, :, into] = acc.reshape(nx, nz, rows, tile).astype(total.dtype)
            return carry

        lax.fori_loop(0, 2, columns, 0)

    def give(i, flow, device):
        @pl.when(i + SLOTS < pieces)
        def _():
            pl.semaphore_signal(credit.at[flow], inc=1, device_id=device, device_id_type=MESH)

    def spend(i, flow):
        @pl.when(i >= SLOTS)
        def _():
            pl.semaphore_wait(credit.at[flow], 1)

    def add(slot, xs, zs, value):
        where = (slot, xs, zs)
        total[where] = (total[where].astype(jnp.float32) + value.astype(jnp.float32)).astype(total.dtype)

    def x_copy(i, up, here):
        low, high = (here + 1, nx) if up else (0, here)
        side = 0 if (up or nx == 2) else 1
        return remote(
            total.at[lax.rem(i, ring), pl.ds(low, high - low)],
            x_in.at[lax.rem(i, SLOTS), side, pl.ds(low - (1 if up else 0), high - low)],
            x_sem.at[0 if up else 1, i],
            x_sem.at[2 if up else 3, i],
            to_x(1 if up else -1),
        )

    def z_copy(i, up, here):
        low, high = (here + 1, nz) if up else (0, here)
        into = zup_in if up else zdown_in
        sems = zup_sem if up else zdown_sem
        return remote(
            total.at[lax.rem(i, ring), x, pl.ds(low, high - low)],
            into.at[lax.rem(i, SLOTS), pl.ds(low - (1 if up else 0), high - low)],
            sems.at[0, i],
            sems.at[1, i],
            to_z(1 if up else -1),
        )

    def x_hop(i, h):
        slot, small = lax.rem(i, ring), lax.rem(i, SLOTS)
        for up in (True, False):
            here = h if up else nx - 1 - h
            side = 0 if (up or nx == 2) else 1

            @pl.when(x == here)
            def _():
                if h > 0:
                    x_copy(i, up, here - 1 if up else here + 1).wait_recv()
                    for target in range(here, nx) if up else range(here + 1):

                        def body(zs, carry):
                            add(slot, target, zs, x_in[small, side, target - (1 if up else 0), zs])
                            return carry

                        lax.fori_loop(0, nz, body, 0)
                    give(i, 0 if up else 1, to_x(-1 if up else 1))
                if h < nx - 1:
                    spend(i, 0 if up else 1)
                    x_copy(i, up, here).start()

    def z_hop(i, h):
        slot, small = lax.rem(i, ring), lax.rem(i, SLOTS)
        for up in (True, False):
            here = h if up else nz - 1 - h

            @pl.when(z == here)
            def _():
                if h > 0:
                    z_copy(i, up, here - 1 if up else here + 1).wait_recv()
                    into = zup_in if up else zdown_in

                    def body(target, carry):
                        add(slot, x, target, into[small, target - (1 if up else 0)])
                        return carry

                    lax.fori_loop(here if up else 0, nz if up else here + 1, body, 0)
                    give(i, 2 if up else 3, to_z(-1 if up else 1))
                if h < nz - 1:
                    spend(i, 2 if up else 3)
                    z_copy(i, up, here).start()

    def f_copy(i):
        return remote(
            total.at[lax.rem(i, ring), x, z], f_in.at[lax.rem(i, SLOTS)], f_sem.at[0, i], f_sem.at[1, i], to_y
        )

    def send_f(i):
        spend(i, 4)
        f_copy(i).start()

    def result_copy(i, replica, into):
        two = lax.rem(i, 2)
        return pltpu.make_async_copy(result.at[two, replica], into, result_sem.at[two, replica])

    def keep_result(i, replica):
        layer, j = place(i)
        for n in range(PIECES):
            for r in range(2):

                @pl.when((j == n) & (replica == r))
                def _():
                    which, part, column = piece_place(n, r)
                    into = outs[which].at[layers - 1 - layer, pl.ds(part * rows, rows), pl.ds(column * width, width)]
                    result_copy(i, r, into).start()

    def result_kept(i):
        for r in range(2):
            result_copy(i, r, outs[5].at[0, :, pl.ds(0, width)]).wait()

    def finish(i):
        slot, small, two = lax.rem(i, ring), lax.rem(i, SLOTS), lax.rem(i, 2)
        f_copy(i).wait_recv()

        @pl.when(i >= 2)
        def _():
            result_kept(i - 2)

        result[two, y] = total[slot, x, z].astype(jnp.float32)
        result[two, 1 - y] = f_in[small].astype(jnp.float32)
        give(i, 4, to_y)
        keep_result(i, 0)
        keep_result(i, 1)
        f_copy(i).wait_send()
        for here in range(nx):

            @pl.when(x == here)
            def _():
                if here < nx - 1:
                    x_copy(i, True, here).wait_send()
                if here > 0:
                    x_copy(i, False, here).wait_send()

        for here in range(nz):

            @pl.when(z == here)
            def _():
                if here < nz - 1:
                    z_copy(i, True, here).wait_send()
                if here > 0:
                    z_copy(i, False, here).wait_send()

    def gain_copy(n, source, device):
        return remote(source, gain_in.at[n], gain_sem.at[0, n], gain_sem.at[1, n], device)

    def gain_start():
        copy = pltpu.make_async_copy(gains, gain_in.at[0], gain_sem.at[0, 0])
        copy.start()
        copy.wait()
        gain_copy(1, gain_in.at[0], to_core).start()

    def gain_pair():
        gain_copy(1, gain_in.at[0], to_core).wait()
        gain_up[0] = gain_in[0] + gain_in[1]
        gain_copy(2, gain_up.at[0], to_y).start()

    def gain_y():
        gain_copy(2, gain_up.at[0], to_y).wait()
        gain_in[0] = gain_up[0] + gain_in[2]

    def gain_hop(h, n, here, to, first, level):
        for up in (True, False):
            buffer = (gain_up if up else gain_down).at[level]
            slot = first if up else first + 1

            @pl.when(here == (h if up else n - 1 - h))
            def _():
                buffer[...] = gain_in[0]
                if h > 0:
                    gain_copy(slot, buffer, to(1 if up else -1)).wait_recv()
                    buffer[...] = gain_in[0] + gain_in[slot]
                if h < n - 1:
                    gain_copy(slot, buffer, to(1 if up else -1)).start()

    def gain_line(n, here, to, first, level):
        @pl.when(here < n - 1)
        def _():
            gain_copy(first, gain_up.at[level], to(1)).wait_send()

        @pl.when(here > 0)
        def _():
            gain_copy(first + 1, gain_down.at[level], to(-1)).wait_send()

        gain_in[0] = gain_up[level] + gain_down[level] - gain_in[0]

    def gain_end():
        copy = pltpu.make_async_copy(gain_in.at[0], gains_out, gain_sem.at[0, 0])
        copy.start()
        copy.wait()

    steps = [gain_start, gain_pair, gain_y]
    for h in range(nx):
        steps.append(functools.partial(gain_hop, h, nx, x, to_x, 3, 1))
    steps.append(functools.partial(gain_line, nx, x, to_x, 3, 1))
    for h in range(nz):
        steps.append(functools.partial(gain_hop, h, nz, z, to_z, 5, 2))
    steps.append(functools.partial(gain_line, nz, z, to_z, 5, 2))
    steps.append(gain_end)

    plan = [[fetch], [], [], [forward], [], [product], [functools.partial(x_hop, h=0)]]
    for h in range(1, nx):
        plan += [[], [functools.partial(x_hop, h=h)]]
    plan[-1].append(functools.partial(z_hop, h=0))
    for h in range(1, nz):
        plan.append([functools.partial(z_hop, h=h)])
    plan[-1].append(send_f)
    plan.append([finish])

    def tick(t, carry):
        for depth in [*range(6, len(plan)), 0, 3, 5]:
            if not plan[depth]:
                continue
            i = t - depth

            @pl.when((i >= 0) & (i < pieces))
            def _():
                for stage in plan[depth]:
                    stage(i)

        for n, step in enumerate(steps):
            pl.when(t == n)(step)
        return carry

    lax.fori_loop(0, pieces + len(plan) - 1, tick, 0)
    result_kept(pieces - 2)
    result_kept(pieces - 1)


def reduce_weights(operands, held, gains, nx, nz, collective_id):
    layers = len(operands)
    flat = [a for layer in operands for a in layer]
    tokens, wide = held.shape
    rows, width = wide // (2 * nx * nz), wide // 2
    pieces = layers * PIECES
    ring = 2 * nx + nz + 1
    sides = 1 if nx == 2 else 2
    low = jnp.bfloat16
    dma = pltpu.SemaphoreType.DMA
    anywhere = pl.BlockSpec(memory_space=pl.ANY)
    return pl.pallas_call(
        functools.partial(reduce_kernel, nx, nz, layers),
        out_shape=[
            jax.ShapeDtypeStruct((layers, rows * below, wide * across), jnp.float32) for across, below in WEIGHT_BLOCKS
        ]
        + [jax.ShapeDtypeStruct(gains.shape, gains.dtype)],
        in_specs=[anywhere] * (len(flat) + 2),
        out_specs=[anywhere] * (len(WEIGHT_BLOCKS) + 1),
        scratch_shapes=[pltpu.VMEM((4, layers, nx, tokens, nz * n * rows), low) for n in LEFT_BLOCKS]
        + [
            pltpu.VMEM((4, layers * RIGHTS, tokens, wide), low),
            pltpu.VMEM((4, max(LEFT_BLOCKS), nx, nz, rows, tokens), low),
            pltpu.VMEM((ring, nx, nz, rows, width), low),
            pltpu.VMEM((SLOTS, sides, nx - 1, nz, rows, width), low),
            pltpu.VMEM((SLOTS, nz - 1, rows, width), low),
            pltpu.VMEM((SLOTS, nz - 1, rows, width), low),
            pltpu.VMEM((SLOTS, rows, width), low),
            pltpu.VMEM((2, 2, rows, width), jnp.float32),
            pltpu.VMEM((7, *gains.shape), gains.dtype),
            pltpu.VMEM((3, *gains.shape), gains.dtype),
            pltpu.VMEM((3, *gains.shape), gains.dtype),
            dma((7, layers * 4, nx)),
            dma((7, layers * RIGHTS)),
            dma((4, pieces)),
            dma((2, pieces)),
            dma((2, pieces)),
            dma((2, pieces)),
            dma((2, 2)),
            dma((2, 7)),
            pltpu.SemaphoreType.REGULAR((5,)),
        ],
        compiler_params=pltpu.CompilerParams(
            collective_id=collective_id, has_side_effects=True, vmem_limit_bytes=56 * 1024 * 1024
        ),
    )(held, *flat, gains)


def segment_of(doc_ends, token_index):
    return jnp.sum((token_index[:, None] >= doc_ends[None, :]).astype(jnp.int32), axis=1)


def doc_layout(doc_ends, token_index):
    token_segment = segment_of(doc_ends, token_index)
    starts = jnp.concatenate([jnp.zeros((1,), jnp.int32), doc_ends])
    labels = jnp.arange(starts.shape[0], dtype=jnp.int32)
    doc_begin = jnp.sum(
        jnp.where(token_segment[:, None] == labels[None, :], starts[None, :], 0), axis=1
    )
    return (token_segment, token_index - doc_begin)


def rotary(positions, head_width):
    middle = head_width // 2
    inv_rates = jnp.exp(
        jnp.arange(middle, dtype=jnp.float32) * jnp.float32(-2.0 * math.log(ROPE_BASE) / head_width)
    )
    angles = positions.astype(jnp.float32)[:, None] * inv_rates[None, :]
    cosine = jnp.cos(angles)
    sine = jnp.sin(angles)
    return (jnp.concatenate([cosine, cosine], axis=1), jnp.concatenate([-sine, sine], axis=1))


def rms_scale(values, gain_vec):
    return (
        values * lax.rsqrt(jnp.mean(values * values, axis=-1, keepdims=True) + NORM_EPS) * gain_vec
    )


def swiglu(gate_pre, upward):
    return jax.nn.silu(gate_pre) * upward


def product(left, right):
    return jnp.dot(left, right, preferred_element_type=jnp.float32)


def product_back(grad, right):
    return lax.dot_general(grad, right, (((1,), (1,)), ((), ())), preferred_element_type=jnp.float32)


def over_replica(values):
    return lax.ppermute(values, "rep", [(0, 1), (1, 0)])


def after(value, others):
    value, *others = lax.optimization_barrier((value, *others))
    return value, others


def layer_back(upstream, hidden, weights, gains, saved, tables, m, which_layer, waiting):
    (
        query_weight,
        key_matrix,
        value_matrix,
        output_weight,
        gate_weight,
        up_weight,
        down_weight,
    ) = weights
    gain_first, gain_second = gains[which_layer], gains[2 + which_layer]
    gain_query, gain_key = gains[4 + which_layer, :HEAD_SIZE], gains[6 + which_layer, :HEAD_SIZE]
    (
        lefts,
        query_proj,
        key_projection,
        query_rows,
        keys_values,
        attended_rows,
        log_sum,
        hidden_mid,
        gate_pre,
        upward,
    ) = saved
    branch_low = upstream.astype(jnp.bfloat16)
    if which_layer == LAYERS - 1:
        waiting.append(over_replica(branch_low))
    grad_act = product_back(branch_low, down_weight)
    ignored, swiglu_back = jax.vjp(swiglu, gate_pre, upward)
    grad_gate_pre, grad_upward = swiglu_back(grad_act)
    gate_low = grad_gate_pre.astype(jnp.bfloat16)
    up_low = grad_upward.astype(jnp.bfloat16)
    grad_normed_two = product_back(gate_low, gate_weight) + product_back(up_low, up_weight)
    ignored, second_back = jax.vjp(rms_scale, hidden_mid, gain_second)
    grad_mid, grad_gain_second = second_back(grad_normed_two)
    upstream_mid = upstream + grad_mid
    attn_low = upstream_mid.astype(jnp.bfloat16)
    grad_attended = product_back(attn_low, output_weight).astype(jnp.bfloat16)
    if which_layer == 0:
        grad_attended, waiting[:1] = after(grad_attended, waiting[:1])
    query_low, key_low, value_low, head_gains = attend_back(
        m,
        query_rows,
        keys_values,
        grad_attended,
        attended_rows,
        log_sum,
        query_proj,
        key_projection,
        gain_query[None],
        gain_key[None],
        *tables,
        3,
    )
    grad_normed = product_back(query_low, query_weight)
    grad_normed = grad_normed + product_back(key_low, key_matrix)
    grad_normed = grad_normed + product_back(value_low, value_matrix)
    ignored, first_back = jax.vjp(rms_scale, hidden, gain_first)
    grad_hidden, grad_gain_first = first_back(grad_normed)
    rights = (branch_low, attn_low, gate_low, up_low, query_low, key_low, value_low)
    gain_grads = (grad_gain_first, head_gains[0], head_gains[1], grad_gain_second)
    return (upstream_mid + grad_hidden, (lefts, rights, gain_grads))


def near_rows(rows, share):
    return min(rows, -(-int(rows * share) // 16) * 16)


NEAR_SHARES = (0.75, 0.75, 0.75, 0.6, 0.5, 0.75, 0.55)
CUTS = (2, 1, 1, 2, 3, 3, 2)
ARRIVAL = [(weight, layer) for layer in range(LAYERS) for weight in (1, 2, 0, 3, 4, 5, 6)]


def run_forward(tokens, tables, weights, gains):
    nx, nz = lax.axis_size("shard") // 2, lax.axis_size("ctx")
    here = lax.axis_index("shard") * nz + lax.axis_index("ctx")
    block = jnp.zeros((16, D), jnp.bfloat16)
    for row, parts in ((0, gains[:2]), (4, gains[2:])):
        part = jnp.concatenate(parts)
        block = lax.dynamic_update_slice(block, part, (row, here * part.shape[1]))
    chunks = [(-1, 0, 0, D, 16, 16)]
    for weight, layer in ARRIVAL:
        rows, columns = weights[weight].shape[1:]
        near = near_rows(rows, NEAR_SHARES[weight])
        width = columns // CUTS[weight]
        for n in range(CUTS[weight]):
            chunks.append((weight, layer, n * width, width, rows, near))
    wholes, outs, saved = forward(block, weights, tokens, tables, tuple(chunks), nx, nz, 0)
    gathered = [[wholes[weight, layer] for weight in range(7)] for layer in range(LAYERS)]
    return gathered, outs, saved


def weight_gradients(operands, held):
    nx, nz = lax.axis_size("shard") // 2, lax.axis_size("ctx")
    shards = 2 * nx * nz
    flat = jnp.concatenate([g for _, gains in operands for g in gains])
    size = -(-flat.shape[0] // 1024) * 1024
    padded = jnp.zeros((size,), flat.dtype).at[: flat.shape[0]].set(flat).reshape(-1, 128)
    *grads, summed = reduce_weights([members for members, _ in operands[::-1]], held, padded, nx, nz, 1)
    summed = summed.reshape(-1)[: flat.shape[0]].reshape(LAYERS, -1)
    here = lax.axis_index("shard") * nz + lax.axis_index("ctx")
    small, used = [], 0
    for size in (D, HEAD_SIZE, HEAD_SIZE, D):
        own = size // shards
        small.append(lax.dynamic_slice_in_dim(summed, used + here * own, own, axis=1))
        used += size
    down, output, gate, up, query, key, value = grads
    return (small[0], query, key, value, small[1], small[2], output, small[3], gate, up, down)


def local(
    tokens,
    lengths,
    norm_one,
    w_query,
    w_key,
    w_value,
    query_gain,
    key_gain,
    w_output,
    norm_two,
    w_gate,
    w_up,
    w_down,
    cotangent,
):
    token_rows = tokens.shape[1]
    nx, nz = lax.axis_size("shard") // 2, lax.axis_size("ctx")
    m = nz // 2
    pairs = []
    for x in range(nx):
        for z in range(m):
            low, high = (2 * x + 1) * nz + z, 2 * x * nz + z + m
            same = (2 * x * nz + z, (2 * x + 1) * nz + z + m)
            pairs += [(low, high), (high, low)] + [(s, s) for s in same]

    def swap(values):
        return lax.ppermute(values, ("shard", "ctx"), pairs)

    lengths = swap(lengths)
    block = lax.axis_index("ctx") % m + (lax.axis_index("shard") % 2) * m
    token_index = block * token_rows + jnp.arange(token_rows, dtype=jnp.int32)
    doc_lengths = lengths[0]
    upto = jnp.arange(doc_lengths.shape[0])
    doc_ends = jnp.sum(jnp.where(upto[:, None] >= upto[None, :], doc_lengths[None, :], 0), axis=1)
    token_segment, positions = doc_layout(doc_ends, token_index)
    cosine, sine = rotary(positions, HEAD_SIZE)
    key_segment = segment_of(doc_ends, jnp.arange(token_rows * nz, dtype=jnp.int32))
    tables = (cosine, sine, jnp.stack([token_segment, token_index], axis=1), key_segment[None, :])
    gathered, (gains, tokens, hidden, last), saved = run_forward(
        tokens[0],
        tables,
        (w_query, w_key, w_value, w_output, w_gate, w_up, w_down),
        (norm_one, norm_two, query_gain, key_gain),
    )
    cotangent = swap(cotangent)
    output = swap(last)[None]
    hiddens = (tokens.astype(jnp.float32), hidden)
    waiting = [over_replica(lefts) for lefts, *_ in saved]
    live_mask = (token_segment < doc_lengths.shape[0]).astype(jnp.float32)
    upstream = cotangent[0].astype(jnp.float32) * live_mask[:, None]
    operands = [None] * LAYERS
    for which_layer in reversed(range(LAYERS)):
        upstream, operands[which_layer] = layer_back(
            upstream,
            hiddens[which_layer],
            gathered[which_layer],
            gains,
            saved[which_layer],
            tables,
            m,
            which_layer,
            waiting,
        )
    grad_tokens = swap(upstream.astype(jnp.bfloat16))[None]
    for which_layer, (lefts, rights, layer_gains) in enumerate(operands):
        operands[which_layer] = ((lefts, waiting[which_layer]) + rights, layer_gains)
    return (output, grad_tokens) + weight_gradients(operands, waiting[-1])


def solution(mesh):
    return jax.shard_map(
        local,
        mesh=mesh,
        in_specs=(
            P(("rep", "shard"), "ctx", None),
            P(("rep", "shard"), None),
            P(None, ("shard", "ctx")),
            P(None, ("shard", "ctx"), None),
            P(None, ("shard", "ctx"), None),
            P(None, ("shard", "ctx"), None),
            P(None, ("shard", "ctx")),
            P(None, ("shard", "ctx")),
            P(None, ("shard", "ctx"), None),
            P(None, ("shard", "ctx")),
            P(None, ("shard", "ctx"), None),
            P(None, ("shard", "ctx"), None),
            P(None, ("shard", "ctx"), None),
            P(("rep", "shard"), "ctx", None),
        ),
        out_specs=(
            P(("rep", "shard"), "ctx", None),
            P(("rep", "shard"), "ctx", None),
            P(None, ("shard", "ctx")),
            P(None, ("shard", "ctx"), None),
            P(None, ("shard", "ctx"), None),
            P(None, ("shard", "ctx"), None),
            P(None, ("shard", "ctx")),
            P(None, ("shard", "ctx")),
            P(None, ("shard", "ctx"), None),
            P(None, ("shard", "ctx")),
            P(None, ("shard", "ctx"), None),
            P(None, ("shard", "ctx"), None),
            P(None, ("shard", "ctx"), None),
        ),
        check_vma=False,
    )
```

```python
import functools
import math

import jax
import jax.numpy as jnp
from jax import lax
from jax.experimental import pallas as pl
from jax.experimental.pallas import tpu as pltpu
from jax.sharding import PartitionSpec as P

D = 1024
QUERY_HEADS = 16
KEYVALUE_HEADS = 8
HEAD_SIZE = 128
LAYERS = 2
QD = 2048
KEY_FEATURES = 1024


NORM_EPS = 1e-06
ROPE_BASE = 1000000.0
VERY_NEGATIVE = -1e30
MESH = pl.DeviceIdType.MESH


CHUNK_HEADS = 2
CHUNKS = KEYVALUE_HEADS // CHUNK_HEADS
CHUNK = CHUNK_HEADS * HEAD_SIZE
BACK_HEADS = 2
BACK_CHUNKS = KEYVALUE_HEADS // BACK_HEADS
BACK_WIDTH = BACK_HEADS * HEAD_SIZE
GROUP = QUERY_HEADS // KEYVALUE_HEADS
SCORE_SCALE = 1.0 / math.sqrt(HEAD_SIZE)


def group_place(m):
    y, shard, z = lax.axis_index("rep"), lax.axis_index("shard"), lax.axis_index("ctx")
    core, zz = lax.rem(shard, 2), lax.rem(z, m)
    to_core = (y, shard + 1 - 2 * core, z)

    def to_line(step):
        return (y, shard, z + step)

    return core, zz, to_core, to_line


def greet(m, zz, to_core, to_line):
    barrier = pltpu.get_barrier_semaphore()
    pl.semaphore_signal(barrier, inc=1, device_id=to_core, device_id_type=MESH)
    for here, there in ((zz > 0, to_line(-1)), (zz < m - 1, to_line(1))):

        @pl.when(here)
        def _():
            pl.semaphore_signal(barrier, inc=1, device_id=there, device_id_type=MESH)

    pl.semaphore_wait(barrier, 1 + (zz > 0).astype(jnp.int32) + (zz < m - 1).astype(jnp.int32))


def remote(src, dst, send_sem, recv_sem, device):
    return pltpu.make_async_remote_copy(
        src_ref=src, dst_ref=dst, send_sem=send_sem, recv_sem=recv_sem, device_id=device, device_id_type=MESH
    )


def head_prepare(v, gain, cosine, sine):
    v = v * lax.rsqrt(jnp.mean(v * v, axis=-1, keepdims=True) + NORM_EPS) * gain
    return v * cosine + pltpu.roll(v, HEAD_SIZE // 2, 1) * sine


def head_prepare_back(grad, v, gain, cosine, sine):
    grad = grad * cosine + pltpu.roll(grad * sine, HEAD_SIZE // 2, 1)
    r = lax.rsqrt(jnp.mean(v * v, axis=-1, keepdims=True) + NORM_EPS)
    unit = v * r
    by_gain = jnp.sum(grad * unit, axis=0, keepdims=True)
    grad = grad * gain
    return r * (grad - unit * jnp.mean(grad * unit, axis=-1, keepdims=True)), by_gain


def attend_back_kernel(m, q, kv, d_att, att, lse, qp, kp, q_gain, k_gain, cosine, sine, place_q, segment_k, dq_low, dk_low, dv_low, gains, partial, core_in, up_in, down_in, core_sem, up_sem, down_sem):
    tokens, length = q.shape[0], kv.shape[0]
    core, zz, to_core, to_line = group_place(m)
    greet(m, zz, to_core, to_line)
    cos, sin = cosine[...], sine[...]
    segment_q = place_q[:, 0:1]
    index_q = place_q[:, 1:2]
    index_k = lax.broadcasted_iota(jnp.int32, (tokens, length), 1)
    allowed = (segment_q == segment_k[...]) & (index_q >= index_k)
    lane = lax.broadcasted_iota(jnp.int32, (tokens, HEAD_SIZE), 1)
    gains[...] = jnp.zeros_like(gains)
    over_rows = (((0,), (0,)), ((), ()))
    over_columns = (((1,), (1,)), ((), ()))

    def core_copy(j):
        return remote(partial.at[j, 1 - core], core_in.at[j], core_sem.at[0, j], core_sem.at[1, j], to_core)

    def line_copy(j, up, here):
        low, high = (here + 1, m) if up else (0, here)
        into, sems = (up_in, up_sem) if up else (down_in, down_sem)
        return remote(
            partial.at[j, core, pl.ds(low, high - low)],
            into.at[j, pl.ds(low - (1 if up else 0), high - low)],
            sems.at[0, j],
            sems.at[1, j],
            to_line(1 if up else -1),
        )

    def add(j, place, value):
        partial[j, core, place] = (partial[j, core, place].astype(jnp.float32) + value.astype(jnp.float32)).astype(partial.dtype)

    def compute(j):
        for n in range(BACK_HEADS):
            one = j * BACK_HEADS + n
            first = lax.div(one, CHUNK_HEADS) * 2 * CHUNK + lax.rem(one, CHUNK_HEADS) * HEAD_SIZE
            keys = kv[:, pl.ds(pl.multiple_of(first, 128), HEAD_SIZE)]
            values = kv[:, pl.ds(pl.multiple_of(first + CHUNK, 128), HEAD_SIZE)]
            dk = dv = None
            for g in range(GROUP):
                h = one * GROUP + g
                at = pl.ds(pl.multiple_of(h * HEAD_SIZE, 128), HEAD_SIZE)
                queries, grad = q[:, at], d_att[:, at]
                total = jnp.sum(jnp.where(lane == h, lse[...], 0.0), axis=-1, keepdims=True)
                delta = jnp.sum(grad.astype(jnp.float32) * att[:, at], axis=-1, keepdims=True)
                s = lax.dot_general(queries, keys, over_columns, preferred_element_type=jnp.float32)
                p = jnp.exp(jnp.where(allowed, s * SCORE_SCALE, VERY_NEGATIVE) - total)
                dp = lax.dot_general(grad, values, over_columns, preferred_element_type=jnp.float32)
                ds = (p * (dp - delta)).astype(queries.dtype)
                dq = jnp.dot(ds, keys, preferred_element_type=jnp.float32) * SCORE_SCALE
                here_k = lax.dot_general(ds, queries, over_rows, preferred_element_type=jnp.float32)
                here_v = lax.dot_general(p.astype(grad.dtype), grad, over_rows, preferred_element_type=jnp.float32)
                dk = here_k if dk is None else dk + here_k
                dv = here_v if dv is None else dv + here_v
                by_head, by_gain = head_prepare_back(dq, qp[:, at], q_gain[...], cos, sin)
                dq_low[:, at] = by_head.astype(dq_low.dtype)
                gains[0:1] += by_gain
            first = n * HEAD_SIZE
            partial[j, :, :, :, first : first + HEAD_SIZE] = (dk * SCORE_SCALE).astype(partial.dtype).reshape(2, m, tokens, HEAD_SIZE)
            first += BACK_WIDTH
            partial[j, :, :, :, first : first + HEAD_SIZE] = dv.astype(partial.dtype).reshape(2, m, tokens, HEAD_SIZE)
        core_copy(j).start()

    def take_core(j):
        core_copy(j).wait_recv()
        for place in range(m):
            add(j, place, core_in[j, place])

    def hop(j, h):
        for up in (True, False):
            here = h if up else m - 1 - h

            @pl.when(zz == here)
            def _():
                if h > 0:
                    line_copy(j, up, here - 1 if up else here + 1).wait_recv()
                    into = up_in if up else down_in
                    for place in range(here, m) if up else range(here + 1):
                        add(j, place, into[j, place - (1 if up else 0)])
                if h < m - 1:
                    line_copy(j, up, here).start()

    def finish(j):
        for n in range(BACK_HEADS):
            at = pl.ds(pl.multiple_of((j * BACK_HEADS + n) * HEAD_SIZE, 128), HEAD_SIZE)
            grad = partial[j, core, zz, :, n * HEAD_SIZE : (n + 1) * HEAD_SIZE].astype(jnp.float32)
            by_head, by_gain = head_prepare_back(grad, kp[:, at], k_gain[...], cos, sin)
            dk_low[:, at] = by_head.astype(dk_low.dtype)
            gains[1:2] += by_gain
        at = pl.ds(pl.multiple_of(j * BACK_WIDTH, 128), BACK_WIDTH)
        dv_low[:, at] = partial[j, core, zz, :, BACK_WIDTH:]
        core_copy(j).wait_send()
        for here in range(m):

            @pl.when(zz == here)
            def _():
                if here < m - 1:
                    line_copy(j, True, here).wait_send()
                if here > 0:
                    line_copy(j, False, here).wait_send()

    plan = [[compute], [take_core, functools.partial(hop, h=0)]]
    for h in range(1, m):
        plan.append([functools.partial(hop, h=h)])
    plan[-1].append(finish)

    def tick(t, carry):
        for depth in range(len(plan)):
            j = t - depth

            @pl.when((j >= 0) & (j < BACK_CHUNKS))
            def _():
                for stage in plan[depth]:
                    stage(j)

        return carry

    lax.fori_loop(0, BACK_CHUNKS + len(plan) - 1, tick, 0)


def attend_back(m, q, kv, d_att, att, lse, qp, kp, q_gain, k_gain, cosine, sine, place_q, segment_k, collective_id):
    tokens = q.shape[0]
    low = jnp.bfloat16
    dma = pltpu.SemaphoreType.DMA
    vmem = pl.BlockSpec(memory_space=pltpu.VMEM)
    return pl.pallas_call(
        functools.partial(attend_back_kernel, m),
        out_shape=[
            jax.ShapeDtypeStruct((tokens, QD), low),
            jax.ShapeDtypeStruct((tokens, KEY_FEATURES), low),
            jax.ShapeDtypeStruct((tokens, KEY_FEATURES), low),
            jax.ShapeDtypeStruct((8, HEAD_SIZE), jnp.float32),
        ],
        in_specs=[vmem] * 13,
        out_specs=[vmem] * 4,
        scratch_shapes=[
            pltpu.VMEM((BACK_CHUNKS, 2, m, tokens, 2 * BACK_WIDTH), low),
            pltpu.VMEM((BACK_CHUNKS, m, tokens, 2 * BACK_WIDTH), low),
            pltpu.VMEM((BACK_CHUNKS, max(m - 1, 1), tokens, 2 * BACK_WIDTH), low),
            pltpu.VMEM((BACK_CHUNKS, max(m - 1, 1), tokens, 2 * BACK_WIDTH), low),
            dma((2, BACK_CHUNKS)),
            dma((2, BACK_CHUNKS)),
            dma((2, BACK_CHUNKS)),
        ],
        compiler_params=pltpu.CompilerParams(
            collective_id=collective_id, has_side_effects=True, vmem_limit_bytes=48 * 1024 * 1024
        ),
    )(q, kv, d_att, att, lse, qp, kp, q_gain, k_gain, cosine, sine, place_q, segment_k)


WIDE_TILE, NARROW_TILE = 512, 256
IDLE = 2


def wholes_of(chunks):
    return list(dict.fromkeys(c[:2] for c in chunks))


def unit_rms(values):
    return values * lax.rsqrt(jnp.mean(values * values, axis=-1, keepdims=True) + NORM_EPS)


def forward_kernel(chunks, nx, nz, *refs):
    count = len(chunks)
    arrays = wholes_of(chunks)
    weights = 7
    gain_shard, shards, refs = refs[0], refs[1 : 1 + weights], refs[1 + weights :]
    tokens_here, cosine, sine, place_q, segment_k, refs = *refs[:5], refs[5:]
    wholes, refs = refs[: len(arrays)], refs[len(arrays) :]
    gains_out, tokens_out, hidden_out, last_out, refs = *refs[:4], refs[4:]
    saved_out, refs = [refs[n * SAVED : (n + 1) * SAVED] for n in range(LAYERS)], refs[LAYERS * SAVED :]
    own_sem, z_sem, x_sem, y_sem, core_sem, out_sem, refs = *refs[:6], refs[6:]
    gain_all, gains, low_tokens, h, normed, qp, kp, v, q, kv, att, att_low, lse, h_mid, n2, gate, up, act, last, refs = (
        *refs[:19],
        refs[19:],
    )
    wide_buf, output_buf, down_buf, refs = *refs[:3], refs[3:]
    tile_sem, save_sem, misc_sem, kv_core_sem, kv_line_sem, kv_core_out, kv_line_out = refs
    tokens, length = q.shape[0], kv.shape[1]
    m = nz // 2
    y = lax.axis_index("rep")
    shard = lax.axis_index("shard")
    z = lax.axis_index("ctx")
    core, x = lax.rem(shard, 2), lax.div(shard, 2)
    to_core = (y, x * 2 + 1 - core, z)
    to_y = (1 - y, shard, z)
    upper = z >= m
    moves = ((core == 0) & upper) | ((core == 1) & (z < m))
    to_swap = (y, x * 2 + 1 - core, jnp.where(upper, z - m, z + m))

    def to_x(step):
        return (y, shard + 2 * step, z)

    def to_z(step):
        return (y, shard, z + step)

    def own_part(k, start, size):
        weight, layer, column, width = chunks[k][:4]
        ref = gain_shard if weight < 0 else shards[weight].at[layer]
        return ref.at[pl.ds(start, size), pl.ds(column, width)]

    def whole_rows(k, first, size):
        weight, layer, column, width = chunks[k][:4]
        return wholes[arrays.index((weight, layer))].at[pl.ds(first, size), pl.ds(column, width)]

    def rows_of(k, xs, zs, start, size, of_core=core):
        first = ((xs * 2 + of_core) * nz + zs) * chunks[k][4] + start
        return whole_rows(k, pl.multiple_of(first, 16), size)

    def inplane(k):
        rows, near = chunks[k][4:]
        return y * (rows - near), near

    def arrived(ref, sem):
        pltpu.make_async_copy(ref, ref, sem).wait()

    def pass_z(k, src, zs, step, kind):
        start, size = inplane(k)
        remote(src, rows_of(k, x, zs, start, size), out_sem.at[k, kind], z_sem.at[k, zs], to_z(step)).start()

    def pass_x(k, src, xs, zs, step, kind):
        start, size = inplane(k)
        into = rows_of(k, xs, zs, start, size)
        remote(src, into, out_sem.at[k, kind], x_sem.at[k, xs * nz + zs], to_x(step)).start()

    def pass_y(k, xs, zs):
        rows, near = chunks[k][4:]
        if rows > near:
            part = rows_of(k, xs, zs, y * near, rows - near)
            remote(part, part, out_sem.at[k, 4], y_sem.at[k, xs * nz + zs], to_y).start()

    def pass_core(k, xs, zs, start, size):
        part = rows_of(k, xs, zs, start, size)
        remote(part, part, out_sem.at[k, 5], core_sem.at[k], to_core).start()

    def stage_own(k):
        rows = chunks[k][4]
        start, size = inplane(k)
        part = own_part(k, pl.multiple_of(start, 16), size)

        @pl.when(z < nz - 1)
        def _():
            pass_z(k, part, z, 1, 0)

        @pl.when(z > 0)
        def _():
            pass_z(k, part, z, -1, 1)

        @pl.when(x < nx - 1)
        def _():
            pass_x(k, part, x, z, 1, 2)

        @pl.when(x > 0)
        def _():
            pass_x(k, part, x, z, -1, 3)

        every = own_part(k, 0, rows)
        remote(every, rows_of(k, x, z, 0, rows), out_sem.at[k, 5], core_sem.at[k], to_core).start()
        pltpu.make_async_copy(every, rows_of(k, x, z, 0, rows), own_sem.at[k]).start()

    def stage_z(k, d):
        start, size = inplane(k)
        for step, kind in ((1, 0), (-1, 1)):
            zs = z - step * d

            @pl.when((zs >= 0) & (zs < nz))
            def _():
                part = rows_of(k, x, zs, start, size)
                arrived(part, z_sem.at[k, zs])

                @pl.when((z + step >= 0) & (z + step < nz))
                def _():
                    pass_z(k, part, zs, step, kind)

                @pl.when(x < nx - 1)
                def _():
                    pass_x(k, part, x, zs, 1, 2)

                @pl.when(x > 0)
                def _():
                    pass_x(k, part, x, zs, -1, 3)

                pass_y(k, x, zs)
                pass_core(k, x, zs, start, size)

    def stage_x(k, d):
        start, size = inplane(k)
        for step, kind in ((1, 2), (-1, 3)):
            xs = x - step * d

            @pl.when((xs >= 0) & (xs < nx))
            def _():
                def body(zs, carry):
                    part = rows_of(k, xs, zs, start, size)
                    arrived(part, x_sem.at[k, xs * nz + zs])
                    if nx > 2:

                        @pl.when((x + step >= 0) & (x + step < nx))
                        def _():
                            pass_x(k, part, xs, zs, step, kind)

                    pass_y(k, xs, zs)
                    pass_core(k, xs, zs, start, size)
                    return carry

                lax.fori_loop(0, nz, body, 0)

    def stage_y(k):
        rows, near = chunks[k][4:]
        if rows > near:

            def body(i, carry):
                xs, zs = lax.div(i, nz), lax.rem(i, nz)

                @pl.when((xs != x) | (zs != z))
                def _():
                    start = (1 - y) * near
                    arrived(rows_of(k, xs, zs, start, rows - near), y_sem.at[k, i])
                    pass_core(k, xs, zs, start, rows - near)

                return carry

            lax.fori_loop(0, nx * nz, body, 0)

    def first_rows(k, size):
        return whole_rows(k, 0, size)

    def complete(k):
        rows = chunks[k][4]
        arrived(first_rows(k, nx * nz * rows), core_sem.at[k])
        arrived(first_rows(k, rows), own_sem.at[k])

    def sent(k):
        rows, near = chunks[k][4:]
        for zz in range(nz):

            @pl.when(z == zz)
            def _():
                if zz < nz - 1:
                    arrived(first_rows(k, (zz + 1) * near), out_sem.at[k, 0])
                if zz > 0:
                    arrived(first_rows(k, (nz - zz) * near), out_sem.at[k, 1])

        for xx in range(nx):

            @pl.when(x == xx)
            def _():
                if xx < nx - 1:
                    arrived(first_rows(k, (xx + 1) * nz * near), out_sem.at[k, 2])
                if xx > 0:
                    arrived(first_rows(k, (nx - xx) * nz * near), out_sem.at[k, 3])

        if rows > near:
            arrived(first_rows(k, (nx * nz - 1) * (rows - near)), out_sem.at[k, 4])
        arrived(first_rows(k, nx * nz * rows), out_sem.at[k, 5])

    barrier = pltpu.get_barrier_semaphore()
    pl.semaphore_signal(barrier, inc=1, device_id=to_core, device_id_type=MESH)
    pl.semaphore_signal(barrier, inc=1, device_id=to_y, device_id_type=MESH)
    meets = ((z > 0, to_z(-1)), (z < nz - 1, to_z(1)), (x > 0, to_x(-1)), (x < nx - 1, to_x(1)), (moves, to_swap))
    greeted = 2
    for here, there in meets:

        @pl.when(here)
        def _():
            pl.semaphore_signal(barrier, inc=1, device_id=there, device_id_type=MESH)

        greeted = greeted + here.astype(jnp.int32)
    pl.semaphore_wait(barrier, greeted)

    def swap_copy():
        return remote(tokens_here, low_tokens, misc_sem.at[0], misc_sem.at[1], to_swap)

    def stay_copy():
        return pltpu.make_async_copy(tokens_here, low_tokens, misc_sem.at[1])

    @pl.when(moves)
    def _():
        swap_copy().start()

    @pl.when(~moves)
    def _():
        stay_copy().start()

    def begin():
        @pl.when(moves)
        def _():
            swap_copy().wait()

        @pl.when(~moves)
        def _():
            stay_copy().wait()

        h[...] = low_tokens[...].astype(jnp.float32)
        pltpu.make_async_copy(low_tokens, tokens_out, misc_sem.at[2]).start()

    def read_gains():
        complete(0)
        copy = pltpu.make_async_copy(wholes[0], gain_all, misc_sem.at[3])
        copy.start()
        copy.wait()
        gains[...] = jnp.zeros_like(gains)

        def body(n, carry):
            gains[...] += gain_all[pl.ds(pl.multiple_of(n * 16, 16), 16)].astype(jnp.float32)
            return carry

        lax.fori_loop(0, 2 * nx * nz, body, 0)
        pltpu.make_async_copy(gains, gains_out, misc_sem.at[4]).start()

    zz = lax.rem(z, m)

    def kv_part(layer, j, source, of_core=core):
        rows = pl.multiple_of((source + of_core * m) * tokens, 16)
        at = j * 2 * CHUNK if isinstance(j, int) else pl.multiple_of(j * 2 * CHUNK, 128)
        return kv.at[layer, pl.ds(rows, tokens), pl.ds(at, 2 * CHUNK)]

    def kv_core(layer, j, source, of_core=core):
        ref = kv_part(layer, j, source, of_core)
        return remote(ref, ref, kv_core_out.at[layer, j, source], kv_core_sem.at[layer, j, source], to_core)

    def kv_line(layer, j, source, step):
        ref = kv_part(layer, j, source)
        send_sem = kv_line_out.at[0 if step > 0 else 1, layer, j, source]
        return remote(ref, ref, send_sem, kv_line_sem.at[layer, j, source], to_z(step))

    def onward(layer, j, source, step, do):
        @pl.when((zz + step >= 0) & (zz + step < m))
        def _():
            do(kv_line(layer, j, source, step))

    start, ended = lambda copy: copy.start(), lambda copy: copy.wait_send()

    def kv_left(layer):
        for j in range(CHUNKS):
            for source in range(m):
                kv_core(layer, j, source).wait_send()
            for d in range(m):
                for step in (1, -1):
                    source = zz - step * d

                    @pl.when((source >= 0) & (source < m))
                    def _():
                        onward(layer, j, source, step, ended)

    saves = (normed, qp, kp, q, None, att, att_low, lse, h_mid, n2, gate, up, act)

    def save_copy(layer, n):
        source = kv.at[layer] if saves[n] is None else saves[n]
        into = saved_out[layer][SAVE_TO[n]]
        if n in LEFT_AT:
            into = into.at[:, pl.ds(LEFT_AT[n] * D, source.shape[1])]
        return pltpu.make_async_copy(source, into, save_sem.at[layer, n])

    def save(layer, *which):
        for n in which:
            save_copy(layer, n).start()

    def reusable(layer, *which):
        if layer > 0:
            for n in which:
                save_copy(layer - 1, n).wait()

    def layer_tasks(layer):
        parts = {w: [k for k, c in enumerate(chunks) if c[:2] == (w, layer)] for w in range(weights)}
        row = lambda n, width=D: gains[n + layer : n + layer + 1, :width]
        tasks = []

        def streamed(weight, buf, base, sems, tile, use, tiles):
            whole = wholes[arrays.index((weight, layer))]

            def copy(i):
                slot = base + i % 2
                source = whole.at[:, pl.ds(i * tile, tile)]
                return pltpu.make_async_copy(source, buf.at[slot], tile_sem.at[sems + i % 2])

            def first():
                for k in parts[weight]:
                    complete(k)
                copy(0).start()
                copy(1).start()

            def one(i):
                copy(i).wait()
                use(i, buf.at[base + i % 2])
                if i + 2 < tiles:
                    copy(i + 2).start()

            return first, [functools.partial(one, i) for i in range(tiles)], max(parts[weight])

        def put(k, *steps):
            tasks.append((k, lambda: [step() for step in steps]))

        def norm_first():
            if layer == 0:
                begin()
                read_gains()
            reusable(layer, 0)
            normed[...] = (unit_rms(h[...]) * row(0)).astype(normed.dtype)
            save(layer, 0)
            if layer > 0:
                pltpu.make_async_copy(h, hidden_out, misc_sem.at[5]).start()

        def keys(i, w):
            if i == 0:
                reusable(layer, 2)
            kp[:, i * WIDE_TILE : (i + 1) * WIDE_TILE] = jnp.dot(normed[...], w[...], preferred_element_type=jnp.float32)
            if i == 1:
                save(layer, 2)

        def values(i, w):
            term = jnp.dot(normed[...], w[...], preferred_element_type=jnp.float32)
            v[:, i * WIDE_TILE : (i + 1) * WIDE_TILE] = term.astype(v.dtype)

        def queries(i, w):
            if i == 0:
                reusable(layer, 1)
            qp[:, i * WIDE_TILE : (i + 1) * WIDE_TILE] = jnp.dot(normed[...], w[...], preferred_element_type=jnp.float32)
            if i == 3:
                save(layer, 1)

        cos = lambda: cosine[...]
        sin = lambda: sine[...]
        own_rows = pl.ds(pl.multiple_of((zz + core * m) * tokens, 16), tokens)

        def send_keys(j):
            for n in range(CHUNK_HEADS):
                hd = j * CHUNK_HEADS + n
                ready = head_prepare(kp[:, hd * HEAD_SIZE : (hd + 1) * HEAD_SIZE], row(6, HEAD_SIZE), cos(), sin())
                first = j * 2 * CHUNK + n * HEAD_SIZE
                kv[layer, own_rows, first : first + HEAD_SIZE] = ready.astype(kv.dtype)
            kv[layer, own_rows, j * 2 * CHUNK + CHUNK : (j + 1) * 2 * CHUNK] = v[:, j * CHUNK : (j + 1) * CHUNK]
            for step in (1, -1):
                onward(layer, j, zz, step, start)
            kv_core(layer, j, zz).start()

        def prepare_queries(part):
            if part == 0:
                reusable(layer, 3)
            for hd in range(part * 4, part * 4 + 4):
                at = slice(hd * HEAD_SIZE, (hd + 1) * HEAD_SIZE)
                q[:, at] = head_prepare(qp[:, at], row(4, HEAD_SIZE), cos(), sin()).astype(q.dtype)
            if part == 3:
                save(layer, 3)

        def arrivals(j):
            for d in range(1, m):
                for step in (1, -1):
                    source = zz - step * d

                    @pl.when((source >= 0) & (source < m))
                    def _():
                        kv_line(layer, j, source, step).wait_recv()
                        onward(layer, j, source, step, start)
                        kv_core(layer, j, source).start()

        def attend(j):
            if j == 0:
                reusable(layer, 5, 6, 7)
                lse[...] = jnp.zeros_like(lse)
            for source in range(m):
                kv_core(layer, j, source, 1 - core).wait_recv()
            index_k = lax.broadcasted_iota(jnp.int32, (tokens, length), 1)
            allowed = (place_q[:, 0:1] == segment_k[...]) & (place_q[:, 1:2] >= index_k)
            lane = lax.broadcasted_iota(jnp.int32, (tokens, HEAD_SIZE), 1)

            def head(n, carry):
                first = j * 2 * CHUNK + lax.div(n, GROUP) * HEAD_SIZE
                their_keys = kv[layer, :, pl.ds(pl.multiple_of(first, 128), HEAD_SIZE)]
                their_values = kv[layer, :, pl.ds(pl.multiple_of(first + CHUNK, 128), HEAD_SIZE)]
                hd = j * CHUNK_HEADS * GROUP + n
                at = pl.ds(pl.multiple_of(hd * HEAD_SIZE, 128), HEAD_SIZE)
                s = lax.dot_general(q[:, at], their_keys, (((1,), (1,)), ((), ())), preferred_element_type=jnp.float32)
                s = jnp.where(allowed, s * SCORE_SCALE, VERY_NEGATIVE)
                top = jnp.max(s, axis=-1, keepdims=True)
                p = jnp.exp(s - top)
                total = jnp.sum(p, axis=-1, keepdims=True)
                o = jnp.dot(p.astype(jnp.bfloat16), their_values, preferred_element_type=jnp.float32) / total
                att[:, at] = o
                att_low[:, at] = o.astype(att_low.dtype)
                lse[...] = jnp.where(lane == hd, top + jnp.log(total), lse[...])
                return carry

            lax.fori_loop(0, CHUNK_HEADS * GROUP, head, 0)
            if j == CHUNKS - 1:
                save(layer, 4, 5, 6, 7)

        def outputs(i, w):
            if i == 0:
                reusable(layer, 8)
            at = slice(i * NARROW_TILE, (i + 1) * NARROW_TILE)
            h_mid[:, at] = h[:, at] + jnp.dot(att_low[...], w[...], preferred_element_type=jnp.float32)
            if i == 3:
                save(layer, 8)

        def norm_second():
            reusable(layer, 9)
            n2[...] = (unit_rms(h_mid[...]) * row(2)).astype(n2.dtype)
            save(layer, 9)

        def gates(i, w):
            if i == 0:
                reusable(layer, 10, 12)
            gate[:, i * WIDE_TILE : (i + 1) * WIDE_TILE] = jnp.dot(n2[...], w[...], preferred_element_type=jnp.float32)

        def ups(i, w):
            if i == 0:
                reusable(layer, 11)
            at = slice(i * WIDE_TILE, (i + 1) * WIDE_TILE)
            term = jnp.dot(n2[...], w[...], preferred_element_type=jnp.float32)
            up[:, at] = term
            opened = gate[:, at]
            act[:, at] = (opened / (1.0 + jnp.exp(-opened)) * term).astype(act.dtype)
            if i == 5:
                save(layer, 10, 11, 12)

        def downs(i, w):
            if layer > 0 and i == 0:
                pltpu.make_async_copy(h, hidden_out, misc_sem.at[5]).wait()
            at = slice(i * NARROW_TILE, (i + 1) * NARROW_TILE)
            h[:, at] = h_mid[:, at] + jnp.dot(act[...], w[...], preferred_element_type=jnp.float32)

        first_k, key_tiles, kk = streamed(1, wide_buf, 0, 0, WIDE_TILE, keys, 2)
        first_v, value_tiles, kv_chunk = streamed(2, wide_buf, 2, 2, WIDE_TILE, values, 2)
        first_q, query_tiles, kq = streamed(0, wide_buf, 4, 8, WIDE_TILE, queries, 4)
        first_o, output_tiles, ko = streamed(3, output_buf, 0, 4, NARROW_TILE, outputs, 4)
        first_g, gate_tiles, kg = streamed(4, wide_buf, 0, 0, WIDE_TILE, gates, 6)
        first_u, up_tiles, ku = streamed(5, wide_buf, 2, 2, WIDE_TILE, ups, 6)
        first_d, down_tiles, kd = streamed(6, down_buf, 0, 6, NARROW_TILE, downs, 4)
        kqkv = max(kk, kv_chunk, kq)
        put(kqkv, first_k, first_v, first_q)
        put(kqkv, norm_first)
        put(kqkv, *key_tiles)
        put(kqkv, *value_tiles)
        put(kqkv, functools.partial(send_keys, 0), functools.partial(send_keys, 1))
        put(kqkv, functools.partial(send_keys, 2), functools.partial(send_keys, 3))
        put(kqkv, *query_tiles[:2])
        put(kqkv, *query_tiles[2:])
        for part in range(4):
            put(kqkv, functools.partial(prepare_queries, part))
        for j in range(CHUNKS):
            for _ in range(IDLE):
                put(kqkv)
            put(kqkv, functools.partial(arrivals, j))
            if j > 0:
                put(kqkv, functools.partial(attend, j - 1))
        for _ in range(IDLE // 2):
            put(kqkv)
        put(ko, first_o)
        put(kqkv, functools.partial(attend, CHUNKS - 1))
        put(ko, *output_tiles[:2])
        put(ko, *output_tiles[2:])
        put(kg, norm_second, first_g)
        for n in range(3):
            put(kg, *gate_tiles[2 * n : 2 * n + 2])
        put(ku, first_u)
        for n in range(3):
            put(ku, *up_tiles[2 * n : 2 * n + 2])
        put(kd, first_d)
        put(kd, *down_tiles[:2])
        put(kd, *down_tiles[2:])
        return tasks

    stages = [stage_own]
    stages += [functools.partial(stage_z, d=d) for d in range(1, nz)]
    stages += [functools.partial(stage_x, d=d) for d in range(1, nx)]
    stages += [stage_y]
    tasks = [task for layer in range(LAYERS) for task in layer_tasks(layer)]
    for tick in range(count + len(stages) - 1):
        for depth, stage in enumerate(stages):
            k = tick - depth
            if 0 <= k < count:
                stage(k)
            if tasks and tasks[0][0] + len(stages) <= tick:
                tasks.pop(0)[1]()
    for _, task in tasks:
        task()
    last[...] = h[...].astype(last.dtype)
    pltpu.make_async_copy(last, last_out, misc_sem.at[6]).start()
    for k in range(count):
        sent(k)
    for layer in range(LAYERS):
        kv_left(layer)
    for n in range(len(saves)):
        save_copy(LAYERS - 1, n).wait()
    save_copy(0, 4).wait()
    pltpu.make_async_copy(low_tokens, tokens_out, misc_sem.at[2]).wait()
    pltpu.make_async_copy(gains, gains_out, misc_sem.at[4]).wait()
    pltpu.make_async_copy(last, last_out, misc_sem.at[6]).wait()


LEFT_AT = {0: 4, 9: 3, 12: 0}
SAVE_TO = (0, 2, 3, 4, 5, 6, 1, 7, 8, 0, 9, 10, 0)
SAVED = 11


def forward(gain_shard, shards, tokens, tables, chunks, nx, nz, collective_id):
    count, m = len(chunks), nz // 2
    rows = tokens.shape[0]
    low, wide = jnp.bfloat16, jnp.float32
    dma, vmem = pltpu.SemaphoreType.DMA, pltpu.VMEM
    anywhere = pl.BlockSpec(memory_space=pl.ANY)
    arrays = [gain_shard if weight < 0 else shards[weight] for weight, _ in wholes_of(chunks)]
    ff = shards[4].shape[-1]
    lefts = [((rows, ff + 2 * D), low), ((rows, QD), low)]
    kept = [((rows, D), low), ((rows, QD), wide), ((rows, KEY_FEATURES), wide), ((rows, QD), low)]
    kept += [((2 * m * rows, 2 * KEY_FEATURES), low), ((rows, QD), wide), ((rows, QD), low), ((rows, HEAD_SIZE), wide)]
    kept += [((rows, D), wide), ((rows, D), low), ((rows, ff), wide), ((rows, ff), wide), ((rows, ff), low)]
    shape = jax.ShapeDtypeStruct
    outs = pl.pallas_call(
        functools.partial(forward_kernel, chunks, nx, nz),
        out_shape=[shape((a.shape[-2] * 2 * nx * nz, a.shape[-1]), low) for a in arrays]
        + [shape((16, D), wide), shape((rows, D), low), shape((rows, D), wide), shape((rows, D), low)]
        + [shape(*k) for k in [*lefts, *kept[1:6], *kept[7:9], *kept[10:12]]] * LAYERS,
        in_specs=[anywhere] * (2 + len(shards)) + [pl.BlockSpec(memory_space=pltpu.VMEM)] * 4,
        out_specs=[anywhere] * (len(arrays) + 4 + SAVED * LAYERS),
        scratch_shapes=[
            dma((count,)),
            dma((count, nz)),
            dma((count, nx * nz)),
            dma((count, nx * nz)),
            dma((count,)),
            dma((count, 6)),
            vmem((16 * 2 * nx * nz, D), low),
            vmem((16, D), wide),
            vmem((rows, D), low),
            vmem((rows, D), wide),
            vmem(*kept[0]),
            vmem(*kept[1]),
            vmem(*kept[2]),
            vmem((rows, KEY_FEATURES), low),
            vmem(*kept[3]),
            vmem((LAYERS, *kept[4][0]), low),
            *[vmem(*k) for k in kept[5:]],
            vmem((rows, D), low),
            vmem((6, D, WIDE_TILE), low),
            vmem((2, QD, NARROW_TILE), low),
            vmem((2, ff, NARROW_TILE), low),
            dma((10,)),
            dma((LAYERS, len(SAVE_TO))),
            dma((7,)),
            dma((LAYERS, CHUNKS, m)),
            dma((LAYERS, CHUNKS, m)),
            dma((LAYERS, CHUNKS, m)),
            dma((2, LAYERS, CHUNKS, m)),
        ],
        compiler_params=pltpu.CompilerParams(
            collective_id=collective_id, has_side_effects=True, vmem_limit_bytes=56 * 1024 * 1024
        ),
    )(gain_shard, *shards, tokens, *tables)
    wholes, outs = outs[: len(arrays)], outs[len(arrays) :]
    return dict(zip(wholes_of(chunks), wholes)), outs[:4], [outs[4 + n * SAVED : 4 + (n + 1) * SAVED] for n in range(LAYERS)]


SLOTS = 4
AHEAD = 6
PIECES = 15
LEFT_BLOCKS = (3, 2, 1, 1)
LEFT_FIRST = (0, 3, 5, 11)
LEFT_BASE = (0, 0, 3, 4)
RIGHTS = 7
RIGHT_FIRST = (0, 3, 5, 7, 9, 11, 13)
WEIGHT_BLOCKS = ((1, 3), (1, 2), (3, 1), (3, 1), (2, 1), (1, 1), (1, 1))


def piece_place(j, replica):
    if j < 2:
        return 0, replica, j
    if j == 2:
        return 0, 2, replica
    if j < 5:
        return 1, replica, j - 3
    if j < 11:
        return 2 + replica, 0, j - 5
    if replica == 0:
        return 4, 0, j - 11
    return (5, 0, j - 11) if j < 13 else (6, 0, j - 13)


def reduce_kernel(nx, nz, layers, *refs):
    per = 2 + 2 + 7
    held, refs = refs[0], refs[1:]
    operands, refs = refs[: layers * per], refs[layers * per :]
    gains, refs = refs[0], refs[1:]
    outs, refs = refs[: len(WEIGHT_BLOCKS)], refs[len(WEIGHT_BLOCKS) :]
    gains_out, left_at, refs = refs[0], refs[1:5], refs[5:]
    right_at, turned, total, x_in, zup_in, zdown_in, f_in, result, landed, refs = *refs[:9], refs[9:]
    gain_in, gain_up, gain_down, refs = *refs[:3], refs[3:]
    left_sem, right_sem, x_sem, zup_sem, zdown_sem, f_sem, result_sem, gain_sem, landed_sem, credit = refs
    rows, width = total.shape[3:]
    tokens, wide = right_at.shape[2:]
    pieces = layers * PIECES
    ring = total.shape[0]
    y = lax.axis_index("rep")
    shard = lax.axis_index("shard")
    z = lax.axis_index("ctx")
    core, x = lax.rem(shard, 2), lax.div(shard, 2)
    to_core = (y, x * 2 + 1 - core, z)
    to_y = (1 - y, shard, z)

    def to_x(step):
        return (y, shard + 2 * step, z)

    def to_z(step):
        return (y, shard, z + step)

    barrier = pltpu.get_barrier_semaphore()
    pl.semaphore_signal(barrier, inc=1, device_id=to_core, device_id_type=MESH)
    pl.semaphore_signal(barrier, inc=1, device_id=to_y, device_id_type=MESH)
    for here, there in ((z > 0, to_z(-1)), (z < nz - 1, to_z(1)), (x > 0, to_x(-1)), (x < nx - 1, to_x(1))):

        @pl.when(here)
        def _():
            pl.semaphore_signal(barrier, inc=1, device_id=there, device_id_type=MESH)

    greeted = 2 + (z > 0).astype(jnp.int32) + (z < nz - 1).astype(jnp.int32)
    greeted = greeted + (x > 0).astype(jnp.int32) + (x < nx - 1).astype(jnp.int32)
    pl.semaphore_wait(barrier, greeted)

    def left_copies(k, layer, sources):
        span = nz * LEFT_BLOCKS[k] * rows
        base = LEFT_BASE[k] * wide
        sems = layer * 4 + k
        for whose, source in zip((0, 2), sources):

            def columns(xs, of_core):
                return source.at[:, pl.ds(pl.multiple_of(base + (xs * 2 + of_core) * span, 128), span)]

            for xs in range(nx):
                yield pltpu.make_async_copy(
                    columns(xs, core), left_at[k].at[whose, layer, xs], left_sem.at[whose, sems, xs]
                )
                yield remote(
                    columns(xs, 1 - core),
                    left_at[k].at[whose + 1, layer, xs],
                    left_sem.at[4 + whose, sems, xs],
                    left_sem.at[whose + 1, sems, xs],
                    to_core,
                )

    def own_right(b, source):
        return pltpu.make_async_copy(source, right_at.at[0, b], right_sem.at[0, b])

    def pair_right(b, source):
        return remote(source, right_at.at[1, b], right_sem.at[4, b], right_sem.at[1, b], to_core)

    def held_right(b, source):
        return pltpu.make_async_copy(source, right_at.at[2, b], right_sem.at[2, b])

    def replica_right(b, source):
        return remote(source, right_at.at[2, b], right_sem.at[5, b], right_sem.at[2, b], to_y)

    def passed_right(b, source):
        return remote(source, right_at.at[3, b], right_sem.at[6, b], right_sem.at[3, b], to_core)

    def attended_copy(layer, source):
        return remote(source, landed.at[layer - 1], landed_sem.at[0, layer], landed_sem.at[1, layer], to_y)

    def fetch(i):
        for layer in range(1, layers):

            @pl.when(i == layer * PIECES - AHEAD)
            def _():
                attended_copy(layer, operands[layer * per + 1]).start()

        for layer in range(layers):
            mine = operands[layer * per : (layer + 1) * per]
            lefts, their_lefts = mine[:2], mine[2:4]
            down, output, gate, up, query, key, value = mine[4:]
            blocks = [((down, 0), (down, 0)), ((output, 0), (output, 0))]
            blocks += [((gate, n), (up, n)) for n in range(3)]
            blocks += [((query, 0), (key, 0)), ((query, 1), (value, 0))]
            for n in range(RIGHTS):

                @pl.when(i == layer * PIECES + RIGHT_FIRST[n])
                def _():
                    fetch_block(layer, n, lefts, their_lefts, blocks[n], held)

    def fetch_block(layer, n, lefts, their_lefts, block, their_down):
        b = layer * RIGHTS + n
        for replica in range(2):

            @pl.when(y == replica)
            def _():
                here, there = (
                    source.at[:, pl.ds(at * wide, wide)] for source, at in (block[replica], block[1 - replica])
                )
                if n > 0 or layer > 0:
                    replica_right(b, there).start()
                own_right(b, here).start()
                pair_right(b, here).start()

        if n == 0 and layer == 0:
            held_right(b, their_down).start()
            passed_right(b, their_down).start()
        for k, first in enumerate(LEFT_FIRST):
            if first == RIGHT_FIRST[n]:
                n_left = 1 if k == 1 else 0
                theirs = their_lefts[n_left]
                if k == 1 and layer > 0:
                    theirs = landed.at[layer - 1]
                    attended_copy(layer, lefts[1]).wait_recv()
                for copy in left_copies(k, layer, (lefts[n_left], theirs)):
                    copy.start()

    def place(i):
        return lax.div(i, PIECES), lax.rem(i, PIECES)

    def right_block(j):
        return jnp.where(j < 3, 0, jnp.where(j < 5, 1, lax.div(j - 1, 2)))

    def any_of(j, values):
        hit = j == values[0]
        for value in values[1:]:
            hit = hit | (j == value)
        return hit

    some_right = operands[4]

    def forward(i):
        layer, j = place(i)

        @pl.when(any_of(j, RIGHT_FIRST) & (i > 0))
        def _():
            b = layer * RIGHTS + right_block(j)
            replica_right(b, some_right).wait_recv()
            passed_right(b, right_at.at[2, b]).start()

    def product(i):
        layer, j = place(i)
        b = layer * RIGHTS + right_block(j)
        for k, first in enumerate(LEFT_FIRST):

            @pl.when(j == first)
            def _():
                for copy in left_copies(k, layer, (operands[int(k == 1)],) * 2):
                    copy.wait()

                for who in range(4):
                    for xs in range(nx):
                        flipped = left_at[k][who, layer, xs].T.reshape(nz, LEFT_BLOCKS[k], rows, tokens)
                        for n in range(LEFT_BLOCKS[k]):
                            turned[who, n, xs] = flipped[:, n]

        @pl.when(any_of(j, RIGHT_FIRST))
        def _():
            own_right(b, some_right).wait()
            pair_right(b, some_right).wait()
            passed_right(b, some_right).wait()

        @pl.when(i == 0)
        def _():
            held_right(b, some_right).wait()

        @pl.when(any_of(j, RIGHT_FIRST) & (i > 0))
        def _():
            replica_right(b, some_right).wait_send()

        slot = lax.rem(i, ring)
        part = jnp.where(j == 2, 2, jnp.where(j < 5, y, 0))
        half = jnp.where(j < 2, j, jnp.where(j == 2, y, lax.rem(j + 1, 2)))
        tile = width // 2

        def columns(c, carry):
            source = pl.ds(pl.multiple_of(half * width + c * tile, tile), tile)
            acc = None
            for who in range(4):
                left = turned[who, part].reshape(nx * nz * rows, tokens)
                term = jnp.dot(left, right_at[who, b, :, source], preferred_element_type=jnp.float32)
                acc = term if acc is None else acc + term
            into = pl.ds(pl.multiple_of(c * tile, tile), tile)
            total[slot, :, :, :, into] = acc.reshape(nx, nz, rows, tile).astype(total.dtype)
            return carry

        lax.fori_loop(0, 2, columns, 0)

    def give(i, flow, device):
        @pl.when(i + SLOTS < pieces)
        def _():
            pl.semaphore_signal(credit.at[flow], inc=1, device_id=device, device_id_type=MESH)

    def spend(i, flow):
        @pl.when(i >= SLOTS)
        def _():
            pl.semaphore_wait(credit.at[flow], 1)

    def add(slot, xs, zs, value):
        where = (slot, xs, zs)
        total[where] = (total[where].astype(jnp.float32) + value.astype(jnp.float32)).astype(total.dtype)

    def x_copy(i, up, here):
        low, high = (here + 1, nx) if up else (0, here)
        side = 0 if (up or nx == 2) else 1
        return remote(
            total.at[lax.rem(i, ring), pl.ds(low, high - low)],
            x_in.at[lax.rem(i, SLOTS), side, pl.ds(low - (1 if up else 0), high - low)],
            x_sem.at[0 if up else 1, i],
            x_sem.at[2 if up else 3, i],
            to_x(1 if up else -1),
        )

    def z_copy(i, up, here):
        low, high = (here + 1, nz) if up else (0, here)
        into = zup_in if up else zdown_in
        sems = zup_sem if up else zdown_sem
        return remote(
            total.at[lax.rem(i, ring), x, pl.ds(low, high - low)],
            into.at[lax.rem(i, SLOTS), pl.ds(low - (1 if up else 0), high - low)],
            sems.at[0, i],
            sems.at[1, i],
            to_z(1 if up else -1),
        )

    def x_hop(i, h):
        slot, small = lax.rem(i, ring), lax.rem(i, SLOTS)
        for up in (True, False):
            here = h if up else nx - 1 - h
            side = 0 if (up or nx == 2) else 1

            @pl.when(x == here)
            def _():
                if h > 0:
                    x_copy(i, up, here - 1 if up else here + 1).wait_recv()
                    for target in range(here, nx) if up else range(here + 1):

                        def body(zs, carry):
                            add(slot, target, zs, x_in[small, side, target - (1 if up else 0), zs])
                            return carry

                        lax.fori_loop(0, nz, body, 0)
                    give(i, 0 if up else 1, to_x(-1 if up else 1))
                if h < nx - 1:
                    spend(i, 0 if up else 1)
                    x_copy(i, up, here).start()

    def z_hop(i, h):
        slot, small = lax.rem(i, ring), lax.rem(i, SLOTS)
        for up in (True, False):
            here = h if up else nz - 1 - h

            @pl.when(z == here)
            def _():
                if h > 0:
                    z_copy(i, up, here - 1 if up else here + 1).wait_recv()
                    into = zup_in if up else zdown_in

                    def body(target, carry):
                        add(slot, x, target, into[small, target - (1 if up else 0)])
                        return carry

                    lax.fori_loop(here if up else 0, nz if up else here + 1, body, 0)
                    give(i, 2 if up else 3, to_z(-1 if up else 1))
                if h < nz - 1:
                    spend(i, 2 if up else 3)
                    z_copy(i, up, here).start()

    def f_copy(i):
        return remote(
            total.at[lax.rem(i, ring), x, z], f_in.at[lax.rem(i, SLOTS)], f_sem.at[0, i], f_sem.at[1, i], to_y
        )

    def send_f(i):
        spend(i, 4)
        f_copy(i).start()

    def result_copy(i, replica, into):
        two = lax.rem(i, 2)
        return pltpu.make_async_copy(result.at[two, replica], into, result_sem.at[two, replica])

    def keep_result(i, replica):
        layer, j = place(i)
        for n in range(PIECES):
            for r in range(2):

                @pl.when((j == n) & (replica == r))
                def _():
                    which, part, column = piece_place(n, r)
                    into = outs[which].at[layers - 1 - layer, pl.ds(part * rows, rows), pl.ds(column * width, width)]
                    result_copy(i, r, into).start()

    def result_kept(i):
        for r in range(2):
            result_copy(i, r, outs[5].at[0, :, pl.ds(0, width)]).wait()

    def finish(i):
        slot, small, two = lax.rem(i, ring), lax.rem(i, SLOTS), lax.rem(i, 2)
        f_copy(i).wait_recv()

        @pl.when(i >= 2)
        def _():
            result_kept(i - 2)

        result[two, y] = total[slot, x, z].astype(jnp.float32)
        result[two, 1 - y] = f_in[small].astype(jnp.float32)
        give(i, 4, to_y)
        keep_result(i, 0)
        keep_result(i, 1)
        f_copy(i).wait_send()
        for here in range(nx):

            @pl.when(x == here)
            def _():
                if here < nx - 1:
                    x_copy(i, True, here).wait_send()
                if here > 0:
                    x_copy(i, False, here).wait_send()

        for here in range(nz):

            @pl.when(z == here)
            def _():
                if here < nz - 1:
                    z_copy(i, True, here).wait_send()
                if here > 0:
                    z_copy(i, False, here).wait_send()

    def gain_copy(n, source, device):
        return remote(source, gain_in.at[n], gain_sem.at[0, n], gain_sem.at[1, n], device)

    def gain_start():
        copy = pltpu.make_async_copy(gains, gain_in.at[0], gain_sem.at[0, 0])
        copy.start()
        copy.wait()
        gain_copy(1, gain_in.at[0], to_core).start()

    def gain_pair():
        gain_copy(1, gain_in.at[0], to_core).wait()
        gain_up[0] = gain_in[0] + gain_in[1]
        gain_copy(2, gain_up.at[0], to_y).start()

    def gain_y():
        gain_copy(2, gain_up.at[0], to_y).wait()
        gain_in[0] = gain_up[0] + gain_in[2]

    def gain_hop(h, n, here, to, first, level):
        for up in (True, False):
            buffer = (gain_up if up else gain_down).at[level]
            slot = first if up else first + 1

            @pl.when(here == (h if up else n - 1 - h))
            def _():
                buffer[...] = gain_in[0]
                if h > 0:
                    gain_copy(slot, buffer, to(1 if up else -1)).wait_recv()
                    buffer[...] = gain_in[0] + gain_in[slot]
                if h < n - 1:
                    gain_copy(slot, buffer, to(1 if up else -1)).start()

    def gain_line(n, here, to, first, level):
        @pl.when(here < n - 1)
        def _():
            gain_copy(first, gain_up.at[level], to(1)).wait_send()

        @pl.when(here > 0)
        def _():
            gain_copy(first + 1, gain_down.at[level], to(-1)).wait_send()

        gain_in[0] = gain_up[level] + gain_down[level] - gain_in[0]

    def gain_end():
        copy = pltpu.make_async_copy(gain_in.at[0], gains_out, gain_sem.at[0, 0])
        copy.start()
        copy.wait()

    steps = [gain_start, gain_pair, gain_y]
    for h in range(nx):
        steps.append(functools.partial(gain_hop, h, nx, x, to_x, 3, 1))
    steps.append(functools.partial(gain_line, nx, x, to_x, 3, 1))
    for h in range(nz):
        steps.append(functools.partial(gain_hop, h, nz, z, to_z, 5, 2))
    steps.append(functools.partial(gain_line, nz, z, to_z, 5, 2))
    steps.append(gain_end)

    plan = [[fetch], [], [], [forward], [], [product], [functools.partial(x_hop, h=0)]]
    for h in range(1, nx):
        plan += [[], [functools.partial(x_hop, h=h)]]
    plan[-1].append(functools.partial(z_hop, h=0))
    for h in range(1, nz):
        plan.append([functools.partial(z_hop, h=h)])
    plan[-1].append(send_f)
    plan += [[], [finish]]

    def tick(t, carry):
        for depth in [*range(6, len(plan)), 0, 3, 5]:
            if not plan[depth]:
                continue
            i = t - depth

            @pl.when((i >= 0) & (i < pieces))
            def _():
                for stage in plan[depth]:
                    stage(i)

        for n, step in enumerate(steps):
            pl.when(t == n)(step)
        return carry

    lax.fori_loop(0, pieces + len(plan) - 1, tick, 0)
    result_kept(pieces - 2)
    result_kept(pieces - 1)
    for layer in range(1, layers):
        attended_copy(layer, operands[layer * per + 1]).wait_send()


def reduce_weights(operands, held, gains, nx, nz, collective_id):
    layers = len(operands)
    flat = [a for layer in operands for a in layer]
    tokens, wide = held.shape
    rows, width = wide // (2 * nx * nz), wide // 2
    pieces = layers * PIECES
    ring = 2 * nx + nz + 2
    sides = 1 if nx == 2 else 2
    low = jnp.bfloat16
    dma = pltpu.SemaphoreType.DMA
    anywhere = pl.BlockSpec(memory_space=pl.ANY)
    return pl.pallas_call(
        functools.partial(reduce_kernel, nx, nz, layers),
        out_shape=[
            jax.ShapeDtypeStruct((layers, rows * below, wide * across), jnp.float32) for across, below in WEIGHT_BLOCKS
        ]
        + [jax.ShapeDtypeStruct(gains.shape, gains.dtype)],
        in_specs=[anywhere] * (len(flat) + 2),
        out_specs=[anywhere] * (len(WEIGHT_BLOCKS) + 1),
        scratch_shapes=[pltpu.VMEM((4, layers, nx, tokens, nz * n * rows), low) for n in LEFT_BLOCKS]
        + [
            pltpu.VMEM((4, layers * RIGHTS, tokens, wide), low),
            pltpu.VMEM((4, max(LEFT_BLOCKS), nx, nz, rows, tokens), low),
            pltpu.VMEM((ring, nx, nz, rows, width), low),
            pltpu.VMEM((SLOTS, sides, nx - 1, nz, rows, width), low),
            pltpu.VMEM((SLOTS, nz - 1, rows, width), low),
            pltpu.VMEM((SLOTS, nz - 1, rows, width), low),
            pltpu.VMEM((SLOTS, rows, width), low),
            pltpu.VMEM((2, 2, rows, width), jnp.float32),
            pltpu.VMEM((layers - 1, tokens, 2 * wide), low),
            pltpu.VMEM((7, *gains.shape), gains.dtype),
            pltpu.VMEM((3, *gains.shape), gains.dtype),
            pltpu.VMEM((3, *gains.shape), gains.dtype),
            dma((7, layers * 4, nx)),
            dma((7, layers * RIGHTS)),
            dma((4, pieces)),
            dma((2, pieces)),
            dma((2, pieces)),
            dma((2, pieces)),
            dma((2, 2)),
            dma((2, 7)),
            dma((2, layers)),
            pltpu.SemaphoreType.REGULAR((5,)),
        ],
        compiler_params=pltpu.CompilerParams(
            collective_id=collective_id, has_side_effects=True, vmem_limit_bytes=56 * 1024 * 1024
        ),
    )(held, *flat, gains)


def segment_of(doc_ends, token_index):
    return jnp.sum((token_index[:, None] >= doc_ends[None, :]).astype(jnp.int32), axis=1)


def doc_layout(doc_ends, token_index):
    token_segment = segment_of(doc_ends, token_index)
    starts = jnp.concatenate([jnp.zeros((1,), jnp.int32), doc_ends])
    labels = jnp.arange(starts.shape[0], dtype=jnp.int32)
    doc_begin = jnp.sum(
        jnp.where(token_segment[:, None] == labels[None, :], starts[None, :], 0), axis=1
    )
    return (token_segment, token_index - doc_begin)


def rotary(positions, head_width):
    middle = head_width // 2
    inv_rates = jnp.exp(
        jnp.arange(middle, dtype=jnp.float32) * jnp.float32(-2.0 * math.log(ROPE_BASE) / head_width)
    )
    angles = positions.astype(jnp.float32)[:, None] * inv_rates[None, :]
    cosine = jnp.cos(angles)
    sine = jnp.sin(angles)
    return (jnp.concatenate([cosine, cosine], axis=1), jnp.concatenate([-sine, sine], axis=1))


def rms_scale(values, gain_vec):
    return (
        values * lax.rsqrt(jnp.mean(values * values, axis=-1, keepdims=True) + NORM_EPS) * gain_vec
    )


def swiglu(gate_pre, upward):
    return jax.nn.silu(gate_pre) * upward


def product(left, right):
    return jnp.dot(left, right, preferred_element_type=jnp.float32)


def product_back(grad, right):
    return lax.dot_general(grad, right, (((1,), (1,)), ((), ())), preferred_element_type=jnp.float32)


def over_replica(values):
    return lax.ppermute(values, "rep", [(0, 1), (1, 0)])


def after(value, others):
    value, *others = lax.optimization_barrier((value, *others))
    return value, others


def layer_back(upstream, hidden, weights, gains, saved, tables, m, which_layer, waiting):
    (
        query_weight,
        key_matrix,
        value_matrix,
        output_weight,
        gate_weight,
        up_weight,
        down_weight,
    ) = weights
    gain_first, gain_second = gains[which_layer], gains[2 + which_layer]
    gain_query, gain_key = gains[4 + which_layer, :HEAD_SIZE], gains[6 + which_layer, :HEAD_SIZE]
    (
        lefts,
        attended_low,
        query_proj,
        key_projection,
        query_rows,
        keys_values,
        attended_rows,
        log_sum,
        hidden_mid,
        gate_pre,
        upward,
    ) = saved
    branch_low = upstream.astype(jnp.bfloat16)
    if which_layer == LAYERS - 1:
        waiting.append(over_replica(branch_low))
    grad_act = product_back(branch_low, down_weight)
    ignored, swiglu_back = jax.vjp(swiglu, gate_pre, upward)
    grad_gate_pre, grad_upward = swiglu_back(grad_act)
    gate_low = grad_gate_pre.astype(jnp.bfloat16)
    up_low = grad_upward.astype(jnp.bfloat16)
    grad_normed_two = product_back(gate_low, gate_weight) + product_back(up_low, up_weight)
    ignored, second_back = jax.vjp(rms_scale, hidden_mid, gain_second)
    grad_mid, grad_gain_second = second_back(grad_normed_two)
    upstream_mid = upstream + grad_mid
    attn_low = upstream_mid.astype(jnp.bfloat16)
    grad_attended = product_back(attn_low, output_weight).astype(jnp.bfloat16)
    if which_layer == 0:
        grad_attended, waiting[:1] = after(grad_attended, waiting[:1])
    query_low, key_low, value_low, head_gains = attend_back(
        m,
        query_rows,
        keys_values,
        grad_attended,
        attended_rows,
        log_sum,
        query_proj,
        key_projection,
        gain_query[None],
        gain_key[None],
        *tables,
        3,
    )
    grad_normed = product_back(query_low, query_weight)
    grad_normed = grad_normed + product_back(key_low, key_matrix)
    grad_normed = grad_normed + product_back(value_low, value_matrix)
    ignored, first_back = jax.vjp(rms_scale, hidden, gain_first)
    grad_hidden, grad_gain_first = first_back(grad_normed)
    rights = (branch_low, attn_low, gate_low, up_low, query_low, key_low, value_low)
    gain_grads = (grad_gain_first, head_gains[0], head_gains[1], grad_gain_second)
    return (upstream_mid + grad_hidden, ((lefts, attended_low), rights, gain_grads))


def near_rows(rows, share):
    return min(rows, -(-int(rows * share) // 16) * 16)


NEAR_SHARES = (0.75, 0.75, 0.75, 0.6, 0.5, 0.75, 0.55)
CUTS = (2, 1, 1, 2, 3, 3, 2)
ARRIVAL = [(weight, layer) for layer in range(LAYERS) for weight in (1, 2, 0, 3, 4, 5, 6)]


def run_forward(tokens, tables, weights, gains):
    nx, nz = lax.axis_size("shard") // 2, lax.axis_size("ctx")
    here = lax.axis_index("shard") * nz + lax.axis_index("ctx")
    block = jnp.zeros((16, D), jnp.bfloat16)
    for row, parts in ((0, gains[:2]), (4, gains[2:])):
        part = jnp.concatenate(parts)
        block = lax.dynamic_update_slice(block, part, (row, here * part.shape[1]))
    chunks = [(-1, 0, 0, D, 16, 16)]
    for weight, layer in ARRIVAL:
        rows, columns = weights[weight].shape[1:]
        near = near_rows(rows, NEAR_SHARES[weight])
        width = columns // CUTS[weight]
        for n in range(CUTS[weight]):
            chunks.append((weight, layer, n * width, width, rows, near))
    wholes, outs, saved = forward(block, weights, tokens, tables, tuple(chunks), nx, nz, 0)
    gathered = [[wholes[weight, layer] for weight in range(7)] for layer in range(LAYERS)]
    return gathered, outs, saved


def weight_gradients(operands, held):
    nx, nz = lax.axis_size("shard") // 2, lax.axis_size("ctx")
    shards = 2 * nx * nz
    flat = jnp.concatenate([g for _, gains in operands for g in gains])
    size = -(-flat.shape[0] // 1024) * 1024
    padded = jnp.zeros((size,), flat.dtype).at[: flat.shape[0]].set(flat).reshape(-1, 128)
    *grads, summed = reduce_weights([members for members, _ in operands[::-1]], held, padded, nx, nz, 1)
    summed = summed.reshape(-1)[: flat.shape[0]].reshape(LAYERS, -1)
    here = lax.axis_index("shard") * nz + lax.axis_index("ctx")
    small, used = [], 0
    for size in (D, HEAD_SIZE, HEAD_SIZE, D):
        own = size // shards
        small.append(lax.dynamic_slice_in_dim(summed, used + here * own, own, axis=1))
        used += size
    down, output, gate, up, query, key, value = grads
    return (small[0], query, key, value, small[1], small[2], output, small[3], gate, up, down)


def local(
    tokens,
    lengths,
    norm_one,
    w_query,
    w_key,
    w_value,
    query_gain,
    key_gain,
    w_output,
    norm_two,
    w_gate,
    w_up,
    w_down,
    cotangent,
):
    token_rows = tokens.shape[1]
    nx, nz = lax.axis_size("shard") // 2, lax.axis_size("ctx")
    m = nz // 2
    pairs = []
    for x in range(nx):
        for z in range(m):
            low, high = (2 * x + 1) * nz + z, 2 * x * nz + z + m
            same = (2 * x * nz + z, (2 * x + 1) * nz + z + m)
            pairs += [(low, high), (high, low)] + [(s, s) for s in same]

    def swap(values):
        return lax.ppermute(values, ("shard", "ctx"), pairs)

    lengths = swap(lengths)
    block = lax.axis_index("ctx") % m + (lax.axis_index("shard") % 2) * m
    token_index = block * token_rows + jnp.arange(token_rows, dtype=jnp.int32)
    doc_lengths = lengths[0]
    upto = jnp.arange(doc_lengths.shape[0])
    doc_ends = jnp.sum(jnp.where(upto[:, None] >= upto[None, :], doc_lengths[None, :], 0), axis=1)
    token_segment, positions = doc_layout(doc_ends, token_index)
    cosine, sine = rotary(positions, HEAD_SIZE)
    key_segment = segment_of(doc_ends, jnp.arange(token_rows * nz, dtype=jnp.int32))
    tables = (cosine, sine, jnp.stack([token_segment, token_index], axis=1), key_segment[None, :])
    gathered, (gains, tokens, hidden, last), saved = run_forward(
        tokens[0],
        tables,
        (w_query, w_key, w_value, w_output, w_gate, w_up, w_down),
        (norm_one, norm_two, query_gain, key_gain),
    )
    cotangent = swap(cotangent)
    output = swap(last)[None]
    hiddens = (tokens.astype(jnp.float32), hidden)
    waiting = [over_replica(lefts) for lefts, *_ in saved]
    their_attended = over_replica(saved[LAYERS - 1][1])
    live_mask = (token_segment < doc_lengths.shape[0]).astype(jnp.float32)
    upstream = cotangent[0].astype(jnp.float32) * live_mask[:, None]
    operands = [None] * LAYERS
    for which_layer in reversed(range(LAYERS)):
        upstream, operands[which_layer] = layer_back(
            upstream,
            hiddens[which_layer],
            gathered[which_layer],
            gains,
            saved[which_layer],
            tables,
            m,
            which_layer,
            waiting,
        )
    grad_tokens = swap(upstream.astype(jnp.bfloat16))[None]
    for which_layer, (lefts, rights, layer_gains) in enumerate(operands):
        operands[which_layer] = (lefts + (waiting[which_layer], their_attended) + rights, layer_gains)
    return (output, grad_tokens) + weight_gradients(operands, waiting[-1])


def solution(mesh):
    return jax.shard_map(
        local,
        mesh=mesh,
        in_specs=(
            P(("rep", "shard"), "ctx", None),
            P(("rep", "shard"), None),
            P(None, ("shard", "ctx")),
            P(None, ("shard", "ctx"), None),
            P(None, ("shard", "ctx"), None),
            P(None, ("shard", "ctx"), None),
            P(None, ("shard", "ctx")),
            P(None, ("shard", "ctx")),
            P(None, ("shard", "ctx"), None),
            P(None, ("shard", "ctx")),
            P(None, ("shard", "ctx"), None),
            P(None, ("shard", "ctx"), None),
            P(None, ("shard", "ctx"), None),
            P(("rep", "shard"), "ctx", None),
        ),
        out_specs=(
            P(("rep", "shard"), "ctx", None),
            P(("rep", "shard"), "ctx", None),
            P(None, ("shard", "ctx")),
            P(None, ("shard", "ctx"), None),
            P(None, ("shard", "ctx"), None),
            P(None, ("shard", "ctx"), None),
            P(None, ("shard", "ctx")),
            P(None, ("shard", "ctx")),
            P(None, ("shard", "ctx"), None),
            P(None, ("shard", "ctx")),
            P(None, ("shard", "ctx"), None),
            P(None, ("shard", "ctx"), None),
            P(None, ("shard", "ctx"), None),
        ),
        check_vma=False,
    )
```

```python
import functools
import math

import jax
import jax.numpy as jnp
from jax import lax
from jax.experimental import pallas as pl
from jax.experimental.pallas import tpu as pltpu
from jax.sharding import PartitionSpec as P

D = 1024
QUERY_HEADS = 16
KEYVALUE_HEADS = 8
HEAD_SIZE = 128
LAYERS = 2
QD = 2048
KEY_FEATURES = 1024


NORM_EPS = 1e-06
ROPE_BASE = 1000000.0
VERY_NEGATIVE = -1e30
MESH = pl.DeviceIdType.MESH


CHUNK_HEADS = 2
CHUNKS = KEYVALUE_HEADS // CHUNK_HEADS
CHUNK = CHUNK_HEADS * HEAD_SIZE
BACK_HEADS = 2
BACK_CHUNKS = KEYVALUE_HEADS // BACK_HEADS
BACK_WIDTH = BACK_HEADS * HEAD_SIZE
GROUP = QUERY_HEADS // KEYVALUE_HEADS
SCORE_SCALE = 1.0 / math.sqrt(HEAD_SIZE)


def group_place(m):
    y, shard, z = lax.axis_index("rep"), lax.axis_index("shard"), lax.axis_index("ctx")
    core, zz = lax.rem(shard, 2), lax.rem(z, m)
    to_core = (y, shard + 1 - 2 * core, z)

    def to_line(step):
        return (y, shard, z + step)

    return core, zz, to_core, to_line


def greet(m, zz, to_core, to_line):
    barrier = pltpu.get_barrier_semaphore()
    pl.semaphore_signal(barrier, inc=1, device_id=to_core, device_id_type=MESH)
    for here, there in ((zz > 0, to_line(-1)), (zz < m - 1, to_line(1))):

        @pl.when(here)
        def _():
            pl.semaphore_signal(barrier, inc=1, device_id=there, device_id_type=MESH)

    pl.semaphore_wait(barrier, 1 + (zz > 0).astype(jnp.int32) + (zz < m - 1).astype(jnp.int32))


def remote(src, dst, send_sem, recv_sem, device):
    return pltpu.make_async_remote_copy(
        src_ref=src, dst_ref=dst, send_sem=send_sem, recv_sem=recv_sem, device_id=device, device_id_type=MESH
    )


def head_prepare(v, gain, cosine, sine):
    v = v * lax.rsqrt(jnp.mean(v * v, axis=-1, keepdims=True) + NORM_EPS) * gain
    return v * cosine + pltpu.roll(v, HEAD_SIZE // 2, 1) * sine


def head_prepare_back(grad, v, gain, cosine, sine):
    grad = grad * cosine + pltpu.roll(grad * sine, HEAD_SIZE // 2, 1)
    r = lax.rsqrt(jnp.mean(v * v, axis=-1, keepdims=True) + NORM_EPS)
    unit = v * r
    by_gain = jnp.sum(grad * unit, axis=0, keepdims=True)
    grad = grad * gain
    return r * (grad - unit * jnp.mean(grad * unit, axis=-1, keepdims=True)), by_gain


def attend_back_kernel(m, q, kv, d_att, att, lse, qp, kp, q_gain, k_gain, cosine, sine, place_q, segment_k, dq_low, dk_low, dv_low, gains, partial, core_in, up_in, down_in, core_sem, up_sem, down_sem):
    tokens, length = q.shape[0], kv.shape[0]
    core, zz, to_core, to_line = group_place(m)
    greet(m, zz, to_core, to_line)
    cos, sin = cosine[...], sine[...]
    segment_q = place_q[:, 0:1]
    index_q = place_q[:, 1:2]
    index_k = lax.broadcasted_iota(jnp.int32, (tokens, length), 1)
    allowed = (segment_q == segment_k[...]) & (index_q >= index_k)
    lane = lax.broadcasted_iota(jnp.int32, (tokens, HEAD_SIZE), 1)
    gains[...] = jnp.zeros_like(gains)
    over_rows = (((0,), (0,)), ((), ()))
    over_columns = (((1,), (1,)), ((), ()))

    def core_copy(j):
        return remote(partial.at[j, 1 - core], core_in.at[j], core_sem.at[0, j], core_sem.at[1, j], to_core)

    def line_copy(j, up, here):
        low, high = (here + 1, m) if up else (0, here)
        into, sems = (up_in, up_sem) if up else (down_in, down_sem)
        return remote(
            partial.at[j, core, pl.ds(low, high - low)],
            into.at[j, pl.ds(low - (1 if up else 0), high - low)],
            sems.at[0, j],
            sems.at[1, j],
            to_line(1 if up else -1),
        )

    def add(j, place, value):
        partial[j, core, place] = (partial[j, core, place].astype(jnp.float32) + value.astype(jnp.float32)).astype(partial.dtype)

    def compute(j):
        for n in range(BACK_HEADS):
            one = j * BACK_HEADS + n
            first = lax.div(one, CHUNK_HEADS) * 2 * CHUNK + lax.rem(one, CHUNK_HEADS) * HEAD_SIZE
            keys = kv[:, pl.ds(pl.multiple_of(first, 128), HEAD_SIZE)]
            values = kv[:, pl.ds(pl.multiple_of(first + CHUNK, 128), HEAD_SIZE)]
            dk = dv = None
            for g in range(GROUP):
                h = one * GROUP + g
                at = pl.ds(pl.multiple_of(h * HEAD_SIZE, 128), HEAD_SIZE)
                queries, grad = q[:, at], d_att[:, at]
                total = jnp.sum(jnp.where(lane == h, lse[...], 0.0), axis=-1, keepdims=True)
                delta = jnp.sum(grad.astype(jnp.float32) * att[:, at], axis=-1, keepdims=True)
                s = lax.dot_general(queries, keys, over_columns, preferred_element_type=jnp.float32)
                p = jnp.exp(jnp.where(allowed, s * SCORE_SCALE, VERY_NEGATIVE) - total)
                dp = lax.dot_general(grad, values, over_columns, preferred_element_type=jnp.float32)
                ds = (p * (dp - delta)).astype(queries.dtype)
                dq = jnp.dot(ds, keys, preferred_element_type=jnp.float32) * SCORE_SCALE
                here_k = lax.dot_general(ds, queries, over_rows, preferred_element_type=jnp.float32)
                here_v = lax.dot_general(p.astype(grad.dtype), grad, over_rows, preferred_element_type=jnp.float32)
                dk = here_k if dk is None else dk + here_k
                dv = here_v if dv is None else dv + here_v
                by_head, by_gain = head_prepare_back(dq, qp[:, at], q_gain[...], cos, sin)
                dq_low[:, at] = by_head.astype(dq_low.dtype)
                gains[0:1] += by_gain
            first = n * HEAD_SIZE
            partial[j, :, :, :, first : first + HEAD_SIZE] = (dk * SCORE_SCALE).astype(partial.dtype).reshape(2, m, tokens, HEAD_SIZE)
            first += BACK_WIDTH
            partial[j, :, :, :, first : first + HEAD_SIZE] = dv.astype(partial.dtype).reshape(2, m, tokens, HEAD_SIZE)
        core_copy(j).start()

    def take_core(j):
        core_copy(j).wait_recv()
        for place in range(m):
            add(j, place, core_in[j, place])

    def hop(j, h):
        for up in (True, False):
            here = h if up else m - 1 - h

            @pl.when(zz == here)
            def _():
                if h > 0:
                    line_copy(j, up, here - 1 if up else here + 1).wait_recv()
                    into = up_in if up else down_in
                    for place in range(here, m) if up else range(here + 1):
                        add(j, place, into[j, place - (1 if up else 0)])
                if h < m - 1:
                    line_copy(j, up, here).start()

    def finish(j):
        for n in range(BACK_HEADS):
            at = pl.ds(pl.multiple_of((j * BACK_HEADS + n) * HEAD_SIZE, 128), HEAD_SIZE)
            grad = partial[j, core, zz, :, n * HEAD_SIZE : (n + 1) * HEAD_SIZE].astype(jnp.float32)
            by_head, by_gain = head_prepare_back(grad, kp[:, at], k_gain[...], cos, sin)
            dk_low[:, at] = by_head.astype(dk_low.dtype)
            gains[1:2] += by_gain
        at = pl.ds(pl.multiple_of(j * BACK_WIDTH, 128), BACK_WIDTH)
        dv_low[:, at] = partial[j, core, zz, :, BACK_WIDTH:]
        core_copy(j).wait_send()
        for here in range(m):

            @pl.when(zz == here)
            def _():
                if here < m - 1:
                    line_copy(j, True, here).wait_send()
                if here > 0:
                    line_copy(j, False, here).wait_send()

    plan = [[compute], [take_core, functools.partial(hop, h=0)]]
    for h in range(1, m):
        plan.append([functools.partial(hop, h=h)])
    plan[-1].append(finish)

    def tick(t, carry):
        for depth in range(len(plan)):
            j = t - depth

            @pl.when((j >= 0) & (j < BACK_CHUNKS))
            def _():
                for stage in plan[depth]:
                    stage(j)

        return carry

    lax.fori_loop(0, BACK_CHUNKS + len(plan) - 1, tick, 0)


def attend_back(m, q, kv, d_att, att, lse, qp, kp, q_gain, k_gain, cosine, sine, place_q, segment_k, collective_id):
    tokens = q.shape[0]
    low = jnp.bfloat16
    dma = pltpu.SemaphoreType.DMA
    vmem = pl.BlockSpec(memory_space=pltpu.VMEM)
    return pl.pallas_call(
        functools.partial(attend_back_kernel, m),
        out_shape=[
            jax.ShapeDtypeStruct((tokens, QD), low),
            jax.ShapeDtypeStruct((tokens, KEY_FEATURES), low),
            jax.ShapeDtypeStruct((tokens, KEY_FEATURES), low),
            jax.ShapeDtypeStruct((8, HEAD_SIZE), jnp.float32),
        ],
        in_specs=[vmem] * 13,
        out_specs=[vmem] * 4,
        scratch_shapes=[
            pltpu.VMEM((BACK_CHUNKS, 2, m, tokens, 2 * BACK_WIDTH), low),
            pltpu.VMEM((BACK_CHUNKS, m, tokens, 2 * BACK_WIDTH), low),
            pltpu.VMEM((BACK_CHUNKS, max(m - 1, 1), tokens, 2 * BACK_WIDTH), low),
            pltpu.VMEM((BACK_CHUNKS, max(m - 1, 1), tokens, 2 * BACK_WIDTH), low),
            dma((2, BACK_CHUNKS)),
            dma((2, BACK_CHUNKS)),
            dma((2, BACK_CHUNKS)),
        ],
        compiler_params=pltpu.CompilerParams(
            collective_id=collective_id, has_side_effects=True, vmem_limit_bytes=48 * 1024 * 1024
        ),
    )(q, kv, d_att, att, lse, qp, kp, q_gain, k_gain, cosine, sine, place_q, segment_k)


WIDE_TILE, NARROW_TILE = 512, 256
IDLE = 2


def wholes_of(chunks):
    return list(dict.fromkeys(c[:2] for c in chunks))


def unit_rms(values):
    return values * lax.rsqrt(jnp.mean(values * values, axis=-1, keepdims=True) + NORM_EPS)


def forward_kernel(chunks, nx, nz, *refs):
    count = len(chunks)
    arrays = wholes_of(chunks)
    weights = 7
    gain_shard, shards, refs = refs[0], refs[1 : 1 + weights], refs[1 + weights :]
    tokens_here, cosine, sine, place_q, segment_k, refs = *refs[:5], refs[5:]
    wholes, refs = refs[: len(arrays)], refs[len(arrays) :]
    gains_out, tokens_out, hidden_out, last_out, refs = *refs[:4], refs[4:]
    saved_out, refs = [refs[n * SAVED : (n + 1) * SAVED] for n in range(LAYERS)], refs[LAYERS * SAVED :]
    own_sem, z_sem, x_sem, y_sem, core_sem, out_sem, refs = *refs[:6], refs[6:]
    gain_all, gains, low_tokens, h, normed, qp, kp, v, q, kv, att, att_low, lse, h_mid, n2, gate, up, act, last, refs = (
        *refs[:19],
        refs[19:],
    )
    wide_buf, output_buf, down_buf, refs = *refs[:3], refs[3:]
    tile_sem, save_sem, misc_sem, kv_core_sem, kv_line_sem, kv_core_out, kv_line_out = refs
    tokens, length = q.shape[0], kv.shape[1]
    m = nz // 2
    y = lax.axis_index("rep")
    shard = lax.axis_index("shard")
    z = lax.axis_index("ctx")
    core, x = lax.rem(shard, 2), lax.div(shard, 2)
    to_core = (y, x * 2 + 1 - core, z)
    to_y = (1 - y, shard, z)
    upper = z >= m
    moves = ((core == 0) & upper) | ((core == 1) & (z < m))
    to_swap = (y, x * 2 + 1 - core, jnp.where(upper, z - m, z + m))

    def to_x(step):
        return (y, shard + 2 * step, z)

    def to_z(step):
        return (y, shard, z + step)

    def own_part(k, start, size):
        weight, layer, column, width = chunks[k][:4]
        ref = gain_shard if weight < 0 else shards[weight].at[layer]
        return ref.at[pl.ds(start, size), pl.ds(column, width)]

    def whole_rows(k, first, size):
        weight, layer, column, width = chunks[k][:4]
        return wholes[arrays.index((weight, layer))].at[pl.ds(first, size), pl.ds(column, width)]

    def rows_of(k, xs, zs, start, size, of_core=core):
        first = ((xs * 2 + of_core) * nz + zs) * chunks[k][4] + start
        return whole_rows(k, pl.multiple_of(first, 16), size)

    def inplane(k):
        rows, near = chunks[k][4:]
        return y * (rows - near), near

    def arrived(ref, sem):
        pltpu.make_async_copy(ref, ref, sem).wait()

    def pass_z(k, src, zs, step, kind):
        start, size = inplane(k)
        remote(src, rows_of(k, x, zs, start, size), out_sem.at[k, kind], z_sem.at[k, zs], to_z(step)).start()

    def pass_x(k, src, xs, zs, step, kind):
        start, size = inplane(k)
        into = rows_of(k, xs, zs, start, size)
        remote(src, into, out_sem.at[k, kind], x_sem.at[k, xs * nz + zs], to_x(step)).start()

    def pass_y(k, xs, zs):
        rows, near = chunks[k][4:]
        if rows > near:
            part = rows_of(k, xs, zs, y * near, rows - near)
            remote(part, part, out_sem.at[k, 4], y_sem.at[k, xs * nz + zs], to_y).start()

    def pass_core(k, xs, zs, start, size):
        part = rows_of(k, xs, zs, start, size)
        remote(part, part, out_sem.at[k, 5], core_sem.at[k], to_core).start()

    def stage_own(k):
        rows = chunks[k][4]
        start, size = inplane(k)
        part = own_part(k, pl.multiple_of(start, 16), size)

        @pl.when(z < nz - 1)
        def _():
            pass_z(k, part, z, 1, 0)

        @pl.when(z > 0)
        def _():
            pass_z(k, part, z, -1, 1)

        @pl.when(x < nx - 1)
        def _():
            pass_x(k, part, x, z, 1, 2)

        @pl.when(x > 0)
        def _():
            pass_x(k, part, x, z, -1, 3)

        every = own_part(k, 0, rows)
        remote(every, rows_of(k, x, z, 0, rows), out_sem.at[k, 5], core_sem.at[k], to_core).start()
        pltpu.make_async_copy(every, rows_of(k, x, z, 0, rows), own_sem.at[k]).start()

    def stage_z(k, d):
        start, size = inplane(k)
        for step, kind in ((1, 0), (-1, 1)):
            zs = z - step * d

            @pl.when((zs >= 0) & (zs < nz))
            def _():
                part = rows_of(k, x, zs, start, size)
                arrived(part, z_sem.at[k, zs])

                @pl.when((z + step >= 0) & (z + step < nz))
                def _():
                    pass_z(k, part, zs, step, kind)

                @pl.when(x < nx - 1)
                def _():
                    pass_x(k, part, x, zs, 1, 2)

                @pl.when(x > 0)
                def _():
                    pass_x(k, part, x, zs, -1, 3)

                pass_y(k, x, zs)
                pass_core(k, x, zs, start, size)

    def stage_x(k, d):
        start, size = inplane(k)
        for step, kind in ((1, 2), (-1, 3)):
            xs = x - step * d

            @pl.when((xs >= 0) & (xs < nx))
            def _():
                def body(zs, carry):
                    part = rows_of(k, xs, zs, start, size)
                    arrived(part, x_sem.at[k, xs * nz + zs])
                    if nx > 2:

                        @pl.when((x + step >= 0) & (x + step < nx))
                        def _():
                            pass_x(k, part, xs, zs, step, kind)

                    pass_y(k, xs, zs)
                    pass_core(k, xs, zs, start, size)
                    return carry

                lax.fori_loop(0, nz, body, 0)

    def stage_y(k):
        rows, near = chunks[k][4:]
        if rows > near:

            def body(i, carry):
                xs, zs = lax.div(i, nz), lax.rem(i, nz)

                @pl.when((xs != x) | (zs != z))
                def _():
                    start = (1 - y) * near
                    arrived(rows_of(k, xs, zs, start, rows - near), y_sem.at[k, i])
                    pass_core(k, xs, zs, start, rows - near)

                return carry

            lax.fori_loop(0, nx * nz, body, 0)

    def first_rows(k, size):
        return whole_rows(k, 0, size)

    def complete(k):
        rows = chunks[k][4]
        arrived(first_rows(k, nx * nz * rows), core_sem.at[k])
        arrived(first_rows(k, rows), own_sem.at[k])

    def sent(k):
        rows, near = chunks[k][4:]
        for zz in range(nz):

            @pl.when(z == zz)
            def _():
                if zz < nz - 1:
                    arrived(first_rows(k, (zz + 1) * near), out_sem.at[k, 0])
                if zz > 0:
                    arrived(first_rows(k, (nz - zz) * near), out_sem.at[k, 1])

        for xx in range(nx):

            @pl.when(x == xx)
            def _():
                if xx < nx - 1:
                    arrived(first_rows(k, (xx + 1) * nz * near), out_sem.at[k, 2])
                if xx > 0:
                    arrived(first_rows(k, (nx - xx) * nz * near), out_sem.at[k, 3])

        if rows > near:
            arrived(first_rows(k, (nx * nz - 1) * (rows - near)), out_sem.at[k, 4])
        arrived(first_rows(k, nx * nz * rows), out_sem.at[k, 5])

    barrier = pltpu.get_barrier_semaphore()
    pl.semaphore_signal(barrier, inc=1, device_id=to_core, device_id_type=MESH)
    pl.semaphore_signal(barrier, inc=1, device_id=to_y, device_id_type=MESH)
    meets = ((z > 0, to_z(-1)), (z < nz - 1, to_z(1)), (x > 0, to_x(-1)), (x < nx - 1, to_x(1)), (moves, to_swap))
    greeted = 2
    for here, there in meets:

        @pl.when(here)
        def _():
            pl.semaphore_signal(barrier, inc=1, device_id=there, device_id_type=MESH)

        greeted = greeted + here.astype(jnp.int32)
    pl.semaphore_wait(barrier, greeted)

    def swap_copy():
        return remote(tokens_here, low_tokens, misc_sem.at[0], misc_sem.at[1], to_swap)

    def stay_copy():
        return pltpu.make_async_copy(tokens_here, low_tokens, misc_sem.at[1])

    @pl.when(moves)
    def _():
        swap_copy().start()

    @pl.when(~moves)
    def _():
        stay_copy().start()

    def begin():
        @pl.when(moves)
        def _():
            swap_copy().wait()

        @pl.when(~moves)
        def _():
            stay_copy().wait()

        h[...] = low_tokens[...].astype(jnp.float32)
        pltpu.make_async_copy(low_tokens, tokens_out, misc_sem.at[2]).start()

    def read_gains():
        complete(0)
        copy = pltpu.make_async_copy(wholes[0], gain_all, misc_sem.at[3])
        copy.start()
        copy.wait()
        gains[...] = jnp.zeros_like(gains)

        def body(n, carry):
            gains[...] += gain_all[pl.ds(pl.multiple_of(n * 16, 16), 16)].astype(jnp.float32)
            return carry

        lax.fori_loop(0, 2 * nx * nz, body, 0)
        pltpu.make_async_copy(gains, gains_out, misc_sem.at[4]).start()

    zz = lax.rem(z, m)

    def kv_part(layer, j, source, of_core=core):
        rows = pl.multiple_of((source + of_core * m) * tokens, 16)
        at = j * 2 * CHUNK if isinstance(j, int) else pl.multiple_of(j * 2 * CHUNK, 128)
        return kv.at[layer, pl.ds(rows, tokens), pl.ds(at, 2 * CHUNK)]

    def kv_core(layer, j, source, of_core=core):
        ref = kv_part(layer, j, source, of_core)
        return remote(ref, ref, kv_core_out.at[layer, j, source], kv_core_sem.at[layer, j, source], to_core)

    def kv_line(layer, j, source, step):
        ref = kv_part(layer, j, source)
        send_sem = kv_line_out.at[0 if step > 0 else 1, layer, j, source]
        return remote(ref, ref, send_sem, kv_line_sem.at[layer, j, source], to_z(step))

    def onward(layer, j, source, step, do):
        @pl.when((zz + step >= 0) & (zz + step < m))
        def _():
            do(kv_line(layer, j, source, step))

    start, ended = lambda copy: copy.start(), lambda copy: copy.wait_send()

    def kv_left(layer):
        for j in range(CHUNKS):
            for source in range(m):
                kv_core(layer, j, source).wait_send()
            for d in range(m):
                for step in (1, -1):
                    source = zz - step * d

                    @pl.when((source >= 0) & (source < m))
                    def _():
                        onward(layer, j, source, step, ended)

    saves = (normed, qp, kp, q, None, att, att_low, lse, h_mid, n2, gate, up, act)

    def save_copy(layer, n):
        source = kv.at[layer] if saves[n] is None else saves[n]
        into = saved_out[layer][SAVE_TO[n]]
        if n in LEFT_AT:
            into = into.at[:, pl.ds(LEFT_AT[n] * D, source.shape[1])]
        return pltpu.make_async_copy(source, into, save_sem.at[layer, n])

    def save(layer, *which):
        for n in which:
            save_copy(layer, n).start()

    def reusable(layer, *which):
        if layer > 0:
            for n in which:
                save_copy(layer - 1, n).wait()

    def layer_tasks(layer):
        parts = {w: [k for k, c in enumerate(chunks) if c[:2] == (w, layer)] for w in range(weights)}
        row = lambda n, width=D: gains[n + layer : n + layer + 1, :width]
        tasks = []

        def streamed(weight, buf, base, sems, tile, use, tiles):
            whole = wholes[arrays.index((weight, layer))]

            def copy(i):
                slot = base + i % 2
                source = whole.at[:, pl.ds(i * tile, tile)]
                return pltpu.make_async_copy(source, buf.at[slot], tile_sem.at[sems + i % 2])

            def first():
                for k in parts[weight]:
                    complete(k)
                copy(0).start()
                copy(1).start()

            def one(i):
                copy(i).wait()
                use(i, buf.at[base + i % 2])
                if i + 2 < tiles:
                    copy(i + 2).start()

            return first, [functools.partial(one, i) for i in range(tiles)], max(parts[weight])

        def put(k, *steps):
            tasks.append((k, lambda: [step() for step in steps]))

        def norm_first():
            if layer == 0:
                begin()
                read_gains()
            reusable(layer, 0)
            normed[...] = (unit_rms(h[...]) * row(0)).astype(normed.dtype)
            save(layer, 0)
            if layer > 0:
                pltpu.make_async_copy(h, hidden_out, misc_sem.at[5]).start()

        def keys(i, w):
            if i == 0:
                reusable(layer, 2)
            kp[:, i * WIDE_TILE : (i + 1) * WIDE_TILE] = jnp.dot(normed[...], w[...], preferred_element_type=jnp.float32)
            if i == 1:
                save(layer, 2)

        def values(i, w):
            term = jnp.dot(normed[...], w[...], preferred_element_type=jnp.float32)
            v[:, i * WIDE_TILE : (i + 1) * WIDE_TILE] = term.astype(v.dtype)

        def queries(i, w):
            if i == 0:
                reusable(layer, 1)
            qp[:, i * WIDE_TILE : (i + 1) * WIDE_TILE] = jnp.dot(normed[...], w[...], preferred_element_type=jnp.float32)
            if i == 3:
                save(layer, 1)

        cos = lambda: cosine[...]
        sin = lambda: sine[...]
        own_rows = pl.ds(pl.multiple_of((zz + core * m) * tokens, 16), tokens)

        def send_keys(j):
            for n in range(CHUNK_HEADS):
                hd = j * CHUNK_HEADS + n
                ready = head_prepare(kp[:, hd * HEAD_SIZE : (hd + 1) * HEAD_SIZE], row(6, HEAD_SIZE), cos(), sin())
                first = j * 2 * CHUNK + n * HEAD_SIZE
                kv[layer, own_rows, first : first + HEAD_SIZE] = ready.astype(kv.dtype)
            kv[layer, own_rows, j * 2 * CHUNK + CHUNK : (j + 1) * 2 * CHUNK] = v[:, j * CHUNK : (j + 1) * CHUNK]
            for step in (1, -1):
                onward(layer, j, zz, step, start)
            kv_core(layer, j, zz).start()

        def prepare_queries(part):
            if part == 0:
                reusable(layer, 3)
            for hd in range(part * 4, part * 4 + 4):
                at = slice(hd * HEAD_SIZE, (hd + 1) * HEAD_SIZE)
                q[:, at] = head_prepare(qp[:, at], row(4, HEAD_SIZE), cos(), sin()).astype(q.dtype)
            if part == 3:
                save(layer, 3)

        def arrivals(j):
            for d in range(1, m):
                for step in (1, -1):
                    source = zz - step * d

                    @pl.when((source >= 0) & (source < m))
                    def _():
                        kv_line(layer, j, source, step).wait_recv()
                        onward(layer, j, source, step, start)
                        kv_core(layer, j, source).start()

        def attend(j):
            if j == 0:
                reusable(layer, 5, 6, 7)
                lse[...] = jnp.zeros_like(lse)
            for source in range(m):
                kv_core(layer, j, source, 1 - core).wait_recv()
            index_k = lax.broadcasted_iota(jnp.int32, (tokens, length), 1)
            allowed = (place_q[:, 0:1] == segment_k[...]) & (place_q[:, 1:2] >= index_k)
            lane = lax.broadcasted_iota(jnp.int32, (tokens, HEAD_SIZE), 1)

            def head(n, carry):
                first = j * 2 * CHUNK + lax.div(n, GROUP) * HEAD_SIZE
                their_keys = kv[layer, :, pl.ds(pl.multiple_of(first, 128), HEAD_SIZE)]
                their_values = kv[layer, :, pl.ds(pl.multiple_of(first + CHUNK, 128), HEAD_SIZE)]
                hd = j * CHUNK_HEADS * GROUP + n
                at = pl.ds(pl.multiple_of(hd * HEAD_SIZE, 128), HEAD_SIZE)
                s = lax.dot_general(q[:, at], their_keys, (((1,), (1,)), ((), ())), preferred_element_type=jnp.float32)
                s = jnp.where(allowed, s * SCORE_SCALE, VERY_NEGATIVE)
                top = jnp.max(s, axis=-1, keepdims=True)
                p = jnp.exp(s - top)
                total = jnp.sum(p, axis=-1, keepdims=True)
                o = jnp.dot(p.astype(jnp.bfloat16), their_values, preferred_element_type=jnp.float32) / total
                att[:, at] = o
                att_low[:, at] = o.astype(att_low.dtype)
                lse[...] = jnp.where(lane == hd, top + jnp.log(total), lse[...])
                return carry

            lax.fori_loop(0, CHUNK_HEADS * GROUP, head, 0)
            if j == CHUNKS - 1:
                save(layer, 4, 5, 6, 7)

        def outputs(i, w):
            if i == 0:
                reusable(layer, 8)
            at = slice(i * NARROW_TILE, (i + 1) * NARROW_TILE)
            h_mid[:, at] = h[:, at] + jnp.dot(att_low[...], w[...], preferred_element_type=jnp.float32)
            if i == 3:
                save(layer, 8)

        def norm_second():
            reusable(layer, 9)
            n2[...] = (unit_rms(h_mid[...]) * row(2)).astype(n2.dtype)
            save(layer, 9)

        def gates(i, w):
            if i == 0:
                reusable(layer, 10, 12)
            gate[:, i * WIDE_TILE : (i + 1) * WIDE_TILE] = jnp.dot(n2[...], w[...], preferred_element_type=jnp.float32)

        def ups(i, w):
            if i == 0:
                reusable(layer, 11)
            at = slice(i * WIDE_TILE, (i + 1) * WIDE_TILE)
            term = jnp.dot(n2[...], w[...], preferred_element_type=jnp.float32)
            up[:, at] = term
            opened = gate[:, at]
            act[:, at] = (opened / (1.0 + jnp.exp(-opened)) * term).astype(act.dtype)
            if i == 5:
                save(layer, 10, 11, 12)

        def downs(i, w):
            if layer > 0 and i == 0:
                pltpu.make_async_copy(h, hidden_out, misc_sem.at[5]).wait()
            at = slice(i * NARROW_TILE, (i + 1) * NARROW_TILE)
            h[:, at] = h_mid[:, at] + jnp.dot(act[...], w[...], preferred_element_type=jnp.float32)

        first_k, key_tiles, kk = streamed(1, wide_buf, 0, 0, WIDE_TILE, keys, 2)
        first_v, value_tiles, kv_chunk = streamed(2, wide_buf, 2, 2, WIDE_TILE, values, 2)
        first_q, query_tiles, kq = streamed(0, wide_buf, 4, 8, WIDE_TILE, queries, 4)
        first_o, output_tiles, ko = streamed(3, output_buf, 0, 4, NARROW_TILE, outputs, 4)
        first_g, gate_tiles, kg = streamed(4, wide_buf, 0, 0, WIDE_TILE, gates, 6)
        first_u, up_tiles, ku = streamed(5, wide_buf, 2, 2, WIDE_TILE, ups, 6)
        first_d, down_tiles, kd = streamed(6, down_buf, 0, 6, NARROW_TILE, downs, 4)
        kqkv = max(kk, kv_chunk, kq)
        put(kqkv, first_k, first_v, first_q)
        put(kqkv, norm_first)
        put(kqkv, *key_tiles)
        put(kqkv, *value_tiles)
        put(kqkv, functools.partial(send_keys, 0), functools.partial(send_keys, 1))
        put(kqkv, functools.partial(send_keys, 2), functools.partial(send_keys, 3))
        put(kqkv, *query_tiles[:2])
        put(kqkv, *query_tiles[2:])
        for part in range(4):
            put(kqkv, functools.partial(prepare_queries, part))
        for j in range(CHUNKS):
            for _ in range(IDLE):
                put(kqkv)
            put(kqkv, functools.partial(arrivals, j))
            if j > 0:
                put(kqkv, functools.partial(attend, j - 1))
        for _ in range(IDLE // 2):
            put(kqkv)
        put(ko, first_o)
        put(kqkv, functools.partial(attend, CHUNKS - 1))
        put(ko, *output_tiles[:2])
        put(ko, *output_tiles[2:])
        put(kg, norm_second, first_g)
        for n in range(3):
            put(kg, *gate_tiles[2 * n : 2 * n + 2])
        put(ku, first_u)
        for n in range(3):
            put(ku, *up_tiles[2 * n : 2 * n + 2])
        put(kd, first_d)
        put(kd, *down_tiles[:2])
        put(kd, *down_tiles[2:])
        return tasks

    stages = [stage_own]
    stages += [functools.partial(stage_z, d=d) for d in range(1, nz)]
    stages += [functools.partial(stage_x, d=d) for d in range(1, nx)]
    stages += [stage_y]
    tasks = [task for layer in range(LAYERS) for task in layer_tasks(layer)]
    for tick in range(count + len(stages) - 1):
        for depth, stage in enumerate(stages):
            k = tick - depth
            if 0 <= k < count:
                stage(k)
            if tasks and tasks[0][0] + len(stages) <= tick:
                tasks.pop(0)[1]()
    for _, task in tasks:
        task()
    last[...] = h[...].astype(last.dtype)
    pltpu.make_async_copy(last, last_out, misc_sem.at[6]).start()
    for k in range(count):
        sent(k)
    for layer in range(LAYERS):
        kv_left(layer)
    for n in range(len(saves)):
        save_copy(LAYERS - 1, n).wait()
    save_copy(0, 4).wait()
    pltpu.make_async_copy(low_tokens, tokens_out, misc_sem.at[2]).wait()
    pltpu.make_async_copy(gains, gains_out, misc_sem.at[4]).wait()
    pltpu.make_async_copy(last, last_out, misc_sem.at[6]).wait()


LEFT_AT = {0: 4, 9: 3, 12: 0}
SAVE_TO = (0, 2, 3, 4, 5, 6, 1, 7, 8, 0, 9, 10, 0)
SAVED = 11


def forward(gain_shard, shards, tokens, tables, chunks, nx, nz, collective_id):
    count, m = len(chunks), nz // 2
    rows = tokens.shape[0]
    low, wide = jnp.bfloat16, jnp.float32
    dma, vmem = pltpu.SemaphoreType.DMA, pltpu.VMEM
    anywhere = pl.BlockSpec(memory_space=pl.ANY)
    arrays = [gain_shard if weight < 0 else shards[weight] for weight, _ in wholes_of(chunks)]
    ff = shards[4].shape[-1]
    lefts = [((rows, ff + 2 * D), low), ((rows, QD), low)]
    kept = [((rows, D), low), ((rows, QD), wide), ((rows, KEY_FEATURES), wide), ((rows, QD), low)]
    kept += [((2 * m * rows, 2 * KEY_FEATURES), low), ((rows, QD), wide), ((rows, QD), low), ((rows, HEAD_SIZE), wide)]
    kept += [((rows, D), wide), ((rows, D), low), ((rows, ff), wide), ((rows, ff), wide), ((rows, ff), low)]
    shape = jax.ShapeDtypeStruct
    outs = pl.pallas_call(
        functools.partial(forward_kernel, chunks, nx, nz),
        out_shape=[shape((a.shape[-2] * 2 * nx * nz, a.shape[-1]), low) for a in arrays]
        + [shape((16, D), wide), shape((rows, D), low), shape((rows, D), wide), shape((rows, D), low)]
        + [shape(*k) for k in [*lefts, *kept[1:6], *kept[7:9], *kept[10:12]]] * LAYERS,
        in_specs=[anywhere] * (2 + len(shards)) + [pl.BlockSpec(memory_space=pltpu.VMEM)] * 4,
        out_specs=[anywhere] * (len(arrays) + 4 + SAVED * LAYERS),
        scratch_shapes=[
            dma((count,)),
            dma((count, nz)),
            dma((count, nx * nz)),
            dma((count, nx * nz)),
            dma((count,)),
            dma((count, 6)),
            vmem((16 * 2 * nx * nz, D), low),
            vmem((16, D), wide),
            vmem((rows, D), low),
            vmem((rows, D), wide),
            vmem(*kept[0]),
            vmem(*kept[1]),
            vmem(*kept[2]),
            vmem((rows, KEY_FEATURES), low),
            vmem(*kept[3]),
            vmem((LAYERS, *kept[4][0]), low),
            *[vmem(*k) for k in kept[5:]],
            vmem((rows, D), low),
            vmem((6, D, WIDE_TILE), low),
            vmem((2, QD, NARROW_TILE), low),
            vmem((2, ff, NARROW_TILE), low),
            dma((10,)),
            dma((LAYERS, len(SAVE_TO))),
            dma((7,)),
            dma((LAYERS, CHUNKS, m)),
            dma((LAYERS, CHUNKS, m)),
            dma((LAYERS, CHUNKS, m)),
            dma((2, LAYERS, CHUNKS, m)),
        ],
        compiler_params=pltpu.CompilerParams(
            collective_id=collective_id, has_side_effects=True, vmem_limit_bytes=56 * 1024 * 1024
        ),
    )(gain_shard, *shards, tokens, *tables)
    wholes, outs = outs[: len(arrays)], outs[len(arrays) :]
    return dict(zip(wholes_of(chunks), wholes)), outs[:4], [outs[4 + n * SAVED : 4 + (n + 1) * SAVED] for n in range(LAYERS)]


SLOTS = 4
AHEAD = 4
PIECES = 15
LEFT_BLOCKS = (3, 2, 1, 1)
LEFT_FIRST = (0, 3, 5, 11)
LEFT_BASE = (0, 0, 3, 4)
RIGHTS = 7
RIGHT_FIRST = (0, 3, 5, 7, 9, 11, 13)
WEIGHT_BLOCKS = ((1, 3), (1, 2), (3, 1), (3, 1), (2, 1), (1, 1), (1, 1))


def piece_place(j, replica):
    if j < 2:
        return 0, replica, j
    if j == 2:
        return 0, 2, replica
    if j < 5:
        return 1, replica, j - 3
    if j < 11:
        return 2 + replica, 0, j - 5
    if replica == 0:
        return 4, 0, j - 11
    return (5, 0, j - 11) if j < 13 else (6, 0, j - 13)


def reduce_kernel(nx, nz, layers, *refs):
    per = 2 + 2 + 7
    held, refs = refs[0], refs[1:]
    operands, refs = refs[: layers * per], refs[layers * per :]
    gains, refs = refs[0], refs[1:]
    outs, refs = refs[: len(WEIGHT_BLOCKS)], refs[len(WEIGHT_BLOCKS) :]
    gains_out, left_at, refs = refs[0], refs[1:5], refs[5:]
    right_at, turned, total, x_in, zup_in, zdown_in, f_in, result, landed, refs = *refs[:9], refs[9:]
    gain_in, gain_up, gain_down, refs = *refs[:3], refs[3:]
    left_sem, right_sem, x_sem, zup_sem, zdown_sem, f_sem, result_sem, gain_sem, landed_sem, credit = refs
    rows, width = total.shape[3:]
    tokens, wide = right_at.shape[2:]
    pieces = layers * PIECES
    ring = total.shape[0]
    y = lax.axis_index("rep")
    shard = lax.axis_index("shard")
    z = lax.axis_index("ctx")
    core, x = lax.rem(shard, 2), lax.div(shard, 2)
    to_core = (y, x * 2 + 1 - core, z)
    to_y = (1 - y, shard, z)

    def to_x(step):
        return (y, shard + 2 * step, z)

    def to_z(step):
        return (y, shard, z + step)

    barrier = pltpu.get_barrier_semaphore()
    pl.semaphore_signal(barrier, inc=1, device_id=to_core, device_id_type=MESH)
    pl.semaphore_signal(barrier, inc=1, device_id=to_y, device_id_type=MESH)
    for here, there in ((z > 0, to_z(-1)), (z < nz - 1, to_z(1)), (x > 0, to_x(-1)), (x < nx - 1, to_x(1))):

        @pl.when(here)
        def _():
            pl.semaphore_signal(barrier, inc=1, device_id=there, device_id_type=MESH)

    greeted = 2 + (z > 0).astype(jnp.int32) + (z < nz - 1).astype(jnp.int32)
    greeted = greeted + (x > 0).astype(jnp.int32) + (x < nx - 1).astype(jnp.int32)
    pl.semaphore_wait(barrier, greeted)

    def left_copies(k, layer, sources):
        span = nz * LEFT_BLOCKS[k] * rows
        base = LEFT_BASE[k] * wide
        sems = layer * 4 + k
        for whose, source in zip((0, 2), sources):

            def columns(xs, of_core):
                return source.at[:, pl.ds(pl.multiple_of(base + (xs * 2 + of_core) * span, 128), span)]

            for xs in range(nx):
                yield pltpu.make_async_copy(
                    columns(xs, core), left_at[k].at[whose, layer, xs], left_sem.at[whose, sems, xs]
                )
                yield remote(
                    columns(xs, 1 - core),
                    left_at[k].at[whose + 1, layer, xs],
                    left_sem.at[4 + whose, sems, xs],
                    left_sem.at[whose + 1, sems, xs],
                    to_core,
                )

    def own_right(b, source):
        return pltpu.make_async_copy(source, right_at.at[0, b], right_sem.at[0, b])

    def pair_right(b, source):
        return remote(source, right_at.at[1, b], right_sem.at[4, b], right_sem.at[1, b], to_core)

    def held_right(b, source):
        return pltpu.make_async_copy(source, right_at.at[2, b], right_sem.at[2, b])

    def replica_right(b, source):
        return remote(source, right_at.at[2, b], right_sem.at[5, b], right_sem.at[2, b], to_y)

    def passed_right(b, source):
        return remote(source, right_at.at[3, b], right_sem.at[6, b], right_sem.at[3, b], to_core)

    def attended_copy(layer, source):
        return remote(source, landed.at[layer - 1], landed_sem.at[0, layer], landed_sem.at[1, layer], to_y)

    def fetch(i):
        for layer in range(1, layers):

            @pl.when(i == layer * PIECES - AHEAD)
            def _():
                attended_copy(layer, operands[layer * per + 1]).start()

        for layer in range(layers):
            mine = operands[layer * per : (layer + 1) * per]
            lefts, their_lefts = mine[:2], mine[2:4]
            down, output, gate, up, query, key, value = mine[4:]
            blocks = [((down, 0), (down, 0)), ((output, 0), (output, 0))]
            blocks += [((gate, n), (up, n)) for n in range(3)]
            blocks += [((query, 0), (key, 0)), ((query, 1), (value, 0))]
            for n in range(RIGHTS):

                @pl.when(i == layer * PIECES + RIGHT_FIRST[n])
                def _():
                    fetch_block(layer, n, lefts, their_lefts, blocks[n], held)

    def fetch_block(layer, n, lefts, their_lefts, block, their_down):
        b = layer * RIGHTS + n
        for replica in range(2):

            @pl.when(y == replica)
            def _():
                here, there = (
                    source.at[:, pl.ds(at * wide, wide)] for source, at in (block[replica], block[1 - replica])
                )
                if n > 0 or layer > 0:
                    replica_right(b, there).start()
                own_right(b, here).start()
                pair_right(b, here).start()

        if n == 0 and layer == 0:
            held_right(b, their_down).start()
            passed_right(b, their_down).start()
        for k, first in enumerate(LEFT_FIRST):
            if first == RIGHT_FIRST[n]:
                n_left = 1 if k == 1 else 0
                theirs = their_lefts[n_left]
                if k == 1 and layer > 0:
                    theirs = landed.at[layer - 1]
                    attended_copy(layer, lefts[1]).wait_recv()
                for copy in left_copies(k, layer, (lefts[n_left], theirs)):
                    copy.start()

    def place(i):
        return lax.div(i, PIECES), lax.rem(i, PIECES)

    def right_block(j):
        return jnp.where(j < 3, 0, jnp.where(j < 5, 1, lax.div(j - 1, 2)))

    def any_of(j, values):
        hit = j == values[0]
        for value in values[1:]:
            hit = hit | (j == value)
        return hit

    some_right = operands[4]

    def forward(i):
        layer, j = place(i)

        @pl.when(any_of(j, RIGHT_FIRST) & (i > 0))
        def _():
            b = layer * RIGHTS + right_block(j)
            replica_right(b, some_right).wait_recv()
            passed_right(b, right_at.at[2, b]).start()

    def product(i):
        layer, j = place(i)
        b = layer * RIGHTS + right_block(j)
        for k, first in enumerate(LEFT_FIRST):

            @pl.when(j == first)
            def _():
                for copy in left_copies(k, layer, (operands[int(k == 1)],) * 2):
                    copy.wait()

                for who in range(4):
                    for xs in range(nx):
                        flipped = left_at[k][who, layer, xs].T.reshape(nz, LEFT_BLOCKS[k], rows, tokens)
                        for n in range(LEFT_BLOCKS[k]):
                            turned[who, n, xs] = flipped[:, n]

        @pl.when(any_of(j, RIGHT_FIRST))
        def _():
            own_right(b, some_right).wait()
            pair_right(b, some_right).wait()
            passed_right(b, some_right).wait()

        @pl.when(i == 0)
        def _():
            held_right(b, some_right).wait()

        @pl.when(any_of(j, RIGHT_FIRST) & (i > 0))
        def _():
            replica_right(b, some_right).wait_send()

        slot = lax.rem(i, ring)
        part = jnp.where(j == 2, 2, jnp.where(j < 5, y, 0))
        half = jnp.where(j < 2, j, jnp.where(j == 2, y, lax.rem(j + 1, 2)))
        tile = width // 2

        def columns(c, carry):
            source = pl.ds(pl.multiple_of(half * width + c * tile, tile), tile)
            acc = None
            for who in range(4):
                left = turned[who, part].reshape(nx * nz * rows, tokens)
                term = jnp.dot(left, right_at[who, b, :, source], preferred_element_type=jnp.float32)
                acc = term if acc is None else acc + term
            into = pl.ds(pl.multiple_of(c * tile, tile), tile)
            total[slot, :, :, :, into] = acc.reshape(nx, nz, rows, tile).astype(total.dtype)
            return carry

        lax.fori_loop(0, 2, columns, 0)

    def give(i, flow, device):
        @pl.when(i + SLOTS < pieces)
        def _():
            pl.semaphore_signal(credit.at[flow], inc=1, device_id=device, device_id_type=MESH)

    def spend(i, flow):
        @pl.when(i >= SLOTS)
        def _():
            pl.semaphore_wait(credit.at[flow], 1)

    def add(slot, xs, zs, value):
        where = (slot, xs, zs)
        total[where] = (total[where].astype(jnp.float32) + value.astype(jnp.float32)).astype(total.dtype)

    def x_copy(i, up, here):
        low, high = (here + 1, nx) if up else (0, here)
        side = 0 if (up or nx == 2) else 1
        return remote(
            total.at[lax.rem(i, ring), pl.ds(low, high - low)],
            x_in.at[lax.rem(i, SLOTS), side, pl.ds(low - (1 if up else 0), high - low)],
            x_sem.at[0 if up else 1, i],
            x_sem.at[2 if up else 3, i],
            to_x(1 if up else -1),
        )

    def z_copy(i, up, here):
        low, high = (here + 1, nz) if up else (0, here)
        into = zup_in if up else zdown_in
        sems = zup_sem if up else zdown_sem
        return remote(
            total.at[lax.rem(i, ring), x, pl.ds(low, high - low)],
            into.at[lax.rem(i, SLOTS), pl.ds(low - (1 if up else 0), high - low)],
            sems.at[0, i],
            sems.at[1, i],
            to_z(1 if up else -1),
        )

    def x_hop(i, h):
        slot, small = lax.rem(i, ring), lax.rem(i, SLOTS)
        for up in (True, False):
            here = h if up else nx - 1 - h
            side = 0 if (up or nx == 2) else 1

            @pl.when(x == here)
            def _():
                if h > 0:
                    x_copy(i, up, here - 1 if up else here + 1).wait_recv()
                    for target in range(here, nx) if up else range(here + 1):

                        def body(zs, carry):
                            add(slot, target, zs, x_in[small, side, target - (1 if up else 0), zs])
                            return carry

                        lax.fori_loop(0, nz, body, 0)
                    give(i, 0 if up else 1, to_x(-1 if up else 1))
                if h < nx - 1:
                    spend(i, 0 if up else 1)
                    x_copy(i, up, here).start()

    def z_hop(i, h):
        slot, small = lax.rem(i, ring), lax.rem(i, SLOTS)
        for up in (True, False):
            here = h if up else nz - 1 - h

            @pl.when(z == here)
            def _():
                if h > 0:
                    z_copy(i, up, here - 1 if up else here + 1).wait_recv()
                    into = zup_in if up else zdown_in

                    def body(target, carry):
                        add(slot, x, target, into[small, target - (1 if up else 0)])
                        return carry

                    lax.fori_loop(here if up else 0, nz if up else here + 1, body, 0)
                    give(i, 2 if up else 3, to_z(-1 if up else 1))
                if h < nz - 1:
                    spend(i, 2 if up else 3)
                    z_copy(i, up, here).start()

    def f_copy(i):
        return remote(
            total.at[lax.rem(i, ring), x, z], f_in.at[lax.rem(i, SLOTS)], f_sem.at[0, i], f_sem.at[1, i], to_y
        )

    def send_f(i):
        spend(i, 4)
        f_copy(i).start()

    def result_copy(i, replica, into):
        two = lax.rem(i, 2)
        return pltpu.make_async_copy(result.at[two, replica], into, result_sem.at[two, replica])

    def keep_result(i, replica):
        layer, j = place(i)
        for n in range(PIECES):
            for r in range(2):

                @pl.when((j == n) & (replica == r))
                def _():
                    which, part, column = piece_place(n, r)
                    into = outs[which].at[layers - 1 - layer, pl.ds(part * rows, rows), pl.ds(column * width, width)]
                    result_copy(i, r, into).start()

    def result_kept(i):
        for r in range(2):
            result_copy(i, r, outs[5].at[0, :, pl.ds(0, width)]).wait()

    def finish(i):
        slot, small, two = lax.rem(i, ring), lax.rem(i, SLOTS), lax.rem(i, 2)
        f_copy(i).wait_recv()

        @pl.when(i >= 2)
        def _():
            result_kept(i - 2)

        result[two, y] = total[slot, x, z].astype(jnp.float32)
        result[two, 1 - y] = f_in[small].astype(jnp.float32)
        give(i, 4, to_y)
        keep_result(i, 0)
        keep_result(i, 1)
        f_copy(i).wait_send()
        for here in range(nx):

            @pl.when(x == here)
            def _():
                if here < nx - 1:
                    x_copy(i, True, here).wait_send()
                if here > 0:
                    x_copy(i, False, here).wait_send()

        for here in range(nz):

            @pl.when(z == here)
            def _():
                if here < nz - 1:
                    z_copy(i, True, here).wait_send()
                if here > 0:
                    z_copy(i, False, here).wait_send()

    def gain_copy(n, source, device):
        return remote(source, gain_in.at[n], gain_sem.at[0, n], gain_sem.at[1, n], device)

    def gain_start():
        copy = pltpu.make_async_copy(gains, gain_in.at[0], gain_sem.at[0, 0])
        copy.start()
        copy.wait()
        gain_copy(1, gain_in.at[0], to_core).start()

    def gain_pair():
        gain_copy(1, gain_in.at[0], to_core).wait()
        gain_up[0] = gain_in[0] + gain_in[1]
        gain_copy(2, gain_up.at[0], to_y).start()

    def gain_y():
        gain_copy(2, gain_up.at[0], to_y).wait()
        gain_in[0] = gain_up[0] + gain_in[2]

    def gain_hop(h, n, here, to, first, level):
        for up in (True, False):
            buffer = (gain_up if up else gain_down).at[level]
            slot = first if up else first + 1

            @pl.when(here == (h if up else n - 1 - h))
            def _():
                buffer[...] = gain_in[0]
                if h > 0:
                    gain_copy(slot, buffer, to(1 if up else -1)).wait_recv()
                    buffer[...] = gain_in[0] + gain_in[slot]
                if h < n - 1:
                    gain_copy(slot, buffer, to(1 if up else -1)).start()

    def gain_line(n, here, to, first, level):
        @pl.when(here < n - 1)
        def _():
            gain_copy(first, gain_up.at[level], to(1)).wait_send()

        @pl.when(here > 0)
        def _():
            gain_copy(first + 1, gain_down.at[level], to(-1)).wait_send()

        gain_in[0] = gain_up[level] + gain_down[level] - gain_in[0]

    def gain_end():
        copy = pltpu.make_async_copy(gain_in.at[0], gains_out, gain_sem.at[0, 0])
        copy.start()
        copy.wait()

    steps = [gain_start, gain_pair, gain_y]
    for h in range(nx):
        steps.append(functools.partial(gain_hop, h, nx, x, to_x, 3, 1))
    steps.append(functools.partial(gain_line, nx, x, to_x, 3, 1))
    for h in range(nz):
        steps.append(functools.partial(gain_hop, h, nz, z, to_z, 5, 2))
    steps.append(functools.partial(gain_line, nz, z, to_z, 5, 2))
    steps.append(gain_end)

    plan = [[fetch], [], [], [forward], [], [product], [functools.partial(x_hop, h=0)]]
    for h in range(1, nx):
        plan += [[], [functools.partial(x_hop, h=h)]]
    plan[-1].append(functools.partial(z_hop, h=0))
    for h in range(1, nz):
        plan.append([functools.partial(z_hop, h=h)])
    plan[-1].append(send_f)
    plan += [[], [finish]]

    def tick(t, carry):
        for depth in [*range(6, len(plan)), 0, 3, 5]:
            if not plan[depth]:
                continue
            i = t - depth

            @pl.when((i >= 0) & (i < pieces))
            def _():
                for stage in plan[depth]:
                    stage(i)

        for n, step in enumerate(steps):
            pl.when(t == n)(step)
        return carry

    lax.fori_loop(0, pieces + len(plan) - 1, tick, 0)
    result_kept(pieces - 2)
    result_kept(pieces - 1)
    for layer in range(1, layers):
        attended_copy(layer, operands[layer * per + 1]).wait_send()


def reduce_weights(operands, held, gains, nx, nz, collective_id):
    layers = len(operands)
    flat = [a for layer in operands for a in layer]
    tokens, wide = held.shape
    rows, width = wide // (2 * nx * nz), wide // 2
    pieces = layers * PIECES
    ring = 2 * nx + nz + 2
    sides = 1 if nx == 2 else 2
    low = jnp.bfloat16
    dma = pltpu.SemaphoreType.DMA
    anywhere = pl.BlockSpec(memory_space=pl.ANY)
    return pl.pallas_call(
        functools.partial(reduce_kernel, nx, nz, layers),
        out_shape=[
            jax.ShapeDtypeStruct((layers, rows * below, wide * across), jnp.float32) for across, below in WEIGHT_BLOCKS
        ]
        + [jax.ShapeDtypeStruct(gains.shape, gains.dtype)],
        in_specs=[anywhere] * (len(flat) + 2),
        out_specs=[anywhere] * (len(WEIGHT_BLOCKS) + 1),
        scratch_shapes=[pltpu.VMEM((4, layers, nx, tokens, nz * n * rows), low) for n in LEFT_BLOCKS]
        + [
            pltpu.VMEM((4, layers * RIGHTS, tokens, wide), low),
            pltpu.VMEM((4, max(LEFT_BLOCKS), nx, nz, rows, tokens), low),
            pltpu.VMEM((ring, nx, nz, rows, width), low),
            pltpu.VMEM((SLOTS, sides, nx - 1, nz, rows, width), low),
            pltpu.VMEM((SLOTS, nz - 1, rows, width), low),
            pltpu.VMEM((SLOTS, nz - 1, rows, width), low),
            pltpu.VMEM((SLOTS, rows, width), low),
            pltpu.VMEM((2, 2, rows, width), jnp.float32),
            pltpu.VMEM((layers - 1, tokens, 2 * wide), low),
            pltpu.VMEM((7, *gains.shape), gains.dtype),
            pltpu.VMEM((3, *gains.shape), gains.dtype),
            pltpu.VMEM((3, *gains.shape), gains.dtype),
            dma((7, layers * 4, nx)),
            dma((7, layers * RIGHTS)),
            dma((4, pieces)),
            dma((2, pieces)),
            dma((2, pieces)),
            dma((2, pieces)),
            dma((2, 2)),
            dma((2, 7)),
            dma((2, layers)),
            pltpu.SemaphoreType.REGULAR((5,)),
        ],
        compiler_params=pltpu.CompilerParams(
            collective_id=collective_id, has_side_effects=True, vmem_limit_bytes=56 * 1024 * 1024
        ),
    )(held, *flat, gains)


def segment_of(doc_ends, token_index):
    return jnp.sum((token_index[:, None] >= doc_ends[None, :]).astype(jnp.int32), axis=1)


def doc_layout(doc_ends, token_index):
    token_segment = segment_of(doc_ends, token_index)
    starts = jnp.concatenate([jnp.zeros((1,), jnp.int32), doc_ends])
    labels = jnp.arange(starts.shape[0], dtype=jnp.int32)
    doc_begin = jnp.sum(
        jnp.where(token_segment[:, None] == labels[None, :], starts[None, :], 0), axis=1
    )
    return (token_segment, token_index - doc_begin)


def rotary(positions, head_width):
    middle = head_width // 2
    inv_rates = jnp.exp(
        jnp.arange(middle, dtype=jnp.float32) * jnp.float32(-2.0 * math.log(ROPE_BASE) / head_width)
    )
    angles = positions.astype(jnp.float32)[:, None] * inv_rates[None, :]
    cosine = jnp.cos(angles)
    sine = jnp.sin(angles)
    return (jnp.concatenate([cosine, cosine], axis=1), jnp.concatenate([-sine, sine], axis=1))


def rms_scale(values, gain_vec):
    return (
        values * lax.rsqrt(jnp.mean(values * values, axis=-1, keepdims=True) + NORM_EPS) * gain_vec
    )


def swiglu(gate_pre, upward):
    return jax.nn.silu(gate_pre) * upward


def product(left, right):
    return jnp.dot(left, right, preferred_element_type=jnp.float32)


def product_back(grad, right):
    return lax.dot_general(grad, right, (((1,), (1,)), ((), ())), preferred_element_type=jnp.float32)


def over_replica(values):
    return lax.ppermute(values, "rep", [(0, 1), (1, 0)])


def after(value, others):
    value, *others = lax.optimization_barrier((value, *others))
    return value, others


def layer_back(upstream, hidden, weights, gains, saved, tables, m, which_layer, waiting):
    (
        query_weight,
        key_matrix,
        value_matrix,
        output_weight,
        gate_weight,
        up_weight,
        down_weight,
    ) = weights
    gain_first, gain_second = gains[which_layer], gains[2 + which_layer]
    gain_query, gain_key = gains[4 + which_layer, :HEAD_SIZE], gains[6 + which_layer, :HEAD_SIZE]
    (
        lefts,
        attended_low,
        query_proj,
        key_projection,
        query_rows,
        keys_values,
        attended_rows,
        log_sum,
        hidden_mid,
        gate_pre,
        upward,
    ) = saved
    branch_low = upstream.astype(jnp.bfloat16)
    if which_layer == LAYERS - 1:
        waiting.append(over_replica(branch_low))
    grad_act = product_back(branch_low, down_weight)
    ignored, swiglu_back = jax.vjp(swiglu, gate_pre, upward)
    grad_gate_pre, grad_upward = swiglu_back(grad_act)
    gate_low = grad_gate_pre.astype(jnp.bfloat16)
    up_low = grad_upward.astype(jnp.bfloat16)
    grad_normed_two = product_back(gate_low, gate_weight) + product_back(up_low, up_weight)
    ignored, second_back = jax.vjp(rms_scale, hidden_mid, gain_second)
    grad_mid, grad_gain_second = second_back(grad_normed_two)
    upstream_mid = upstream + grad_mid
    attn_low = upstream_mid.astype(jnp.bfloat16)
    grad_attended = product_back(attn_low, output_weight).astype(jnp.bfloat16)
    if which_layer == 0:
        grad_attended, waiting[:1] = after(grad_attended, waiting[:1])
    query_low, key_low, value_low, head_gains = attend_back(
        m,
        query_rows,
        keys_values,
        grad_attended,
        attended_rows,
        log_sum,
        query_proj,
        key_projection,
        gain_query[None],
        gain_key[None],
        *tables,
        3,
    )
    grad_normed = product_back(query_low, query_weight)
    grad_normed = grad_normed + product_back(key_low, key_matrix)
    grad_normed = grad_normed + product_back(value_low, value_matrix)
    ignored, first_back = jax.vjp(rms_scale, hidden, gain_first)
    grad_hidden, grad_gain_first = first_back(grad_normed)
    rights = (branch_low, attn_low, gate_low, up_low, query_low, key_low, value_low)
    gain_grads = (grad_gain_first, head_gains[0], head_gains[1], grad_gain_second)
    return (upstream_mid + grad_hidden, ((lefts, attended_low), rights, gain_grads))


def near_rows(rows, share):
    return min(rows, -(-int(rows * share) // 16) * 16)


NEAR_SHARES = (0.75, 0.75, 0.75, 0.6, 0.5, 0.75, 0.55)
CUTS = (2, 1, 1, 2, 3, 3, 2)
ARRIVAL = [(weight, layer) for layer in range(LAYERS) for weight in (1, 2, 0, 3, 4, 5, 6)]


def run_forward(tokens, tables, weights, gains):
    nx, nz = lax.axis_size("shard") // 2, lax.axis_size("ctx")
    here = lax.axis_index("shard") * nz + lax.axis_index("ctx")
    block = jnp.zeros((16, D), jnp.bfloat16)
    for row, parts in ((0, gains[:2]), (4, gains[2:])):
        part = jnp.concatenate(parts)
        block = lax.dynamic_update_slice(block, part, (row, here * part.shape[1]))
    chunks = [(-1, 0, 0, D, 16, 16)]
    for weight, layer in ARRIVAL:
        rows, columns = weights[weight].shape[1:]
        near = near_rows(rows, NEAR_SHARES[weight])
        width = columns // CUTS[weight]
        for n in range(CUTS[weight]):
            chunks.append((weight, layer, n * width, width, rows, near))
    wholes, outs, saved = forward(block, weights, tokens, tables, tuple(chunks), nx, nz, 0)
    gathered = [[wholes[weight, layer] for weight in range(7)] for layer in range(LAYERS)]
    return gathered, outs, saved


def weight_gradients(operands, held):
    nx, nz = lax.axis_size("shard") // 2, lax.axis_size("ctx")
    shards = 2 * nx * nz
    flat = jnp.concatenate([g for _, gains in operands for g in gains])
    size = -(-flat.shape[0] // 1024) * 1024
    padded = jnp.zeros((size,), flat.dtype).at[: flat.shape[0]].set(flat).reshape(-1, 128)
    *grads, summed = reduce_weights([members for members, _ in operands[::-1]], held, padded, nx, nz, 1)
    summed = summed.reshape(-1)[: flat.shape[0]].reshape(LAYERS, -1)
    here = lax.axis_index("shard") * nz + lax.axis_index("ctx")
    small, used = [], 0
    for size in (D, HEAD_SIZE, HEAD_SIZE, D):
        own = size // shards
        small.append(lax.dynamic_slice_in_dim(summed, used + here * own, own, axis=1))
        used += size
    down, output, gate, up, query, key, value = grads
    return (small[0], query, key, value, small[1], small[2], output, small[3], gate, up, down)


def local(
    tokens,
    lengths,
    norm_one,
    w_query,
    w_key,
    w_value,
    query_gain,
    key_gain,
    w_output,
    norm_two,
    w_gate,
    w_up,
    w_down,
    cotangent,
):
    token_rows = tokens.shape[1]
    nx, nz = lax.axis_size("shard") // 2, lax.axis_size("ctx")
    m = nz // 2
    pairs = []
    for x in range(nx):
        for z in range(m):
            low, high = (2 * x + 1) * nz + z, 2 * x * nz + z + m
            same = (2 * x * nz + z, (2 * x + 1) * nz + z + m)
            pairs += [(low, high), (high, low)] + [(s, s) for s in same]

    def swap(values):
        return lax.ppermute(values, ("shard", "ctx"), pairs)

    lengths = swap(lengths)
    block = lax.axis_index("ctx") % m + (lax.axis_index("shard") % 2) * m
    token_index = block * token_rows + jnp.arange(token_rows, dtype=jnp.int32)
    doc_lengths = lengths[0]
    upto = jnp.arange(doc_lengths.shape[0])
    doc_ends = jnp.sum(jnp.where(upto[:, None] >= upto[None, :], doc_lengths[None, :], 0), axis=1)
    token_segment, positions = doc_layout(doc_ends, token_index)
    cosine, sine = rotary(positions, HEAD_SIZE)
    key_segment = segment_of(doc_ends, jnp.arange(token_rows * nz, dtype=jnp.int32))
    tables = (cosine, sine, jnp.stack([token_segment, token_index], axis=1), key_segment[None, :])
    gathered, (gains, tokens, hidden, last), saved = run_forward(
        tokens[0],
        tables,
        (w_query, w_key, w_value, w_output, w_gate, w_up, w_down),
        (norm_one, norm_two, query_gain, key_gain),
    )
    cotangent = swap(cotangent)
    output = swap(last)[None]
    hiddens = (tokens.astype(jnp.float32), hidden)
    waiting = [over_replica(lefts) for lefts, *_ in saved]
    their_attended = over_replica(saved[LAYERS - 1][1])
    live_mask = (token_segment < doc_lengths.shape[0]).astype(jnp.float32)
    upstream = cotangent[0].astype(jnp.float32) * live_mask[:, None]
    operands = [None] * LAYERS
    for which_layer in reversed(range(LAYERS)):
        upstream, operands[which_layer] = layer_back(
            upstream,
            hiddens[which_layer],
            gathered[which_layer],
            gains,
            saved[which_layer],
            tables,
            m,
            which_layer,
            waiting,
        )
    grad_tokens = swap(upstream.astype(jnp.bfloat16))[None]
    for which_layer, (lefts, rights, layer_gains) in enumerate(operands):
        operands[which_layer] = (lefts + (waiting[which_layer], their_attended) + rights, layer_gains)
    return (output, grad_tokens) + weight_gradients(operands, waiting[-1])


def solution(mesh):
    return jax.shard_map(
        local,
        mesh=mesh,
        in_specs=(
            P(("rep", "shard"), "ctx", None),
            P(("rep", "shard"), None),
            P(None, ("shard", "ctx")),
            P(None, ("shard", "ctx"), None),
            P(None, ("shard", "ctx"), None),
            P(None, ("shard", "ctx"), None),
            P(None, ("shard", "ctx")),
            P(None, ("shard", "ctx")),
            P(None, ("shard", "ctx"), None),
            P(None, ("shard", "ctx")),
            P(None, ("shard", "ctx"), None),
            P(None, ("shard", "ctx"), None),
            P(None, ("shard", "ctx"), None),
            P(("rep", "shard"), "ctx", None),
        ),
        out_specs=(
            P(("rep", "shard"), "ctx", None),
            P(("rep", "shard"), "ctx", None),
            P(None, ("shard", "ctx")),
            P(None, ("shard", "ctx"), None),
            P(None, ("shard", "ctx"), None),
            P(None, ("shard", "ctx"), None),
            P(None, ("shard", "ctx")),
            P(None, ("shard", "ctx")),
            P(None, ("shard", "ctx"), None),
            P(None, ("shard", "ctx")),
            P(None, ("shard", "ctx"), None),
            P(None, ("shard", "ctx"), None),
            P(None, ("shard", "ctx"), None),
        ),
        check_vma=False,
    )
```
